32 devices in a mesh: section: 2 (over x), dp: 16 (over z, y, core).
Axes of the slice: x: 2, y: 2, z: 4, core: 2. Of those that a mesh axis runs over, the one named last changes fastest.
Arguments:
- tokens: bfloat16 [8192, 1024], P('dp'), may hold values from -6 to 6
- segment_ids: int32 [32, 256], P('dp'), may hold values from 0 to 3, never falling along the last dimension, each value on 1 to 128 neighbouring positions
- cotangent: bfloat16 [8192, 1024], P('dp'), may hold values from -6 to 6
- w_qkv: bfloat16 [2, 1024, 3072], P('section', 'dp'), may hold values from -0.1875 to 0.1875
- w_attn_out: bfloat16 [2, 1024, 1024], P('section', 'dp'), may hold values from -0.75 to 0.75
- w_fc: bfloat16 [2, 1024, 4096], P('section', 'dp'), may hold values from -0.1875 to 0.1875
- w_proj: bfloat16 [2, 4096, 1024], P('section', 'dp'), may hold values from -0.09375 to 0.09375
- gains: bfloat16 [2, 2, 1024], P('section', None, 'dp'), may hold values from 0.5 to 1.5
- biases: bfloat16 [2, 11264], P('section', 'dp'), may hold values from -1.1953125 to 1.1953125
- prefix_embed: bfloat16 [10, 1024], replicated, may hold values from -6 to 6
- reparam_in: bfloat16 [1024, 512], replicated, may hold values from -0.1875 to 0.1875
- reparam_in_bias: bfloat16 [512], replicated, may hold values from -3 to 3
- reparam_out: bfloat16 [512, 4096], P(None, 'section'), may hold values from -0.25 to 0.25
- reparam_out_bias: bfloat16 [4096], P('section'), may hold values from -3 to 3
Outputs:
- layer_outs: bfloat16 [2, 8192, 1024], P('section', 'dp')
- input_grads: bfloat16 [2, 8192, 1024], P('section', 'dp')
- grad_w_qkv: float32 [2, 1024, 3072], P('section', 'dp')
- grad_w_attn_out: float32 [2, 1024, 1024], P('section', 'dp')
- grad_w_fc: float32 [2, 1024, 4096], P('section', 'dp')
- grad_w_proj: float32 [2, 4096, 1024], P('section', 'dp')
- grad_gains: float32 [2, 2, 1024], P('section', None, 'dp')
- grad_biases: float32 [2, 11264], P('section', 'dp')
- grad_prefix_embed: float32 [10, 1024], replicated
- grad_reparam_in: float32 [1024, 512], replicated
- grad_reparam_in_bias: float32 [512], replicated
- grad_reparam_out: float32 [512, 4096], P(None, 'section')
- grad_reparam_out_bias: float32 [4096], P('section')
The draws below stay inside these ranges and needn't reach their ends.
Inputs may be any that keep to these rules, and one draw needn't show every extreme that they name: `segment_ids`: within each packed row the ids never fall, every id appears, each segment has 1 to 128 tokens and one has exactly 128.
All inputs are finite; a program needn't handle non-finite values.
Results may differ from the reference program's by a relative error of at most 0.019.
Values may be sent and summed in bfloat16 or wider, within the bound.
A program may use at most 320 MiB of HBM per device.

```python
import math
import jax
import jax.numpy as jnp
import numpy as np
from jax import lax

D = 1024
HEADS = 16
HEAD_DIM = 64
FF = 4096
PREFIX = 10
RW = 512
SEGMENTS = 4
ROW_LEN = 256
ROWS = 32
TOKENS = 8192


def block_levels(rng, shape, cuts, least, high):
    level, own = 1.0, jax.random.fold_in(rng, 6)
    for dim, blocks in cuts:
        steps = jnp.exp(jax.random.uniform(jax.random.fold_in(own, dim), (blocks,), jnp.float32, least / len(cuts), high / len(cuts)))
        level = level * jnp.repeat(steps, shape[dim] // blocks).reshape([-1 if axis == dim else 1 for axis in range(len(shape))])
    return level


def length_profile(count, total, reach, lean):
    portions = [(1 << 20) // math.isqrt(grade ** lean) + 1 for grade in range(2, count + 1)]
    rest, counts = total - reach - (count - 1), [1] * (count - 1)
    while rest > 0:
        free = [i for i in range(count - 1) if counts[i] < reach]
        pool, left = sum([portions[i] for i in free]), rest
        for i in free:
            more = min(reach - counts[i], max(1, left * portions[i] // pool), rest)
            counts[i] = counts[i] + more
            rest = rest - more
    return np.array([reach] + counts)


def ragged(rng, amount, total, reach, slope):
    if amount == 2:
        one = jax.random.randint(rng, (), max(1, total - reach), min(reach, total - 1) + 1)
        return jnp.stack([one, total - one])
    tallies = jnp.asarray(length_profile(amount, total, reach, slope), jnp.int32)
    pairs = (amount - 1) // 2
    donor, receiver = tallies[1:1 + 2 * pairs:2], tallies[2:2 + 2 * pairs:2]
    margin = jnp.minimum(donor - 1, reach - receiver)
    moved = jax.random.randint(jax.random.fold_in(rng, 1), (pairs,), 0, 1 << 20) % (margin + 1)
    tallies = tallies.at[1:1 + 2 * pairs:2].set(donor - moved).at[2:2 + 2 * pairs:2].set(receiver + moved)
    return tallies[jax.random.permutation(jax.random.fold_in(rng, 2), amount)]


def noise(key, extent, width, limit, cuts=(), kind=jnp.bfloat16):
    level = block_levels(key, extent, cuts, -0.22, 0.18) if cuts else 1.0
    values = jax.random.normal(key, extent, jnp.float32) * width * level
    return jnp.minimum(jnp.maximum(values, -limit), limit).astype(kind)


def setup_inputs(seed: int = 0) -> dict:
    key_list = jax.random.split(jax.random.key(seed), 15)
    return {
        "tokens": noise(key_list[0], (TOKENS, D), 1.0, 6.0, ((0, 16),)),
        "segment_ids": jax.vmap(lambda own: jnp.searchsorted(jnp.cumsum(ragged(own, SEGMENTS, ROW_LEN, ROW_LEN // 2, 0)), jnp.arange(ROW_LEN), side="right"))(jax.random.split(key_list[1], ROWS)).reshape((ROWS, ROW_LEN)).astype(jnp.int32),
        "cotangent": noise(key_list[2], (TOKENS, D), 1.0, 6.0, ((0, 16),)),
        "w_qkv": noise(key_list[3], (2, D, 3 * D), D ** -0.5, 0.1875, ((0, 2), (1, 16))),
        "w_attn_out": noise(key_list[4], (2, D, D), (D // 16) ** -0.5, 0.75, ((0, 2), (1, 16))),
        "w_fc": noise(key_list[5], (2, D, FF), D ** -0.5, 0.1875, ((0, 2), (1, 16))),
        "w_proj": noise(key_list[6], (2, FF, D), FF ** -0.5, 0.09375, ((0, 2), (1, 16))),
        "gains": jnp.clip(1.0 + 0.1 * jax.random.normal(key_list[7], (2, 2, D), jnp.float32), 0.5, 1.5).astype(jnp.bfloat16),
        "biases": noise(key_list[8], (2, 11 * D), 0.2, 1.1953125, ((0, 2), (1, 16))),
        "prefix_embed": noise(key_list[9], (PREFIX, D), 1.0, 6.0),
        "reparam_in": noise(key_list[10], (D, RW), D ** -0.5, 0.1875),
        "reparam_in_bias": noise(key_list[11], (RW,), 0.5, 3.0),
        "reparam_out": noise(key_list[12], (RW, 4 * D), RW ** -0.5, 0.25, ((1, 2),)),
        "reparam_out_bias": noise(key_list[13], (4 * D,), 0.5, 3.0, ((0, 2),)),
    }


@jax.custom_vjp
def low(v):
    return lax.optimization_barrier(v.astype(jnp.bfloat16)).astype(jnp.float32)

@jax.custom_vjp
def low_back(v):
    return v

def low_keep(v):
    return (low(v), None)

def low_pass(kept, grad):
    return (grad,)

def back_keep(v):
    return (v, None)

def back_low(kept, grad):
    return (low(grad),)
low.defvjp(low_keep, low_pass)
low_back.defvjp(back_keep, back_low)
HIGH = lax.Precision.HIGHEST
EPS = 1e-05
NEG = -1000000000.0

def norm_rows(v, gain, shift):
    mean = lax.optimization_barrier(jnp.mean(v, axis=-1, keepdims=True))
    cent = v - mean
    var = lax.optimization_barrier(jnp.mean(cent * cent, axis=-1, keepdims=True))
    return cent * lax.rsqrt(var + EPS) * gain + shift

def attend_row(query, keys, values, pkey, pval, segs):
    scale = 1.0 / math.sqrt(HEAD_DIM)
    s_tok = low_back(jnp.einsum('lhe,mhe->hlm', query, keys, precision=HIGH) * scale)
    s_pre = low_back(jnp.einsum('lhe,phe->hlp', query, pkey, precision=HIGH) * scale)
    place = jnp.arange(segs.shape[0])
    allowed = (segs[:, None] == segs[None, :]) & (place[None, :] <= place[:, None])
    s_tok = jnp.where(allowed[None], s_tok, NEG)
    top = jnp.maximum(lax.optimization_barrier(jnp.max(s_tok, axis=-1, keepdims=True)), lax.optimization_barrier(jnp.max(s_pre, axis=-1, keepdims=True)))
    e_tok = jnp.exp(s_tok - top)
    e_pre = jnp.exp(s_pre - top)
    total = lax.optimization_barrier(jnp.sum(e_tok, axis=-1, keepdims=True)) + lax.optimization_barrier(jnp.sum(e_pre, axis=-1, keepdims=True))
    p_tok = low(e_tok / total)
    p_pre = low(e_pre / total)
    return jnp.einsum('hlm,mhe->lhe', p_tok, values, precision=HIGH) + jnp.einsum('hlp,phe->lhe', p_pre, pval, precision=HIGH)

def layer(h, segs, pkey, pval, w_q, w_o, w_f, w_p, gain_pair, bias_all):
    rows, length = segs.shape
    a1 = low(norm_rows(h, gain_pair[0], bias_all[9 * D:10 * D]))
    qkv = low_back(low(jnp.einsum('rld,dc->rlc', a1, w_q, precision=HIGH) + bias_all[:3 * D]))
    split = qkv.reshape(rows, length, 3, HEADS, HEAD_DIM)
    mixed = jax.vmap(attend_row, in_axes=(0, 0, 0, None, None, 0))(split[:, :, 0], split[:, :, 1], split[:, :, 2], pkey, pval, segs)
    mixed = low_back(low(mixed.reshape(rows, length, D)))
    branch = low_back(jnp.einsum('rld,de->rle', mixed, w_o, precision=HIGH) + bias_all[3 * D:4 * D])
    resid = h + branch
    a2 = low(norm_rows(resid, gain_pair[1], bias_all[10 * D:11 * D]))
    pre_act = low_back(jnp.einsum('rld,df->rlf', a2, w_f, precision=HIGH) + bias_all[4 * D:8 * D])
    act = low(jax.nn.gelu(pre_act, approximate=True))
    second = low_back(jnp.einsum('rlf,fd->rld', act, w_p, precision=HIGH) + bias_all[8 * D:9 * D])
    return resid + second

def reference(tokens, segment_ids, cotangent, w_qkv, w_attn_out, w_fc, w_proj, gains, biases, prefix_embed, reparam_in, reparam_in_bias, reparam_out, reparam_out_bias):
    block = math.gcd(ROWS, max(1, 4096 // ROW_LEN))
    blocks = ROWS // block
    segs_blocks = segment_ids.reshape(blocks, block, ROW_LEN)

    def forward(tok, w_q, w_o, w_f, w_p, gain_all, bias_all, embed, w_in, b_in, w_out, b_out, probe):
        hidden = low(jnp.tanh(low_back(jnp.dot(embed, w_in, precision=HIGH) + b_in)))
        prefix_kv = low_back(low(jnp.dot(hidden, w_out, precision=HIGH) + b_out))
        prefix_kv = prefix_kv.reshape(PREFIX, 2, 2, HEADS, HEAD_DIM)

        def block_fn(carry, item):
            tok_block, probe_block, seg_block = item
            first = layer(tok_block, seg_block, prefix_kv[:, 0, 0], prefix_kv[:, 0, 1], w_q[0], w_o[0], w_f[0], w_p[0], gain_all[0], bias_all[0])
            first = low_back(low(first) + probe_block)
            second = layer(first, seg_block, prefix_kv[:, 1, 0], prefix_kv[:, 1, 1], w_q[1], w_o[1], w_f[1], w_p[1], gain_all[1], bias_all[1])
            return (carry, (first, second))
        items = (tok.reshape(blocks, block, ROW_LEN, D), probe.reshape(blocks, block, ROW_LEN, D), segs_blocks)
        _, (firsts, seconds) = lax.scan(jax.checkpoint(block_fn), None, items)
        return (seconds.reshape(TOKENS, D), firsts.reshape(TOKENS, D))
    f32 = jnp.float32
    inputs = (tokens.astype(f32), w_qkv.astype(f32), w_attn_out.astype(f32), w_fc.astype(f32), w_proj.astype(f32), gains.astype(f32), biases.astype(f32), prefix_embed.astype(f32), reparam_in.astype(f32), reparam_in_bias.astype(f32), reparam_out.astype(f32), reparam_out_bias.astype(f32), jnp.zeros((TOKENS, D), f32))
    second, back_fn, first = jax.vjp(forward, *inputs, has_aux=True)
    grads = back_fn(cotangent.astype(f32))
    layer_outs = jnp.stack([first.astype(jnp.bfloat16), second.astype(jnp.bfloat16)])
    input_grads = jnp.stack([grads[0].astype(jnp.bfloat16), grads[12].astype(jnp.bfloat16)])
    return (layer_outs, input_grads, grads[1], grads[2], grads[3], grads[4], grads[5], grads[6], grads[7], grads[8], grads[9], grads[10], grads[11])
```

```python
import math

import jax
import jax.numpy as jnp
from jax import lax
from jax.experimental import pallas as pl
from jax.experimental.pallas import tpu as pltpu
from jax.sharding import PartitionSpec as P

HEADS = 16
MESH = pl.DeviceIdType.MESH

NP = 12

def place():
    s = lax.axis_index("section"); d = lax.axis_index("dp")
    return s, d, d // 4, (d // 2) % 2, d % 2

def greet(s, z, y, c, cross=False):
    bar = pltpu.get_barrier_semaphore()
    def hello(dev):
        pl.semaphore_signal(bar, 1, device_id=dev, device_id_type=MESH)
    hello((s, z*4+y*2+(1-c)))
    hello((s, z*4+(1-y)*2+c))
    if cross: hello((1-s, z*4+y*2+c))
    @pl.when(z > 0)
    def _(): hello((s, (z-1)*4+y*2+c))
    @pl.when(z < 3)
    def _(): hello((s, (z+1)*4+y*2+c))
    pl.semaphore_wait(bar, 3 + (1 if cross else 0) + ((z + 1) // 2) % 2)

class Gather:
    def __init__(self, W, ssem, rsem):
        self.W, self.ssem, self.rsem = W, ssem, rsem
        self.s, self.d, self.z, self.y, self.c = place()
    def blk(self, k, d):
        i = k // 8
        row = (1-i)*(1024*k+64*d) + i*(8192+256*d+64*(k-8))
        return self.W.at[pl.ds(pl.multiple_of(row, 64), 64)]
    def cp(self, k, origin, target, slot):
        b = self.blk(k, origin)
        return pltpu.make_async_remote_copy(src_ref=b, dst_ref=b, send_sem=self.ssem.at[k, slot], recv_sem=self.rsem.at[k, origin],
            device_id=(self.s, target), device_id_type=MESH)
    def dev(self, z, y, c): return z*4+y*2+c
    def arrived(self, k, origin): self.cp(k, origin, origin, 0).wait_recv()
    def to_up(self, k, zo, op):
        op(self.cp(k, self.dev(zo, self.y, self.c), self.dev(self.z+1, self.y, self.c), zo))
    def to_down(self, k, zo, op):
        op(self.cp(k, self.dev(zo, self.y, self.c), self.dev(self.z-1, self.y, self.c), 4+zo))
    def to_y(self, k, zo, op):
        op(self.cp(k, self.dev(zo, self.y, self.c), self.dev(self.z, 1-self.y, self.c), 8+zo))
    def to_c(self, k, zo, yo, op):
        op(self.cp(k, self.dev(zo, yo, self.c), self.dev(self.z, self.y, 1-self.c), 12+zo*2+yo))
    def step(self, t, own):
        z, y, c = self.z, self.y, self.c
        start = lambda cp: cp.start()
        @pl.when(t < NP)
        def _():
            own(t)
            self.to_y(t, z, start)
            @pl.when(z < 3)
            def _(): self.to_up(t, z, start)
            @pl.when(z > 0)
            def _(): self.to_down(t, z, start)
            self.to_c(t, z, y, start)
        for q in (1, 2, 3, 4):
            k = t - q
            ok = (k >= 0) & (k < NP)
            if q < 4:
                @pl.when(ok & (z - q >= 0))
                def _():
                    self.arrived(k, self.dev(z-q, y, c))
                    @pl.when(z < 3)
                    def _(): self.to_up(k, z-q, start)
                    self.to_y(k, z-q, start)
                    self.to_c(k, z-q, y, start)
                @pl.when(ok & (z + q <= 3))
                def _():
                    self.arrived(k, self.dev(z+q, y, c))
                    @pl.when(z > 0)
                    def _(): self.to_down(k, z+q, start)
                    self.to_y(k, z+q, start)
                    self.to_c(k, z+q, y, start)
            e = q - 1
            def side(zo):
                self.arrived(k, self.dev(zo, 1-y, c))
                self.to_c(k, zo, 1-y, start)
            if e == 0:
                @pl.when(ok)
                def _(): side(z)
            else:
                @pl.when(ok & (z - e >= 0))
                def _(): side(z-e)
                @pl.when(ok & (z + e <= 3))
                def _(): side(z+e)
    def complete(self, k):
        for i in range(8):
            self.arrived(k, 2*i + 1-self.c)
    def drain(self):
        fin = lambda cp: cp.wait_send()
        z, y = self.z, self.y
        @pl.loop(0, NP)
        def _(k):
            for zo in range(4):
                @pl.when((zo <= z) & (z < 3))
                def _(): self.to_up(k, zo, fin)
                @pl.when((zo >= z) & (z > 0))
                def _(): self.to_down(k, zo, fin)
                self.to_y(k, zo, fin)
                for yo in range(2): self.to_c(k, zo, yo, fin)

def own_copies(wq, wo, wf, wp, g, sem):
    out = []
    for k in range(NP):
        if k < 3: src = wq.at[0, :, pl.ds(1024*k, 1024)]
        elif k == 3: src = wo.at[0]
        elif k < 8: src = wf.at[0, :, pl.ds(1024*(k-4), 1024)]
        else: src = wp.at[0, pl.ds(64*(k-8), 64)]
        out.append(pltpu.make_async_copy(src, g.blk(jnp.int32(k), g.d), sem.at[k]))
    return out

def ag_kernel(wq, wo, wf, wp, W, own_sem, ssem, rsem):
    g = Gather(W, ssem, rsem)
    for cp in own_copies(wq, wo, wf, wp, g, own_sem): cp.start()
    greet(g.s, g.z, g.y, g.c)
    def own(t):
        b = g.blk(t, g.d)
        pltpu.make_async_copy(b, b, own_sem.at[t]).wait()
    @pl.loop(0, NP + 6)
    def _(t):
        g.step(t, own)
        @pl.when(t >= 6)
        def _(): g.complete(t - 6)
    g.drain()

def all_gather_weights(wq, wo, wf, wp):
    any_ = pl.BlockSpec(memory_space=pl.ANY)
    return pl.pallas_call(ag_kernel, out_shape=jax.ShapeDtypeStruct((NP*1024, 1024), jnp.bfloat16), in_specs=[any_]*4, out_specs=any_,
        scratch_shapes=[pltpu.SemaphoreType.DMA((NP,)), pltpu.SemaphoreType.DMA((NP, 20)), pltpu.SemaphoreType.DMA((NP, 16))],
        compiler_params=pltpu.CompilerParams(collective_id=0, has_side_effects=True))(wq, wo, wf, wp)

def rs_kernel(G, oq, oo, of, op_, V, RC, RY, RU, RD, T, lsem, osem, cs, cr, ys, yr, us, ur, ds_, dr):
    s, d, z, y, c = place()
    loads = [pltpu.make_async_copy(G.at[k], V.at[k], lsem.at[k]) for k in range(NP)]
    for cp in loads: cp.start()
    greet(s, z, y, c)
    F = jnp.float32
    def C(k): return pltpu.make_async_remote_copy(V.at[k, :, 1-c], RC.at[k], cs.at[k], cr.at[k], device_id=(s, z*4+y*2+1-c), device_id_type=MESH)
    def Y(k): return pltpu.make_async_remote_copy(V.at[k, pl.ds(4*(1-y), 4), c], RY.at[k], ys.at[k], yr.at[k], device_id=(s, z*4+(1-y)*2+c), device_id_type=MESH)
    def U(k, n, zz):
        return pltpu.make_async_remote_copy(V.at[k, pl.ds(4*y+zz+1, n), c], RU.at[k, pl.ds(zz, n)], us.at[k], ur.at[k], device_id=(s, (z+1)*4+y*2+c), device_id_type=MESH)
    def D(k, n):
        return pltpu.make_async_remote_copy(V.at[k, pl.ds(4*y, n), c], RD.at[k, pl.ds(0, n)], ds_.at[k], dr.at[k], device_id=(s, (z-1)*4+y*2+c), device_id_type=MESH)
    def addc(k):
        @pl.loop(0, 8)
        def _(i): V[k, i, c] = (V[k, i, c].astype(F) + RC[k, i].astype(F)).astype(jnp.bfloat16)
    def addy(k):
        @pl.loop(0, 4)
        def _(i): V[k, 4*y+i, c] = (V[k, 4*y+i, c].astype(F) + RY[k, i].astype(F)).astype(jnp.bfloat16)
    def out_cp(k):
        def q(): return pltpu.make_async_copy(T.at[k], oq.at[0, :, pl.ds(pl.multiple_of(1024*k, 1024), 1024)], osem.at[k])
        def o(): return pltpu.make_async_copy(T.at[k], oo.at[0], osem.at[k])
        def f(): return pltpu.make_async_copy(T.at[k], of.at[0, :, pl.ds(pl.multiple_of(1024*(k-4), 1024), 1024)], osem.at[k])
        def p(): return pltpu.make_async_copy(T.at[k], op_.at[0, pl.ds(pl.multiple_of(64*(k-8), 64), 64)], osem.at[k])
        return q, o, f, p
    def each_out(k, act):
        q, o, f, p = out_cp(k)
        @pl.when(k < 3)
        def _(): act(q())
        @pl.when(k == 3)
        def _(): act(o())
        @pl.when((k > 3) & (k < 8))
        def _(): act(f())
        @pl.when(k >= 8)
        def _(): act(p())
    @pl.loop(0, NP + 6)
    def _(t):
        @pl.when(t < NP)
        def _():
            k = NP - 1 - t
            pltpu.make_async_copy(G.at[k], V.at[k], lsem.at[k]).wait()
            C(k).start()
        @pl.when((t >= 1) & (t - 1 < NP))
        def _():
            k = NP - t
            C(k).wait_recv(); addc(k); Y(k).start()
        @pl.when((t >= 2) & (t - 2 < NP))
        def _():
            k = NP + 1 - t
            Y(k).wait_recv(); addy(k)
            @pl.when(z == 0)
            def _(): U(k, 3, 0).start()
            @pl.when(z == 3)
            def _(): D(k, 3).start()
        for q in (1, 2, 3):
            @pl.when((t >= 2 + q) & (t - 2 - q < NP))
            def _():
                k = NP + 1 + q - t
                @pl.when(z == q)
                def _():
                    n = 4 - q
                    U(k, n, q - 1).wait_recv()
                    for i in range(1, n):
                        V[k, 4*y+q+i, c] = (V[k, 4*y+q+i, c].astype(F) + RU[k, q-1+i].astype(F)).astype(jnp.bfloat16)
                    if n > 1: U(k, n-1, q).start()
                @pl.when(z == 3 - q)
                def _():
                    n = 4 - q
                    D(k, n).wait_recv()
                    for i in range(0, n-1):
                        V[k, 4*y+i, c] = (V[k, 4*y+i, c].astype(F) + RD[k, i].astype(F)).astype(jnp.bfloat16)
                    if n > 1: D(k, n-1).start()
        @pl.when(t >= 6)
        def _(): pass
        @pl.when((t >= 5) & (t - 5 < NP))
        def _():
            k = NP + 4 - t
            T[k] = V[k, 4*y+z, c].astype(F)
            @pl.when(z > 0)
            def _(): T[k] += RU[k, z-1].astype(F)
            @pl.when(z < 3)
            def _(): T[k] += RD[k, z].astype(F)
            each_out(k, lambda cp: cp.start())
    @pl.loop(0, NP)
    def _(k):
        each_out(k, lambda cp: cp.wait())
        C(k).wait_send(); Y(k).wait_send()
        for q in range(3):
            @pl.when(z == q)
            def _(): U(k, 3-q, q).wait_send()
            @pl.when(z == q + 1)
            def _(): D(k, q+1).wait_send()

def reduce_scatter_grads(G):
    any_ = pl.BlockSpec(memory_space=pl.ANY)
    B = jnp.bfloat16; Dm = pltpu.SemaphoreType.DMA
    return pl.pallas_call(rs_kernel, out_shape=[jax.ShapeDtypeStruct(sh, jnp.float32) for sh in ((1,64,3072),(1,64,1024),(1,64,4096),(1,256,1024))],
        in_specs=[any_], out_specs=[any_]*4,
        scratch_shapes=[pltpu.VMEM((NP,8,2,64,1024),B), pltpu.VMEM((NP,8,64,1024),B), pltpu.VMEM((NP,4,64,1024),B), pltpu.VMEM((NP,3,64,1024),B), pltpu.VMEM((NP,3,64,1024),B),
          pltpu.VMEM((NP,64,1024),jnp.float32)] + [Dm((NP,))]*10,
        compiler_params=pltpu.CompilerParams(collective_id=1, has_side_effects=True, vmem_limit_bytes=62<<20))(G)


def gather_params(w_qkv, w_attn_out, w_fc, w_proj, gains, biases, fused):
    small = (
        lax.all_gather(gains, "dp", axis=2, tiled=True)[0],
        lax.all_gather(biases, "dp", axis=1, tiled=True)[0],
    )
    if not fused:
        return tuple(
            lax.all_gather(w, "dp", axis=1, tiled=True)[0] for w in (w_qkv, w_attn_out, w_fc, w_proj)
        ) + small
    W = all_gather_weights(w_qkv, w_attn_out, w_fc, w_proj)
    part = [W[1024 * k : 1024 * (k + 1)] for k in range(8)]
    return (
        jnp.concatenate(part[:3], axis=1),
        part[3],
        jnp.concatenate(part[4:], axis=1),
        W[8192:],
    ) + small


def scatter_grads(grads, fused):
    gq, go, gf, gp, gg, gb = grads
    small = (
        lax.psum_scatter(gg[None], "dp", scatter_dimension=2, tiled=True),
        lax.psum_scatter(gb[None], "dp", scatter_dimension=1, tiled=True),
    )
    if not fused:
        return tuple(
            lax.psum_scatter(g[None], "dp", scatter_dimension=1, tiled=True) for g in (gq, go, gf, gp)
        ) + small

    def cut(block):
        block = block.astype(jnp.bfloat16).reshape(4, 2, 2, 64, 1024)
        return block.transpose(1, 0, 2, 3, 4).reshape(8, 2, 64, 1024)

    pieces = [cut(gq[:, 1024 * k : 1024 * (k + 1)]) for k in range(3)] + [cut(go)]
    pieces += [cut(gf[:, 1024 * k : 1024 * (k + 1)]) for k in range(4)]
    rows = gp.reshape(16, 4, 64, 1024)
    pieces += [cut(rows[:, j].reshape(1024, 1024)) for j in range(4)]
    return tuple(reduce_scatter_grads(jnp.stack(pieces))) + small


EPS = 1e-05
NEG = -1000000000.0


def passed_along(shard, axis, by):
    size = lax.axis_size(axis)
    pairs = [(i, i + by) for i in range(size) if 0 <= i + by < size]
    return lax.ppermute(shard, axis, pairs)


def norm_rows(v, gain, shift):
    mean = jnp.mean(v, axis=-1, keepdims=True)
    cent = v - mean
    var = jnp.mean(cent * cent, axis=-1, keepdims=True)
    return cent * lax.rsqrt(var + EPS) * gain + shift


def gelu_tanh(v):
    return jax.nn.gelu(v, approximate=True)


def forward_layer(h_b, segs, pkey, pval, params):
    w_q, w_o, w_f, w_p, gain_pair, bias_all = params
    width = w_o.shape[0]
    length = h_b.shape[0]
    heads, head_dim = (pkey.shape[1], pkey.shape[2])
    scale = 1.0 / math.sqrt(head_dim)
    gain_f = gain_pair.astype(jnp.float32)
    bias_f = bias_all.astype(jnp.float32)
    hf = h_b.astype(jnp.float32)
    a1b = norm_rows(hf, gain_f[0], bias_f[9 * width : 10 * width]).astype(jnp.bfloat16)
    qkv_b = (jnp.dot(a1b, w_q, preferred_element_type=jnp.float32) + bias_f[: 3 * width]).astype(
        jnp.bfloat16
    )
    split = qkv_b.reshape(length, 3, heads, head_dim)
    query, keys, values = (split[:, 0], split[:, 1], split[:, 2])
    s_tok = jnp.einsum("lhe,mhe->hlm", query, keys, preferred_element_type=jnp.float32) * scale
    s_pre = jnp.einsum("lhe,phe->hlp", query, pkey, preferred_element_type=jnp.float32) * scale
    place = jnp.arange(length)
    allowed = (segs[:, None] == segs[None, :]) & (place[None, :] <= place[:, None])
    s_tok = jnp.where(allowed[None], s_tok, NEG)
    top = jnp.maximum(
        jnp.max(s_tok, axis=-1, keepdims=True), jnp.max(s_pre, axis=-1, keepdims=True)
    )
    e_tok = jnp.exp(s_tok - top)
    e_pre = jnp.exp(s_pre - top)
    total = jnp.sum(e_tok, axis=-1, keepdims=True) + jnp.sum(e_pre, axis=-1, keepdims=True)
    p_tok = e_tok / total
    p_pre = e_pre / total
    mixed = jnp.einsum(
        "hlm,mhe->lhe", p_tok.astype(jnp.bfloat16), values, preferred_element_type=jnp.float32
    ) + jnp.einsum(
        "hlp,phe->lhe", p_pre.astype(jnp.bfloat16), pval, preferred_element_type=jnp.float32
    )
    attn_b = mixed.reshape(length, width).astype(jnp.bfloat16)
    resid = hf + (
        jnp.dot(attn_b, w_o, preferred_element_type=jnp.float32) + bias_f[3 * width : 4 * width]
    )
    a2b = norm_rows(resid, gain_f[1], bias_f[10 * width : 11 * width]).astype(jnp.bfloat16)
    pre_act = jnp.dot(a2b, w_f, preferred_element_type=jnp.float32) + bias_f[4 * width : 8 * width]
    act_b = gelu_tanh(pre_act).astype(jnp.bfloat16)
    result = resid + (
        jnp.dot(act_b, w_p, preferred_element_type=jnp.float32) + bias_f[8 * width : 9 * width]
    )
    return (result, (hf, a1b, qkv_b, p_tok, p_pre, attn_b, resid, a2b, pre_act, act_b))


def backward_ffn(grad_out, keep, params):
    w_q, w_o, w_f, w_p, gain_pair, bias_all = params
    hf, a1b, qkv_b, p_tok, p_pre, attn_b, resid, a2b, pre_act, act_b = keep
    width = w_o.shape[0]
    gain_f = gain_pair.astype(jnp.float32)
    bias_f = bias_all.astype(jnp.float32)
    dm_b = grad_out.astype(jnp.bfloat16)
    grad_wp = jnp.einsum("lf,ld->fd", act_b, dm_b, preferred_element_type=jnp.float32)
    grad_bp = jnp.sum(dm_b.astype(jnp.float32), axis=0)
    d_act = jnp.dot(dm_b, w_p.T, preferred_element_type=jnp.float32)
    dpre_b = jax.vjp(gelu_tanh, pre_act)[1](d_act)[0].astype(jnp.bfloat16)
    grad_wf = jnp.einsum("ld,lf->df", a2b, dpre_b, preferred_element_type=jnp.float32)
    grad_bf = jnp.sum(dpre_b.astype(jnp.float32), axis=0)
    d_a2 = jnp.dot(dpre_b, w_f.T, preferred_element_type=jnp.float32)
    norm_back = jax.vjp(norm_rows, resid, gain_f[1], bias_f[10 * width : 11 * width])[1]
    d_resid_norm, grad_g2, grad_c2 = norm_back(d_a2)
    d_resid = grad_out + d_resid_norm
    return (d_resid, (grad_wf, grad_wp), (grad_bf, grad_bp, grad_g2, grad_c2))


def backward_attn(d_resid, keep, pkey, pval, params):
    w_q, w_o, w_f, w_p, gain_pair, bias_all = params
    hf, a1b, qkv_b, p_tok, p_pre, attn_b, resid, a2b, pre_act, act_b = keep
    width = w_o.shape[0]
    length = hf.shape[0]
    heads, head_dim = (pkey.shape[1], pkey.shape[2])
    prefix_len = pkey.shape[0]
    scale = 1.0 / math.sqrt(head_dim)
    gain_f = gain_pair.astype(jnp.float32)
    bias_f = bias_all.astype(jnp.float32)
    split = qkv_b.reshape(length, 3, heads, head_dim)
    query, keys, values = (split[:, 0], split[:, 1], split[:, 2])
    dat_b = d_resid.astype(jnp.bfloat16)
    grad_wo = jnp.einsum("ld,le->de", attn_b, dat_b, preferred_element_type=jnp.float32)
    grad_bo = jnp.sum(dat_b.astype(jnp.float32), axis=0)
    dattn_b = jnp.dot(dat_b, w_o.T, preferred_element_type=jnp.float32).astype(jnp.bfloat16)
    dattn_b = dattn_b.reshape(length, heads, head_dim)
    dp_tok = jnp.einsum("lhe,mhe->hlm", dattn_b, values, preferred_element_type=jnp.float32)
    dp_pre = jnp.einsum("lhe,phe->hlp", dattn_b, pval, preferred_element_type=jnp.float32)
    row_dot = jnp.sum(p_tok * dp_tok, axis=-1, keepdims=True) + jnp.sum(
        p_pre * dp_pre, axis=-1, keepdims=True
    )
    ds_tok = (p_tok * (dp_tok - row_dot)).astype(jnp.bfloat16)
    ds_pre = (p_pre * (dp_pre - row_dot)).astype(jnp.bfloat16)
    d_query = (
        jnp.einsum("hlm,mhe->lhe", ds_tok, keys, preferred_element_type=jnp.float32)
        + jnp.einsum("hlp,phe->lhe", ds_pre, pkey, preferred_element_type=jnp.float32)
    ) * scale
    d_keys = jnp.einsum("hlm,lhe->mhe", ds_tok, query, preferred_element_type=jnp.float32) * scale
    d_values = jnp.einsum(
        "hlm,lhe->mhe", p_tok.astype(jnp.bfloat16), dattn_b, preferred_element_type=jnp.float32
    )
    grad_pkey = (
        jnp.einsum("hlp,lhe->phe", ds_pre, query, preferred_element_type=jnp.float32) * scale
    )
    grad_pval = jnp.einsum(
        "hlp,lhe->phe", p_pre.astype(jnp.bfloat16), dattn_b, preferred_element_type=jnp.float32
    )
    dqkv_b = (
        jnp.stack([d_query, d_keys, d_values], axis=1)
        .reshape(length, 3 * width)
        .astype(jnp.bfloat16)
    )
    grad_wq = jnp.einsum("ld,lc->dc", a1b, dqkv_b, preferred_element_type=jnp.float32)
    grad_bq = jnp.sum(dqkv_b.astype(jnp.float32), axis=0)
    d_a1 = jnp.dot(dqkv_b, w_q.T, preferred_element_type=jnp.float32)
    norm_back_first = jax.vjp(norm_rows, hf, gain_f[0], bias_f[9 * width : 10 * width])[1]
    d_in_norm, grad_g1, grad_c1 = norm_back_first(d_a1)
    d_input = d_resid + d_in_norm
    grad_prefix = jnp.concatenate(
        [grad_pkey.reshape(prefix_len, width), grad_pval.reshape(prefix_len, width)], axis=1
    )
    return (d_input, (grad_wq, grad_wo), (grad_bq, grad_bo, grad_g1, grad_c1), grad_prefix)


def assemble(ffn_mats, ffn_small, attn_mats, attn_small):
    grad_bf, grad_bp, grad_g2, grad_c2 = ffn_small
    grad_bq, grad_bo, grad_g1, grad_c1 = attn_small
    grad_gains = jnp.stack([grad_g1, grad_g2])
    grad_bias = jnp.concatenate([grad_bq, grad_bo, grad_bf, grad_bp, grad_c1, grad_c2])
    return (attn_mats[0], attn_mats[1], ffn_mats[0], ffn_mats[1], grad_gains, grad_bias)


def on_device(
    tokens,
    segment_ids,
    cotangent,
    w_qkv,
    w_attn_out,
    w_fc,
    w_proj,
    gains,
    biases,
    prefix_embed,
    reparam_in,
    reparam_in_bias,
    reparam_out,
    reparam_out_bias,
):
    section = lax.axis_index("section")
    micro, row_len = segment_ids.shape
    width = tokens.shape[1]
    prefix_len = prefix_embed.shape[0]
    head_dim = width // HEADS
    fused = lax.axis_size("dp") == 16
    params = gather_params(w_qkv, w_attn_out, w_fc, w_proj, gains, biases, fused)
    pre_hidden = jnp.dot(
        prefix_embed, reparam_in, preferred_element_type=jnp.float32
    ) + reparam_in_bias.astype(jnp.float32)
    hidden = jnp.tanh(pre_hidden)
    hidden_b = hidden.astype(jnp.bfloat16)
    prefix_kv = (
        jnp.dot(hidden_b, reparam_out, preferred_element_type=jnp.float32)
        + reparam_out_bias.astype(jnp.float32)
    ).astype(jnp.bfloat16)
    pkey = prefix_kv[:, :width].reshape(prefix_len, HEADS, head_dim)
    pval = prefix_kv[:, width:].reshape(prefix_len, HEADS, head_dim)
    token_rows = tokens.reshape(micro, row_len, width)
    cot_rows = cotangent.reshape(micro, row_len, width)
    received = jnp.zeros((row_len, width), jnp.bfloat16)
    outputs = jnp.zeros((micro, row_len, width), jnp.bfloat16)
    stored = []
    for tick in range(micro + 1):
        index = tick - section
        active = (index >= 0) & (index < micro)
        slot = jnp.clip(index, 0, micro - 1)
        segs = segment_ids[slot]
        h_b = jnp.where(section == 0, token_rows[slot], received)
        result, keep = forward_layer(h_b, segs, pkey, pval, params)
        result_b = result.astype(jnp.bfloat16)
        outputs = jnp.where(active, outputs.at[slot].set(result_b), outputs)
        stored.append(keep)
        if tick < micro:
            received = passed_along(result_b, "section", 1)
    params_back = params
    stacked = jax.tree.map(lambda *items: jnp.stack(items), *stored)
    coming = jnp.zeros((row_len, width), jnp.bfloat16)
    in_grads = jnp.zeros((micro, row_len, width), jnp.bfloat16)
    grad_total = None
    prefix_total = None
    for tick in range(micro + 1):
        index = micro - tick - section
        active = (index >= 0) & (index < micro)
        slot = jnp.clip(index, 0, micro - 1)
        segs = segment_ids[slot]
        saved = jax.tree.map(lambda item: item[slot + section], stacked)
        grad_out = jnp.where(
            section == 1, cot_rows[slot].astype(jnp.float32), coming.astype(jnp.float32)
        )
        keep = saved
        d_resid, ffn_mats, ffn_small = backward_ffn(grad_out, keep, params_back)
        ffn_mats = jax.tree.map(
            lambda item: jnp.where(active, item, jnp.zeros_like(item)), ffn_mats
        )
        ffn_small = jax.tree.map(
            lambda item: jnp.where(active, item, jnp.zeros_like(item)), ffn_small
        )
        d_input, attn_mats, attn_small, grad_prefix = backward_attn(
            d_resid, keep, pkey, pval, params_back
        )
        attn_mats = jax.tree.map(
            lambda item: jnp.where(active, item, jnp.zeros_like(item)), attn_mats
        )
        attn_small = jax.tree.map(
            lambda item: jnp.where(active, item, jnp.zeros_like(item)), attn_small
        )
        grad_prefix = jnp.where(active, grad_prefix, jnp.zeros_like(grad_prefix))
        grads = assemble(ffn_mats, ffn_small, attn_mats, attn_small)
        if grad_total is None:
            grad_total = grads
            prefix_total = grad_prefix
        else:
            grad_total = jax.tree.map(lambda left, right: left + right, grad_total, grads)
            prefix_total = prefix_total + grad_prefix
        d_input_b = d_input.astype(jnp.bfloat16)
        in_grads = jnp.where(active, in_grads.at[slot].set(d_input_b), in_grads)
        if tick < micro:
            coming = passed_along(d_input_b, "section", -1)
    weight_grads = scatter_grads(grad_total, fused)
    prefix_grad = lax.psum(prefix_total, "dp")
    prefix_grad_b = prefix_grad.astype(jnp.bfloat16)
    grad_reparam_out = jnp.einsum(
        "pr,pc->rc", hidden_b, prefix_grad_b, preferred_element_type=jnp.float32
    )
    grad_reparam_out_bias = jnp.sum(prefix_grad_b.astype(jnp.float32), axis=0)
    hidden_part = jnp.dot(prefix_grad_b, reparam_out.T, preferred_element_type=jnp.float32)
    hidden_grad = lax.psum(hidden_part, "section")
    dpre_hidden_b = (hidden_grad * (1.0 - hidden * hidden)).astype(jnp.bfloat16)
    grad_reparam_in = jnp.einsum(
        "pd,pr->dr", prefix_embed, dpre_hidden_b, preferred_element_type=jnp.float32
    )
    grad_reparam_in_bias = jnp.sum(dpre_hidden_b.astype(jnp.float32), axis=0)
    grad_prefix_embed = jnp.dot(dpre_hidden_b, reparam_in.T, preferred_element_type=jnp.float32)
    layer_outs = outputs.reshape(1, micro * row_len, width)
    input_grads = in_grads.reshape(1, micro * row_len, width)
    return (
        layer_outs,
        input_grads,
        weight_grads[0],
        weight_grads[1],
        weight_grads[2],
        weight_grads[3],
        weight_grads[4],
        weight_grads[5],
        grad_prefix_embed,
        grad_reparam_in,
        grad_reparam_in_bias,
        grad_reparam_out,
        grad_reparam_out_bias,
    )


def solution(mesh):
    return jax.shard_map(
        on_device,
        mesh=mesh,
        in_specs=(
            P("dp", None),
            P("dp", None),
            P("dp", None),
            P("section", "dp", None),
            P("section", "dp", None),
            P("section", "dp", None),
            P("section", "dp", None),
            P("section", None, "dp"),
            P("section", "dp"),
            P(),
            P(),
            P(),
            P(None, "section"),
            P("section"),
        ),
        out_specs=(
            P("section", "dp", None),
            P("section", "dp", None),
            P("section", "dp", None),
            P("section", "dp", None),
            P("section", "dp", None),
            P("section", "dp", None),
            P("section", None, "dp"),
            P("section", "dp"),
            P(),
            P(),
            P(),
            P(None, "section"),
            P("section"),
        ),
        check_vma=False,
    )
```

```python
import math

import jax
import jax.numpy as jnp
from jax import lax
from jax.experimental import pallas as pl
from jax.experimental.pallas import tpu as pltpu
from jax.sharding import PartitionSpec as P

HEADS = 16
EPS = 1e-05
NEG = -1000000000.0
MESH = pl.DeviceIdType.MESH
F32 = jnp.float32
B16 = jnp.bfloat16
NP = 12


def place():
    s = lax.axis_index("section"); d = lax.axis_index("dp")
    return s, d, d // 4, (d // 2) % 2, d % 2

def greet(s, z, y, c, cross=False):
    bar = pltpu.get_barrier_semaphore()
    def hello(dev):
        pl.semaphore_signal(bar, 1, device_id=dev, device_id_type=MESH)
    hello((s, z*4+y*2+(1-c)))
    hello((s, z*4+(1-y)*2+c))
    if cross: hello((1-s, z*4+y*2+c))
    @pl.when(z > 0)
    def _(): hello((s, (z-1)*4+y*2+c))
    @pl.when(z < 3)
    def _(): hello((s, (z+1)*4+y*2+c))
    pl.semaphore_wait(bar, 3 + (1 if cross else 0) + ((z + 1) // 2) % 2)

class Gather:
    def __init__(self, W, ssem, rsem):
        self.W, self.ssem, self.rsem = W, ssem, rsem
        self.s, self.d, self.z, self.y, self.c = place()
    def blk(self, k, d):
        i = k // 8
        row = (1-i)*(1024*k+64*d) + i*(8192+256*d+64*(k-8))
        return self.W.at[pl.ds(pl.multiple_of(row, 64), 64)]
    def cp(self, k, origin, target, slot):
        b = self.blk(k, origin)
        return pltpu.make_async_remote_copy(src_ref=b, dst_ref=b, send_sem=self.ssem.at[k, slot], recv_sem=self.rsem.at[k, origin],
            device_id=(self.s, target), device_id_type=MESH)
    def dev(self, z, y, c): return z*4+y*2+c
    def arrived(self, k, origin): self.cp(k, origin, origin, 0).wait_recv()
    def to_up(self, k, zo, op):
        op(self.cp(k, self.dev(zo, self.y, self.c), self.dev(self.z+1, self.y, self.c), zo))
    def to_down(self, k, zo, op):
        op(self.cp(k, self.dev(zo, self.y, self.c), self.dev(self.z-1, self.y, self.c), 4+zo))
    def to_y(self, k, zo, op):
        op(self.cp(k, self.dev(zo, self.y, self.c), self.dev(self.z, 1-self.y, self.c), 8+zo))
    def to_c(self, k, zo, yo, op):
        op(self.cp(k, self.dev(zo, yo, self.c), self.dev(self.z, self.y, 1-self.c), 12+zo*2+yo))
    def step(self, t, own):
        z, y, c = self.z, self.y, self.c
        start = lambda cp: cp.start()
        @pl.when(t < NP)
        def _():
            own(t)
            self.to_y(t, z, start)
            @pl.when(z < 3)
            def _(): self.to_up(t, z, start)
            @pl.when(z > 0)
            def _(): self.to_down(t, z, start)
            self.to_c(t, z, y, start)
        for q in (1, 2, 3, 4):
            k = t - q
            ok = (k >= 0) & (k < NP)
            if q < 4:
                @pl.when(ok & (z - q >= 0))
                def _():
                    self.arrived(k, self.dev(z-q, y, c))
                    @pl.when(z < 3)
                    def _(): self.to_up(k, z-q, start)
                    self.to_y(k, z-q, start)
                    self.to_c(k, z-q, y, start)
                @pl.when(ok & (z + q <= 3))
                def _():
                    self.arrived(k, self.dev(z+q, y, c))
                    @pl.when(z > 0)
                    def _(): self.to_down(k, z+q, start)
                    self.to_y(k, z+q, start)
                    self.to_c(k, z+q, y, start)
            e = q - 1
            def side(zo):
                self.arrived(k, self.dev(zo, 1-y, c))
                self.to_c(k, zo, 1-y, start)
            if e == 0:
                @pl.when(ok)
                def _(): side(z)
            else:
                @pl.when(ok & (z - e >= 0))
                def _(): side(z-e)
                @pl.when(ok & (z + e <= 3))
                def _(): side(z+e)
    def complete(self, k):
        for i in range(8):
            self.arrived(k, 2*i + 1-self.c)
    def drain(self):
        fin = lambda cp: cp.wait_send()
        z, y = self.z, self.y
        @pl.loop(0, NP)
        def _(k):
            for zo in range(4):
                @pl.when((zo <= z) & (z < 3))
                def _(): self.to_up(k, zo, fin)
                @pl.when((zo >= z) & (z > 0))
                def _(): self.to_down(k, zo, fin)
                self.to_y(k, zo, fin)
                for yo in range(2): self.to_c(k, zo, yo, fin)

def own_copies(wq, wo, wf, wp, g, sem):
    out = []
    for k in range(NP):
        if k < 3: src = wq.at[0, :, pl.ds(1024*k, 1024)]
        elif k == 3: src = wo.at[0]
        elif k < 8: src = wf.at[0, :, pl.ds(1024*(k-4), 1024)]
        else: src = wp.at[0, pl.ds(64*(k-8), 64)]
        out.append(pltpu.make_async_copy(src, g.blk(jnp.int32(k), g.d), sem.at[k]))
    return out


HALF = 256
STAGES = 12
GELU_C = math.sqrt(2.0 / math.pi)


def dot_nn(a, b):
    return lax.dot_general(a, b, (((1,), (0,)), ((), ())), preferred_element_type=F32)


def dot_nt(a, b):
    return lax.dot_general(a, b, (((1,), (1,)), ((), ())), preferred_element_type=F32)


def dot_tn(a, b):
    return lax.dot_general(a, b, (((0,), (0,)), ((), ())), preferred_element_type=F32)


def whiten(v):
    mean = jnp.mean(v, axis=-1, keepdims=True)
    cent = v - mean
    rstd = lax.rsqrt(jnp.mean(cent * cent, axis=-1, keepdims=True) + EPS)
    return cent * rstd, rstd


def split_heads(pair):
    left = lax.broadcasted_iota(jnp.int32, pair.shape, 1) < 64
    zero = jnp.zeros_like(pair)
    return jnp.concatenate([jnp.where(left, pair, zero), jnp.where(left, zero, pair)], axis=0)


def forward_kernel(
    wq, wo, wf, wp, tokens, small, mask, pkey, pval,
    W_o, out_o, h_o, a1_o, qkv_o, prob_o, ppre_o, att_o, res_o, a2_o, gp_o, act_o,
    W, H, A1, QKV, PROB, PPRE, ATT, RES, A2, GP, ACT, OUT, SPRE, ACC,
    own_sem, ssem, rsem, hsem, xs, xr, save_sem,
):
    g = Gather(W, ssem, rsem)
    s = g.s
    for cp in own_copies(wq, wo, wf, wp, g, own_sem):
        cp.start()
    greet(s, g.z, g.y, g.c, cross=True)

    def tokens_in():
        return pltpu.make_async_copy(tokens, H, hsem)

    def half(b):
        return pl.ds(pl.multiple_of(b * HALF, HALF), HALF)

    def cross(b):
        return pltpu.make_async_remote_copy(
            OUT.at[half(b)], H.at[half(b)], xs.at[b], xr.at[b], device_id=(1 - s, g.d), device_id_type=MESH
        )

    @pl.when(s == 0)
    def _():
        tokens_in().start()

    def own(t):
        b = g.blk(t, g.d)
        pltpu.make_async_copy(b, b, own_sem.at[t]).wait()

    def rows_of(k):
        return pl.ds(pl.multiple_of(k * 1024, 1024), 1024)

    def saves(b):
        r = half(b)
        pairs = [
            (H.at[r], h_o.at[r]), (A1.at[r], a1_o.at[r]), (QKV.at[:, r], qkv_o.at[:, r]), (PROB.at[pl.ds(2 * b, 2)], prob_o.at[pl.ds(2 * b, 2)]),
            (PPRE.at[b], ppre_o.at[b]), (ATT.at[r], att_o.at[r]), (RES.at[r], res_o.at[r]), (A2.at[r], a2_o.at[r]),
            (GP.at[:, r], gp_o.at[:, r]), (ACT.at[:, r], act_o.at[:, r]), (OUT.at[r], out_o.at[r]),
        ]
        return [pltpu.make_async_copy(src, dst, save_sem.at[b, i]) for i, (src, dst) in enumerate(pairs)]

    def piece_out(k):
        return pltpu.make_async_copy(W.at[rows_of(k)], W_o.at[rows_of(k)], save_sem.at[2, k])

    def norm_in(b):
        @pl.when(s == 0)
        def _():
            @pl.when(b == 0)
            def _():
                tokens_in().wait()

        @pl.when(s == 1)
        def _():
            cross(b).wait_recv()

        xhat, _ = whiten(H[half(b)].astype(F32))
        A1[half(b)] = (xhat * small[11:12] + small[9:10]).astype(B16)
        saves(b)[0].start()
        saves(b)[1].start()

    def project(i, b):
        v = dot_nn(A1[half(b)], W[rows_of(i)]) + small[pl.ds(i, 1)]
        v = v.astype(B16)
        QKV[i, half(b)] = v * jnp.where(i == 0, 0.125, 1.0).astype(B16)

        @pl.when(i == 2)
        def _():
            saves(b)[2].start()

    def attend(part, b):
        @pl.when(part == 0)
        def _():
            sp = dot_nt(pkey[...], QKV[0, half(b)])
            there = lax.broadcasted_iota(jnp.int32, sp.shape, 0) % 16 < 10
            SPRE[b] = jnp.where(there, sp, NEG)

        @pl.loop(part * 4, part * 4 + 4)
        def _(p):
            cols = pl.ds(pl.multiple_of(p * 128, 128), 128)
            q2, k2, v2 = QKV[0, half(b), cols], QKV[1, half(b), cols], QKV[2, half(b), cols]
            st = dot_nt(split_heads(k2), q2)
            probs, pres = [], []
            for e in range(2):
                sh = st[e * HALF : (e + 1) * HALF] + mask[b]
                sp = SPRE[b, pl.ds(pl.multiple_of(p * 32 + e * 16, 16), 16)]
                top = jnp.maximum(jnp.max(sh, axis=0, keepdims=True), jnp.max(sp, axis=0, keepdims=True))
                et, ep = jnp.exp(sh - top), jnp.exp(sp - top)
                inv = 1.0 / (jnp.sum(et, axis=0, keepdims=True) + jnp.sum(ep, axis=0, keepdims=True))
                probs.append((et * inv).astype(B16))
                pres.append((ep * inv).astype(B16))
            pr = jnp.concatenate(probs, axis=0)
            PROB[2 * b + p // 4, :, pl.ds(pl.multiple_of((p % 4) * HALF, HALF), HALF)] = pr
            PPRE[b, pl.ds(pl.multiple_of(p * 32, 32), 32)] = jnp.concatenate(pres, axis=0)
            ACC[half(b), cols] = dot_tn(pr, split_heads(v2))

        @pl.when(part == 1)
        def _():
            ATT[half(b)] = (ACC[half(b)] + dot_tn(PPRE[b], pval[...])).astype(B16)
            saves(b)[3].start()
            saves(b)[4].start()
            saves(b)[5].start()

    def mix(b):
        r = H[half(b)].astype(F32) + (dot_nn(ATT[half(b)], W[rows_of(3)]) + small[3:4])
        RES[half(b)] = r
        xhat, _ = whiten(r)
        A2[half(b)] = (xhat * small[12:13] + small[10:11]).astype(B16)
        saves(b)[6].start()
        saves(b)[7].start()

    def widen(j, b):
        x = dot_nn(A2[half(b)], W[rows_of(4 + j)]) + small[pl.ds(4 + j, 1)]
        x2 = x * x
        t = jnp.tanh(GELU_C * (x + 0.044715 * (x2 * x)))
        ACT[j, half(b)] = (0.5 * x * (1.0 + t)).astype(B16)
        GP[j, half(b)] = (
            0.5 * (1.0 + t) + (0.5 * GELU_C) * x * (1.0 - t * t) * (1.0 + (3 * 0.044715) * x2)
        ).astype(B16)

        @pl.when(j == 3)
        def _():
            saves(b)[8].start()
            saves(b)[9].start()

    def narrow(b):
        v = RES[half(b)] + small[8:9]
        for j in range(4):
            v = v + dot_nn(ACT[j, half(b)], W[rows_of(8 + j)])
        OUT[half(b)] = v.astype(B16)

        @pl.when(s == 0)
        def _():
            cross(b).start()

        saves(b)[10].start()

    @pl.loop(0, NP + 5 + 2 * STAGES)
    def _(tick):
        @pl.when(tick < NP + 5)
        def _():
            g.step(tick, own)

            @pl.when(tick >= 5)
            def _():
                g.complete(tick - 5)

                @pl.when(tick < 13)
                def _():
                    piece_out(tick - 5).start()

                @pl.when(tick == NP + 4)
                def _():
                    for k in range(8, NP):
                        piece_out(k).start()

        late = tick - (NP + 5)
        stage = (1 - s) * (tick - 5) + s * ((late + STAGES) % STAGES - STAGES * (late < 0).astype(jnp.int32))
        lo = s * (late // STAGES)
        hi = (1 - s) * 2 + s * (late // STAGES + 1)

        def when(i, body):
            @pl.when(stage == i)
            def _():
                pl.loop(lo, hi)(body)

        when(0, norm_in)

        @pl.when((stage >= 1) & (stage < 4))
        def _():
            pl.loop(lo, hi)(lambda b: project(stage - 1, b))

        @pl.when((stage >= 4) & (stage < 6))
        def _():
            pl.loop(lo, hi)(lambda b: attend(stage - 4, b))

        when(6, mix)

        @pl.when((stage >= 7) & (stage < 11))
        def _():
            pl.loop(lo, hi)(lambda b: widen(stage - 7, b))

        when(11, narrow)

    g.drain()

    @pl.loop(0, NP)
    def _(k):
        piece_out(k).wait()

    @pl.loop(0, 2)
    def _(b):
        for cp in saves(b):
            cp.wait()

        @pl.when(s == 0)
        def _():
            cross(b).wait_send()


def forward_call(wq, wo, wf, wp, tokens, small, mask, pkey, pval):
    any_, vm = pl.BlockSpec(memory_space=pl.ANY), pl.BlockSpec(memory_space=pltpu.VMEM)
    n, d = tokens.shape
    kept = [
        ((NP * d, d), B16), ((n, d), B16), ((n, d), B16), ((n, d), B16), ((3, n, d), B16), ((4, n, d), B16),
        ((2, HALF, HALF), B16), ((n, d), B16), ((n, d), F32), ((n, d), B16), ((4, n, d), B16), ((4, n, d), B16),
    ]
    dma = pltpu.SemaphoreType.DMA
    order = [0, 2, 3, 4, 5, 6, 7, 8, 9, 10, 11, 1]
    scratch = [pltpu.VMEM(*kept[i]) for i in order]
    return pl.pallas_call(
        forward_kernel,
        out_shape=[jax.ShapeDtypeStruct(*k) for k in kept],
        in_specs=[any_] * 5 + [vm] * 4,
        out_specs=[any_] * len(kept),
        scratch_shapes=scratch
        + [pltpu.VMEM((2, HALF, HALF), F32), pltpu.VMEM((n, d), F32)]
        + [dma((NP,)), dma((NP, 20)), dma((NP, 16)), dma, dma((2,)), dma((2,)), dma((3, NP))],
        compiler_params=pltpu.CompilerParams(collective_id=0, has_side_effects=True, vmem_limit_bytes=62 << 20),
    )(wq, wo, wf, wp, tokens, small, mask, pkey, pval)

SPLIT = 6
BACK_TICKS = 2 + 2 * SPLIT + NP + 6


def unwhiten(grad, xhat, rstd):
    return rstd * (
        grad
        - jnp.mean(grad, axis=-1, keepdims=True)
        - xhat * jnp.mean(grad * xhat, axis=-1, keepdims=True)
    )


def column_sum(v):
    return jnp.sum(v.astype(F32), axis=0, keepdims=True)


def backward_kernel(
    W_i, h_i, a1_i, qkv_i, prob_i, ppre_i, att_i, res_i, a2_i, gp_i, act_i, cot, small, pkey, pval,
    dh_o, oq, oo, of, op_, SG, DKV,
    WG, H, A1, QKV, BIG, PPRE, ATT, RES, A2, GP, DM, DAT, DATT, DPP, DSP, ACC,
    RC, RY, RU, RD, T,
    wsem, lsem, osem, cs, cr, ys, yr, us, ur, ds_, dr, xs, xr, hs,
):
    s, d, z, y, c = place()
    for k in (8, 9, 10, 11, 4, 5, 6, 7, 3, 2, 1, 0):
        pltpu.make_async_copy(W_i.at[k], WG.at[k], wsem.at[k]).start()

    def loads():
        pairs = [
            (gp_i, GP), (a2_i, A2), (res_i, RES), (att_i, ATT), (qkv_i, QKV), (ppre_i, PPRE), (a1_i, A1), (h_i, H),
            (act_i, BIG), (prob_i, BIG), (cot, DM),
        ]
        return [pltpu.make_async_copy(a, b, lsem.at[i]) for i, (a, b) in enumerate(pairs)]

    L_GP, L_A2, L_RES, L_ATT, L_QKV, L_PPRE, L_A1, L_H, L_ACT, L_PROB, L_COT = range(11)

    @pl.when(s == 1)
    def _():
        loads()[L_COT].start()

    loads()[L_GP].start()
    for i in (L_A2, L_RES, L_ATT, L_QKV, L_PPRE):
        loads()[i].start()

    @pl.when(s == 0)
    def _():
        loads()[L_ACT].start()

    @pl.when(s == 1)
    def _():
        loads()[L_PROB].start()

    for i in (L_A1, L_H):
        loads()[i].start()
    SG[...] = jnp.zeros_like(SG)
    DKV[...] = jnp.zeros_like(DKV)
    greet(s, z, y, c, cross=True)

    def weights(ks):
        for k in ks:
            pltpu.make_async_copy(W_i.at[k], WG.at[k], wsem.at[k]).wait()

    def half(b):
        return pl.ds(pl.multiple_of(b * HALF, HALF), HALF)

    def weight(k):
        return WG[k].reshape(1024, 1024)

    def cross(b):
        return pltpu.make_async_remote_copy(
            H.at[half(b)], DM.at[half(b)], xs.at[b], xr.at[b], device_id=(1 - s, d), device_id_type=MESH
        )

    def dh_out(b):
        return pltpu.make_async_copy(H.at[half(b)], dh_o.at[half(b)], hs.at[b])

    def ffn_in(b):
        first = (b == 0)

        @pl.when(first)
        def _():
            @pl.when(s == 1)
            def _():
                loads()[L_COT].wait()

            weights((8, 9, 10, 11))
            loads()[L_GP].wait()

        @pl.when(s == 0)
        def _():
            cross(b).wait_recv()

        for j in range(4):
            GP[j, half(b)] = (dot_nt(DM[half(b)], weight(8 + j)) * GP[j, half(b)].astype(F32)).astype(B16)

    def ffn_norm(b):
        @pl.when(b == 0)
        def _():
            weights((4, 5, 6, 7))
            loads()[L_A2].wait()
            loads()[L_RES].wait()

        grad = dot_nt(GP[0, half(b)], weight(4))
        for j in range(1, 4):
            grad = grad + dot_nt(GP[j, half(b)], weight(4 + j))
        xhat, rstd = whiten(RES[half(b)])
        SG[10:11] += jnp.sum(grad, axis=0, keepdims=True)
        SG[12:13] += jnp.sum(grad * xhat, axis=0, keepdims=True)
        res = DM[half(b)].astype(F32) + unwhiten(grad * small[12:13], xhat, rstd)
        RES[half(b)] = res
        DAT[half(b)] = res.astype(B16)

    def attn_out(b):
        @pl.when(b == 0)
        def _():
            weights((3,))
            for i in (L_ATT, L_QKV, L_PPRE):
                loads()[i].wait()

            loads()[L_PROB].wait()

        DATT[...] = dot_nt(DAT[half(b)], weight(3)).astype(B16)
        DPP[...] = dot_nt(pval[...], DATT[...])

    def attn_back(part, b):
        @pl.loop(part * 4, part * 4 + 4)
        def _(p):
            cols = pl.ds(pl.multiple_of(p * 128, 128), 128)
            q2, k2, v2 = QKV[0, half(b), cols], QKV[1, half(b), cols], QKV[2, half(b), cols]
            do2 = DATT[:, cols]
            pr = BIG[2 * b + p // 4, :, pl.ds(pl.multiple_of((p % 4) * HALF, HALF), HALF)]
            dp = dot_nt(split_heads(v2), do2)
            dss, pres = [], []
            for e in range(2):
                ph = pr[e * HALF : (e + 1) * HALF].astype(F32)
                dh = dp[e * HALF : (e + 1) * HALF]
                at = pl.ds(pl.multiple_of(p * 32 + e * 16, 16), 16)
                pp, dpp = PPRE[b, at].astype(F32), DPP[at]
                dot = jnp.sum(ph * dh, axis=0, keepdims=True) + jnp.sum(pp * dpp, axis=0, keepdims=True)
                dss.append((ph * (dh - dot)).astype(B16))
                pres.append((pp * (dpp - dot)).astype(B16))
            ds = jnp.concatenate(dss, axis=0)
            DSP[pl.ds(pl.multiple_of(p * 32, 32), 32)] = jnp.concatenate(pres, axis=0)
            left = lax.broadcasted_iota(jnp.int32, (HALF, 128), 1) < 64
            ACC[:, cols] = dot_tn(ds, split_heads(k2))
            dk = dot_nn(ds, q2)
            dv = dot_nn(pr, do2)
            QKV[1, half(b), cols] = jnp.where(left, dk[:HALF], dk[HALF:]).astype(B16)
            QKV[2, half(b), cols] = jnp.where(left, dv[:HALF], dv[HALF:]).astype(B16)

        @pl.when(part == 1)
        def _():
            def own_rows(full):
                out = jnp.zeros((16, 1024), F32)
                head = lax.broadcasted_iota(jnp.int32, (16, 1024), 1) // 64
                for i in range(16):
                    out = out + jnp.where(head == i, full[16 * i : 16 * i + 16], 0.0)
                return out

            DKV[0:16] += own_rows(dot_nn(DSP[...], QKV[0, half(b)]))
            DKV[16:32] += own_rows(dot_nn(PPRE[b], DATT[...]))
            QKV[0, half(b)] = ((ACC[...] + dot_tn(DSP[...], pkey[...])) * 0.125).astype(B16)

    def attn_norm(b):
        @pl.when(b == 0)
        def _():
            weights((0, 1, 2))
            loads()[L_A1].wait()
            loads()[L_H].wait()

        @pl.when((s == 1) & (b == 1))
        def _():
            loads()[L_ACT].start()

        grad = dot_nt(QKV[0, half(b)], weight(0))
        for i in range(1, 3):
            grad = grad + dot_nt(QKV[i, half(b)], weight(i))
        xhat, rstd = whiten(H[half(b)].astype(F32))
        SG[9:10] += jnp.sum(grad, axis=0, keepdims=True)
        SG[11:12] += jnp.sum(grad * xhat, axis=0, keepdims=True)
        H[half(b)] = (RES[half(b)] + unwhiten(grad * small[11:12], xhat, rstd)).astype(B16)

        @pl.when(s == 1)
        def _():
            cross(b).start()

        dh_out(b).start()

    def grad_proj():
        loads()[L_ACT].wait()
        SG[8:9] = column_sum(DM[...])

        @pl.loop(0, 4)
        def _(i):
            for u in range(2):
                v = dot_tn(BIG[i, :, 512 * u : 512 * (u + 1)], DM[...]).astype(B16).reshape(2, 4, 64, 1024)
                for j in range(4):
                    WG[8 + j, i, u] = v[:, j]

        @pl.when(s == 0)
        def _():
            loads()[L_PROB].start()

    def put(k, a, v):
        for i in range(2):
            part = dot_tn(a[:, 512 * i : 512 * (i + 1)], v[...])
            WG[k, 2 * i : 2 * i + 2] = part.astype(B16).reshape(2, 2, 2, 64, 1024)

    def grad_fc(j):
        SG[pl.ds(4 + j, 1)] = column_sum(GP[j])
        put(4 + j, A2, GP.at[j])

    def grad_out():
        SG[3:4] = column_sum(DAT[...])
        put(3, ATT, DAT)

    def grad_qkv(i):
        SG[pl.ds(i, 1)] = column_sum(QKV[i])
        put(i, A1, QKV.at[i])

    def held(r):
        a = r // 4
        return ((2 - a) * (1 - a) // 2) * (r + 8) + a * (2 - a) * r + (a * (a - 1) // 2) * (11 - r)

    def across_c(r):
        return pltpu.make_async_remote_copy(
            WG.at[held(r), :, :, 1 - c], RC.at[r % 4], cs.at[r], cr.at[r],
            device_id=(s, z * 4 + y * 2 + 1 - c), device_id_type=MESH,
        )

    def across_y(r):
        return pltpu.make_async_remote_copy(
            WG.at[held(r), :, 1 - y, c], RY.at[r % 4], ys.at[r], yr.at[r],
            device_id=(s, z * 4 + (1 - y) * 2 + c), device_id_type=MESH,
        )

    def up(r, n, first):
        return pltpu.make_async_remote_copy(
            WG.at[held(r), pl.ds(first, n), y, c], RU.at[r % 7, pl.ds(first - 1, n)], us.at[r], ur.at[r],
            device_id=(s, (z + 1) * 4 + y * 2 + c), device_id_type=MESH,
        )

    def down(r, n):
        return pltpu.make_async_remote_copy(
            WG.at[held(r), pl.ds(0, n), y, c], RD.at[r % 7, pl.ds(0, n)], ds_.at[r], dr.at[r],
            device_id=(s, (z - 1) * 4 + y * 2 + c), device_id_type=MESH,
        )

    def each_out(r, act):
        k = held(r)
        src = T.at[r % 2]

        @pl.when(r < 4)
        def _():
            act(pltpu.make_async_copy(src, op_.at[0, pl.ds(pl.multiple_of(64 * r, 64), 64)], osem.at[r]))

        @pl.when((r >= 4) & (r < 8))
        def _():
            act(pltpu.make_async_copy(src, of.at[0, :, pl.ds(pl.multiple_of(1024 * (r - 4), 1024), 1024)], osem.at[r]))

        @pl.when(r == 8)
        def _():
            act(pltpu.make_async_copy(src, oo.at[0], osem.at[r]))

        @pl.when(r > 8)
        def _():
            act(pltpu.make_async_copy(src, oq.at[0, :, pl.ds(pl.multiple_of(1024 * (11 - r), 1024), 1024)], osem.at[r]))

    def start(cp):
        cp.start()

    def add(k, i, j, other):
        WG[k, i, j, c] = (WG[k, i, j, c].astype(F32) + other.astype(F32)).astype(B16)

    def live(r):
        return (r >= 0) & (r < NP)

    def scatter_step(t):
        @pl.when(live(t))
        def _():
            across_c(t).start()

        @pl.when(live(t - 1))
        def _():
            r = t - 1
            k = held(r)
            across_c(r).wait_recv()

            @pl.loop(0, 4)
            def _(i):
                add(k, i, 1 - y, RC[r % 4, i, 1 - y])

            across_y(r).start()

            @pl.loop(0, 4)
            def _(i):
                add(k, i, y, RC[r % 4, i, y])

        @pl.when(live(t - 2))
        def _():
            r = t - 2
            k = held(r)
            across_y(r).wait_recv()

            @pl.loop(0, 4)
            def _(i):
                add(k, i, y, RY[r % 4, i])

            @pl.when(z == 0)
            def _():
                up(r, 3, 1).start()

            @pl.when(z == 3)
            def _():
                down(r, 3).start()

        for q in (1, 2, 3):
            n = 4 - q

            @pl.when(live(t - 2 - q))
            def _():
                r = t - 2 - q
                k = held(r)

                @pl.when(z == q)
                def _():
                    up_here = pltpu.make_async_remote_copy(
                        WG.at[k, pl.ds(q, n), y, c], RU.at[r % 7, pl.ds(q - 1, n)], us.at[r], ur.at[r],
                        device_id=(s, d), device_id_type=MESH,
                    )
                    up_here.wait_recv()
                    for i in range(q + 1, 4):
                        add(k, i, y, RU[r % 7, i - 1])
                    if n > 1:
                        up(r, n - 1, q + 1).start()

                @pl.when(z == 3 - q)
                def _():
                    down(r, n).wait_recv()
                    for i in range(n - 1):
                        add(k, i, y, RD[r % 7, i])
                    if n > 1:
                        down(r, n - 1).start()

        @pl.when(live(t - 5))
        def _():
            r = t - 5
            k = held(r)

            @pl.when(r >= 2)
            def _():
                each_out(r - 2, lambda cp: cp.wait())

            T[r % 2] = WG[k, z, y, c].astype(F32)

            @pl.when(z > 0)
            def _():
                T[r % 2] += RU[r % 7, z - 1].astype(F32)

            @pl.when(z < 3)
            def _():
                T[r % 2] += RD[r % 7, z].astype(F32)

            each_out(r, start)

    @pl.loop(0, BACK_TICKS)
    def _(tick):
        turn = tick // SPLIT

        def when(i, at, body):
            mine = ((s == 0) & (tick == at)) | ((s == 1) & ((tick == i) | (tick == SPLIT + i)))

            @pl.when(mine)
            def _():
                pl.loop(s * turn, (1 - s) * 2 + s * (turn + 1))(body)

        @pl.when(((s == 0) & (tick < 2)) | ((s == 1) & ((tick == 0) | (tick == SPLIT))))
        def _():
            ffn_in((1 - s) * tick + s * turn)

        when(1, 3, ffn_norm)
        first = 5 - 3 * s + 3 * (1 - s) * ((tick - 5) // 3) + s * SPLIT * turn
        b0 = (1 - s) * ((tick - 5) // 3) + s * turn
        in_turn = ((s == 0) & (tick >= 5) & (tick < 11)) | ((s == 1) & (tick < 2 * SPLIT))

        @pl.when(in_turn & (tick == first))
        def _():
            attn_out(b0)

        @pl.when(in_turn & ((tick == first + 1) | (tick == first + 2)))
        def _():
            attn_back(tick - first - 1, b0)

        when(5, 11, attn_norm)
        r = tick - 2 - (2 * SPLIT - 2) * s

        @pl.when(r == 0)
        def _():
            grad_proj()

        @pl.when((r >= 4) & (r < 8))
        def _():
            grad_fc(r - 4)

        @pl.when(r == 8)
        def _():
            grad_out()

        @pl.when((r > 8) & (r < 12))
        def _():
            grad_qkv(11 - r)

        scatter_step(r)

    @pl.loop(0, NP)
    def _(r):
        @pl.when(r >= NP - 2)
        def _():
            each_out(r, lambda cp: cp.wait())

        across_c(r).wait_send()
        across_y(r).wait_send()
        for q in range(3):

            @pl.when(z == q)
            def _():
                up(r, 3 - q, q + 1).wait_send()

            @pl.when(z == q + 1)
            def _():
                down(r, q + 1).wait_send()

    @pl.loop(0, 2)
    def _(b):
        dh_out(b).wait()

        @pl.when(s == 1)
        def _():
            cross(b).wait_send()


def backward_call(kept, cot, small, pkey, pval):
    W, h, a1, qkv, prob, ppre, att, res, a2, gp, act = kept
    any_, vm = pl.BlockSpec(memory_space=pl.ANY), pl.BlockSpec(memory_space=pltpu.VMEM)
    n, d = h.shape
    dma = pltpu.SemaphoreType.DMA
    wide = (4, 2, 2, 64, d)
    prob = prob.reshape(4, 512, 1024)
    outs = [((n, d), B16), ((1, 64, 3 * d), F32), ((1, 64, d), F32), ((1, 64, 4 * d), F32), ((1, 256, d), F32), ((16, d), F32), ((32, d), F32)]
    scratch = [
        ((NP,) + wide, B16), ((n, d), B16), ((n, d), B16), ((3, n, d), B16), ((4, n, d), B16), ((2, HALF, HALF), B16), ((n, d), B16),
        ((n, d), F32), ((n, d), B16), ((4, n, d), B16), ((n, d), B16), ((n, d), B16), ((HALF, d), B16), ((HALF, HALF), F32),
        ((HALF, HALF), B16), ((HALF, d), F32),
        ((4, 4, 2, 64, d), B16), ((4, 4, 64, d), B16), ((7, 3, 64, d), B16), ((7, 3, 64, d), B16), ((2, 64, d), F32),
    ]
    return pl.pallas_call(
        backward_kernel,
        out_shape=[jax.ShapeDtypeStruct(*o) for o in outs],
        in_specs=[any_] * 12 + [vm] * 3,
        out_specs=[any_] * 5 + [vm] * 2,
        scratch_shapes=[pltpu.VMEM(*v) for v in scratch] + [dma((NP,))] * 11 + [dma((2,))] * 3,
        compiler_params=pltpu.CompilerParams(collective_id=1, has_side_effects=True, vmem_limit_bytes=64 << 20),
    )(W.reshape((NP,) + wide), h, a1, qkv, prob, ppre, att, res, a2, gp, act, cot, small, pkey, pval)

def swap_kernel(src, dst, ss, rs):
    s, d = lax.axis_index("section"), lax.axis_index("dp")
    bar = pltpu.get_barrier_semaphore()
    for i in range(1, 16):
        pl.semaphore_signal(bar, 1, device_id=(s, (d + i) % 16), device_id_type=MESH)
    dst[d] = src[d]
    pl.semaphore_wait(bar, 15)

    def cp(i, frm):
        return pltpu.make_async_remote_copy(
            src.at[(d + i) % 16], dst.at[frm], ss.at[i], rs.at[i], device_id=(s, (d + i) % 16), device_id_type=MESH
        )

    for i in range(1, 16):
        cp(i, d).start()
    for i in range(1, 16):
        cp(i, (d + 16 - i) % 16).wait()


def swap_blocks(x, cid):
    vm = pl.BlockSpec(memory_space=pltpu.VMEM)
    return pl.pallas_call(
        swap_kernel,
        out_shape=jax.ShapeDtypeStruct(x.shape, x.dtype),
        in_specs=[vm],
        out_specs=vm,
        scratch_shapes=[pltpu.SemaphoreType.DMA((16,))] * 2,
        compiler_params=pltpu.CompilerParams(collective_id=cid, has_side_effects=True),
    )(x)


def gather_small(gains, biases):
    own = jnp.concatenate([biases.reshape(704), gains.reshape(128)])
    own = jnp.pad(own, (0, 2048 - 832)).reshape(1, 16, 128)
    got = swap_blocks(jnp.broadcast_to(own, (16, 16, 128)), 2).reshape(16, 2048).astype(F32)
    bias = got[:, :704].reshape(11, 1024)
    gain = got[:, 704:832].reshape(16, 2, 64).transpose(1, 0, 2).reshape(2, 1024)
    return jnp.concatenate([bias, gain, jnp.zeros((3, 1024), F32)])


def prefix_blocks(rows):
    rows = jnp.pad(rows, ((0, 6), (0, 0)))
    big = jnp.broadcast_to(rows[None], (16, 16, 1024)).reshape(256, 1024)
    head = lax.broadcasted_iota(jnp.int32, (256, 1024), 0) // 16
    return jnp.where(head == lax.broadcasted_iota(jnp.int32, (256, 1024), 1) // 64, big, jnp.zeros_like(big))


def row_mask(segs):
    at = jnp.arange(segs.shape[1])
    ok = (segs[:, :, None] == segs[:, None, :]) & (at[:, None] <= at[None, :])
    return jnp.where(ok, 0.0, NEG).astype(F32)

def small_sums(sums, dkv):
    bias = sums[:11].reshape(16, 704)
    gain = sums[11:13].reshape(2, 16, 64).transpose(1, 0, 2).reshape(16, 128)
    both = jnp.concatenate([dkv[:10], dkv[16:26]], axis=1)
    pref = both.reshape(10, 16, 128).transpose(1, 0, 2).reshape(16, 1280)
    parts = jnp.concatenate([bias, gain, pref], axis=1)
    parts = jnp.pad(parts, ((0, 0), (0, 3072 - 2112))).reshape(16, 24, 128)
    mine = jnp.sum(swap_blocks(parts, 3), axis=0).reshape(3072)
    pref = mine[832:2112].reshape(10, 128).astype(B16)
    pref = jnp.pad(pref, ((0, 6), (0, 0)))
    got = swap_blocks(jnp.broadcast_to(pref[None], (16, 16, 128)), 4)
    got = got[:, :10].transpose(1, 0, 2).reshape(10, 2048)
    return mine[:704].reshape(1, 704), mine[704:832].reshape(1, 2, 64), got


def on_device(
    tokens,
    segment_ids,
    cotangent,
    w_qkv,
    w_attn_out,
    w_fc,
    w_proj,
    gains,
    biases,
    prefix_embed,
    reparam_in,
    reparam_in_bias,
    reparam_out,
    reparam_out_bias,
):
    pre_hidden = jnp.dot(prefix_embed, reparam_in, preferred_element_type=F32) + reparam_in_bias.astype(F32)
    hidden = jnp.tanh(pre_hidden)
    hidden_b = hidden.astype(B16)
    prefix_kv = (
        jnp.dot(hidden_b, reparam_out, preferred_element_type=F32) + reparam_out_bias.astype(F32)
    ).astype(B16)
    pkey, pval = prefix_blocks(prefix_kv[:, :1024]), prefix_blocks(prefix_kv[:, 1024:])
    small = gather_small(gains, biases)
    kept = forward_call(w_qkv, w_attn_out, w_fc, w_proj, tokens, small, row_mask(segment_ids), pkey, pval)
    dh, gq, go, gf, gp, sums, dkv = backward_call(kept[:1] + kept[2:], cotangent, small, pkey, pval)
    grad_biases, grad_gains, prefix_grad_b = small_sums(sums, dkv)
    grad_reparam_out = jnp.einsum("pr,pc->rc", hidden_b, prefix_grad_b, preferred_element_type=F32)
    grad_reparam_out_bias = jnp.sum(prefix_grad_b.astype(F32), axis=0)
    hidden_part = jnp.dot(prefix_grad_b, reparam_out.T, preferred_element_type=F32)
    hidden_grad = hidden_part + lax.ppermute(hidden_part, "section", [(0, 1), (1, 0)])
    dpre_hidden_b = (hidden_grad * (1.0 - hidden * hidden)).astype(B16)
    grad_reparam_in = jnp.einsum("pd,pr->dr", prefix_embed, dpre_hidden_b, preferred_element_type=F32)
    grad_reparam_in_bias = jnp.sum(dpre_hidden_b.astype(F32), axis=0)
    grad_prefix_embed = jnp.dot(dpre_hidden_b, reparam_in.T, preferred_element_type=F32)
    return (
        kept[1][None],
        dh[None],
        gq,
        go,
        gf,
        gp,
        grad_gains,
        grad_biases,
        grad_prefix_embed,
        grad_reparam_in,
        grad_reparam_in_bias,
        grad_reparam_out,
        grad_reparam_out_bias,
    )


def passed_along(shard, axis, by):
    size = lax.axis_size(axis)
    pairs = [(i, i + by) for i in range(size) if 0 <= i + by < size]
    return lax.ppermute(shard, axis, pairs)


def norm_rows(v, gain, shift):
    mean = jnp.mean(v, axis=-1, keepdims=True)
    cent = v - mean
    var = jnp.mean(cent * cent, axis=-1, keepdims=True)
    return cent * lax.rsqrt(var + EPS) * gain + shift


def gelu_tanh(v):
    return jax.nn.gelu(v, approximate=True)


def forward_layer(h_b, segs, pkey, pval, params):
    w_q, w_o, w_f, w_p, gain_pair, bias_all = params
    width = w_o.shape[0]
    length = h_b.shape[0]
    heads, head_dim = (pkey.shape[1], pkey.shape[2])
    scale = 1.0 / math.sqrt(head_dim)
    gain_f = gain_pair.astype(jnp.float32)
    bias_f = bias_all.astype(jnp.float32)
    hf = h_b.astype(jnp.float32)
    a1b = norm_rows(hf, gain_f[0], bias_f[9 * width : 10 * width]).astype(jnp.bfloat16)
    qkv_b = (jnp.dot(a1b, w_q, preferred_element_type=jnp.float32) + bias_f[: 3 * width]).astype(
        jnp.bfloat16
    )
    split = qkv_b.reshape(length, 3, heads, head_dim)
    query, keys, values = (split[:, 0], split[:, 1], split[:, 2])
    s_tok = jnp.einsum("lhe,mhe->hlm", query, keys, preferred_element_type=jnp.float32) * scale
    s_pre = jnp.einsum("lhe,phe->hlp", query, pkey, preferred_element_type=jnp.float32) * scale
    place = jnp.arange(length)
    allowed = (segs[:, None] == segs[None, :]) & (place[None, :] <= place[:, None])
    s_tok = jnp.where(allowed[None], s_tok, NEG)
    top = jnp.maximum(
        jnp.max(s_tok, axis=-1, keepdims=True), jnp.max(s_pre, axis=-1, keepdims=True)
    )
    e_tok = jnp.exp(s_tok - top)
    e_pre = jnp.exp(s_pre - top)
    total = jnp.sum(e_tok, axis=-1, keepdims=True) + jnp.sum(e_pre, axis=-1, keepdims=True)
    p_tok = e_tok / total
    p_pre = e_pre / total
    mixed = jnp.einsum(
        "hlm,mhe->lhe", p_tok.astype(jnp.bfloat16), values, preferred_element_type=jnp.float32
    ) + jnp.einsum(
        "hlp,phe->lhe", p_pre.astype(jnp.bfloat16), pval, preferred_element_type=jnp.float32
    )
    attn_b = mixed.reshape(length, width).astype(jnp.bfloat16)
    resid = hf + (
        jnp.dot(attn_b, w_o, preferred_element_type=jnp.float32) + bias_f[3 * width : 4 * width]
    )
    a2b = norm_rows(resid, gain_f[1], bias_f[10 * width : 11 * width]).astype(jnp.bfloat16)
    pre_act = jnp.dot(a2b, w_f, preferred_element_type=jnp.float32) + bias_f[4 * width : 8 * width]
    act_b = gelu_tanh(pre_act).astype(jnp.bfloat16)
    result = resid + (
        jnp.dot(act_b, w_p, preferred_element_type=jnp.float32) + bias_f[8 * width : 9 * width]
    )
    return (result, (hf, a1b, qkv_b, p_tok, p_pre, attn_b, resid, a2b, pre_act, act_b))


def backward_ffn(grad_out, keep, params):
    w_q, w_o, w_f, w_p, gain_pair, bias_all = params
    hf, a1b, qkv_b, p_tok, p_pre, attn_b, resid, a2b, pre_act, act_b = keep
    width = w_o.shape[0]
    gain_f = gain_pair.astype(jnp.float32)
    bias_f = bias_all.astype(jnp.float32)
    dm_b = grad_out.astype(jnp.bfloat16)
    grad_wp = jnp.einsum("lf,ld->fd", act_b, dm_b, preferred_element_type=jnp.float32)
    grad_bp = jnp.sum(dm_b.astype(jnp.float32), axis=0)
    d_act = jnp.dot(dm_b, w_p.T, preferred_element_type=jnp.float32)
    dpre_b = jax.vjp(gelu_tanh, pre_act)[1](d_act)[0].astype(jnp.bfloat16)
    grad_wf = jnp.einsum("ld,lf->df", a2b, dpre_b, preferred_element_type=jnp.float32)
    grad_bf = jnp.sum(dpre_b.astype(jnp.float32), axis=0)
    d_a2 = jnp.dot(dpre_b, w_f.T, preferred_element_type=jnp.float32)
    norm_back = jax.vjp(norm_rows, resid, gain_f[1], bias_f[10 * width : 11 * width])[1]
    d_resid_norm, grad_g2, grad_c2 = norm_back(d_a2)
    d_resid = grad_out + d_resid_norm
    return (d_resid, (grad_wf, grad_wp), (grad_bf, grad_bp, grad_g2, grad_c2))


def backward_attn(d_resid, keep, pkey, pval, params):
    w_q, w_o, w_f, w_p, gain_pair, bias_all = params
    hf, a1b, qkv_b, p_tok, p_pre, attn_b, resid, a2b, pre_act, act_b = keep
    width = w_o.shape[0]
    length = hf.shape[0]
    heads, head_dim = (pkey.shape[1], pkey.shape[2])
    prefix_len = pkey.shape[0]
    scale = 1.0 / math.sqrt(head_dim)
    gain_f = gain_pair.astype(jnp.float32)
    bias_f = bias_all.astype(jnp.float32)
    split = qkv_b.reshape(length, 3, heads, head_dim)
    query, keys, values = (split[:, 0], split[:, 1], split[:, 2])
    dat_b = d_resid.astype(jnp.bfloat16)
    grad_wo = jnp.einsum("ld,le->de", attn_b, dat_b, preferred_element_type=jnp.float32)
    grad_bo = jnp.sum(dat_b.astype(jnp.float32), axis=0)
    dattn_b = jnp.dot(dat_b, w_o.T, preferred_element_type=jnp.float32).astype(jnp.bfloat16)
    dattn_b = dattn_b.reshape(length, heads, head_dim)
    dp_tok = jnp.einsum("lhe,mhe->hlm", dattn_b, values, preferred_element_type=jnp.float32)
    dp_pre = jnp.einsum("lhe,phe->hlp", dattn_b, pval, preferred_element_type=jnp.float32)
    row_dot = jnp.sum(p_tok * dp_tok, axis=-1, keepdims=True) + jnp.sum(
        p_pre * dp_pre, axis=-1, keepdims=True
    )
    ds_tok = (p_tok * (dp_tok - row_dot)).astype(jnp.bfloat16)
    ds_pre = (p_pre * (dp_pre - row_dot)).astype(jnp.bfloat16)
    d_query = (
        jnp.einsum("hlm,mhe->lhe", ds_tok, keys, preferred_element_type=jnp.float32)
        + jnp.einsum("hlp,phe->lhe", ds_pre, pkey, preferred_element_type=jnp.float32)
    ) * scale
    d_keys = jnp.einsum("hlm,lhe->mhe", ds_tok, query, preferred_element_type=jnp.float32) * scale
    d_values = jnp.einsum(
        "hlm,lhe->mhe", p_tok.astype(jnp.bfloat16), dattn_b, preferred_element_type=jnp.float32
    )
    grad_pkey = (
        jnp.einsum("hlp,lhe->phe", ds_pre, query, preferred_element_type=jnp.float32) * scale
    )
    grad_pval = jnp.einsum(
        "hlp,lhe->phe", p_pre.astype(jnp.bfloat16), dattn_b, preferred_element_type=jnp.float32
    )
    dqkv_b = (
        jnp.stack([d_query, d_keys, d_values], axis=1)
        .reshape(length, 3 * width)
        .astype(jnp.bfloat16)
    )
    grad_wq = jnp.einsum("ld,lc->dc", a1b, dqkv_b, preferred_element_type=jnp.float32)
    grad_bq = jnp.sum(dqkv_b.astype(jnp.float32), axis=0)
    d_a1 = jnp.dot(dqkv_b, w_q.T, preferred_element_type=jnp.float32)
    norm_back_first = jax.vjp(norm_rows, hf, gain_f[0], bias_f[9 * width : 10 * width])[1]
    d_in_norm, grad_g1, grad_c1 = norm_back_first(d_a1)
    d_input = d_resid + d_in_norm
    grad_prefix = jnp.concatenate(
        [grad_pkey.reshape(prefix_len, width), grad_pval.reshape(prefix_len, width)], axis=1
    )
    return (d_input, (grad_wq, grad_wo), (grad_bq, grad_bo, grad_g1, grad_c1), grad_prefix)


def assemble(ffn_mats, ffn_small, attn_mats, attn_small):
    grad_bf, grad_bp, grad_g2, grad_c2 = ffn_small
    grad_bq, grad_bo, grad_g1, grad_c1 = attn_small
    grad_gains = jnp.stack([grad_g1, grad_g2])
    grad_bias = jnp.concatenate([grad_bq, grad_bo, grad_bf, grad_bp, grad_c1, grad_c2])
    return (attn_mats[0], attn_mats[1], ffn_mats[0], ffn_mats[1], grad_gains, grad_bias)


def on_device_general(
    tokens,
    segment_ids,
    cotangent,
    w_qkv,
    w_attn_out,
    w_fc,
    w_proj,
    gains,
    biases,
    prefix_embed,
    reparam_in,
    reparam_in_bias,
    reparam_out,
    reparam_out_bias,
):
    section = lax.axis_index("section")
    micro, row_len = segment_ids.shape
    width = tokens.shape[1]
    prefix_len = prefix_embed.shape[0]
    head_dim = width // HEADS
    gathered = (
        lax.all_gather(w_qkv, "dp", axis=1, tiled=True),
        lax.all_gather(w_attn_out, "dp", axis=1, tiled=True),
        lax.all_gather(w_fc, "dp", axis=1, tiled=True),
        lax.all_gather(w_proj, "dp", axis=1, tiled=True),
        lax.all_gather(gains, "dp", axis=2, tiled=True),
        lax.all_gather(biases, "dp", axis=1, tiled=True),
    )
    params = tuple((item[0] for item in gathered))
    pre_hidden = jnp.dot(
        prefix_embed, reparam_in, preferred_element_type=jnp.float32
    ) + reparam_in_bias.astype(jnp.float32)
    hidden = jnp.tanh(pre_hidden)
    hidden_b = hidden.astype(jnp.bfloat16)
    prefix_kv = (
        jnp.dot(hidden_b, reparam_out, preferred_element_type=jnp.float32)
        + reparam_out_bias.astype(jnp.float32)
    ).astype(jnp.bfloat16)
    pkey = prefix_kv[:, :width].reshape(prefix_len, HEADS, head_dim)
    pval = prefix_kv[:, width:].reshape(prefix_len, HEADS, head_dim)
    token_rows = tokens.reshape(micro, row_len, width)
    cot_rows = cotangent.reshape(micro, row_len, width)
    received = jnp.zeros((row_len, width), jnp.bfloat16)
    outputs = jnp.zeros((micro, row_len, width), jnp.bfloat16)
    stored = []
    for tick in range(micro + 1):
        index = tick - section
        active = (index >= 0) & (index < micro)
        slot = jnp.clip(index, 0, micro - 1)
        segs = segment_ids[slot]
        h_b = jnp.where(section == 0, token_rows[slot], received)
        result, keep = forward_layer(h_b, segs, pkey, pval, params)
        result_b = result.astype(jnp.bfloat16)
        outputs = jnp.where(active, outputs.at[slot].set(result_b), outputs)
        stored.append(keep)
        if tick < micro:
            received = passed_along(result_b, "section", 1)
    regathered = (
        lax.all_gather(w_qkv, "dp", axis=1, tiled=True),
        lax.all_gather(w_attn_out, "dp", axis=1, tiled=True),
        lax.all_gather(w_fc, "dp", axis=1, tiled=True),
        lax.all_gather(w_proj, "dp", axis=1, tiled=True),
        lax.all_gather(gains, "dp", axis=2, tiled=True),
        lax.all_gather(biases, "dp", axis=1, tiled=True),
    )
    params_back = tuple((item[0] for item in regathered))
    stacked = jax.tree.map(lambda *items: jnp.stack(items), *stored)
    coming = jnp.zeros((row_len, width), jnp.bfloat16)
    in_grads = jnp.zeros((micro, row_len, width), jnp.bfloat16)
    grad_total = None
    prefix_total = None
    for tick in range(micro + 1):
        index = micro - tick - section
        active = (index >= 0) & (index < micro)
        slot = jnp.clip(index, 0, micro - 1)
        segs = segment_ids[slot]
        saved = jax.tree.map(lambda item: item[slot + section], stacked)
        grad_out = jnp.where(
            section == 1, cot_rows[slot].astype(jnp.float32), coming.astype(jnp.float32)
        )
        keep = saved
        d_resid, ffn_mats, ffn_small = backward_ffn(grad_out, keep, params_back)
        ffn_mats = jax.tree.map(
            lambda item: jnp.where(active, item, jnp.zeros_like(item)), ffn_mats
        )
        ffn_small = jax.tree.map(
            lambda item: jnp.where(active, item, jnp.zeros_like(item)), ffn_small
        )
        d_input, attn_mats, attn_small, grad_prefix = backward_attn(
            d_resid, keep, pkey, pval, params_back
        )
        attn_mats = jax.tree.map(
            lambda item: jnp.where(active, item, jnp.zeros_like(item)), attn_mats
        )
        attn_small = jax.tree.map(
            lambda item: jnp.where(active, item, jnp.zeros_like(item)), attn_small
        )
        grad_prefix = jnp.where(active, grad_prefix, jnp.zeros_like(grad_prefix))
        grads = assemble(ffn_mats, ffn_small, attn_mats, attn_small)
        if grad_total is None:
            grad_total = grads
            prefix_total = grad_prefix
        else:
            grad_total = jax.tree.map(lambda left, right: left + right, grad_total, grads)
            prefix_total = prefix_total + grad_prefix
        d_input_b = d_input.astype(jnp.bfloat16)
        in_grads = jnp.where(active, in_grads.at[slot].set(d_input_b), in_grads)
        if tick < micro:
            coming = passed_along(d_input_b, "section", -1)
    lifted = tuple((item[None] for item in grad_total))
    weight_grads = (
        lax.psum_scatter(lifted[0], "dp", scatter_dimension=1, tiled=True),
        lax.psum_scatter(lifted[1], "dp", scatter_dimension=1, tiled=True),
        lax.psum_scatter(lifted[2], "dp", scatter_dimension=1, tiled=True),
        lax.psum_scatter(lifted[3], "dp", scatter_dimension=1, tiled=True),
        lax.psum_scatter(lifted[4], "dp", scatter_dimension=2, tiled=True),
        lax.psum_scatter(lifted[5], "dp", scatter_dimension=1, tiled=True),
    )
    prefix_grad = lax.psum(prefix_total, "dp")
    prefix_grad_b = prefix_grad.astype(jnp.bfloat16)
    grad_reparam_out = jnp.einsum(
        "pr,pc->rc", hidden_b, prefix_grad_b, preferred_element_type=jnp.float32
    )
    grad_reparam_out_bias = jnp.sum(prefix_grad_b.astype(jnp.float32), axis=0)
    hidden_part = jnp.dot(prefix_grad_b, reparam_out.T, preferred_element_type=jnp.float32)
    hidden_grad = lax.psum(hidden_part, "section")
    dpre_hidden_b = (hidden_grad * (1.0 - hidden * hidden)).astype(jnp.bfloat16)
    grad_reparam_in = jnp.einsum(
        "pd,pr->dr", prefix_embed, dpre_hidden_b, preferred_element_type=jnp.float32
    )
    grad_reparam_in_bias = jnp.sum(dpre_hidden_b.astype(jnp.float32), axis=0)
    grad_prefix_embed = jnp.dot(dpre_hidden_b, reparam_in.T, preferred_element_type=jnp.float32)
    layer_outs = outputs.reshape(1, micro * row_len, width)
    input_grads = in_grads.reshape(1, micro * row_len, width)
    return (
        layer_outs,
        input_grads,
        weight_grads[0],
        weight_grads[1],
        weight_grads[2],
        weight_grads[3],
        weight_grads[4],
        weight_grads[5],
        grad_prefix_embed,
        grad_reparam_in,
        grad_reparam_in_bias,
        grad_reparam_out,
        grad_reparam_out_bias,
    )


def solution(mesh):
    return jax.shard_map(
        on_device if mesh.shape["dp"] == 16 else on_device_general,
        mesh=mesh,
        in_specs=(
            P("dp", None),
            P("dp", None),
            P("dp", None),
            P("section", "dp", None),
            P("section", "dp", None),
            P("section", "dp", None),
            P("section", "dp", None),
            P("section", None, "dp"),
            P("section", "dp"),
            P(),
            P(),
            P(),
            P(None, "section"),
            P("section"),
        ),
        out_specs=(
            P("section", "dp", None),
            P("section", "dp", None),
            P("section", "dp", None),
            P("section", "dp", None),
            P("section", "dp", None),
            P("section", "dp", None),
            P("section", None, "dp"),
            P("section", "dp"),
            P(),
            P(),
            P(),
            P(None, "section"),
            P("section"),
        ),
        check_vma=False,
    )
```

```python
import math

import jax
import jax.numpy as jnp
from jax import lax
from jax.experimental import pallas as pl
from jax.experimental.pallas import tpu as pltpu
from jax.sharding import PartitionSpec as P

HEADS = 16
EPS = 1e-05
NEG = -1000000000.0
MESH = pl.DeviceIdType.MESH
F32 = jnp.float32
B16 = jnp.bfloat16
NP = 12


def place():
    s = lax.axis_index("section"); d = lax.axis_index("dp")
    return s, d, d // 4, (d // 2) % 2, d % 2

def greet(s, d):
    bar = pltpu.get_barrier_semaphore()
    for i in range(1, 16):
        pl.semaphore_signal(bar, 1, device_id=(s, (d + i) % 16), device_id_type=MESH)
    pl.semaphore_signal(bar, 1, device_id=(1 - s, d), device_id_type=MESH)
    pl.semaphore_wait(bar, 16)


def to_all(src, dst, ss, rs):
    s, d = lax.axis_index("section"), lax.axis_index("dp")

    def cp(i, frm):
        to = (d + i) % 16
        return pltpu.make_async_remote_copy(
            src(to), dst.at[frm], ss.at[i], rs.at[i], device_id=(s, to), device_id_type=MESH
        )

    def start():
        for i in range(1, 16):
            cp(i, d).start()

    def arrive():
        for i in range(1, 16):
            cp(i, (d + 16 - i) % 16).wait_recv()

    def finish():
        for i in range(1, 16):
            cp(i, d).wait_send()

    return start, arrive, finish


class Gather:
    def __init__(self, W, ssem, rsem):
        self.W, self.ssem, self.rsem = W, ssem, rsem
        self.s, self.d, self.z, self.y, self.c = place()
    def blk(self, k, d):
        i = k // 8
        row = (1-i)*(1024*k+64*d) + i*(8192+256*d+64*(k-8))
        return self.W.at[pl.ds(pl.multiple_of(row, 64), 64)]
    def cp(self, k, origin, target, slot):
        b = self.blk(k, origin)
        return pltpu.make_async_remote_copy(src_ref=b, dst_ref=b, send_sem=self.ssem.at[k, slot], recv_sem=self.rsem.at[k, origin],
            device_id=(self.s, target), device_id_type=MESH)
    def dev(self, z, y, c): return z*4+y*2+c
    def arrived(self, k, origin): self.cp(k, origin, origin, 0).wait_recv()
    def to_up(self, k, zo, op):
        op(self.cp(k, self.dev(zo, self.y, self.c), self.dev(self.z+1, self.y, self.c), zo))
    def to_down(self, k, zo, op):
        op(self.cp(k, self.dev(zo, self.y, self.c), self.dev(self.z-1, self.y, self.c), 4+zo))
    def to_y(self, k, zo, op):
        op(self.cp(k, self.dev(zo, self.y, self.c), self.dev(self.z, 1-self.y, self.c), 8+zo))
    def to_c(self, k, zo, yo, op):
        op(self.cp(k, self.dev(zo, yo, self.c), self.dev(self.z, self.y, 1-self.c), 12+zo*2+yo))
    def step(self, t, own):
        z, y, c = self.z, self.y, self.c
        start = lambda cp: cp.start()
        @pl.when(t < NP)
        def _():
            own(t)
            self.to_y(t, z, start)
            @pl.when(z < 3)
            def _(): self.to_up(t, z, start)
            @pl.when(z > 0)
            def _(): self.to_down(t, z, start)
            self.to_c(t, z, y, start)
        for q in (1, 2, 3, 4):
            k = t - q
            ok = (k >= 0) & (k < NP)
            if q < 4:
                @pl.when(ok & (z - q >= 0))
                def _():
                    self.arrived(k, self.dev(z-q, y, c))
                    @pl.when(z < 3)
                    def _(): self.to_up(k, z-q, start)
                    self.to_y(k, z-q, start)
                    self.to_c(k, z-q, y, start)
                @pl.when(ok & (z + q <= 3))
                def _():
                    self.arrived(k, self.dev(z+q, y, c))
                    @pl.when(z > 0)
                    def _(): self.to_down(k, z+q, start)
                    self.to_y(k, z+q, start)
                    self.to_c(k, z+q, y, start)
            e = q - 1
            def side(zo):
                self.arrived(k, self.dev(zo, 1-y, c))
                self.to_c(k, zo, 1-y, start)
            if e == 0:
                @pl.when(ok)
                def _(): side(z)
            else:
                @pl.when(ok & (z - e >= 0))
                def _(): side(z-e)
                @pl.when(ok & (z + e <= 3))
                def _(): side(z+e)
    def complete(self, k):
        for i in range(8):
            self.arrived(k, 2*i + 1-self.c)
    def drain(self):
        fin = lambda cp: cp.wait_send()
        z, y = self.z, self.y
        @pl.loop(0, NP)
        def _(k):
            for zo in range(4):
                @pl.when((zo <= z) & (z < 3))
                def _(): self.to_up(k, zo, fin)
                @pl.when((zo >= z) & (z > 0))
                def _(): self.to_down(k, zo, fin)
                self.to_y(k, zo, fin)
                for yo in range(2): self.to_c(k, zo, yo, fin)

def own_copies(wq, wo, wf, wp, g, sem):
    out = []
    for k in range(NP):
        if k < 3: src = wq.at[0, :, pl.ds(1024*k, 1024)]
        elif k == 3: src = wo.at[0]
        elif k < 8: src = wf.at[0, :, pl.ds(1024*(k-4), 1024)]
        else: src = wp.at[0, pl.ds(64*(k-8), 64)]
        out.append(pltpu.make_async_copy(src, g.blk(jnp.int32(k), g.d), sem.at[k]))
    return out


HALF = 256
STAGES = 12
GELU_C = math.sqrt(2.0 / math.pi)


def dot_nn(a, b):
    return lax.dot_general(a, b, (((1,), (0,)), ((), ())), preferred_element_type=F32)


def dot_nt(a, b):
    return lax.dot_general(a, b, (((1,), (1,)), ((), ())), preferred_element_type=F32)


def dot_tn(a, b):
    return lax.dot_general(a, b, (((0,), (0,)), ((), ())), preferred_element_type=F32)


def whiten(v):
    mean = jnp.mean(v, axis=-1, keepdims=True)
    cent = v - mean
    rstd = lax.rsqrt(jnp.mean(cent * cent, axis=-1, keepdims=True) + EPS)
    return cent * rstd, rstd


def split_heads(pair):
    left = lax.broadcasted_iota(jnp.int32, pair.shape, 1) < 64
    zero = jnp.zeros_like(pair)
    return jnp.concatenate([jnp.where(left, pair, zero), jnp.where(left, zero, pair)], axis=0)


def forward_kernel(
    wq, wo, wf, wp, tokens, segs, pack, aux, r_in, r_out,
    W_o, out_o, h_o, a1_o, qkv_o, prob_o, ppre_o, att_o, res_o, a2_o, gp_o, act_o, small_o, pkey_o, pval_o, hid_o,
    W, H, A1, QKV, PROB, PPRE, ATT, RES, A2, GP, ACT, OUT, SPRE, ACC, small, pkey, pval, hid, mask, PACKS, ROWS,
    own_sem, ssem, rsem, hsem, xs, xr, save_sem, ps, pr, psem,
):
    g = Gather(W, ssem, rsem)
    s = g.s
    for cp in own_copies(wq, wo, wf, wp, g, own_sem):
        cp.start()
    r_in_parts = [pltpu.make_async_copy(r_in.at[pl.ds(512 * i, 512)], ACT.at[2, :, pl.ds(512 * i, 512)], psem.at[i]) for i in range(2)]
    r_out_parts = [pltpu.make_async_copy(r_out.at[:, pl.ds(1024 * i, 1024)], ACT.at[i], psem.at[2 + i]) for i in range(2)]
    for cp in r_in_parts + r_out_parts:
        cp.start()
    greet(s, g.d)
    send_packs, packs_in, packs_out = to_all(lambda to: pack, PACKS, ps, pr)

    def prep_saves():
        pairs = [(small, small_o), (pkey, pkey_o), (pval, pval_o), (hid, hid_o)]
        return [pltpu.make_async_copy(a, b, psem.at[4 + i]) for i, (a, b) in enumerate(pairs)]

    def prepare():
        for cp in r_in_parts + r_out_parts:
            cp.wait()
        ph = dot_nn(aux[:, :512], ACT[2, :, :512]) + dot_nn(aux[:, 512:], ACT[2, :, 512:])
        hid[...] = jnp.tanh(ph + aux[10:11, :512].astype(F32))
        hb = hid[...].astype(B16)
        head = lax.broadcasted_iota(jnp.int32, (16, 1024), 1) // 64
        for i, big in enumerate((pkey, pval)):
            kv = (dot_nn(hb, ACT[i]) + aux[11 + i : 12 + i].astype(F32)).astype(B16)
            for h in range(16):
                big[16 * h : 16 * h + 16] = jnp.where(head == h, kv, jnp.zeros_like(kv))
        key = lax.broadcasted_iota(jnp.int32, (HALF, HALF), 0)
        query = lax.broadcasted_iota(jnp.int32, (HALF, HALF), 1)
        for b in range(2):
            by_query = jnp.broadcast_to(segs[b : b + 1].astype(F32), (HALF, HALF))
            ok = (by_query.T == by_query) & (key <= query)
            mask[b] = jnp.where(ok, 0.0, NEG)
        packs_in()
        ROWS[...] = PACKS[...].astype(F32)
        left = lax.broadcasted_iota(jnp.int32, (1, 128), 1) < 64
        small[...] = jnp.zeros_like(small)
        for n in range(104):
            row, at = n // 8, 128 * (n % 8)
            if row < 11:
                (d0, r0), (d1, r1) = divmod(2 * n, 11), divmod(2 * n + 1, 11)
            else:
                (d0, r0), (d1, r1) = (2 * (n % 8), row), (2 * (n % 8) + 1, row)
            small[row : row + 1, at : at + 128] = jnp.where(left, ROWS[d0, r0 : r0 + 1], ROWS[d1, r1 : r1 + 1])
        for cp in prep_saves():
            cp.start()

    send_packs()
    PACKS[g.d] = pack[...]

    def tokens_in():
        return pltpu.make_async_copy(tokens, H, hsem)

    def half(b):
        return pl.ds(pl.multiple_of(b * HALF, HALF), HALF)

    def cross(b):
        return pltpu.make_async_remote_copy(
            OUT.at[half(b)], H.at[half(b)], xs.at[b], xr.at[b], device_id=(1 - s, g.d), device_id_type=MESH
        )

    @pl.when(s == 0)
    def _():
        tokens_in().start()

    def own(t):
        b = g.blk(t, g.d)
        pltpu.make_async_copy(b, b, own_sem.at[t]).wait()

    def rows_of(k):
        return pl.ds(pl.multiple_of(k * 1024, 1024), 1024)

    def saves(b):
        r = half(b)
        pairs = [
            (H.at[r], h_o.at[r]), (A1.at[r], a1_o.at[r]), (QKV.at[:, r], qkv_o.at[:, r]), (PROB.at[pl.ds(2 * b, 2)], prob_o.at[pl.ds(2 * b, 2)]),
            (PPRE.at[b], ppre_o.at[b]), (ATT.at[r], att_o.at[r]), (RES.at[r], res_o.at[r]), (A2.at[r], a2_o.at[r]),
            (GP.at[:, r], gp_o.at[:, r]), (ACT.at[:, r], act_o.at[:, r]), (OUT.at[r], out_o.at[r]),
        ]
        return [pltpu.make_async_copy(src, dst, save_sem.at[b, i]) for i, (src, dst) in enumerate(pairs)]

    def piece_out(k):
        return pltpu.make_async_copy(W.at[rows_of(k)], W_o.at[rows_of(k)], save_sem.at[2, k])

    def norm_in(b):
        @pl.when(s == 0)
        def _():
            @pl.when(b == 0)
            def _():
                tokens_in().wait()

        @pl.when(s == 1)
        def _():
            cross(b).wait_recv()

        xhat, _ = whiten(H[half(b)].astype(F32))
        A1[half(b)] = (xhat * small[11:12] + small[9:10]).astype(B16)
        saves(b)[0].start()
        saves(b)[1].start()

    def project(i, b):
        v = dot_nn(A1[half(b)], W[rows_of(i)]) + small[pl.ds(i, 1)]
        v = v.astype(B16)
        QKV[i, half(b)] = v * jnp.where(i == 0, 0.125, 1.0).astype(B16)

        @pl.when(i == 2)
        def _():
            saves(b)[2].start()

    def attend(part, b):
        @pl.when(part == 0)
        def _():
            sp = dot_nt(pkey[...], QKV[0, half(b)])
            there = lax.broadcasted_iota(jnp.int32, sp.shape, 0) % 16 < 10
            SPRE[b] = jnp.where(there, sp, NEG)

        @pl.loop(part * 4, part * 4 + 4)
        def _(p):
            cols = pl.ds(pl.multiple_of(p * 128, 128), 128)
            q2, k2, v2 = QKV[0, half(b), cols], QKV[1, half(b), cols], QKV[2, half(b), cols]
            st = dot_nt(split_heads(k2), q2)
            probs, pres = [], []
            for e in range(2):
                sh = st[e * HALF : (e + 1) * HALF] + mask[b]
                sp = SPRE[b, pl.ds(pl.multiple_of(p * 32 + e * 16, 16), 16)]
                top = jnp.maximum(jnp.max(sh, axis=0, keepdims=True), jnp.max(sp, axis=0, keepdims=True))
                et, ep = jnp.exp(sh - top), jnp.exp(sp - top)
                inv = 1.0 / (jnp.sum(et, axis=0, keepdims=True) + jnp.sum(ep, axis=0, keepdims=True))
                probs.append((et * inv).astype(B16))
                pres.append((ep * inv).astype(B16))
            pr = jnp.concatenate(probs, axis=0)
            PROB[2 * b + p // 4, :, pl.ds(pl.multiple_of((p % 4) * HALF, HALF), HALF)] = pr
            PPRE[b, pl.ds(pl.multiple_of(p * 32, 32), 32)] = jnp.concatenate(pres, axis=0)
            ACC[half(b), cols] = dot_tn(pr, split_heads(v2))

        @pl.when(part == 1)
        def _():
            ATT[half(b)] = (ACC[half(b)] + dot_tn(PPRE[b], pval[...])).astype(B16)
            saves(b)[3].start()
            saves(b)[4].start()
            saves(b)[5].start()

    def mix(b):
        r = H[half(b)].astype(F32) + (dot_nn(ATT[half(b)], W[rows_of(3)]) + small[3:4])
        RES[half(b)] = r
        xhat, _ = whiten(r)
        A2[half(b)] = (xhat * small[12:13] + small[10:11]).astype(B16)
        saves(b)[6].start()
        saves(b)[7].start()

    def widen(j, b):
        x = dot_nn(A2[half(b)], W[rows_of(4 + j)]) + small[pl.ds(4 + j, 1)]
        x2 = x * x
        t = jnp.tanh(GELU_C * (x + 0.044715 * (x2 * x)))
        ACT[j, half(b)] = (0.5 * x * (1.0 + t)).astype(B16)
        GP[j, half(b)] = (
            0.5 * (1.0 + t) + (0.5 * GELU_C) * x * (1.0 - t * t) * (1.0 + (3 * 0.044715) * x2)
        ).astype(B16)

        @pl.when(j == 3)
        def _():
            saves(b)[8].start()
            saves(b)[9].start()

    def narrow(b):
        v = RES[half(b)] + small[8:9]
        for j in range(4):
            v = v + dot_nn(ACT[j, half(b)], W[rows_of(8 + j)])
        OUT[half(b)] = v.astype(B16)

        @pl.when(s == 0)
        def _():
            cross(b).start()

        saves(b)[10].start()

    @pl.loop(0, NP + 5 + 2 * STAGES)
    def _(tick):
        @pl.when(tick < NP + 5)
        def _():
            g.step(tick, own)

            @pl.when(tick == 3)
            def _():
                prepare()

            @pl.when(tick >= 5)
            def _():
                g.complete(tick - 5)

                @pl.when(tick < 13)
                def _():
                    piece_out(tick - 5).start()

                @pl.when(tick == NP + 4)
                def _():
                    for k in range(8, NP):
                        piece_out(k).start()

        late = tick - (NP + 5)
        stage = (1 - s) * (tick - 5) + s * ((late + STAGES) % STAGES - STAGES * (late < 0).astype(jnp.int32))
        lo = s * (late // STAGES)
        hi = (1 - s) * 2 + s * (late // STAGES + 1)

        def when(i, body):
            @pl.when(stage == i)
            def _():
                pl.loop(lo, hi)(body)

        when(0, norm_in)

        @pl.when((stage >= 1) & (stage < 4))
        def _():
            pl.loop(lo, hi)(lambda b: project(stage - 1, b))

        @pl.when((stage >= 4) & (stage < 6))
        def _():
            pl.loop(lo, hi)(lambda b: attend(stage - 4, b))

        when(6, mix)

        @pl.when((stage >= 7) & (stage < 11))
        def _():
            pl.loop(lo, hi)(lambda b: widen(stage - 7, b))

        when(11, narrow)

    g.drain()
    packs_out()
    for cp in prep_saves():
        cp.wait()

    @pl.loop(0, NP)
    def _(k):
        piece_out(k).wait()

    @pl.loop(0, 2)
    def _(b):
        for cp in saves(b):
            cp.wait()

        @pl.when(s == 0)
        def _():
            cross(b).wait_send()


def forward_call(wq, wo, wf, wp, tokens, segs, pack, aux, r_in, r_out):
    any_, vm = pl.BlockSpec(memory_space=pl.ANY), pl.BlockSpec(memory_space=pltpu.VMEM)
    n, d = tokens.shape
    kept = [
        ((NP * d, d), B16), ((n, d), B16), ((n, d), B16), ((n, d), B16), ((3, n, d), B16), ((4, n, d), B16),
        ((2, HALF, HALF), B16), ((n, d), B16), ((n, d), F32), ((n, d), B16), ((4, n, d), B16), ((4, n, d), B16),
    ]
    shared = [((16, d), F32), ((HALF, d), B16), ((HALF, d), B16), ((16, 512), F32)]
    dma = pltpu.SemaphoreType.DMA
    order = [0, 2, 3, 4, 5, 6, 7, 8, 9, 10, 11, 1]
    scratch = [kept[i] for i in order] + [((2, HALF, HALF), F32), ((n, d), F32)] + shared
    scratch += [((2, HALF, HALF), F32), ((16, 16, 128), B16), ((16, 16, 128), F32)]
    return pl.pallas_call(
        forward_kernel,
        out_shape=[jax.ShapeDtypeStruct(*k) for k in kept + shared],
        in_specs=[any_] * 5 + [vm] * 3 + [any_] * 2,
        out_specs=[any_] * len(kept + shared),
        scratch_shapes=[pltpu.VMEM(*v) for v in scratch]
        + [dma((NP,)), dma((NP, 20)), dma((NP, 16)), dma, dma((2,)), dma((2,)), dma((3, NP)), dma((16,)), dma((16,)), dma((8,))],
        compiler_params=pltpu.CompilerParams(collective_id=0, has_side_effects=True, vmem_limit_bytes=62 << 20),
    )(wq, wo, wf, wp, tokens, segs, pack, aux, r_in, r_out)


def own_pack(gains, biases):
    rows = jnp.concatenate([biases.reshape(11, 64), gains.reshape(2, 64), jnp.zeros((3, 64), B16)])
    return jnp.concatenate([rows, rows], axis=1)


def prefix_rows(embed, in_bias, out_bias):
    in_bias = jnp.pad(in_bias, (0, 512)).reshape(1, 1024)
    return jnp.concatenate([embed, in_bias, out_bias.reshape(2, 1024), jnp.zeros((3, 1024), B16)])


SPLIT = 6
BACK_TICKS = 2 + 2 * SPLIT + NP + 6


def unwhiten(grad, xhat, rstd):
    return rstd * (
        grad
        - jnp.mean(grad, axis=-1, keepdims=True)
        - xhat * jnp.mean(grad * xhat, axis=-1, keepdims=True)
    )


def column_sum(v):
    return jnp.sum(v.astype(F32), axis=0, keepdims=True)


def backward_kernel(
    W_i, h_i, a1_i, qkv_i, prob_i, ppre_i, att_i, res_i, a2_i, gp_i, act_i, cot, r_out, small, pkey, pval,
    dh_o, oq, oo, of, op_, own_sums, KVB, HSUM,
    WG, H, A1, QKV, BIG, PPRE, ATT, RES, A2, GP, DM, DAT, DATT, DPP, DSP, ACC,
    RC, RY, RU, RD, T, SG, DKV, SB, RB, PF, PG, HP, HPR,
    wsem, lsem, osem, cs, cr, ys, yr, us, ur, ds_, dr, xs, xr, hs, bs, br, ps, pr, hx,
):
    s, d, z, y, c = place()
    for k in (8, 9, 10, 11, 4, 5, 6, 7, 3, 2, 1, 0):
        pltpu.make_async_copy(W_i.at[k], WG.at[k], wsem.at[k]).start()

    def loads():
        pairs = [
            (gp_i, GP), (a2_i, A2), (res_i, RES), (att_i, ATT), (qkv_i, QKV), (ppre_i, PPRE), (a1_i, A1), (h_i, H),
            (act_i, BIG), (prob_i, BIG), (cot, DM),
        ]
        return [pltpu.make_async_copy(a, b, lsem.at[i]) for i, (a, b) in enumerate(pairs)]

    L_GP, L_A2, L_RES, L_ATT, L_QKV, L_PPRE, L_A1, L_H, L_ACT, L_PROB, L_COT = range(11)

    @pl.when(s == 1)
    def _():
        loads()[L_COT].start()

    loads()[L_GP].start()
    for i in (L_A2, L_RES, L_ATT, L_QKV, L_PPRE):
        loads()[i].start()

    @pl.when(s == 0)
    def _():
        loads()[L_ACT].start()

    @pl.when(s == 1)
    def _():
        loads()[L_PROB].start()

    for i in (L_A1, L_H):
        loads()[i].start()
    SG[...] = jnp.zeros_like(SG)
    DKV[...] = jnp.zeros_like(DKV)
    SB[...] = jnp.zeros_like(SB)
    greet(s, d)

    def weights(ks):
        for k in ks:
            pltpu.make_async_copy(W_i.at[k], WG.at[k], wsem.at[k]).wait()

    def half(b):
        return pl.ds(pl.multiple_of(b * HALF, HALF), HALF)

    def weight(k):
        return WG[k].reshape(1024, 1024)

    def cross(b):
        return pltpu.make_async_remote_copy(
            H.at[half(b)], DM.at[half(b)], xs.at[b], xr.at[b], device_id=(1 - s, d), device_id_type=MESH
        )

    def dh_out(b):
        return pltpu.make_async_copy(H.at[half(b)], dh_o.at[half(b)], hs.at[b])

    def ffn_in(b):
        first = (b == 0)

        @pl.when(first)
        def _():
            @pl.when(s == 1)
            def _():
                loads()[L_COT].wait()

            weights((8, 9, 10, 11))
            loads()[L_GP].wait()

        @pl.when(s == 0)
        def _():
            cross(b).wait_recv()

        for j in range(4):
            GP[j, half(b)] = (dot_nt(DM[half(b)], weight(8 + j)) * GP[j, half(b)].astype(F32)).astype(B16)

    def ffn_norm(b):
        @pl.when(b == 0)
        def _():
            weights((4, 5, 6, 7))
            loads()[L_A2].wait()
            loads()[L_RES].wait()

        grad = dot_nt(GP[0, half(b)], weight(4))
        for j in range(1, 4):
            grad = grad + dot_nt(GP[j, half(b)], weight(4 + j))
        xhat, rstd = whiten(RES[half(b)])
        SG[10:11] += jnp.sum(grad, axis=0, keepdims=True)
        SG[12:13] += jnp.sum(grad * xhat, axis=0, keepdims=True)
        res = DM[half(b)].astype(F32) + unwhiten(grad * small[12:13], xhat, rstd)
        RES[half(b)] = res
        DAT[half(b)] = res.astype(B16)

    def attn_out(b):
        @pl.when(b == 0)
        def _():
            weights((3,))
            for i in (L_ATT, L_QKV, L_PPRE):
                loads()[i].wait()

            loads()[L_PROB].wait()

        DATT[...] = dot_nt(DAT[half(b)], weight(3)).astype(B16)
        DPP[...] = dot_nt(pval[...], DATT[...])

    def attn_back(part, b):
        @pl.loop(part * 4, part * 4 + 4)
        def _(p):
            cols = pl.ds(pl.multiple_of(p * 128, 128), 128)
            q2, k2, v2 = QKV[0, half(b), cols], QKV[1, half(b), cols], QKV[2, half(b), cols]
            do2 = DATT[:, cols]
            pr = BIG[2 * b + p // 4, :, pl.ds(pl.multiple_of((p % 4) * HALF, HALF), HALF)]
            dp = dot_nt(split_heads(v2), do2)
            dss, pres = [], []
            for e in range(2):
                ph = pr[e * HALF : (e + 1) * HALF].astype(F32)
                dh = dp[e * HALF : (e + 1) * HALF]
                at = pl.ds(pl.multiple_of(p * 32 + e * 16, 16), 16)
                pp, dpp = PPRE[b, at].astype(F32), DPP[at]
                dot = jnp.sum(ph * dh, axis=0, keepdims=True) + jnp.sum(pp * dpp, axis=0, keepdims=True)
                dss.append((ph * (dh - dot)).astype(B16))
                pres.append((pp * (dpp - dot)).astype(B16))
            ds = jnp.concatenate(dss, axis=0)
            DSP[pl.ds(pl.multiple_of(p * 32, 32), 32)] = jnp.concatenate(pres, axis=0)
            left = lax.broadcasted_iota(jnp.int32, (HALF, 128), 1) < 64
            ACC[:, cols] = dot_tn(ds, split_heads(k2))
            dk = dot_nn(ds, q2)
            dv = dot_nn(pr, do2)
            QKV[1, half(b), cols] = jnp.where(left, dk[:HALF], dk[HALF:]).astype(B16)
            QKV[2, half(b), cols] = jnp.where(left, dv[:HALF], dv[HALF:]).astype(B16)

        @pl.when(part == 1)
        def _():
            def own_rows(full):
                out = jnp.zeros((16, 1024), F32)
                head = lax.broadcasted_iota(jnp.int32, (16, 1024), 1) // 64
                for i in range(16):
                    out = out + jnp.where(head == i, full[16 * i : 16 * i + 16], 0.0)
                return out

            DKV[0:16] += own_rows(dot_nn(DSP[...], QKV[0, half(b)]))
            DKV[16:32] += own_rows(dot_nn(PPRE[b], DATT[...]))
            QKV[0, half(b)] = ((ACC[...] + dot_tn(DSP[...], pkey[...])) * 0.125).astype(B16)

    def attn_norm(b):
        @pl.when(b == 0)
        def _():
            weights((0, 1, 2))
            loads()[L_A1].wait()
            loads()[L_H].wait()

        @pl.when((s == 1) & (b == 1))
        def _():
            loads()[L_ACT].start()

        grad = dot_nt(QKV[0, half(b)], weight(0))
        for i in range(1, 3):
            grad = grad + dot_nt(QKV[i, half(b)], weight(i))
        xhat, rstd = whiten(H[half(b)].astype(F32))
        SG[9:10] += jnp.sum(grad, axis=0, keepdims=True)
        SG[11:12] += jnp.sum(grad * xhat, axis=0, keepdims=True)
        H[half(b)] = (RES[half(b)] + unwhiten(grad * small[11:12], xhat, rstd)).astype(B16)

        @pl.when(s == 1)
        def _():
            cross(b).start()

        dh_out(b).start()

    def grad_proj():
        loads()[L_ACT].wait()
        @pl.loop(0, 4)
        def _(i):
            for u in range(2):
                v = dot_tn(BIG[i, :, 512 * u : 512 * (u + 1)], DM[...]).astype(B16).reshape(2, 4, 64, 1024)
                for j in range(4):
                    WG[8 + j, i, u] = v[:, j]

        @pl.when(s == 0)
        def _():
            loads()[L_PROB].start()

    def put(k, a, v):
        for i in range(2):
            part = dot_tn(a[:, 512 * i : 512 * (i + 1)], v[...])
            WG[k, 2 * i : 2 * i + 2] = part.astype(B16).reshape(2, 2, 2, 64, 1024)

    def grad_fc(j):
        put(4 + j, A2, GP.at[j])

    def grad_out():
        put(3, ATT, DAT)

    def grad_qkv(i):
        put(i, A1, QKV.at[i])

    send_sums, sums_in, sums_out = to_all(lambda to: SB.at[to], RB, bs, br)
    send_pref, pref_in, pref_out = to_all(lambda to: PF, PG, ps, pr)

    def r_out_in():
        return [pltpu.make_async_copy(r_out.at[:, pl.ds(1024 * i, 1024)], BIG.at[i], hx.at[i]) for i in range(2)]

    def hidden_across():
        return pltpu.make_async_remote_copy(HP, HPR, hx.at[2], hx.at[3], device_id=(1 - s, d), device_id_type=MESH)

    def small_first():
        for cp in r_out_in():
            cp.start()
        for i in range(3):
            SG[i : i + 1] = column_sum(QKV[i])
        SG[3:4] = column_sum(DAT[...])
        for j in range(4):
            SG[4 + j : 5 + j] = column_sum(GP[j])
        SG[8:9] = column_sum(DM[...])
        for i in range(16):
            for n in range(13):
                m = 11 * i + n
                row, at = (m // 16, 128 * (m % 16 // 2)) if n < 11 else (n, 128 * (i // 2))
                SB[i, n : n + 1] = SG[row : row + 1, at : at + 128]
            SB[i, 16:32] = DKV[16 * (i // 8) : 16 * (i // 8) + 16, 128 * (i % 8) : 128 * (i % 8) + 128]
        send_sums()
        RB[d] = SB[d]

    def small_second():
        sums_in()
        total = RB[0]
        for i in range(1, 16):
            total = total + RB[i]
        row = lax.broadcasted_iota(jnp.int32, (16, 128), 0)
        odd = jnp.where(row < 11, d + row, d) % 2 == 1
        own_sums[...] = jnp.where(odd, pltpu.roll(total[:16], 64, 1), total[:16])
        PF[...] = total[16:].astype(B16)
        send_pref()
        PG[d] = PF[...]

    def small_third():
        pref_in()
        for i in range(16):
            KVB[:, 128 * i : 128 * i + 128] = PG[i]
        for cp in r_out_in():
            cp.wait()
        HP[...] = dot_nt(KVB[:, :1024], BIG[0]) + dot_nt(KVB[:, 1024:], BIG[1])
        hidden_across().start()

    def small_last():
        hidden_across().wait()
        HSUM[...] = HP[...] + HPR[...]

    def held(r):
        a = r // 4
        return ((2 - a) * (1 - a) // 2) * (r + 8) + a * (2 - a) * r + (a * (a - 1) // 2) * (11 - r)

    def across_c(r):
        return pltpu.make_async_remote_copy(
            WG.at[held(r), :, :, 1 - c], RC.at[r % 4], cs.at[r], cr.at[r],
            device_id=(s, z * 4 + y * 2 + 1 - c), device_id_type=MESH,
        )

    def across_y(r):
        return pltpu.make_async_remote_copy(
            WG.at[held(r), :, 1 - y, c], RY.at[r % 4], ys.at[r], yr.at[r],
            device_id=(s, z * 4 + (1 - y) * 2 + c), device_id_type=MESH,
        )

    def up(r, n, first):
        return pltpu.make_async_remote_copy(
            WG.at[held(r), pl.ds(first, n), y, c], RU.at[r % 7, pl.ds(first - 1, n)], us.at[r], ur.at[r],
            device_id=(s, (z + 1) * 4 + y * 2 + c), device_id_type=MESH,
        )

    def down(r, n):
        return pltpu.make_async_remote_copy(
            WG.at[held(r), pl.ds(0, n), y, c], RD.at[r % 7, pl.ds(0, n)], ds_.at[r], dr.at[r],
            device_id=(s, (z - 1) * 4 + y * 2 + c), device_id_type=MESH,
        )

    def each_out(r, act):
        k = held(r)
        src = T.at[r % 2]

        @pl.when(r < 4)
        def _():
            act(pltpu.make_async_copy(src, op_.at[0, pl.ds(pl.multiple_of(64 * r, 64), 64)], osem.at[r]))

        @pl.when((r >= 4) & (r < 8))
        def _():
            act(pltpu.make_async_copy(src, of.at[0, :, pl.ds(pl.multiple_of(1024 * (r - 4), 1024), 1024)], osem.at[r]))

        @pl.when(r == 8)
        def _():
            act(pltpu.make_async_copy(src, oo.at[0], osem.at[r]))

        @pl.when(r > 8)
        def _():
            act(pltpu.make_async_copy(src, oq.at[0, :, pl.ds(pl.multiple_of(1024 * (11 - r), 1024), 1024)], osem.at[r]))

    def start(cp):
        cp.start()

    def add(k, i, j, other):
        WG[k, i, j, c] = (WG[k, i, j, c].astype(F32) + other.astype(F32)).astype(B16)

    def live(r):
        return (r >= 0) & (r < NP)

    def scatter_step(t):
        @pl.when(live(t))
        def _():
            across_c(t).start()

        @pl.when(live(t - 1))
        def _():
            r = t - 1
            k = held(r)
            across_c(r).wait_recv()

            @pl.loop(0, 4)
            def _(i):
                add(k, i, 1 - y, RC[r % 4, i, 1 - y])

            across_y(r).start()

            @pl.loop(0, 4)
            def _(i):
                add(k, i, y, RC[r % 4, i, y])

        @pl.when(live(t - 2))
        def _():
            r = t - 2
            k = held(r)
            across_y(r).wait_recv()

            @pl.loop(0, 4)
            def _(i):
                add(k, i, y, RY[r % 4, i])

            @pl.when(z == 0)
            def _():
                up(r, 3, 1).start()

            @pl.when(z == 3)
            def _():
                down(r, 3).start()

        for q in (1, 2, 3):
            n = 4 - q

            @pl.when(live(t - 2 - q))
            def _():
                r = t - 2 - q
                k = held(r)

                @pl.when(z == q)
                def _():
                    up_here = pltpu.make_async_remote_copy(
                        WG.at[k, pl.ds(q, n), y, c], RU.at[r % 7, pl.ds(q - 1, n)], us.at[r], ur.at[r],
                        device_id=(s, d), device_id_type=MESH,
                    )
                    up_here.wait_recv()
                    for i in range(q + 1, 4):
                        add(k, i, y, RU[r % 7, i - 1])
                    if n > 1:
                        up(r, n - 1, q + 1).start()

                @pl.when(z == 3 - q)
                def _():
                    down(r, n).wait_recv()
                    for i in range(n - 1):
                        add(k, i, y, RD[r % 7, i])
                    if n > 1:
                        down(r, n - 1).start()

        @pl.when(live(t - 5))
        def _():
            r = t - 5
            k = held(r)

            @pl.when(r >= 2)
            def _():
                each_out(r - 2, lambda cp: cp.wait())

            T[r % 2] = WG[k, z, y, c].astype(F32)

            @pl.when(z > 0)
            def _():
                T[r % 2] += RU[r % 7, z - 1].astype(F32)

            @pl.when(z < 3)
            def _():
                T[r % 2] += RD[r % 7, z].astype(F32)

            each_out(r, start)

    @pl.loop(0, BACK_TICKS)
    def _(tick):
        turn = tick // SPLIT

        def when(i, at, body):
            mine = ((s == 0) & (tick == at)) | ((s == 1) & ((tick == i) | (tick == SPLIT + i)))

            @pl.when(mine)
            def _():
                pl.loop(s * turn, (1 - s) * 2 + s * (turn + 1))(body)

        @pl.when(((s == 0) & (tick < 2)) | ((s == 1) & ((tick == 0) | (tick == SPLIT))))
        def _():
            ffn_in((1 - s) * tick + s * turn)

        when(1, 3, ffn_norm)
        first = 5 - 3 * s + 3 * (1 - s) * ((tick - 5) // 3) + s * SPLIT * turn
        b0 = (1 - s) * ((tick - 5) // 3) + s * turn
        in_turn = ((s == 0) & (tick >= 5) & (tick < 11)) | ((s == 1) & (tick < 2 * SPLIT))

        @pl.when(in_turn & (tick == first))
        def _():
            attn_out(b0)

        @pl.when(in_turn & ((tick == first + 1) | (tick == first + 2)))
        def _():
            attn_back(tick - first - 1, b0)

        when(5, 11, attn_norm)
        r = tick - 2 - (2 * SPLIT - 2) * s

        @pl.when(r == 0)
        def _():
            grad_proj()

        @pl.when((r >= 4) & (r < 8))
        def _():
            grad_fc(r - 4)

        @pl.when(r == 8)
        def _():
            grad_out()

        @pl.when((r > 8) & (r < 12))
        def _():
            grad_qkv(11 - r)

        scatter_step(r)
        for at, body in ((10, small_first), (11, small_second), (13, small_third), (16, small_last)):
            pl.when(r == at)(body)

    @pl.loop(0, NP)
    def _(r):
        @pl.when(r >= NP - 2)
        def _():
            each_out(r, lambda cp: cp.wait())

        across_c(r).wait_send()
        across_y(r).wait_send()
        for q in range(3):

            @pl.when(z == q)
            def _():
                up(r, 3 - q, q + 1).wait_send()

            @pl.when(z == q + 1)
            def _():
                down(r, q + 1).wait_send()

    sums_out()
    pref_out()

    @pl.loop(0, 2)
    def _(b):
        dh_out(b).wait()

        @pl.when(s == 1)
        def _():
            cross(b).wait_send()


def backward_call(kept, cot, r_out, small, pkey, pval):
    W, h, a1, qkv, prob, ppre, att, res, a2, gp, act = kept
    any_, vm = pl.BlockSpec(memory_space=pl.ANY), pl.BlockSpec(memory_space=pltpu.VMEM)
    n, d = h.shape
    dma = pltpu.SemaphoreType.DMA
    wide = (4, 2, 2, 64, d)
    outs = [
        ((n, d), B16), ((1, 64, 3 * d), F32), ((1, 64, d), F32), ((1, 64, 4 * d), F32), ((1, 256, d), F32),
        ((16, 128), F32), ((16, 2 * d), B16), ((16, 512), F32),
    ]
    scratch = [
        ((NP,) + wide, B16), ((n, d), B16), ((n, d), B16), ((3, n, d), B16), ((4, n, d), B16), ((2, HALF, HALF), B16), ((n, d), B16),
        ((n, d), F32), ((n, d), B16), ((4, n, d), B16), ((n, d), B16), ((n, d), B16), ((HALF, d), B16), ((HALF, HALF), F32),
        ((HALF, HALF), B16), ((HALF, d), F32),
        ((4, 4, 2, 64, d), B16), ((4, 4, 64, d), B16), ((7, 3, 64, d), B16), ((7, 3, 64, d), B16), ((2, 64, d), F32),
        ((16, d), F32), ((32, d), F32), ((16, 32, 128), F32), ((16, 32, 128), F32), ((16, 128), B16), ((16, 16, 128), B16),
        ((16, 512), F32), ((16, 512), F32),
    ]
    return pl.pallas_call(
        backward_kernel,
        out_shape=[jax.ShapeDtypeStruct(*o) for o in outs],
        in_specs=[any_] * 13 + [vm] * 3,
        out_specs=[any_] * 5 + [vm] * 3,
        scratch_shapes=[pltpu.VMEM(*v) for v in scratch] + [dma((NP,))] * 11 + [dma((2,))] * 3 + [dma((16,))] * 4 + [dma((4,))],
        compiler_params=pltpu.CompilerParams(collective_id=1, has_side_effects=True, vmem_limit_bytes=64 << 20),
    )(W.reshape((NP,) + wide), h, a1, qkv, prob, ppre, att, res, a2, gp, act, cot, r_out, small, pkey, pval)


def finish_kernel(
    o0, o1, o2, o3, o4, o5, hid, kvb, hsum, aux, r_in,
    c0, c1, c2, c3, c4, c5, g_embed, g_in, g_in_bias, g_out, g_out_bias,
    G_IN, G_OUT, sem,
):
    moves = [pltpu.make_async_copy(a, b, sem.at[i]) for i, (a, b) in enumerate(zip((o0, o1, o2, o3, o4, o5), (c0, c1, c2, c3, c4, c5)))]
    for cp in moves:
        cp.start()
    h = hid[...]
    kv = kvb[...]
    G_OUT[...] = dot_tn(h.astype(B16), kv)
    out_cp = pltpu.make_async_copy(G_OUT, g_out, sem.at[6])
    out_cp.start()
    g_out_bias[...] = column_sum(kv)
    dp = (hsum[...] * (1.0 - h * h)).astype(B16)
    G_IN[...] = dot_tn(aux[...], dp)
    in_cp = pltpu.make_async_copy(G_IN, g_in, sem.at[7])
    in_cp.start()
    g_in_bias[...] = column_sum(dp)
    g_embed[...] = dot_nt(dp, r_in[...])[:10]
    for cp in moves + [out_cp, in_cp]:
        cp.wait()


def finish_call(large, hid, kvb, hsum, aux, r_in):
    any_, vm = pl.BlockSpec(memory_space=pl.ANY), pl.BlockSpec(memory_space=pltpu.VMEM)
    d = r_in.shape[0]
    outs = [jax.ShapeDtypeStruct(x.shape, x.dtype) for x in large]
    outs += [jax.ShapeDtypeStruct(x, F32) for x in ((10, d), (d, 512), (1, 512), (512, 2 * d), (1, 2 * d))]
    return pl.pallas_call(
        finish_kernel,
        out_shape=outs,
        in_specs=[any_] * 6 + [vm] * 5,
        out_specs=[any_] * 6 + [vm, any_, vm, any_, vm],
        scratch_shapes=[pltpu.VMEM((d, 512), F32), pltpu.VMEM((512, 2 * d), F32), pltpu.SemaphoreType.DMA((8,))],
        compiler_params=pltpu.CompilerParams(vmem_limit_bytes=40 << 20),
    )(*large, hid, kvb, hsum, aux, r_in)


def on_device(
    tokens,
    segment_ids,
    cotangent,
    w_qkv,
    w_attn_out,
    w_fc,
    w_proj,
    gains,
    biases,
    prefix_embed,
    reparam_in,
    reparam_in_bias,
    reparam_out,
    reparam_out_bias,
):
    aux = prefix_rows(prefix_embed, reparam_in_bias, reparam_out_bias)
    pack = own_pack(gains, biases)
    kept = forward_call(w_qkv, w_attn_out, w_fc, w_proj, tokens, segment_ids, pack, aux, reparam_in, reparam_out)
    small, pkey, pval, hid = kept[12:]
    *large, sums, kvb, hsum = backward_call(kept[:1] + kept[2:12], cotangent, reparam_out, small, pkey, pval)
    done = finish_call([kept[1]] + large, hid, kvb, hsum, aux, reparam_in)
    return (
        done[0][None],
        done[1][None],
        *done[2:6],
        sums[11:13, :64][None],
        sums[:11, :64].reshape(1, 704),
        done[6],
        done[7],
        done[8][0],
        done[9],
        done[10][0],
    )


def passed_along(shard, axis, by):
    size = lax.axis_size(axis)
    pairs = [(i, i + by) for i in range(size) if 0 <= i + by < size]
    return lax.ppermute(shard, axis, pairs)


def norm_rows(v, gain, shift):
    mean = jnp.mean(v, axis=-1, keepdims=True)
    cent = v - mean
    var = jnp.mean(cent * cent, axis=-1, keepdims=True)
    return cent * lax.rsqrt(var + EPS) * gain + shift


def gelu_tanh(v):
    return jax.nn.gelu(v, approximate=True)


def forward_layer(h_b, segs, pkey, pval, params):
    w_q, w_o, w_f, w_p, gain_pair, bias_all = params
    width = w_o.shape[0]
    length = h_b.shape[0]
    heads, head_dim = (pkey.shape[1], pkey.shape[2])
    scale = 1.0 / math.sqrt(head_dim)
    gain_f = gain_pair.astype(jnp.float32)
    bias_f = bias_all.astype(jnp.float32)
    hf = h_b.astype(jnp.float32)
    a1b = norm_rows(hf, gain_f[0], bias_f[9 * width : 10 * width]).astype(jnp.bfloat16)
    qkv_b = (jnp.dot(a1b, w_q, preferred_element_type=jnp.float32) + bias_f[: 3 * width]).astype(
        jnp.bfloat16
    )
    split = qkv_b.reshape(length, 3, heads, head_dim)
    query, keys, values = (split[:, 0], split[:, 1], split[:, 2])
    s_tok = jnp.einsum("lhe,mhe->hlm", query, keys, preferred_element_type=jnp.float32) * scale
    s_pre = jnp.einsum("lhe,phe->hlp", query, pkey, preferred_element_type=jnp.float32) * scale
    place = jnp.arange(length)
    allowed = (segs[:, None] == segs[None, :]) & (place[None, :] <= place[:, None])
    s_tok = jnp.where(allowed[None], s_tok, NEG)
    top = jnp.maximum(
        jnp.max(s_tok, axis=-1, keepdims=True), jnp.max(s_pre, axis=-1, keepdims=True)
    )
    e_tok = jnp.exp(s_tok - top)
    e_pre = jnp.exp(s_pre - top)
    total = jnp.sum(e_tok, axis=-1, keepdims=True) + jnp.sum(e_pre, axis=-1, keepdims=True)
    p_tok = e_tok / total
    p_pre = e_pre / total
    mixed = jnp.einsum(
        "hlm,mhe->lhe", p_tok.astype(jnp.bfloat16), values, preferred_element_type=jnp.float32
    ) + jnp.einsum(
        "hlp,phe->lhe", p_pre.astype(jnp.bfloat16), pval, preferred_element_type=jnp.float32
    )
    attn_b = mixed.reshape(length, width).astype(jnp.bfloat16)
    resid = hf + (
        jnp.dot(attn_b, w_o, preferred_element_type=jnp.float32) + bias_f[3 * width : 4 * width]
    )
    a2b = norm_rows(resid, gain_f[1], bias_f[10 * width : 11 * width]).astype(jnp.bfloat16)
    pre_act = jnp.dot(a2b, w_f, preferred_element_type=jnp.float32) + bias_f[4 * width : 8 * width]
    act_b = gelu_tanh(pre_act).astype(jnp.bfloat16)
    result = resid + (
        jnp.dot(act_b, w_p, preferred_element_type=jnp.float32) + bias_f[8 * width : 9 * width]
    )
    return (result, (hf, a1b, qkv_b, p_tok, p_pre, attn_b, resid, a2b, pre_act, act_b))


def backward_ffn(grad_out, keep, params):
    w_q, w_o, w_f, w_p, gain_pair, bias_all = params
    hf, a1b, qkv_b, p_tok, p_pre, attn_b, resid, a2b, pre_act, act_b = keep
    width = w_o.shape[0]
    gain_f = gain_pair.astype(jnp.float32)
    bias_f = bias_all.astype(jnp.float32)
    dm_b = grad_out.astype(jnp.bfloat16)
    grad_wp = jnp.einsum("lf,ld->fd", act_b, dm_b, preferred_element_type=jnp.float32)
    grad_bp = jnp.sum(dm_b.astype(jnp.float32), axis=0)
    d_act = jnp.dot(dm_b, w_p.T, preferred_element_type=jnp.float32)
    dpre_b = jax.vjp(gelu_tanh, pre_act)[1](d_act)[0].astype(jnp.bfloat16)
    grad_wf = jnp.einsum("ld,lf->df", a2b, dpre_b, preferred_element_type=jnp.float32)
    grad_bf = jnp.sum(dpre_b.astype(jnp.float32), axis=0)
    d_a2 = jnp.dot(dpre_b, w_f.T, preferred_element_type=jnp.float32)
    norm_back = jax.vjp(norm_rows, resid, gain_f[1], bias_f[10 * width : 11 * width])[1]
    d_resid_norm, grad_g2, grad_c2 = norm_back(d_a2)
    d_resid = grad_out + d_resid_norm
    return (d_resid, (grad_wf, grad_wp), (grad_bf, grad_bp, grad_g2, grad_c2))


def backward_attn(d_resid, keep, pkey, pval, params):
    w_q, w_o, w_f, w_p, gain_pair, bias_all = params
    hf, a1b, qkv_b, p_tok, p_pre, attn_b, resid, a2b, pre_act, act_b = keep
    width = w_o.shape[0]
    length = hf.shape[0]
    heads, head_dim = (pkey.shape[1], pkey.shape[2])
    prefix_len = pkey.shape[0]
    scale = 1.0 / math.sqrt(head_dim)
    gain_f = gain_pair.astype(jnp.float32)
    bias_f = bias_all.astype(jnp.float32)
    split = qkv_b.reshape(length, 3, heads, head_dim)
    query, keys, values = (split[:, 0], split[:, 1], split[:, 2])
    dat_b = d_resid.astype(jnp.bfloat16)
    grad_wo = jnp.einsum("ld,le->de", attn_b, dat_b, preferred_element_type=jnp.float32)
    grad_bo = jnp.sum(dat_b.astype(jnp.float32), axis=0)
    dattn_b = jnp.dot(dat_b, w_o.T, preferred_element_type=jnp.float32).astype(jnp.bfloat16)
    dattn_b = dattn_b.reshape(length, heads, head_dim)
    dp_tok = jnp.einsum("lhe,mhe->hlm", dattn_b, values, preferred_element_type=jnp.float32)
    dp_pre = jnp.einsum("lhe,phe->hlp", dattn_b, pval, preferred_element_type=jnp.float32)
    row_dot = jnp.sum(p_tok * dp_tok, axis=-1, keepdims=True) + jnp.sum(
        p_pre * dp_pre, axis=-1, keepdims=True
    )
    ds_tok = (p_tok * (dp_tok - row_dot)).astype(jnp.bfloat16)
    ds_pre = (p_pre * (dp_pre - row_dot)).astype(jnp.bfloat16)
    d_query = (
        jnp.einsum("hlm,mhe->lhe", ds_tok, keys, preferred_element_type=jnp.float32)
        + jnp.einsum("hlp,phe->lhe", ds_pre, pkey, preferred_element_type=jnp.float32)
    ) * scale
    d_keys = jnp.einsum("hlm,lhe->mhe", ds_tok, query, preferred_element_type=jnp.float32) * scale
    d_values = jnp.einsum(
        "hlm,lhe->mhe", p_tok.astype(jnp.bfloat16), dattn_b, preferred_element_type=jnp.float32
    )
    grad_pkey = (
        jnp.einsum("hlp,lhe->phe", ds_pre, query, preferred_element_type=jnp.float32) * scale
    )
    grad_pval = jnp.einsum(
        "hlp,lhe->phe", p_pre.astype(jnp.bfloat16), dattn_b, preferred_element_type=jnp.float32
    )
    dqkv_b = (
        jnp.stack([d_query, d_keys, d_values], axis=1)
        .reshape(length, 3 * width)
        .astype(jnp.bfloat16)
    )
    grad_wq = jnp.einsum("ld,lc->dc", a1b, dqkv_b, preferred_element_type=jnp.float32)
    grad_bq = jnp.sum(dqkv_b.astype(jnp.float32), axis=0)
    d_a1 = jnp.dot(dqkv_b, w_q.T, preferred_element_type=jnp.float32)
    norm_back_first = jax.vjp(norm_rows, hf, gain_f[0], bias_f[9 * width : 10 * width])[1]
    d_in_norm, grad_g1, grad_c1 = norm_back_first(d_a1)
    d_input = d_resid + d_in_norm
    grad_prefix = jnp.concatenate(
        [grad_pkey.reshape(prefix_len, width), grad_pval.reshape(prefix_len, width)], axis=1
    )
    return (d_input, (grad_wq, grad_wo), (grad_bq, grad_bo, grad_g1, grad_c1), grad_prefix)


def assemble(ffn_mats, ffn_small, attn_mats, attn_small):
    grad_bf, grad_bp, grad_g2, grad_c2 = ffn_small
    grad_bq, grad_bo, grad_g1, grad_c1 = attn_small
    grad_gains = jnp.stack([grad_g1, grad_g2])
    grad_bias = jnp.concatenate([grad_bq, grad_bo, grad_bf, grad_bp, grad_c1, grad_c2])
    return (attn_mats[0], attn_mats[1], ffn_mats[0], ffn_mats[1], grad_gains, grad_bias)


def on_device_general(
    tokens,
    segment_ids,
    cotangent,
    w_qkv,
    w_attn_out,
    w_fc,
    w_proj,
    gains,
    biases,
    prefix_embed,
    reparam_in,
    reparam_in_bias,
    reparam_out,
    reparam_out_bias,
):
    section = lax.axis_index("section")
    micro, row_len = segment_ids.shape
    width = tokens.shape[1]
    prefix_len = prefix_embed.shape[0]
    head_dim = width // HEADS
    gathered = (
        lax.all_gather(w_qkv, "dp", axis=1, tiled=True),
        lax.all_gather(w_attn_out, "dp", axis=1, tiled=True),
        lax.all_gather(w_fc, "dp", axis=1, tiled=True),
        lax.all_gather(w_proj, "dp", axis=1, tiled=True),
        lax.all_gather(gains, "dp", axis=2, tiled=True),
        lax.all_gather(biases, "dp", axis=1, tiled=True),
    )
    params = tuple((item[0] for item in gathered))
    pre_hidden = jnp.dot(
        prefix_embed, reparam_in, preferred_element_type=jnp.float32
    ) + reparam_in_bias.astype(jnp.float32)
    hidden = jnp.tanh(pre_hidden)
    hidden_b = hidden.astype(jnp.bfloat16)
    prefix_kv = (
        jnp.dot(hidden_b, reparam_out, preferred_element_type=jnp.float32)
        + reparam_out_bias.astype(jnp.float32)
    ).astype(jnp.bfloat16)
    pkey = prefix_kv[:, :width].reshape(prefix_len, HEADS, head_dim)
    pval = prefix_kv[:, width:].reshape(prefix_len, HEADS, head_dim)
    token_rows = tokens.reshape(micro, row_len, width)
    cot_rows = cotangent.reshape(micro, row_len, width)
    received = jnp.zeros((row_len, width), jnp.bfloat16)
    outputs = jnp.zeros((micro, row_len, width), jnp.bfloat16)
    stored = []
    for tick in range(micro + 1):
        index = tick - section
        active = (index >= 0) & (index < micro)
        slot = jnp.clip(index, 0, micro - 1)
        segs = segment_ids[slot]
        h_b = jnp.where(section == 0, token_rows[slot], received)
        result, keep = forward_layer(h_b, segs, pkey, pval, params)
        result_b = result.astype(jnp.bfloat16)
        outputs = jnp.where(active, outputs.at[slot].set(result_b), outputs)
        stored.append(keep)
        if tick < micro:
            received = passed_along(result_b, "section", 1)
    regathered = (
        lax.all_gather(w_qkv, "dp", axis=1, tiled=True),
        lax.all_gather(w_attn_out, "dp", axis=1, tiled=True),
        lax.all_gather(w_fc, "dp", axis=1, tiled=True),
        lax.all_gather(w_proj, "dp", axis=1, tiled=True),
        lax.all_gather(gains, "dp", axis=2, tiled=True),
        lax.all_gather(biases, "dp", axis=1, tiled=True),
    )
    params_back = tuple((item[0] for item in regathered))
    stacked = jax.tree.map(lambda *items: jnp.stack(items), *stored)
    coming = jnp.zeros((row_len, width), jnp.bfloat16)
    in_grads = jnp.zeros((micro, row_len, width), jnp.bfloat16)
    grad_total = None
    prefix_total = None
    for tick in range(micro + 1):
        index = micro - tick - section
        active = (index >= 0) & (index < micro)
        slot = jnp.clip(index, 0, micro - 1)
        segs = segment_ids[slot]
        saved = jax.tree.map(lambda item: item[slot + section], stacked)
        grad_out = jnp.where(
            section == 1, cot_rows[slot].astype(jnp.float32), coming.astype(jnp.float32)
        )
        keep = saved
        d_resid, ffn_mats, ffn_small = backward_ffn(grad_out, keep, params_back)
        ffn_mats = jax.tree.map(
            lambda item: jnp.where(active, item, jnp.zeros_like(item)), ffn_mats
        )
        ffn_small = jax.tree.map(
            lambda item: jnp.where(active, item, jnp.zeros_like(item)), ffn_small
        )
        d_input, attn_mats, attn_small, grad_prefix = backward_attn(
            d_resid, keep, pkey, pval, params_back
        )
        attn_mats = jax.tree.map(
            lambda item: jnp.where(active, item, jnp.zeros_like(item)), attn_mats
        )
        attn_small = jax.tree.map(
            lambda item: jnp.where(active, item, jnp.zeros_like(item)), attn_small
        )
        grad_prefix = jnp.where(active, grad_prefix, jnp.zeros_like(grad_prefix))
        grads = assemble(ffn_mats, ffn_small, attn_mats, attn_small)
        if grad_total is None:
            grad_total = grads
            prefix_total = grad_prefix
        else:
            grad_total = jax.tree.map(lambda left, right: left + right, grad_total, grads)
            prefix_total = prefix_total + grad_prefix
        d_input_b = d_input.astype(jnp.bfloat16)
        in_grads = jnp.where(active, in_grads.at[slot].set(d_input_b), in_grads)
        if tick < micro:
            coming = passed_along(d_input_b, "section", -1)
    lifted = tuple((item[None] for item in grad_total))
    weight_grads = (
        lax.psum_scatter(lifted[0], "dp", scatter_dimension=1, tiled=True),
        lax.psum_scatter(lifted[1], "dp", scatter_dimension=1, tiled=True),
        lax.psum_scatter(lifted[2], "dp", scatter_dimension=1, tiled=True),
        lax.psum_scatter(lifted[3], "dp", scatter_dimension=1, tiled=True),
        lax.psum_scatter(lifted[4], "dp", scatter_dimension=2, tiled=True),
        lax.psum_scatter(lifted[5], "dp", scatter_dimension=1, tiled=True),
    )
    prefix_grad = lax.psum(prefix_total, "dp")
    prefix_grad_b = prefix_grad.astype(jnp.bfloat16)
    grad_reparam_out = jnp.einsum(
        "pr,pc->rc", hidden_b, prefix_grad_b, preferred_element_type=jnp.float32
    )
    grad_reparam_out_bias = jnp.sum(prefix_grad_b.astype(jnp.float32), axis=0)
    hidden_part = jnp.dot(prefix_grad_b, reparam_out.T, preferred_element_type=jnp.float32)
    hidden_grad = lax.psum(hidden_part, "section")
    dpre_hidden_b = (hidden_grad * (1.0 - hidden * hidden)).astype(jnp.bfloat16)
    grad_reparam_in = jnp.einsum(
        "pd,pr->dr", prefix_embed, dpre_hidden_b, preferred_element_type=jnp.float32
    )
    grad_reparam_in_bias = jnp.sum(dpre_hidden_b.astype(jnp.float32), axis=0)
    grad_prefix_embed = jnp.dot(dpre_hidden_b, reparam_in.T, preferred_element_type=jnp.float32)
    layer_outs = outputs.reshape(1, micro * row_len, width)
    input_grads = in_grads.reshape(1, micro * row_len, width)
    return (
        layer_outs,
        input_grads,
        weight_grads[0],
        weight_grads[1],
        weight_grads[2],
        weight_grads[3],
        weight_grads[4],
        weight_grads[5],
        grad_prefix_embed,
        grad_reparam_in,
        grad_reparam_in_bias,
        grad_reparam_out,
        grad_reparam_out_bias,
    )


def solution(mesh):
    return jax.shard_map(
        on_device if mesh.shape["dp"] == 16 else on_device_general,
        mesh=mesh,
        in_specs=(
            P("dp", None),
            P("dp", None),
            P("dp", None),
            P("section", "dp", None),
            P("section", "dp", None),
            P("section", "dp", None),
            P("section", "dp", None),
            P("section", None, "dp"),
            P("section", "dp"),
            P(),
            P(),
            P(),
            P(None, "section"),
            P("section"),
        ),
        out_specs=(
            P("section", "dp", None),
            P("section", "dp", None),
            P("section", "dp", None),
            P("section", "dp", None),
            P("section", "dp", None),
            P("section", "dp", None),
            P("section", None, "dp"),
            P("section", "dp"),
            P(),
            P(),
            P(),
            P(None, "section"),
            P("section"),
        ),
        check_vma=False,
    )
```

```python
import math

import jax
import jax.numpy as jnp
from jax import lax
from jax.experimental import pallas as pl
from jax.experimental.pallas import tpu as pltpu
from jax.sharding import PartitionSpec as P

HEADS = 16
EPS = 1e-05
NEG = -1000000000.0
MESH = pl.DeviceIdType.MESH
F32 = jnp.float32
B16 = jnp.bfloat16
NP = 12
AHEAD = 1


def place():
    s = lax.axis_index("section"); d = lax.axis_index("dp")
    return s, d, d // 4, (d // 2) % 2, d % 2

def greet(s, d):
    bar = pltpu.get_barrier_semaphore()
    for i in range(1, 16):
        pl.semaphore_signal(bar, 1, device_id=(s, (d + i) % 16), device_id_type=MESH)
    pl.semaphore_signal(bar, 1, device_id=(1 - s, d), device_id_type=MESH)
    pl.semaphore_wait(bar, 16)


def to_all(src, dst, ss, rs):
    s, d = lax.axis_index("section"), lax.axis_index("dp")

    def cp(i, frm):
        to = (d + i) % 16
        return pltpu.make_async_remote_copy(
            src(to), dst.at[frm], ss.at[i], rs.at[i], device_id=(s, to), device_id_type=MESH
        )

    def start():
        for i in range(1, 16):
            cp(i, d).start()

    def arrive():
        for i in range(1, 16):
            cp(i, (d + 16 - i) % 16).wait_recv()

    def finish():
        for i in range(1, 16):
            cp(i, d).wait_send()

    return start, arrive, finish


class Gather:
    def __init__(self, W, ssem, rsem):
        self.W, self.ssem, self.rsem = W, ssem, rsem
        self.s, self.d, self.z, self.y, self.c = place()
    def blk(self, k, d):
        i = k // 8
        row = (1-i)*(1024*k+64*d) + i*(8192+256*d+64*(k-8))
        return self.W.at[pl.ds(pl.multiple_of(row, 64), 64)]
    def cp(self, k, origin, target, slot):
        b = self.blk(k, origin)
        return pltpu.make_async_remote_copy(src_ref=b, dst_ref=b, send_sem=self.ssem.at[k, slot], recv_sem=self.rsem.at[k, origin],
            device_id=(self.s, target), device_id_type=MESH)
    def dev(self, z, y, c): return z*4+y*2+c
    def arrived(self, k, origin): self.cp(k, origin, origin, 0).wait_recv()
    def to_up(self, k, zo, op):
        op(self.cp(k, self.dev(zo, self.y, self.c), self.dev(self.z+1, self.y, self.c), zo))
    def to_down(self, k, zo, op):
        op(self.cp(k, self.dev(zo, self.y, self.c), self.dev(self.z-1, self.y, self.c), 4+zo))
    def to_y(self, k, zo, op):
        op(self.cp(k, self.dev(zo, self.y, self.c), self.dev(self.z, 1-self.y, self.c), 8+zo))
    def to_c(self, k, zo, yo, op):
        op(self.cp(k, self.dev(zo, yo, self.c), self.dev(self.z, self.y, 1-self.c), 12+zo*2+yo))
    def step(self, t, own):
        z, y, c = self.z, self.y, self.c
        start = lambda cp: cp.start()
        def fresh(k):
            own(k)
            self.to_y(k, z, start)
            @pl.when(z < 3)
            def _(): self.to_up(k, z, start)
            @pl.when(z > 0)
            def _(): self.to_down(k, z, start)
            self.to_c(k, z, y, start)
        @pl.when(t == 0)
        def _():
            for k in range(AHEAD): fresh(k)
        @pl.when(t + AHEAD < NP)
        def _(): fresh(t + AHEAD)
        for q in (1, 2, 3, 4):
            k = t - q
            ok = (k >= 0) & (k < NP)
            if q < 4:
                @pl.when(ok & (z - q >= 0))
                def _():
                    self.arrived(k, self.dev(z-q, y, c))
                    @pl.when(z < 3)
                    def _(): self.to_up(k, z-q, start)
                    self.to_y(k, z-q, start)
                    self.to_c(k, z-q, y, start)
                @pl.when(ok & (z + q <= 3))
                def _():
                    self.arrived(k, self.dev(z+q, y, c))
                    @pl.when(z > 0)
                    def _(): self.to_down(k, z+q, start)
                    self.to_y(k, z+q, start)
                    self.to_c(k, z+q, y, start)
            e = q - 1
            def side(zo):
                self.arrived(k, self.dev(zo, 1-y, c))
                self.to_c(k, zo, 1-y, start)
            if e == 0:
                @pl.when(ok)
                def _(): side(z)
            else:
                @pl.when(ok & (z - e >= 0))
                def _(): side(z-e)
                @pl.when(ok & (z + e <= 3))
                def _(): side(z+e)
    def complete(self, k):
        for i in range(8):
            self.arrived(k, 2*i + 1-self.c)
    def drain(self):
        fin = lambda cp: cp.wait_send()
        z, y = self.z, self.y
        @pl.loop(0, NP)
        def _(k):
            for zo in range(4):
                @pl.when((zo <= z) & (z < 3))
                def _(): self.to_up(k, zo, fin)
                @pl.when((zo >= z) & (z > 0))
                def _(): self.to_down(k, zo, fin)
                self.to_y(k, zo, fin)
                for yo in range(2): self.to_c(k, zo, yo, fin)

def own_copies(wq, wo, wf, wp, g, sem):
    out = []
    for k in range(NP):
        if k < 3: src = wq.at[0, :, pl.ds(1024*k, 1024)]
        elif k == 3: src = wo.at[0]
        elif k < 8: src = wf.at[0, :, pl.ds(1024*(k-4), 1024)]
        else: src = wp.at[0, pl.ds(64*(k-8), 64)]
        out.append(pltpu.make_async_copy(src, g.blk(jnp.int32(k), g.d), sem.at[k]))
    return out


HALF = 256
STAGES = 12
GELU_C = math.sqrt(2.0 / math.pi)


def dot_nn(a, b):
    return lax.dot_general(a, b, (((1,), (0,)), ((), ())), preferred_element_type=F32)


def dot_nt(a, b):
    return lax.dot_general(a, b, (((1,), (1,)), ((), ())), preferred_element_type=F32)


def dot_tn(a, b):
    return lax.dot_general(a, b, (((0,), (0,)), ((), ())), preferred_element_type=F32)


def whiten(v):
    mean = jnp.mean(v, axis=-1, keepdims=True)
    cent = v - mean
    rstd = lax.rsqrt(jnp.mean(cent * cent, axis=-1, keepdims=True) + EPS)
    return cent * rstd, rstd


def split_heads(pair):
    left = lax.broadcasted_iota(jnp.int32, pair.shape, 1) < 64
    zero = jnp.zeros_like(pair)
    return jnp.concatenate([jnp.where(left, pair, zero), jnp.where(left, zero, pair)], axis=0)


def forward_kernel(
    wq, wo, wf, wp, tokens, segs, pack, aux, r_in, r_out,
    W_o, out_o, h_o, a1_o, qkv_o, prob_o, ppre_o, att_o, res_o, a2_o, gp_o, act_o, small_o, pkey_o, pval_o, hid_o,
    W, H, A1, QKV, PROB, PPRE, ATT, RES, A2, GP, ACT, OUT, SPRE, ACC, small, pkey, pval, hid, mask, PACKS, ROWS,
    own_sem, ssem, rsem, hsem, xs, xr, save_sem, ps, pr, psem,
):
    g = Gather(W, ssem, rsem)
    s = g.s
    for cp in own_copies(wq, wo, wf, wp, g, own_sem):
        cp.start()
    r_in_parts = [pltpu.make_async_copy(r_in.at[pl.ds(512 * i, 512)], ACT.at[2, :, pl.ds(512 * i, 512)], psem.at[i]) for i in range(2)]
    r_out_parts = [pltpu.make_async_copy(r_out.at[:, pl.ds(1024 * i, 1024)], ACT.at[i], psem.at[2 + i]) for i in range(2)]
    for cp in r_in_parts + r_out_parts:
        cp.start()
    greet(s, g.d)
    send_packs, packs_in, packs_out = to_all(lambda to: pack, PACKS, ps, pr)

    def prep_saves():
        pairs = [(small, small_o), (pkey, pkey_o), (pval, pval_o), (hid, hid_o)]
        return [pltpu.make_async_copy(a, b, psem.at[4 + i]) for i, (a, b) in enumerate(pairs)]

    def prepare():
        for cp in r_in_parts + r_out_parts:
            cp.wait()
        ph = dot_nn(aux[:, :512], ACT[2, :, :512]) + dot_nn(aux[:, 512:], ACT[2, :, 512:])
        hid[...] = jnp.tanh(ph + aux[10:11, :512].astype(F32))
        hb = hid[...].astype(B16)
        head = lax.broadcasted_iota(jnp.int32, (16, 1024), 1) // 64
        for i, big in enumerate((pkey, pval)):
            kv = (dot_nn(hb, ACT[i]) + aux[11 + i : 12 + i].astype(F32)).astype(B16)
            for h in range(16):
                big[16 * h : 16 * h + 16] = jnp.where(head == h, kv, jnp.zeros_like(kv))
        key = lax.broadcasted_iota(jnp.int32, (HALF, HALF), 0)
        query = lax.broadcasted_iota(jnp.int32, (HALF, HALF), 1)
        for b in range(2):
            by_query = jnp.broadcast_to(segs[b : b + 1].astype(F32), (HALF, HALF))
            ok = (by_query.T == by_query) & (key <= query)
            mask[b] = jnp.where(ok, 0.0, NEG)
        packs_in()
        ROWS[...] = PACKS[...].astype(F32)
        left = lax.broadcasted_iota(jnp.int32, (1, 128), 1) < 64
        small[...] = jnp.zeros_like(small)
        for n in range(104):
            row, at = n // 8, 128 * (n % 8)
            if row < 11:
                (d0, r0), (d1, r1) = divmod(2 * n, 11), divmod(2 * n + 1, 11)
            else:
                (d0, r0), (d1, r1) = (2 * (n % 8), row), (2 * (n % 8) + 1, row)
            small[row : row + 1, at : at + 128] = jnp.where(left, ROWS[d0, r0 : r0 + 1], ROWS[d1, r1 : r1 + 1])
        for cp in prep_saves():
            cp.start()

    send_packs()
    PACKS[g.d] = pack[...]

    def tokens_in():
        return pltpu.make_async_copy(tokens, H, hsem)

    def half(b):
        return pl.ds(pl.multiple_of(b * HALF, HALF), HALF)

    def cross(b):
        return pltpu.make_async_remote_copy(
            OUT.at[half(b)], H.at[half(b)], xs.at[b], xr.at[b], device_id=(1 - s, g.d), device_id_type=MESH
        )

    @pl.when(s == 0)
    def _():
        tokens_in().start()

    def own(t):
        b = g.blk(t, g.d)
        pltpu.make_async_copy(b, b, own_sem.at[t]).wait()

    def rows_of(k):
        return pl.ds(pl.multiple_of(k * 1024, 1024), 1024)

    def saves(b):
        r = half(b)
        pairs = [
            (H.at[r], h_o.at[r]), (A1.at[r], a1_o.at[r]), (QKV.at[:, r], qkv_o.at[:, r]), (PROB.at[pl.ds(2 * b, 2)], prob_o.at[pl.ds(2 * b, 2)]),
            (PPRE.at[b], ppre_o.at[b]), (ATT.at[r], att_o.at[r]), (RES.at[r], res_o.at[r]), (A2.at[r], a2_o.at[r]),
            (GP.at[:, r], gp_o.at[:, r]), (ACT.at[:, r], act_o.at[:, r]), (OUT.at[r], out_o.at[r]),
        ]
        return [pltpu.make_async_copy(src, dst, save_sem.at[b, i]) for i, (src, dst) in enumerate(pairs)]

    def piece_out(k):
        return pltpu.make_async_copy(W.at[rows_of(k)], W_o.at[rows_of(k)], save_sem.at[2, k])

    def norm_in(b):
        @pl.when(s == 0)
        def _():
            @pl.when(b == 0)
            def _():
                tokens_in().wait()

        @pl.when(s == 1)
        def _():
            cross(b).wait_recv()

        xhat, _ = whiten(H[half(b)].astype(F32))
        A1[half(b)] = (xhat * small[11:12] + small[9:10]).astype(B16)
        saves(b)[0].start()
        saves(b)[1].start()

    def project(i, b):
        v = dot_nn(A1[half(b)], W[rows_of(i)]) + small[pl.ds(i, 1)]
        v = v.astype(B16)
        QKV[i, half(b)] = v * jnp.where(i == 0, 0.125, 1.0).astype(B16)

        @pl.when(i == 2)
        def _():
            saves(b)[2].start()

    def attend(part, b):
        @pl.when(part == 0)
        def _():
            sp = dot_nt(pkey[...], QKV[0, half(b)])
            there = lax.broadcasted_iota(jnp.int32, sp.shape, 0) % 16 < 10
            SPRE[b] = jnp.where(there, sp, NEG)

        def pair(p):
            cols = pl.ds(pl.multiple_of(p * 128, 128), 128)
            q2, k2, v2 = QKV[0, half(b), cols], QKV[1, half(b), cols], QKV[2, half(b), cols]
            st = dot_nt(split_heads(k2), q2)
            probs, pres = [], []
            for e in range(2):
                sh = st[e * HALF : (e + 1) * HALF] + mask[b]
                sp = SPRE[b, pl.ds(pl.multiple_of(p * 32 + e * 16, 16), 16)]
                top = jnp.maximum(jnp.max(sh, axis=0, keepdims=True), jnp.max(sp, axis=0, keepdims=True))
                et, ep = jnp.exp(sh - top), jnp.exp(sp - top)
                inv = 1.0 / (jnp.sum(et, axis=0, keepdims=True) + jnp.sum(ep, axis=0, keepdims=True))
                probs.append((et * inv).astype(B16))
                pres.append((ep * inv).astype(B16))
            pr = jnp.concatenate(probs, axis=0)
            PROB[2 * b + p // 4, :, pl.ds(pl.multiple_of((p % 4) * HALF, HALF), HALF)] = pr
            PPRE[b, pl.ds(pl.multiple_of(p * 32, 32), 32)] = jnp.concatenate(pres, axis=0)
            ACC[half(b), cols] = dot_tn(pr, split_heads(v2))

        for p in range(4):
            pair(part * 4 + p)

        @pl.when(part == 1)
        def _():
            ATT[half(b)] = (ACC[half(b)] + dot_tn(PPRE[b], pval[...])).astype(B16)
            saves(b)[3].start()
            saves(b)[4].start()
            saves(b)[5].start()

    def mix(b):
        r = H[half(b)].astype(F32) + (dot_nn(ATT[half(b)], W[rows_of(3)]) + small[3:4])
        RES[half(b)] = r
        xhat, _ = whiten(r)
        A2[half(b)] = (xhat * small[12:13] + small[10:11]).astype(B16)
        saves(b)[6].start()
        saves(b)[7].start()

    def widen(j, b):
        x = dot_nn(A2[half(b)], W[rows_of(4 + j)]) + small[pl.ds(4 + j, 1)]
        x2 = x * x
        h = 0.5 + 0.5 * jnp.tanh(x * (GELU_C + (0.044715 * GELU_C) * x2))
        act = x * h
        ACT[j, half(b)] = act.astype(B16)
        GP[j, half(b)] = (h + act * (1.0 - h) * (2.0 * GELU_C + (6 * 0.044715 * GELU_C) * x2)).astype(B16)

        @pl.when(j == 3)
        def _():
            saves(b)[8].start()
            saves(b)[9].start()

    def narrow(b):
        v = RES[half(b)] + small[8:9]
        for j in range(4):
            v = v + dot_nn(ACT[j, half(b)], W[rows_of(8 + j)])
        OUT[half(b)] = v.astype(B16)

        @pl.when(s == 0)
        def _():
            cross(b).start()

        saves(b)[10].start()

    @pl.loop(0, NP + 5 + 2 * STAGES)
    def _(tick):
        @pl.when(tick < NP + 5)
        def _():
            g.step(tick, own)

            @pl.when(tick == 3)
            def _():
                prepare()

            @pl.when(tick >= 5)
            def _():
                g.complete(tick - 5)

                @pl.when(tick < 13)
                def _():
                    piece_out(tick - 5).start()

                @pl.when(tick == NP + 4)
                def _():
                    for k in range(8, NP):
                        piece_out(k).start()

        late = tick - (NP + 5)
        stage = (1 - s) * (tick - 5) + s * ((late + STAGES) % STAGES - STAGES * (late < 0).astype(jnp.int32))
        lo = s * (late // STAGES)
        hi = (1 - s) * 2 + s * (late // STAGES + 1)

        def when(i, body):
            @pl.when(stage == i)
            def _():
                pl.loop(lo, hi)(body)

        when(0, norm_in)

        @pl.when((stage >= 1) & (stage < 4))
        def _():
            pl.loop(lo, hi)(lambda b: project(stage - 1, b))

        @pl.when((stage >= 4) & (stage < 6))
        def _():
            pl.loop(lo, hi)(lambda b: attend(stage - 4, b))

        when(6, mix)

        @pl.when((stage >= 7) & (stage < 11))
        def _():
            pl.loop(lo, hi)(lambda b: widen(stage - 7, b))

        when(11, narrow)

    g.drain()
    packs_out()
    for cp in prep_saves():
        cp.wait()

    @pl.loop(0, NP)
    def _(k):
        piece_out(k).wait()

    @pl.loop(0, 2)
    def _(b):
        for cp in saves(b):
            cp.wait()

        @pl.when(s == 0)
        def _():
            cross(b).wait_send()


def forward_call(wq, wo, wf, wp, tokens, segs, pack, aux, r_in, r_out):
    any_, vm = pl.BlockSpec(memory_space=pl.ANY), pl.BlockSpec(memory_space=pltpu.VMEM)
    n, d = tokens.shape
    kept = [
        ((NP * d, d), B16), ((n, d), B16), ((n, d), B16), ((n, d), B16), ((3, n, d), B16), ((4, n, d), B16),
        ((2, HALF, HALF), B16), ((n, d), B16), ((n, d), F32), ((n, d), B16), ((4, n, d), B16), ((4, n, d), B16),
    ]
    shared = [((16, d), F32), ((HALF, d), B16), ((HALF, d), B16), ((16, 512), F32)]
    dma = pltpu.SemaphoreType.DMA
    order = [0, 2, 3, 4, 5, 6, 7, 8, 9, 10, 11, 1]
    scratch = [kept[i] for i in order] + [((2, HALF, HALF), F32), ((n, d), F32)] + shared
    scratch += [((2, HALF, HALF), F32), ((16, 16, 128), B16), ((16, 16, 128), F32)]
    return pl.pallas_call(
        forward_kernel,
        out_shape=[jax.ShapeDtypeStruct(*k) for k in kept + shared],
        in_specs=[any_] * 5 + [vm] * 3 + [any_] * 2,
        out_specs=[any_] * len(kept + shared),
        scratch_shapes=[pltpu.VMEM(*v) for v in scratch]
        + [dma((NP,)), dma((NP, 20)), dma((NP, 16)), dma, dma((2,)), dma((2,)), dma((3, NP)), dma((16,)), dma((16,)), dma((8,))],
        compiler_params=pltpu.CompilerParams(collective_id=0, has_side_effects=True, vmem_limit_bytes=62 << 20),
    )(wq, wo, wf, wp, tokens, segs, pack, aux, r_in, r_out)


def own_pack(gains, biases):
    rows = jnp.concatenate([biases.reshape(11, 64), gains.reshape(2, 64), jnp.zeros((3, 64), B16)])
    return jnp.concatenate([rows, rows], axis=1)


def prefix_rows(embed, in_bias, out_bias):
    in_bias = jnp.pad(in_bias, (0, 512)).reshape(1, 1024)
    return jnp.concatenate([embed, in_bias, out_bias.reshape(2, 1024), jnp.zeros((3, 1024), B16)])


SPLIT = 6
BACK_TICKS = 2 + 2 * SPLIT + NP + 6


def unwhiten(grad, xhat, rstd):
    return rstd * (
        grad
        - jnp.mean(grad, axis=-1, keepdims=True)
        - xhat * jnp.mean(grad * xhat, axis=-1, keepdims=True)
    )


def column_sum(v):
    return jnp.sum(v.astype(F32), axis=0, keepdims=True)


def backward_kernel(
    W_i, h_i, a1_i, qkv_i, prob_i, ppre_i, att_i, res_i, a2_i, gp_i, act_i, cot, r_out, small, pkey, pval,
    dh_o, oq, oo, of, op_, own_sums, KVB, HSUM,
    WG, H, A1, QKV, BIG, PPRE, ATT, RES, A2, GP, DM, DAT, DATT, DPP, DSP, ACC,
    RC, RY, RU, RD, T, SG, DKV, SB, RB, PF, PG, HP, HPR,
    wsem, lsem, osem, cs, cr, ys, yr, us, ur, ds_, dr, xs, xr, hs, bs, br, ps, pr, hx,
):
    s, d, z, y, c = place()

    def slot(k):
        return k + 8 * (1 - s) if k < 4 else k

    def fetch(ks):
        return [pltpu.make_async_copy(W_i.at[k], WG.at[slot(k)], wsem.at[k]) for k in ks]

    def begin(cps):
        for cp in cps:
            cp.start()

    def loads():
        pairs = [
            (gp_i, GP), (a2_i, A2), (res_i, RES), (att_i, ATT), (qkv_i, QKV), (ppre_i, PPRE), (a1_i, A1), (h_i, H),
            (act_i, BIG), (prob_i, BIG), (cot, DM),
        ]
        return [pltpu.make_async_copy(a, b, lsem.at[i]) for i, (a, b) in enumerate(pairs)]

    L_GP, L_A2, L_RES, L_ATT, L_QKV, L_PPRE, L_A1, L_H, L_ACT, L_PROB, L_COT = range(11)

    def begin_loads(which):
        begin([loads()[i] for i in which])

    pl.when(s == 1)(lambda: begin_loads((L_COT,)))
    begin(fetch((8, 9, 10, 11)))
    begin_loads((L_GP,))
    pl.when(s == 0)(lambda: begin_loads((L_ACT,)))
    SG[...] = jnp.zeros_like(SG)
    DKV[...] = jnp.zeros_like(DKV)
    SB[...] = jnp.zeros_like(SB)
    greet(s, d)

    def weights(ks):
        for cp in fetch(ks):
            cp.wait()

    def half(b):
        return pl.ds(pl.multiple_of(b * HALF, HALF), HALF)

    def weight(k):
        return WG[slot(k)].reshape(1024, 1024)

    def cross(b):
        return pltpu.make_async_remote_copy(
            H.at[half(b)], DM.at[half(b)], xs.at[b], xr.at[b], device_id=(1 - s, d), device_id_type=MESH
        )

    def dh_out(b):
        return pltpu.make_async_copy(H.at[half(b)], dh_o.at[half(b)], hs.at[b])

    def ffn_in(b):
        first = (b == 0)

        @pl.when(first)
        def _():
            @pl.when(s == 1)
            def _():
                loads()[L_COT].wait()

            weights((8, 9, 10, 11))
            loads()[L_GP].wait()
            begin(fetch((4, 5, 6, 7)))
            begin_loads((L_A2, L_RES))

            @pl.when(s == 1)
            def _():
                begin(fetch((3,)))
                begin_loads((L_QKV, L_PPRE, L_PROB))

            @pl.when(s == 0)
            def _():
                cross(0).wait_recv()

        for j in range(4):
            GP[j, half(b)] = (dot_nt(DM[half(b)], weight(8 + j)) * GP[j, half(b)].astype(F32)).astype(B16)

        @pl.when((s == 0) & (b == 1))
        def _():
            begin(fetch((3, 0, 1, 2)))

    def ffn_norm(b):
        @pl.when(b == 0)
        def _():
            weights((4, 5, 6, 7))
            loads()[L_A2].wait()
            loads()[L_RES].wait()
            begin_loads((L_ATT, L_A1, L_H))

            @pl.when(s == 0)
            def _():
                begin_loads((L_QKV, L_PPRE))

            @pl.when(s == 1)
            def _():
                begin(fetch((0, 1, 2)))

        grad = dot_nt(GP[0, half(b)], weight(4))
        for j in range(1, 4):
            grad = grad + dot_nt(GP[j, half(b)], weight(4 + j))
        xhat, rstd = whiten(RES[half(b)])
        SG[10:11] += jnp.sum(grad, axis=0, keepdims=True)
        SG[12:13] += jnp.sum(grad * xhat, axis=0, keepdims=True)
        res = DM[half(b)].astype(F32) + unwhiten(grad * small[12:13], xhat, rstd)
        RES[half(b)] = res
        DAT[half(b)] = res.astype(B16)

    def attn_out(b):
        @pl.when(b == 0)
        def _():
            weights((3,))
            for i in (L_ATT, L_QKV, L_PPRE):
                loads()[i].wait()

            loads()[L_PROB].wait()

        DATT[...] = dot_nt(DAT[half(b)], weight(3)).astype(B16)
        DPP[...] = dot_nt(pval[...], DATT[...])

    def attn_back(part, b):
        @pl.loop(part * 4, part * 4 + 4)
        def _(p):
            cols = pl.ds(pl.multiple_of(p * 128, 128), 128)
            q2, k2, v2 = QKV[0, half(b), cols], QKV[1, half(b), cols], QKV[2, half(b), cols]
            do2 = DATT[:, cols]
            pr = BIG[2 * b + p // 4, :, pl.ds(pl.multiple_of((p % 4) * HALF, HALF), HALF)]
            dp = dot_nt(split_heads(v2), do2)
            dss, pres = [], []
            for e in range(2):
                ph = pr[e * HALF : (e + 1) * HALF].astype(F32)
                dh = dp[e * HALF : (e + 1) * HALF]
                at = pl.ds(pl.multiple_of(p * 32 + e * 16, 16), 16)
                pp, dpp = PPRE[b, at].astype(F32), DPP[at]
                dot = jnp.sum(ph * dh, axis=0, keepdims=True) + jnp.sum(pp * dpp, axis=0, keepdims=True)
                dss.append((ph * (dh - dot)).astype(B16))
                pres.append((pp * (dpp - dot)).astype(B16))
            ds = jnp.concatenate(dss, axis=0)
            DSP[pl.ds(pl.multiple_of(p * 32, 32), 32)] = jnp.concatenate(pres, axis=0)
            left = lax.broadcasted_iota(jnp.int32, (HALF, 128), 1) < 64
            ACC[:, cols] = dot_tn(ds, split_heads(k2))
            dk = dot_nn(ds, q2)
            dv = dot_nn(pr, do2)
            QKV[1, half(b), cols] = jnp.where(left, dk[:HALF], dk[HALF:]).astype(B16)
            QKV[2, half(b), cols] = jnp.where(left, dv[:HALF], dv[HALF:]).astype(B16)

        @pl.when(part == 1)
        def _():
            def own_rows(full):
                out = jnp.zeros((16, 1024), F32)
                head = lax.broadcasted_iota(jnp.int32, (16, 1024), 1) // 64
                for i in range(16):
                    out = out + jnp.where(head == i, full[16 * i : 16 * i + 16], 0.0)
                return out

            DKV[0:16] += own_rows(dot_nn(DSP[...], QKV[0, half(b)]))
            DKV[16:32] += own_rows(dot_nn(PPRE[b], DATT[...]))
            QKV[0, half(b)] = ((ACC[...] + dot_tn(DSP[...], pkey[...])) * 0.125).astype(B16)

    def attn_norm(b):
        @pl.when(b == 0)
        def _():
            weights((0, 1, 2))
            loads()[L_A1].wait()
            loads()[L_H].wait()

        @pl.when((s == 1) & (b == 1))
        def _():
            loads()[L_ACT].start()

        grad = dot_nt(QKV[0, half(b)], weight(0))
        for i in range(1, 3):
            grad = grad + dot_nt(QKV[i, half(b)], weight(i))
        xhat, rstd = whiten(H[half(b)].astype(F32))
        SG[9:10] += jnp.sum(grad, axis=0, keepdims=True)
        SG[11:12] += jnp.sum(grad * xhat, axis=0, keepdims=True)
        H[half(b)] = (RES[half(b)] + unwhiten(grad * small[11:12], xhat, rstd)).astype(B16)

        @pl.when(s == 1)
        def _():
            cross(b).start()

        dh_out(b).start()

    def grad_proj():
        loads()[L_ACT].wait()

        @pl.when(s == 0)
        def _():
            cross(1).wait_recv()
        @pl.loop(0, 4)
        def _(i):
            for u in range(2):
                v = dot_tn(BIG[i, :, 512 * u : 512 * (u + 1)], DM[...]).astype(B16).reshape(2, 4, 64, 1024)
                for j in range(4):
                    WG[8 * s + j, i, u] = v[:, j]

        @pl.when(s == 0)
        def _():
            loads()[L_PROB].start()

    def put(k, a, v):
        for i in range(2):
            part = dot_tn(a[:, 512 * i : 512 * (i + 1)], v[...])
            WG[k, 2 * i : 2 * i + 2] = part.astype(B16).reshape(2, 2, 2, 64, 1024)

    def grad_fc(j):
        put(4 + j, A2, GP.at[j])

    def grad_out():
        put(slot(3), ATT, DAT)

    def grad_qkv(i):
        put(i + 8 * (1 - s), A1, QKV.at[i])

    send_sums, sums_in, sums_out = to_all(lambda to: SB.at[to], RB, bs, br)
    send_pref, pref_in, pref_out = to_all(lambda to: PF, PG, ps, pr)

    def r_out_in():
        return [pltpu.make_async_copy(r_out.at[:, pl.ds(1024 * i, 1024)], BIG.at[i], hx.at[i]) for i in range(2)]

    def hidden_across():
        return pltpu.make_async_remote_copy(HP, HPR, hx.at[2], hx.at[3], device_id=(1 - s, d), device_id_type=MESH)

    def small_first():
        for cp in r_out_in():
            cp.start()
        for i in range(3):
            SG[i : i + 1] = column_sum(QKV[i])
        SG[3:4] = column_sum(DAT[...])
        for j in range(4):
            SG[4 + j : 5 + j] = column_sum(GP[j])
        SG[8:9] = column_sum(DM[...])
        for i in range(16):
            for n in range(13):
                m = 11 * i + n
                row, at = (m // 16, 128 * (m % 16 // 2)) if n < 11 else (n, 128 * (i // 2))
                SB[i, n : n + 1] = SG[row : row + 1, at : at + 128]
            SB[i, 16:32] = DKV[16 * (i // 8) : 16 * (i // 8) + 16, 128 * (i % 8) : 128 * (i % 8) + 128]
        send_sums()
        RB[d] = SB[d]

    def small_second():
        sums_in()
        total = RB[0]
        for i in range(1, 16):
            total = total + RB[i]
        row = lax.broadcasted_iota(jnp.int32, (16, 128), 0)
        odd = jnp.where(row < 11, d + row, d) % 2 == 1
        own_sums[...] = jnp.where(odd, pltpu.roll(total[:16], 64, 1), total[:16])
        PF[...] = total[16:].astype(B16)
        send_pref()
        PG[d] = PF[...]

    def small_third():
        pref_in()
        for i in range(16):
            KVB[:, 128 * i : 128 * i + 128] = PG[i]
        for cp in r_out_in():
            cp.wait()
        HP[...] = dot_nt(KVB[:, :1024], BIG[0]) + dot_nt(KVB[:, 1024:], BIG[1])
        hidden_across().start()

    def small_last():
        hidden_across().wait()
        HSUM[...] = HP[...] + HPR[...]

    def held(r):
        a = r // 4
        return ((2 - a) * (1 - a) // 2) * (r + 8 * s) + a * (2 - a) * r + (a * (a - 1) // 2) * (11 - r + 8 * (1 - s))

    def across_c(r):
        return pltpu.make_async_remote_copy(
            WG.at[held(r), :, :, 1 - c], RC.at[r % 4], cs.at[r], cr.at[r],
            device_id=(s, z * 4 + y * 2 + 1 - c), device_id_type=MESH,
        )

    def across_y(r):
        return pltpu.make_async_remote_copy(
            WG.at[held(r), :, 1 - y, c], RY.at[r % 4], ys.at[r], yr.at[r],
            device_id=(s, z * 4 + (1 - y) * 2 + c), device_id_type=MESH,
        )

    def up(r, i):
        return pltpu.make_async_remote_copy(
            WG.at[held(r), i, y, c], RU.at[r % 7, i - 1], us.at[r, i - 1], ur.at[r, i - 1],
            device_id=(s, (z + 1) * 4 + y * 2 + c), device_id_type=MESH,
        )

    def down(r, i):
        return pltpu.make_async_remote_copy(
            WG.at[held(r), i, y, c], RD.at[r % 7, i], ds_.at[r, i], dr.at[r, i],
            device_id=(s, (z - 1) * 4 + y * 2 + c), device_id_type=MESH,
        )

    def each_out(r, act):
        k = held(r)
        src = T.at[r % 2]

        @pl.when(r < 4)
        def _():
            act(pltpu.make_async_copy(src, op_.at[0, pl.ds(pl.multiple_of(64 * r, 64), 64)], osem.at[r]))

        @pl.when((r >= 4) & (r < 8))
        def _():
            act(pltpu.make_async_copy(src, of.at[0, :, pl.ds(pl.multiple_of(1024 * (r - 4), 1024), 1024)], osem.at[r]))

        @pl.when(r == 8)
        def _():
            act(pltpu.make_async_copy(src, oo.at[0], osem.at[r]))

        @pl.when(r > 8)
        def _():
            act(pltpu.make_async_copy(src, oq.at[0, :, pl.ds(pl.multiple_of(1024 * (11 - r), 1024), 1024)], osem.at[r]))

    def start(cp):
        cp.start()

    def add(k, i, j, other):
        WG[k, i, j, c] = (WG[k, i, j, c].astype(F32) + other.astype(F32)).astype(B16)

    def live(r):
        return (r >= 0) & (r < NP)

    def scatter_step(t):
        @pl.when(live(t))
        def _():
            across_c(t).start()

        @pl.when(live(t - 1))
        def _():
            r = t - 1
            k = held(r)
            across_c(r).wait_recv()

            @pl.loop(0, 4)
            def _(i):
                add(k, i, 1 - y, RC[r % 4, i, 1 - y])

            across_y(r).start()

            @pl.loop(0, 4)
            def _(i):
                add(k, i, y, RC[r % 4, i, y])

        @pl.when(live(t - 2))
        def _():
            r = t - 2
            k = held(r)
            across_y(r).wait_recv()

            @pl.loop(0, 4)
            def _(i):
                add(k, i, y, RY[r % 4, i])

            @pl.when(z == 0)
            def _():
                for i in (3, 2, 1):
                    up(r, i).start()

            @pl.when(z == 3)
            def _():
                for i in (0, 1, 2):
                    down(r, i).start()

        for q in (1, 2, 3):
            n = 4 - q

            @pl.when(live(t - 2 - q))
            def _():
                r = t - 2 - q
                k = held(r)

                @pl.when(z == q)
                def _():
                    for i in range(3, q - 1, -1):
                        up(r, i).wait_recv()
                        if i > q:
                            add(k, i, y, RU[r % 7, i - 1])
                            up(r, i).start()

                @pl.when(z == 3 - q)
                def _():
                    for i in range(n):
                        down(r, i).wait_recv()
                        if i < n - 1:
                            add(k, i, y, RD[r % 7, i])
                            down(r, i).start()

        @pl.when(live(t - 5))
        def _():
            r = t - 5
            k = held(r)

            @pl.when(r >= 2)
            def _():
                each_out(r - 2, lambda cp: cp.wait())

            T[r % 2] = WG[k, z, y, c].astype(F32)

            @pl.when(z > 0)
            def _():
                T[r % 2] += RU[r % 7, z - 1].astype(F32)

            @pl.when(z < 3)
            def _():
                T[r % 2] += RD[r % 7, z].astype(F32)

            each_out(r, start)

    @pl.loop(0, BACK_TICKS)
    def _(tick):
        turn = tick // SPLIT

        @pl.when((tick == 0) | (tick == 2 * (1 - s) + SPLIT * s))
        def _():
            ffn_in((tick > 0).astype(jnp.int32))

        def when(i, at0, at1, body):
            early = (1 - s) * at0 + s * i
            late = (1 - s) * at1 + s * (SPLIT + i)

            @pl.when((tick == early) | (tick == late))
            def _():
                body((tick == late).astype(jnp.int32))

        when(1, 3, 4, ffn_norm)
        when(2, 5, 7, attn_out)
        first = (tick - 3) % SPLIT * s + (tick - 5) % 2 * (1 - s)

        @pl.when(((s == 0) & (tick >= 5) & (tick < 9)) | ((s == 1) & (tick < 2 * SPLIT) & (first < 2)))
        def _():
            attn_back(first, (1 - s) * ((tick - 5) // 2) + s * turn)

        when(5, 9, 10, attn_norm)
        r = tick - 1 - (2 * SPLIT - 1) * s

        @pl.when(r == 0)
        def _():
            grad_proj()

        @pl.when((r >= 4) & (r < 8))
        def _():
            grad_fc(r - 4)

        @pl.when(r == 8)
        def _():
            grad_out()

        @pl.when((r > 8) & (r < 12))
        def _():
            grad_qkv(11 - r)

        scatter_step(r)
        for at, body in ((10, small_first), (11, small_second), (13, small_third), (16, small_last)):
            pl.when(r == at)(body)

    @pl.loop(0, NP)
    def _(r):
        @pl.when(r >= NP - 2)
        def _():
            each_out(r, lambda cp: cp.wait())

        across_c(r).wait_send()
        across_y(r).wait_send()
        for q in range(3):

            @pl.when(z == q)
            def _():
                for i in range(q + 1, 4):
                    up(r, i).wait_send()

            @pl.when(z == q + 1)
            def _():
                for i in range(q + 1):
                    down(r, i).wait_send()

    sums_out()
    pref_out()

    @pl.loop(0, 2)
    def _(b):
        dh_out(b).wait()

        @pl.when(s == 1)
        def _():
            cross(b).wait_send()


def backward_call(kept, cot, r_out, small, pkey, pval):
    W, h, a1, qkv, prob, ppre, att, res, a2, gp, act = kept
    any_, vm = pl.BlockSpec(memory_space=pl.ANY), pl.BlockSpec(memory_space=pltpu.VMEM)
    n, d = h.shape
    dma = pltpu.SemaphoreType.DMA
    wide = (4, 2, 2, 64, d)
    outs = [
        ((n, d), B16), ((1, 64, 3 * d), F32), ((1, 64, d), F32), ((1, 64, 4 * d), F32), ((1, 256, d), F32),
        ((16, 128), F32), ((16, 2 * d), B16), ((16, 512), F32),
    ]
    scratch = [
        ((NP,) + wide, B16), ((n, d), B16), ((n, d), B16), ((3, n, d), B16), ((4, n, d), B16), ((2, HALF, HALF), B16), ((n, d), B16),
        ((n, d), F32), ((n, d), B16), ((4, n, d), B16), ((n, d), B16), ((n, d), B16), ((HALF, d), B16), ((HALF, HALF), F32),
        ((HALF, HALF), B16), ((HALF, d), F32),
        ((4, 4, 2, 64, d), B16), ((4, 4, 64, d), B16), ((7, 3, 64, d), B16), ((7, 3, 64, d), B16), ((2, 64, d), F32),
        ((16, d), F32), ((32, d), F32), ((16, 32, 128), F32), ((16, 32, 128), F32), ((16, 128), B16), ((16, 16, 128), B16),
        ((16, 512), F32), ((16, 512), F32),
    ]
    return pl.pallas_call(
        backward_kernel,
        out_shape=[jax.ShapeDtypeStruct(*o) for o in outs],
        in_specs=[any_] * 13 + [vm] * 3,
        out_specs=[any_] * 5 + [vm] * 3,
        scratch_shapes=[pltpu.VMEM(*v) for v in scratch] + [dma((NP,))] * 7 + [dma((NP, 3))] * 4 + [dma((2,))] * 3 + [dma((16,))] * 4 + [dma((4,))],
        compiler_params=pltpu.CompilerParams(collective_id=1, has_side_effects=True, vmem_limit_bytes=64 << 20),
    )(W.reshape((NP,) + wide), h, a1, qkv, prob, ppre, att, res, a2, gp, act, cot, r_out, small, pkey, pval)


def finish_kernel(
    o0, o1, o2, o3, o4, o5, hid, kvb, hsum, aux, r_in, sums,
    c0, c1, c2, c3, c4, c5, g_embed, g_in, g_in_bias, g_out, g_out_bias, g_gains, g_bias,
    G_IN, G_OUT, M0, M1, M2, M3, M4, M5, sem,
):
    held = (M0, M1, M2, M3, M4, M5)
    here = [pltpu.make_async_copy(a, m, sem.at[i]) for i, (a, m) in enumerate(zip((o0, o1, o2, o3, o4, o5), held))]
    away = [pltpu.make_async_copy(m, c, sem.at[8 + i]) for i, (m, c) in enumerate(zip(held, (c0, c1, c2, c3, c4, c5)))]
    for cp in here:
        cp.start()
    h = hid[...]
    kv = kvb[...]
    G_OUT[...] = dot_tn(h.astype(B16), kv)
    out_cp = pltpu.make_async_copy(G_OUT, g_out, sem.at[6])
    out_cp.start()
    g_out_bias[...] = column_sum(kv)
    for cp, out in zip(here, away):
        cp.wait()
        out.start()
    dp = (hsum[...] * (1.0 - h * h)).astype(B16)
    G_IN[...] = dot_tn(aux[...], dp)
    in_cp = pltpu.make_async_copy(G_IN, g_in, sem.at[7])
    in_cp.start()
    g_in_bias[...] = column_sum(dp)
    g_embed[...] = dot_nt(dp, r_in[...])[:10]
    g_gains[0] = sums[11:13, :64]
    for i in range(11):
        g_bias[:, 64 * i : 64 * i + 64] = sums[i : i + 1, :64]
    for cp in away + [out_cp, in_cp]:
        cp.wait()


def finish_call(large, hid, kvb, hsum, aux, r_in, sums):
    any_, vm = pl.BlockSpec(memory_space=pl.ANY), pl.BlockSpec(memory_space=pltpu.VMEM)
    d = r_in.shape[0]
    outs = [jax.ShapeDtypeStruct(x.shape, x.dtype) for x in large]
    outs += [jax.ShapeDtypeStruct(x, F32) for x in ((10, d), (d, 512), (1, 512), (512, 2 * d), (1, 2 * d), (1, 2, 64), (1, 704))]
    return pl.pallas_call(
        finish_kernel,
        out_shape=outs,
        in_specs=[any_] * 6 + [vm] * 6,
        out_specs=[any_] * 6 + [vm, any_, vm, any_, vm, vm, vm],
        scratch_shapes=[pltpu.VMEM((d, 512), F32), pltpu.VMEM((512, 2 * d), F32)]
        + [pltpu.VMEM(x.shape, x.dtype) for x in large]
        + [pltpu.SemaphoreType.DMA((14,))],
        compiler_params=pltpu.CompilerParams(vmem_limit_bytes=63 << 20),
    )(*large, hid, kvb, hsum, aux, r_in, sums)


def on_device(
    tokens,
    segment_ids,
    cotangent,
    w_qkv,
    w_attn_out,
    w_fc,
    w_proj,
    gains,
    biases,
    prefix_embed,
    reparam_in,
    reparam_in_bias,
    reparam_out,
    reparam_out_bias,
):
    aux = prefix_rows(prefix_embed, reparam_in_bias, reparam_out_bias)
    pack = own_pack(gains, biases)
    kept = forward_call(w_qkv, w_attn_out, w_fc, w_proj, tokens, segment_ids, pack, aux, reparam_in, reparam_out)
    small, pkey, pval, hid = kept[12:]
    *large, sums, kvb, hsum = backward_call(kept[:1] + kept[2:12], cotangent, reparam_out, small, pkey, pval)
    done = finish_call([kept[1]] + large, hid, kvb, hsum, aux, reparam_in, sums)
    return (
        done[0][None],
        done[1][None],
        *done[2:6],
        done[11],
        done[12],
        done[6],
        done[7],
        done[8][0],
        done[9],
        done[10][0],
    )


def passed_along(shard, axis, by):
    size = lax.axis_size(axis)
    pairs = [(i, i + by) for i in range(size) if 0 <= i + by < size]
    return lax.ppermute(shard, axis, pairs)


def norm_rows(v, gain, shift):
    mean = jnp.mean(v, axis=-1, keepdims=True)
    cent = v - mean
    var = jnp.mean(cent * cent, axis=-1, keepdims=True)
    return cent * lax.rsqrt(var + EPS) * gain + shift


def gelu_tanh(v):
    return jax.nn.gelu(v, approximate=True)


def forward_layer(h_b, segs, pkey, pval, params):
    w_q, w_o, w_f, w_p, gain_pair, bias_all = params
    width = w_o.shape[0]
    length = h_b.shape[0]
    heads, head_dim = (pkey.shape[1], pkey.shape[2])
    scale = 1.0 / math.sqrt(head_dim)
    gain_f = gain_pair.astype(jnp.float32)
    bias_f = bias_all.astype(jnp.float32)
    hf = h_b.astype(jnp.float32)
    a1b = norm_rows(hf, gain_f[0], bias_f[9 * width : 10 * width]).astype(jnp.bfloat16)
    qkv_b = (jnp.dot(a1b, w_q, preferred_element_type=jnp.float32) + bias_f[: 3 * width]).astype(
        jnp.bfloat16
    )
    split = qkv_b.reshape(length, 3, heads, head_dim)
    query, keys, values = (split[:, 0], split[:, 1], split[:, 2])
    s_tok = jnp.einsum("lhe,mhe->hlm", query, keys, preferred_element_type=jnp.float32) * scale
    s_pre = jnp.einsum("lhe,phe->hlp", query, pkey, preferred_element_type=jnp.float32) * scale
    place = jnp.arange(length)
    allowed = (segs[:, None] == segs[None, :]) & (place[None, :] <= place[:, None])
    s_tok = jnp.where(allowed[None], s_tok, NEG)
    top = jnp.maximum(
        jnp.max(s_tok, axis=-1, keepdims=True), jnp.max(s_pre, axis=-1, keepdims=True)
    )
    e_tok = jnp.exp(s_tok - top)
    e_pre = jnp.exp(s_pre - top)
    total = jnp.sum(e_tok, axis=-1, keepdims=True) + jnp.sum(e_pre, axis=-1, keepdims=True)
    p_tok = e_tok / total
    p_pre = e_pre / total
    mixed = jnp.einsum(
        "hlm,mhe->lhe", p_tok.astype(jnp.bfloat16), values, preferred_element_type=jnp.float32
    ) + jnp.einsum(
        "hlp,phe->lhe", p_pre.astype(jnp.bfloat16), pval, preferred_element_type=jnp.float32
    )
    attn_b = mixed.reshape(length, width).astype(jnp.bfloat16)
    resid = hf + (
        jnp.dot(attn_b, w_o, preferred_element_type=jnp.float32) + bias_f[3 * width : 4 * width]
    )
    a2b = norm_rows(resid, gain_f[1], bias_f[10 * width : 11 * width]).astype(jnp.bfloat16)
    pre_act = jnp.dot(a2b, w_f, preferred_element_type=jnp.float32) + bias_f[4 * width : 8 * width]
    act_b = gelu_tanh(pre_act).astype(jnp.bfloat16)
    result = resid + (
        jnp.dot(act_b, w_p, preferred_element_type=jnp.float32) + bias_f[8 * width : 9 * width]
    )
    return (result, (hf, a1b, qkv_b, p_tok, p_pre, attn_b, resid, a2b, pre_act, act_b))


def backward_ffn(grad_out, keep, params):
    w_q, w_o, w_f, w_p, gain_pair, bias_all = params
    hf, a1b, qkv_b, p_tok, p_pre, attn_b, resid, a2b, pre_act, act_b = keep
    width = w_o.shape[0]
    gain_f = gain_pair.astype(jnp.float32)
    bias_f = bias_all.astype(jnp.float32)
    dm_b = grad_out.astype(jnp.bfloat16)
    grad_wp = jnp.einsum("lf,ld->fd", act_b, dm_b, preferred_element_type=jnp.float32)
    grad_bp = jnp.sum(dm_b.astype(jnp.float32), axis=0)
    d_act = jnp.dot(dm_b, w_p.T, preferred_element_type=jnp.float32)
    dpre_b = jax.vjp(gelu_tanh, pre_act)[1](d_act)[0].astype(jnp.bfloat16)
    grad_wf = jnp.einsum("ld,lf->df", a2b, dpre_b, preferred_element_type=jnp.float32)
    grad_bf = jnp.sum(dpre_b.astype(jnp.float32), axis=0)
    d_a2 = jnp.dot(dpre_b, w_f.T, preferred_element_type=jnp.float32)
    norm_back = jax.vjp(norm_rows, resid, gain_f[1], bias_f[10 * width : 11 * width])[1]
    d_resid_norm, grad_g2, grad_c2 = norm_back(d_a2)
    d_resid = grad_out + d_resid_norm
    return (d_resid, (grad_wf, grad_wp), (grad_bf, grad_bp, grad_g2, grad_c2))


def backward_attn(d_resid, keep, pkey, pval, params):
    w_q, w_o, w_f, w_p, gain_pair, bias_all = params
    hf, a1b, qkv_b, p_tok, p_pre, attn_b, resid, a2b, pre_act, act_b = keep
    width = w_o.shape[0]
    length = hf.shape[0]
    heads, head_dim = (pkey.shape[1], pkey.shape[2])
    prefix_len = pkey.shape[0]
    scale = 1.0 / math.sqrt(head_dim)
    gain_f = gain_pair.astype(jnp.float32)
    bias_f = bias_all.astype(jnp.float32)
    split = qkv_b.reshape(length, 3, heads, head_dim)
    query, keys, values = (split[:, 0], split[:, 1], split[:, 2])
    dat_b = d_resid.astype(jnp.bfloat16)
    grad_wo = jnp.einsum("ld,le->de", attn_b, dat_b, preferred_element_type=jnp.float32)
    grad_bo = jnp.sum(dat_b.astype(jnp.float32), axis=0)
    dattn_b = jnp.dot(dat_b, w_o.T, preferred_element_type=jnp.float32).astype(jnp.bfloat16)
    dattn_b = dattn_b.reshape(length, heads, head_dim)
    dp_tok = jnp.einsum("lhe,mhe->hlm", dattn_b, values, preferred_element_type=jnp.float32)
    dp_pre = jnp.einsum("lhe,phe->hlp", dattn_b, pval, preferred_element_type=jnp.float32)
    row_dot = jnp.sum(p_tok * dp_tok, axis=-1, keepdims=True) + jnp.sum(
        p_pre * dp_pre, axis=-1, keepdims=True
    )
    ds_tok = (p_tok * (dp_tok - row_dot)).astype(jnp.bfloat16)
    ds_pre = (p_pre * (dp_pre - row_dot)).astype(jnp.bfloat16)
    d_query = (
        jnp.einsum("hlm,mhe->lhe", ds_tok, keys, preferred_element_type=jnp.float32)
        + jnp.einsum("hlp,phe->lhe", ds_pre, pkey, preferred_element_type=jnp.float32)
    ) * scale
    d_keys = jnp.einsum("hlm,lhe->mhe", ds_tok, query, preferred_element_type=jnp.float32) * scale
    d_values = jnp.einsum(
        "hlm,lhe->mhe", p_tok.astype(jnp.bfloat16), dattn_b, preferred_element_type=jnp.float32
    )
    grad_pkey = (
        jnp.einsum("hlp,lhe->phe", ds_pre, query, preferred_element_type=jnp.float32) * scale
    )
    grad_pval = jnp.einsum(
        "hlp,lhe->phe", p_pre.astype(jnp.bfloat16), dattn_b, preferred_element_type=jnp.float32
    )
    dqkv_b = (
        jnp.stack([d_query, d_keys, d_values], axis=1)
        .reshape(length, 3 * width)
        .astype(jnp.bfloat16)
    )
    grad_wq = jnp.einsum("ld,lc->dc", a1b, dqkv_b, preferred_element_type=jnp.float32)
    grad_bq = jnp.sum(dqkv_b.astype(jnp.float32), axis=0)
    d_a1 = jnp.dot(dqkv_b, w_q.T, preferred_element_type=jnp.float32)
    norm_back_first = jax.vjp(norm_rows, hf, gain_f[0], bias_f[9 * width : 10 * width])[1]
    d_in_norm, grad_g1, grad_c1 = norm_back_first(d_a1)
    d_input = d_resid + d_in_norm
    grad_prefix = jnp.concatenate(
        [grad_pkey.reshape(prefix_len, width), grad_pval.reshape(prefix_len, width)], axis=1
    )
    return (d_input, (grad_wq, grad_wo), (grad_bq, grad_bo, grad_g1, grad_c1), grad_prefix)


def assemble(ffn_mats, ffn_small, attn_mats, attn_small):
    grad_bf, grad_bp, grad_g2, grad_c2 = ffn_small
    grad_bq, grad_bo, grad_g1, grad_c1 = attn_small
    grad_gains = jnp.stack([grad_g1, grad_g2])
    grad_bias = jnp.concatenate([grad_bq, grad_bo, grad_bf, grad_bp, grad_c1, grad_c2])
    return (attn_mats[0], attn_mats[1], ffn_mats[0], ffn_mats[1], grad_gains, grad_bias)


def on_device_general(
    tokens,
    segment_ids,
    cotangent,
    w_qkv,
    w_attn_out,
    w_fc,
    w_proj,
    gains,
    biases,
    prefix_embed,
    reparam_in,
    reparam_in_bias,
    reparam_out,
    reparam_out_bias,
):
    section = lax.axis_index("section")
    micro, row_len = segment_ids.shape
    width = tokens.shape[1]
    prefix_len = prefix_embed.shape[0]
    head_dim = width // HEADS
    gathered = (
        lax.all_gather(w_qkv, "dp", axis=1, tiled=True),
        lax.all_gather(w_attn_out, "dp", axis=1, tiled=True),
        lax.all_gather(w_fc, "dp", axis=1, tiled=True),
        lax.all_gather(w_proj, "dp", axis=1, tiled=True),
        lax.all_gather(gains, "dp", axis=2, tiled=True),
        lax.all_gather(biases, "dp", axis=1, tiled=True),
    )
    params = tuple((item[0] for item in gathered))
    pre_hidden = jnp.dot(
        prefix_embed, reparam_in, preferred_element_type=jnp.float32
    ) + reparam_in_bias.astype(jnp.float32)
    hidden = jnp.tanh(pre_hidden)
    hidden_b = hidden.astype(jnp.bfloat16)
    prefix_kv = (
        jnp.dot(hidden_b, reparam_out, preferred_element_type=jnp.float32)
        + reparam_out_bias.astype(jnp.float32)
    ).astype(jnp.bfloat16)
    pkey = prefix_kv[:, :width].reshape(prefix_len, HEADS, head_dim)
    pval = prefix_kv[:, width:].reshape(prefix_len, HEADS, head_dim)
    token_rows = tokens.reshape(micro, row_len, width)
    cot_rows = cotangent.reshape(micro, row_len, width)
    received = jnp.zeros((row_len, width), jnp.bfloat16)
    outputs = jnp.zeros((micro, row_len, width), jnp.bfloat16)
    stored = []
    for tick in range(micro + 1):
        index = tick - section
        active = (index >= 0) & (index < micro)
        slot = jnp.clip(index, 0, micro - 1)
        segs = segment_ids[slot]
        h_b = jnp.where(section == 0, token_rows[slot], received)
        result, keep = forward_layer(h_b, segs, pkey, pval, params)
        result_b = result.astype(jnp.bfloat16)
        outputs = jnp.where(active, outputs.at[slot].set(result_b), outputs)
        stored.append(keep)
        if tick < micro:
            received = passed_along(result_b, "section", 1)
    regathered = (
        lax.all_gather(w_qkv, "dp", axis=1, tiled=True),
        lax.all_gather(w_attn_out, "dp", axis=1, tiled=True),
        lax.all_gather(w_fc, "dp", axis=1, tiled=True),
        lax.all_gather(w_proj, "dp", axis=1, tiled=True),
        lax.all_gather(gains, "dp", axis=2, tiled=True),
        lax.all_gather(biases, "dp", axis=1, tiled=True),
    )
    params_back = tuple((item[0] for item in regathered))
    stacked = jax.tree.map(lambda *items: jnp.stack(items), *stored)
    coming = jnp.zeros((row_len, width), jnp.bfloat16)
    in_grads = jnp.zeros((micro, row_len, width), jnp.bfloat16)
    grad_total = None
    prefix_total = None
    for tick in range(micro + 1):
        index = micro - tick - section
        active = (index >= 0) & (index < micro)
        slot = jnp.clip(index, 0, micro - 1)
        segs = segment_ids[slot]
        saved = jax.tree.map(lambda item: item[slot + section], stacked)
        grad_out = jnp.where(
            section == 1, cot_rows[slot].astype(jnp.float32), coming.astype(jnp.float32)
        )
        keep = saved
        d_resid, ffn_mats, ffn_small = backward_ffn(grad_out, keep, params_back)
        ffn_mats = jax.tree.map(
            lambda item: jnp.where(active, item, jnp.zeros_like(item)), ffn_mats
        )
        ffn_small = jax.tree.map(
            lambda item: jnp.where(active, item, jnp.zeros_like(item)), ffn_small
        )
        d_input, attn_mats, attn_small, grad_prefix = backward_attn(
            d_resid, keep, pkey, pval, params_back
        )
        attn_mats = jax.tree.map(
            lambda item: jnp.where(active, item, jnp.zeros_like(item)), attn_mats
        )
        attn_small = jax.tree.map(
            lambda item: jnp.where(active, item, jnp.zeros_like(item)), attn_small
        )
        grad_prefix = jnp.where(active, grad_prefix, jnp.zeros_like(grad_prefix))
        grads = assemble(ffn_mats, ffn_small, attn_mats, attn_small)
        if grad_total is None:
            grad_total = grads
            prefix_total = grad_prefix
        else:
            grad_total = jax.tree.map(lambda left, right: left + right, grad_total, grads)
            prefix_total = prefix_total + grad_prefix
        d_input_b = d_input.astype(jnp.bfloat16)
        in_grads = jnp.where(active, in_grads.at[slot].set(d_input_b), in_grads)
        if tick < micro:
            coming = passed_along(d_input_b, "section", -1)
    lifted = tuple((item[None] for item in grad_total))
    weight_grads = (
        lax.psum_scatter(lifted[0], "dp", scatter_dimension=1, tiled=True),
        lax.psum_scatter(lifted[1], "dp", scatter_dimension=1, tiled=True),
        lax.psum_scatter(lifted[2], "dp", scatter_dimension=1, tiled=True),
        lax.psum_scatter(lifted[3], "dp", scatter_dimension=1, tiled=True),
        lax.psum_scatter(lifted[4], "dp", scatter_dimension=2, tiled=True),
        lax.psum_scatter(lifted[5], "dp", scatter_dimension=1, tiled=True),
    )
    prefix_grad = lax.psum(prefix_total, "dp")
    prefix_grad_b = prefix_grad.astype(jnp.bfloat16)
    grad_reparam_out = jnp.einsum(
        "pr,pc->rc", hidden_b, prefix_grad_b, preferred_element_type=jnp.float32
    )
    grad_reparam_out_bias = jnp.sum(prefix_grad_b.astype(jnp.float32), axis=0)
    hidden_part = jnp.dot(prefix_grad_b, reparam_out.T, preferred_element_type=jnp.float32)
    hidden_grad = lax.psum(hidden_part, "section")
    dpre_hidden_b = (hidden_grad * (1.0 - hidden * hidden)).astype(jnp.bfloat16)
    grad_reparam_in = jnp.einsum(
        "pd,pr->dr", prefix_embed, dpre_hidden_b, preferred_element_type=jnp.float32
    )
    grad_reparam_in_bias = jnp.sum(dpre_hidden_b.astype(jnp.float32), axis=0)
    grad_prefix_embed = jnp.dot(dpre_hidden_b, reparam_in.T, preferred_element_type=jnp.float32)
    layer_outs = outputs.reshape(1, micro * row_len, width)
    input_grads = in_grads.reshape(1, micro * row_len, width)
    return (
        layer_outs,
        input_grads,
        weight_grads[0],
        weight_grads[1],
        weight_grads[2],
        weight_grads[3],
        weight_grads[4],
        weight_grads[5],
        grad_prefix_embed,
        grad_reparam_in,
        grad_reparam_in_bias,
        grad_reparam_out,
        grad_reparam_out_bias,
    )


def solution(mesh):
    return jax.shard_map(
        on_device if mesh.shape["dp"] == 16 else on_device_general,
        mesh=mesh,
        in_specs=(
            P("dp", None),
            P("dp", None),
            P("dp", None),
            P("section", "dp", None),
            P("section", "dp", None),
            P("section", "dp", None),
            P("section", "dp", None),
            P("section", None, "dp"),
            P("section", "dp"),
            P(),
            P(),
            P(),
            P(None, "section"),
            P("section"),
        ),
        out_specs=(
            P("section", "dp", None),
            P("section", "dp", None),
            P("section", "dp", None),
            P("section", "dp", None),
            P("section", "dp", None),
            P("section", "dp", None),
            P("section", None, "dp"),
            P("section", "dp"),
            P(),
            P(),
            P(),
            P(None, "section"),
            P("section"),
        ),
        check_vma=False,
    )
```

```python
import math

import jax
import jax.numpy as jnp
from jax import lax
from jax.experimental import pallas as pl
from jax.experimental.pallas import tpu as pltpu
from jax.sharding import PartitionSpec as P

HEADS = 16
EPS = 1e-05
NEG = -1000000000.0
MESH = pl.DeviceIdType.MESH
F32 = jnp.float32
B16 = jnp.bfloat16
NP = 12
MAIN = 896
AHEAD = 1


def place():
    s = lax.axis_index("section"); d = lax.axis_index("dp")
    return s, d, d // 4, (d // 2) % 2, d % 2

def greet(s, d):
    bar = pltpu.get_barrier_semaphore()
    for i in range(1, 16):
        pl.semaphore_signal(bar, 1, device_id=(s, (d + i) % 16), device_id_type=MESH)
    pl.semaphore_signal(bar, 1, device_id=(1 - s, d), device_id_type=MESH)
    pl.semaphore_wait(bar, 16)


def to_all(src, dst, ss, rs):
    s, d = lax.axis_index("section"), lax.axis_index("dp")

    def cp(i, frm):
        to = (d + i) % 16
        return pltpu.make_async_remote_copy(
            src(to), dst.at[frm], ss.at[i], rs.at[i], device_id=(s, to), device_id_type=MESH
        )

    def start():
        for i in range(1, 16):
            cp(i, d).start()

    def arrive():
        for i in range(1, 16):
            cp(i, (d + 16 - i) % 16).wait_recv()

    def finish():
        for i in range(1, 16):
            cp(i, d).wait_send()

    return start, arrive, finish


class Gather:
    def __init__(self, W, ssem, rsem, tsem, qsem):
        self.W, self.ssem, self.rsem, self.tsem, self.qsem = W, ssem, rsem, tsem, qsem
        self.s, self.d, self.z, self.y, self.c = place()
    def blk(self, k, d):
        i = k // 8
        row = (1-i)*(1024*k+64*d) + i*(8192+256*d+64*(k-8))
        return self.W.at[pl.ds(pl.multiple_of(row, 64), 64)]
    def cp(self, k, origin, target, slot, width=1024):
        b = self.blk(k, origin)
        if width < 1024: b = b.at[:, pl.ds(0, width)]
        return pltpu.make_async_remote_copy(src_ref=b, dst_ref=b, send_sem=self.ssem.at[k, slot], recv_sem=self.rsem.at[k, origin],
            device_id=(self.s, target), device_id_type=MESH)
    def dev(self, z, y, c): return z*4+y*2+c
    def arrived(self, k, origin): self.cp(k, origin, origin, 0).wait_recv()
    def to_up(self, k, zo, op):
        op(self.cp(k, self.dev(zo, self.y, self.c), self.dev(self.z+1, self.y, self.c), zo))
    def to_down(self, k, zo, op):
        op(self.cp(k, self.dev(zo, self.y, self.c), self.dev(self.z-1, self.y, self.c), 4+zo))
    def to_y(self, k, zo, op, width=MAIN):
        op(self.cp(k, self.dev(zo, self.y, self.c), self.dev(self.z, 1-self.y, self.c), 8+zo, width))
    def strip(self, k, zo, to, slot):
        b = self.blk(k, self.dev(zo, 1-self.y, self.c)).at[:, pl.ds(MAIN, 1024-MAIN)]
        return pltpu.make_async_remote_copy(src_ref=b, dst_ref=b, send_sem=self.tsem.at[k, slot], recv_sem=self.qsem.at[k, zo],
            device_id=(self.s, self.dev(to, self.y, self.c)), device_id_type=MESH)
    def strip_up(self, k, zo, op): op(self.strip(k, zo, self.z+1, zo))
    def strip_down(self, k, zo, op): op(self.strip(k, zo, self.z-1, 4+zo))
    def to_c(self, k, zo, yo, op):
        op(self.cp(k, self.dev(zo, yo, self.c), self.dev(self.z, self.y, 1-self.c), 12+zo*2+yo))
    def step(self, t, own):
        z, y, c = self.z, self.y, self.c
        start = lambda cp: cp.start()
        def fresh(k):
            own(k)
            self.to_y(k, z, start, 1024)
            @pl.when(z < 3)
            def _(): self.to_up(k, z, start)
            @pl.when(z > 0)
            def _(): self.to_down(k, z, start)
            self.to_c(k, z, y, start)
        @pl.when(t == 0)
        def _():
            for k in range(AHEAD): fresh(k)
        @pl.when(t + AHEAD < NP)
        def _(): fresh(t + AHEAD)
        for q in (1, 2, 3, 4):
            k = t - q
            ok = (k >= 0) & (k < NP)
            if q < 4:
                @pl.when(ok & (z - q >= 0))
                def _():
                    self.arrived(k, self.dev(z-q, y, c))
                    @pl.when(z < 3)
                    def _(): self.to_up(k, z-q, start)
                    self.to_y(k, z-q, start)
                    self.to_c(k, z-q, y, start)
                @pl.when(ok & (z + q <= 3))
                def _():
                    self.arrived(k, self.dev(z+q, y, c))
                    @pl.when(z > 0)
                    def _(): self.to_down(k, z+q, start)
                    self.to_y(k, z+q, start)
                    self.to_c(k, z+q, y, start)
            e = q - 1
            def side(zo):
                o = self.dev(zo, 1-y, c)
                self.cp(k, o, o, 0, MAIN).wait_recv()
                self.to_c(k, zo, 1-y, start)
            if e == 0:
                @pl.when(ok)
                def _():
                    self.arrived(k, self.dev(z, 1-y, c))
                    @pl.when(z < 3)
                    def _(): self.strip_up(k, z, start)
                    @pl.when(z > 0)
                    def _(): self.strip_down(k, z, start)
                    self.to_c(k, z, 1-y, start)
            else:
                @pl.when(ok & (z - e >= 0))
                def _():
                    self.strip(k, z-e, z, 0).wait_recv()
                    @pl.when(z < 3)
                    def _(): self.strip_up(k, z-e, start)
                    side(z-e)
                @pl.when(ok & (z + e <= 3))
                def _():
                    self.strip(k, z+e, z, 0).wait_recv()
                    @pl.when(z > 0)
                    def _(): self.strip_down(k, z+e, start)
                    side(z+e)
    def complete(self, k):
        for i in range(8):
            self.arrived(k, 2*i + 1-self.c)
    def drain(self):
        fin = lambda cp: cp.wait_send()
        z, y = self.z, self.y
        @pl.loop(0, NP)
        def _(k):
            for zo in range(4):
                @pl.when((zo <= z) & (z < 3))
                def _(): self.to_up(k, zo, fin)
                @pl.when((zo >= z) & (z > 0))
                def _(): self.to_down(k, zo, fin)
                @pl.when(zo == z)
                def _(): self.to_y(k, zo, fin, 1024)
                @pl.when(zo != z)
                def _(): self.to_y(k, zo, fin)
                @pl.when((zo <= z) & (z < 3))
                def _(): self.strip_up(k, zo, fin)
                @pl.when((zo >= z) & (z > 0))
                def _(): self.strip_down(k, zo, fin)
                for yo in range(2): self.to_c(k, zo, yo, fin)

def own_copies(wq, wo, wf, wp, g, sem):
    out = []
    for k in range(NP):
        if k < 3: src = wq.at[0, :, pl.ds(1024*k, 1024)]
        elif k == 3: src = wo.at[0]
        elif k < 8: src = wf.at[0, :, pl.ds(1024*(k-4), 1024)]
        else: src = wp.at[0, pl.ds(64*(k-8), 64)]
        out.append(pltpu.make_async_copy(src, g.blk(jnp.int32(k), g.d), sem.at[k]))
    return out


HALF = 256
STAGES = 12
GELU_C = math.sqrt(2.0 / math.pi)


def dot_nn(a, b):
    return lax.dot_general(a, b, (((1,), (0,)), ((), ())), preferred_element_type=F32)


def dot_nt(a, b):
    return lax.dot_general(a, b, (((1,), (1,)), ((), ())), preferred_element_type=F32)


def dot_tn(a, b):
    return lax.dot_general(a, b, (((0,), (0,)), ((), ())), preferred_element_type=F32)


def whiten(v):
    mean = jnp.mean(v, axis=-1, keepdims=True)
    cent = v - mean
    rstd = lax.rsqrt(jnp.mean(cent * cent, axis=-1, keepdims=True) + EPS)
    return cent * rstd, rstd


def split_heads(pair):
    left = lax.broadcasted_iota(jnp.int32, pair.shape, 1) < 64
    zero = jnp.zeros_like(pair)
    return jnp.concatenate([jnp.where(left, pair, zero), jnp.where(left, zero, pair)], axis=0)


def forward_kernel(
    wq, wo, wf, wp, tokens, segs, pack, aux, r_in, r_out,
    W_o, out_o, h_o, a1_o, qkv_o, prob_o, ppre_o, att_o, res_o, a2_o, gp_o, act_o, small_o, pkey_o, pval_o, hid_o,
    W, H, A1, QKV, PROB, PPRE, ATT, RES, A2, GP, ACT, OUT, SPRE, ACC, small, pkey, pval, hid, mask, PACKS, ROWS,
    own_sem, ssem, rsem, tsem, qsem, hsem, xs, xr, save_sem, ps, pr, psem,
):
    g = Gather(W, ssem, rsem, tsem, qsem)
    s = g.s
    for cp in own_copies(wq, wo, wf, wp, g, own_sem):
        cp.start()
    r_in_parts = [pltpu.make_async_copy(r_in.at[pl.ds(512 * i, 512)], ACT.at[2, :, pl.ds(512 * i, 512)], psem.at[i]) for i in range(2)]
    r_out_parts = [pltpu.make_async_copy(r_out.at[:, pl.ds(1024 * i, 1024)], ACT.at[i], psem.at[2 + i]) for i in range(2)]
    for cp in r_in_parts + r_out_parts:
        cp.start()
    greet(s, g.d)
    send_packs, packs_in, packs_out = to_all(lambda to: pack, PACKS, ps, pr)

    def prep_saves():
        pairs = [(small, small_o), (pkey, pkey_o), (pval, pval_o), (hid, hid_o)]
        return [pltpu.make_async_copy(a, b, psem.at[4 + i]) for i, (a, b) in enumerate(pairs)]

    def prepare():
        for cp in r_in_parts + r_out_parts:
            cp.wait()
        ph = dot_nn(aux[:, :512], ACT[2, :, :512]) + dot_nn(aux[:, 512:], ACT[2, :, 512:])
        hid[...] = jnp.tanh(ph + aux[10:11, :512].astype(F32))
        hb = hid[...].astype(B16)
        head = lax.broadcasted_iota(jnp.int32, (16, 1024), 1) // 64
        for i, big in enumerate((pkey, pval)):
            kv = (dot_nn(hb, ACT[i]) + aux[11 + i : 12 + i].astype(F32)).astype(B16)
            for h in range(16):
                big[16 * h : 16 * h + 16] = jnp.where(head == h, kv, jnp.zeros_like(kv))
        key = lax.broadcasted_iota(jnp.int32, (HALF, HALF), 0)
        query = lax.broadcasted_iota(jnp.int32, (HALF, HALF), 1)
        for b in range(2):
            by_query = jnp.broadcast_to(segs[b : b + 1].astype(F32), (HALF, HALF))
            ok = (by_query.T == by_query) & (key <= query)
            mask[b] = jnp.where(ok, 0.0, NEG)
        packs_in()
        ROWS[...] = PACKS[...].astype(F32)
        left = lax.broadcasted_iota(jnp.int32, (1, 128), 1) < 64
        small[...] = jnp.zeros_like(small)
        for n in range(104):
            row, at = n // 8, 128 * (n % 8)
            if row < 11:
                (d0, r0), (d1, r1) = divmod(2 * n, 11), divmod(2 * n + 1, 11)
            else:
                (d0, r0), (d1, r1) = (2 * (n % 8), row), (2 * (n % 8) + 1, row)
            small[row : row + 1, at : at + 128] = jnp.where(left, ROWS[d0, r0 : r0 + 1], ROWS[d1, r1 : r1 + 1])
        for cp in prep_saves():
            cp.start()

    send_packs()
    PACKS[g.d] = pack[...]

    def tokens_in():
        return pltpu.make_async_copy(tokens, H, hsem)

    def half(b):
        return pl.ds(pl.multiple_of(b * HALF, HALF), HALF)

    def cross(b):
        return pltpu.make_async_remote_copy(
            OUT.at[half(b)], H.at[half(b)], xs.at[b], xr.at[b], device_id=(1 - s, g.d), device_id_type=MESH
        )

    @pl.when(s == 0)
    def _():
        tokens_in().start()

    def own(t):
        b = g.blk(t, g.d)
        pltpu.make_async_copy(b, b, own_sem.at[t]).wait()

    def rows_of(k):
        return pl.ds(pl.multiple_of(k * 1024, 1024), 1024)

    def saves(b):
        r = half(b)
        pairs = [
            (H.at[r], h_o.at[r]), (A1.at[r], a1_o.at[r]), (QKV.at[:, r], qkv_o.at[:, r]), (PROB.at[pl.ds(2 * b, 2)], prob_o.at[pl.ds(2 * b, 2)]),
            (PPRE.at[b], ppre_o.at[b]), (ATT.at[r], att_o.at[r]), (RES.at[r], res_o.at[r]), (A2.at[r], a2_o.at[r]),
            (GP.at[:, r], gp_o.at[:, r]), (ACT.at[:, r], act_o.at[:, r]), (OUT.at[r], out_o.at[r]),
        ]
        return [pltpu.make_async_copy(src, dst, save_sem.at[b, i]) for i, (src, dst) in enumerate(pairs)]

    def piece_out(k):
        return pltpu.make_async_copy(W.at[rows_of(k)], W_o.at[rows_of(k)], save_sem.at[2, k])

    def norm_in(b):
        @pl.when(s == 0)
        def _():
            @pl.when(b == 0)
            def _():
                tokens_in().wait()

        @pl.when(s == 1)
        def _():
            cross(b).wait_recv()

        xhat, _ = whiten(H[half(b)].astype(F32))
        A1[half(b)] = (xhat * small[11:12] + small[9:10]).astype(B16)
        saves(b)[0].start()
        saves(b)[1].start()

    def project(i, b):
        v = dot_nn(A1[half(b)], W[rows_of(i)]) + small[pl.ds(i, 1)]
        v = v.astype(B16)
        QKV[i, half(b)] = v * jnp.where(i == 0, 0.125, 1.0).astype(B16)

        @pl.when(i == 2)
        def _():
            saves(b)[2].start()

    def attend(part, b):
        @pl.when(part == 0)
        def _():
            sp = dot_nt(pkey[...], QKV[0, half(b)])
            there = lax.broadcasted_iota(jnp.int32, sp.shape, 0) % 16 < 10
            SPRE[b] = jnp.where(there, sp, NEG)

        def pair(p):
            cols = pl.ds(pl.multiple_of(p * 128, 128), 128)
            q2, k2, v2 = QKV[0, half(b), cols], QKV[1, half(b), cols], QKV[2, half(b), cols]
            st = dot_nt(split_heads(k2), q2)
            probs, pres = [], []
            for e in range(2):
                sh = st[e * HALF : (e + 1) * HALF] + mask[b]
                sp = SPRE[b, pl.ds(pl.multiple_of(p * 32 + e * 16, 16), 16)]
                top = jnp.maximum(jnp.max(sh, axis=0, keepdims=True), jnp.max(sp, axis=0, keepdims=True))
                et, ep = jnp.exp(sh - top), jnp.exp(sp - top)
                inv = 1.0 / (jnp.sum(et, axis=0, keepdims=True) + jnp.sum(ep, axis=0, keepdims=True))
                probs.append((et * inv).astype(B16))
                pres.append((ep * inv).astype(B16))
            pr = jnp.concatenate(probs, axis=0)
            PROB[2 * b + p // 4, :, pl.ds(pl.multiple_of((p % 4) * HALF, HALF), HALF)] = pr
            PPRE[b, pl.ds(pl.multiple_of(p * 32, 32), 32)] = jnp.concatenate(pres, axis=0)
            ACC[half(b), cols] = dot_tn(pr, split_heads(v2))

        for p in range(4):
            pair(part * 4 + p)

        @pl.when(part == 1)
        def _():
            ATT[half(b)] = (ACC[half(b)] + dot_tn(PPRE[b], pval[...])).astype(B16)
            saves(b)[3].start()
            saves(b)[4].start()
            saves(b)[5].start()

    def mix(b):
        r = H[half(b)].astype(F32) + (dot_nn(ATT[half(b)], W[rows_of(3)]) + small[3:4])
        RES[half(b)] = r
        xhat, _ = whiten(r)
        A2[half(b)] = (xhat * small[12:13] + small[10:11]).astype(B16)
        saves(b)[6].start()
        saves(b)[7].start()

    def widen(j, b):
        x = dot_nn(A2[half(b)], W[rows_of(4 + j)]) + small[pl.ds(4 + j, 1)]
        x2 = x * x
        h = 0.5 + 0.5 * jnp.tanh(x * (GELU_C + (0.044715 * GELU_C) * x2))
        act = x * h
        ACT[j, half(b)] = act.astype(B16)
        GP[j, half(b)] = (h + act * (1.0 - h) * (2.0 * GELU_C + (6 * 0.044715 * GELU_C) * x2)).astype(B16)

        @pl.when(j == 3)
        def _():
            saves(b)[8].start()
            saves(b)[9].start()

    def narrow(b):
        v = RES[half(b)] + small[8:9]
        for j in range(4):
            v = v + dot_nn(ACT[j, half(b)], W[rows_of(8 + j)])
        OUT[half(b)] = v.astype(B16)

        @pl.when(s == 0)
        def _():
            cross(b).start()

        saves(b)[10].start()

    @pl.loop(0, NP + 5 + 2 * STAGES)
    def _(tick):
        @pl.when(tick < NP + 5)
        def _():
            g.step(tick, own)

            @pl.when(tick == 3)
            def _():
                prepare()

            @pl.when(tick >= 5)
            def _():
                g.complete(tick - 5)

                @pl.when(tick < 13)
                def _():
                    piece_out(tick - 5).start()

                @pl.when(tick == NP + 4)
                def _():
                    for k in range(8, NP):
                        piece_out(k).start()

        late = tick - (NP + 5)
        stage = (1 - s) * (tick - 5) + s * ((late + STAGES) % STAGES - STAGES * (late < 0).astype(jnp.int32))
        lo = s * (late // STAGES)
        hi = (1 - s) * 2 + s * (late // STAGES + 1)

        def when(i, body):
            @pl.when(stage == i)
            def _():
                pl.loop(lo, hi)(body)

        when(0, norm_in)

        @pl.when((stage >= 1) & (stage < 4))
        def _():
            pl.loop(lo, hi)(lambda b: project(stage - 1, b))

        @pl.when((stage >= 4) & (stage < 6))
        def _():
            pl.loop(lo, hi)(lambda b: attend(stage - 4, b))

        when(6, mix)

        @pl.when((stage >= 7) & (stage < 11))
        def _():
            pl.loop(lo, hi)(lambda b: widen(stage - 7, b))

        when(11, narrow)

    g.drain()
    packs_out()
    for cp in prep_saves():
        cp.wait()

    @pl.loop(0, NP)
    def _(k):
        piece_out(k).wait()

    @pl.loop(0, 2)
    def _(b):
        for cp in saves(b):
            cp.wait()

        @pl.when(s == 0)
        def _():
            cross(b).wait_send()


def forward_call(wq, wo, wf, wp, tokens, segs, pack, aux, r_in, r_out):
    any_, vm = pl.BlockSpec(memory_space=pl.ANY), pl.BlockSpec(memory_space=pltpu.VMEM)
    n, d = tokens.shape
    kept = [
        ((NP * d, d), B16), ((n, d), B16), ((n, d), B16), ((n, d), B16), ((3, n, d), B16), ((4, n, d), B16),
        ((2, HALF, HALF), B16), ((n, d), B16), ((n, d), F32), ((n, d), B16), ((4, n, d), B16), ((4, n, d), B16),
    ]
    shared = [((16, d), F32), ((HALF, d), B16), ((HALF, d), B16), ((16, 512), F32)]
    dma = pltpu.SemaphoreType.DMA
    order = [0, 2, 3, 4, 5, 6, 7, 8, 9, 10, 11, 1]
    scratch = [kept[i] for i in order] + [((2, HALF, HALF), F32), ((n, d), F32)] + shared
    scratch += [((2, HALF, HALF), F32), ((16, 16, 128), B16), ((16, 16, 128), F32)]
    return pl.pallas_call(
        forward_kernel,
        out_shape=[jax.ShapeDtypeStruct(*k) for k in kept + shared],
        in_specs=[any_] * 5 + [vm] * 3 + [any_] * 2,
        out_specs=[any_] * len(kept + shared),
        scratch_shapes=[pltpu.VMEM(*v) for v in scratch]
        + [dma((NP,)), dma((NP, 20)), dma((NP, 16)), dma((NP, 8)), dma((NP, 4)), dma, dma((2,)), dma((2,)), dma((3, NP)), dma((16,)), dma((16,)), dma((8,))],
        compiler_params=pltpu.CompilerParams(collective_id=0, has_side_effects=True, vmem_limit_bytes=62 << 20),
    )(wq, wo, wf, wp, tokens, segs, pack, aux, r_in, r_out)


def own_pack(gains, biases):
    rows = jnp.concatenate([biases.reshape(11, 64), gains.reshape(2, 64), jnp.zeros((3, 64), B16)])
    return jnp.concatenate([rows, rows], axis=1)


def prefix_rows(embed, in_bias, out_bias):
    in_bias = jnp.pad(in_bias, (0, 512)).reshape(1, 1024)
    return jnp.concatenate([embed, in_bias, out_bias.reshape(2, 1024), jnp.zeros((3, 1024), B16)])


SPLIT = 6
BACK_TICKS = 2 + 2 * SPLIT + NP + 6


def unwhiten(grad, xhat, rstd):
    return rstd * (
        grad
        - jnp.mean(grad, axis=-1, keepdims=True)
        - xhat * jnp.mean(grad * xhat, axis=-1, keepdims=True)
    )


def column_sum(v):
    return jnp.sum(v.astype(F32), axis=0, keepdims=True)


def backward_kernel(
    W_i, h_i, a1_i, qkv_i, prob_i, ppre_i, att_i, res_i, a2_i, gp_i, act_i, cot, r_out, small, pkey, pval,
    dh_o, oq, oo, of, op_, own_sums, KVB, HSUM,
    WG, H, A1, QKV, BIG, PPRE, ATT, RES, A2, GP, DM, DAT, DATT, DPP, DSP, ACC,
    RC, RY, RU, RD, RUS, RDS, RYS, T, SG, DKV, SB, RB, PF, PG, HP, HPR,
    wsem, lsem, osem, cs, cr, ys, yr, us, ur, ds_, dr, yss, ysr, xs, xr, hs, bs, br, ps, pr, hx,
):
    s, d, z, y, c = place()

    def slot(k):
        return k + 8 * (1 - s) if k < 4 else k

    def fetch(ks):
        return [pltpu.make_async_copy(W_i.at[k], WG.at[slot(k)], wsem.at[k]) for k in ks]

    def begin(cps):
        for cp in cps:
            cp.start()

    def loads():
        pairs = [
            (gp_i, GP), (a2_i, A2), (res_i, RES), (att_i, ATT), (qkv_i, QKV), (ppre_i, PPRE), (a1_i, A1), (h_i, H),
            (act_i, BIG), (prob_i, BIG), (cot, DM),
        ]
        return [pltpu.make_async_copy(a, b, lsem.at[i]) for i, (a, b) in enumerate(pairs)]

    L_GP, L_A2, L_RES, L_ATT, L_QKV, L_PPRE, L_A1, L_H, L_ACT, L_PROB, L_COT = range(11)

    def begin_loads(which):
        begin([loads()[i] for i in which])

    pl.when(s == 1)(lambda: begin_loads((L_COT,)))
    begin(fetch((8, 9, 10, 11)))
    begin_loads((L_GP,))
    pl.when(s == 0)(lambda: begin_loads((L_ACT,)))
    SG[...] = jnp.zeros_like(SG)
    DKV[...] = jnp.zeros_like(DKV)
    SB[...] = jnp.zeros_like(SB)
    greet(s, d)

    def weights(ks):
        for cp in fetch(ks):
            cp.wait()

    def half(b):
        return pl.ds(pl.multiple_of(b * HALF, HALF), HALF)

    def weight(k):
        return WG[slot(k)].reshape(1024, 1024)

    def cross(b):
        return pltpu.make_async_remote_copy(
            H.at[half(b)], DM.at[half(b)], xs.at[b], xr.at[b], device_id=(1 - s, d), device_id_type=MESH
        )

    def dh_out(b):
        return pltpu.make_async_copy(H.at[half(b)], dh_o.at[half(b)], hs.at[b])

    def ffn_in(b):
        first = (b == 0)

        @pl.when(first)
        def _():
            @pl.when(s == 1)
            def _():
                loads()[L_COT].wait()

            weights((8, 9, 10, 11))
            loads()[L_GP].wait()
            begin(fetch((4, 5, 6, 7)))
            begin_loads((L_A2, L_RES))

            @pl.when(s == 1)
            def _():
                begin(fetch((3,)))
                begin_loads((L_QKV, L_PPRE, L_PROB))

            @pl.when(s == 0)
            def _():
                cross(0).wait_recv()

        for j in range(4):
            GP[j, half(b)] = (dot_nt(DM[half(b)], weight(8 + j)) * GP[j, half(b)].astype(F32)).astype(B16)

        @pl.when((s == 0) & (b == 1))
        def _():
            begin(fetch((3, 0, 1, 2)))

    def ffn_norm(b):
        @pl.when(b == 0)
        def _():
            weights((4, 5, 6, 7))
            loads()[L_A2].wait()
            loads()[L_RES].wait()
            begin_loads((L_ATT, L_A1, L_H))

            @pl.when(s == 0)
            def _():
                begin_loads((L_QKV, L_PPRE))

            @pl.when(s == 1)
            def _():
                begin(fetch((0, 1, 2)))

        grad = dot_nt(GP[0, half(b)], weight(4))
        for j in range(1, 4):
            grad = grad + dot_nt(GP[j, half(b)], weight(4 + j))
        xhat, rstd = whiten(RES[half(b)])
        SG[10:11] += jnp.sum(grad, axis=0, keepdims=True)
        SG[12:13] += jnp.sum(grad * xhat, axis=0, keepdims=True)
        res = DM[half(b)].astype(F32) + unwhiten(grad * small[12:13], xhat, rstd)
        RES[half(b)] = res
        DAT[half(b)] = res.astype(B16)

    def attn_out(b):
        @pl.when(b == 0)
        def _():
            weights((3,))
            for i in (L_ATT, L_QKV, L_PPRE):
                loads()[i].wait()

            loads()[L_PROB].wait()

        DATT[...] = dot_nt(DAT[half(b)], weight(3)).astype(B16)
        DPP[...] = dot_nt(pval[...], DATT[...])

    def attn_back(part, b):
        @pl.loop(part * 4, part * 4 + 4)
        def _(p):
            cols = pl.ds(pl.multiple_of(p * 128, 128), 128)
            q2, k2, v2 = QKV[0, half(b), cols], QKV[1, half(b), cols], QKV[2, half(b), cols]
            do2 = DATT[:, cols]
            pr = BIG[2 * b + p // 4, :, pl.ds(pl.multiple_of((p % 4) * HALF, HALF), HALF)]
            dp = dot_nt(split_heads(v2), do2)
            dss, pres = [], []
            for e in range(2):
                ph = pr[e * HALF : (e + 1) * HALF].astype(F32)
                dh = dp[e * HALF : (e + 1) * HALF]
                at = pl.ds(pl.multiple_of(p * 32 + e * 16, 16), 16)
                pp, dpp = PPRE[b, at].astype(F32), DPP[at]
                dot = jnp.sum(ph * dh, axis=0, keepdims=True) + jnp.sum(pp * dpp, axis=0, keepdims=True)
                dss.append((ph * (dh - dot)).astype(B16))
                pres.append((pp * (dpp - dot)).astype(B16))
            ds = jnp.concatenate(dss, axis=0)
            DSP[pl.ds(pl.multiple_of(p * 32, 32), 32)] = jnp.concatenate(pres, axis=0)
            left = lax.broadcasted_iota(jnp.int32, (HALF, 128), 1) < 64
            ACC[:, cols] = dot_tn(ds, split_heads(k2))
            dk = dot_nn(ds, q2)
            dv = dot_nn(pr, do2)
            QKV[1, half(b), cols] = jnp.where(left, dk[:HALF], dk[HALF:]).astype(B16)
            QKV[2, half(b), cols] = jnp.where(left, dv[:HALF], dv[HALF:]).astype(B16)

        @pl.when(part == 1)
        def _():
            def own_rows(full):
                out = jnp.zeros((16, 1024), F32)
                head = lax.broadcasted_iota(jnp.int32, (16, 1024), 1) // 64
                for i in range(16):
                    out = out + jnp.where(head == i, full[16 * i : 16 * i + 16], 0.0)
                return out

            DKV[0:16] += own_rows(dot_nn(DSP[...], QKV[0, half(b)]))
            DKV[16:32] += own_rows(dot_nn(PPRE[b], DATT[...]))
            QKV[0, half(b)] = ((ACC[...] + dot_tn(DSP[...], pkey[...])) * 0.125).astype(B16)

    def attn_norm(b):
        @pl.when(b == 0)
        def _():
            weights((0, 1, 2))
            loads()[L_A1].wait()
            loads()[L_H].wait()

        @pl.when((s == 1) & (b == 1))
        def _():
            loads()[L_ACT].start()

        grad = dot_nt(QKV[0, half(b)], weight(0))
        for i in range(1, 3):
            grad = grad + dot_nt(QKV[i, half(b)], weight(i))
        xhat, rstd = whiten(H[half(b)].astype(F32))
        SG[9:10] += jnp.sum(grad, axis=0, keepdims=True)
        SG[11:12] += jnp.sum(grad * xhat, axis=0, keepdims=True)
        H[half(b)] = (RES[half(b)] + unwhiten(grad * small[11:12], xhat, rstd)).astype(B16)

        @pl.when(s == 1)
        def _():
            cross(b).start()

        dh_out(b).start()

    def grad_proj():
        loads()[L_ACT].wait()

        @pl.when(s == 0)
        def _():
            cross(1).wait_recv()
        @pl.loop(0, 4)
        def _(i):
            for u in range(2):
                v = dot_tn(BIG[i, :, 512 * u : 512 * (u + 1)], DM[...]).astype(B16).reshape(2, 4, 64, 1024)
                for j in range(4):
                    WG[8 * s + j, i, u] = v[:, j]

        @pl.when(s == 0)
        def _():
            loads()[L_PROB].start()

    def put(k, a, v):
        for i in range(2):
            part = dot_tn(a[:, 512 * i : 512 * (i + 1)], v[...])
            WG[k, 2 * i : 2 * i + 2] = part.astype(B16).reshape(2, 2, 2, 64, 1024)

    def grad_fc(j):
        put(4 + j, A2, GP.at[j])

    def grad_out():
        put(slot(3), ATT, DAT)

    def grad_qkv(i):
        put(i + 8 * (1 - s), A1, QKV.at[i])

    send_sums, sums_in, sums_out = to_all(lambda to: SB.at[to], RB, bs, br)
    send_pref, pref_in, pref_out = to_all(lambda to: PF, PG, ps, pr)

    def r_out_in():
        return [pltpu.make_async_copy(r_out.at[:, pl.ds(1024 * i, 1024)], BIG.at[i], hx.at[i]) for i in range(2)]

    def hidden_across():
        return pltpu.make_async_remote_copy(HP, HPR, hx.at[2], hx.at[3], device_id=(1 - s, d), device_id_type=MESH)

    def small_first():
        for cp in r_out_in():
            cp.start()
        for i in range(3):
            SG[i : i + 1] = column_sum(QKV[i])
        SG[3:4] = column_sum(DAT[...])
        for j in range(4):
            SG[4 + j : 5 + j] = column_sum(GP[j])
        SG[8:9] = column_sum(DM[...])
        for i in range(16):
            for n in range(13):
                m = 11 * i + n
                row, at = (m // 16, 128 * (m % 16 // 2)) if n < 11 else (n, 128 * (i // 2))
                SB[i, n : n + 1] = SG[row : row + 1, at : at + 128]
            SB[i, 16:32] = DKV[16 * (i // 8) : 16 * (i // 8) + 16, 128 * (i % 8) : 128 * (i % 8) + 128]
        send_sums()
        RB[d] = SB[d]

    def small_second():
        sums_in()
        total = RB[0]
        for i in range(1, 16):
            total = total + RB[i]
        row = lax.broadcasted_iota(jnp.int32, (16, 128), 0)
        odd = jnp.where(row < 11, d + row, d) % 2 == 1
        own_sums[...] = jnp.where(odd, pltpu.roll(total[:16], 64, 1), total[:16])
        PF[...] = total[16:].astype(B16)
        send_pref()
        PG[d] = PF[...]

    def small_third():
        pref_in()
        for i in range(16):
            KVB[:, 128 * i : 128 * i + 128] = PG[i]
        for cp in r_out_in():
            cp.wait()
        HP[...] = dot_nt(KVB[:, :1024], BIG[0]) + dot_nt(KVB[:, 1024:], BIG[1])
        hidden_across().start()

    def small_last():
        hidden_across().wait()
        HSUM[...] = HP[...] + HPR[...]

    def held(r):
        a = r // 4
        return ((2 - a) * (1 - a) // 2) * (r + 8 * s) + a * (2 - a) * r + (a * (a - 1) // 2) * (11 - r + 8 * (1 - s))

    def across_c(r):
        return pltpu.make_async_remote_copy(
            WG.at[held(r), :, :, 1 - c], RC.at[r % 4], cs.at[r], cr.at[r],
            device_id=(s, z * 4 + y * 2 + 1 - c), device_id_type=MESH,
        )

    def across_y(r):
        return pltpu.make_async_remote_copy(
            WG.at[held(r), :, 1 - y, c, :, pl.ds(0, MAIN)], RY.at[r % 4], ys.at[r], yr.at[r],
            device_id=(s, z * 4 + (1 - y) * 2 + c), device_id_type=MESH,
        )

    def up(r, i):
        return pltpu.make_async_remote_copy(
            WG.at[held(r), i, y, c], RU.at[r % 7, i - 1], us.at[r, i - 1], ur.at[r, i - 1],
            device_id=(s, (z + 1) * 4 + y * 2 + c), device_id_type=MESH,
        )

    def down(r, i):
        return pltpu.make_async_remote_copy(
            WG.at[held(r), i, y, c], RD.at[r % 7, i], ds_.at[r, i], dr.at[r, i],
            device_id=(s, (z - 1) * 4 + y * 2 + c), device_id_type=MESH,
        )

    def strip_up(r, i):
        return pltpu.make_async_remote_copy(
            WG.at[held(r), i, 1 - y, c, :, pl.ds(MAIN, 1024 - MAIN)], RUS.at[r % 7, i - 1], us.at[r, 2 + i], ur.at[r, 2 + i],
            device_id=(s, (z + 1) * 4 + y * 2 + c), device_id_type=MESH,
        )

    def strip_down(r, i):
        return pltpu.make_async_remote_copy(
            WG.at[held(r), i, 1 - y, c, :, pl.ds(MAIN, 1024 - MAIN)], RDS.at[r % 7, i], ds_.at[r, 3 + i], dr.at[r, 3 + i],
            device_id=(s, (z - 1) * 4 + y * 2 + c), device_id_type=MESH,
        )

    def strip_y(r):
        return pltpu.make_async_remote_copy(
            WG.at[held(r), z, 1 - y, c, :, pl.ds(MAIN, 1024 - MAIN)], RYS.at[r % 4], yss.at[r], ysr.at[r],
            device_id=(s, z * 4 + (1 - y) * 2 + c), device_id_type=MESH,
        )

    def each_out(r, act):
        k = held(r)
        src = T.at[r % 2]

        @pl.when(r < 4)
        def _():
            act(pltpu.make_async_copy(src, op_.at[0, pl.ds(pl.multiple_of(64 * r, 64), 64)], osem.at[r]))

        @pl.when((r >= 4) & (r < 8))
        def _():
            act(pltpu.make_async_copy(src, of.at[0, :, pl.ds(pl.multiple_of(1024 * (r - 4), 1024), 1024)], osem.at[r]))

        @pl.when(r == 8)
        def _():
            act(pltpu.make_async_copy(src, oo.at[0], osem.at[r]))

        @pl.when(r > 8)
        def _():
            act(pltpu.make_async_copy(src, oq.at[0, :, pl.ds(pl.multiple_of(1024 * (11 - r), 1024), 1024)], osem.at[r]))

    def start(cp):
        cp.start()

    def add(k, i, j, other):
        WG[k, i, j, c] = (WG[k, i, j, c].astype(F32) + other.astype(F32)).astype(B16)

    def add_main(k, i, other):
        WG[k, i, y, c, :, :MAIN] = (WG[k, i, y, c, :, :MAIN].astype(F32) + other.astype(F32)).astype(B16)

    def add_strip(k, i, *others):
        total = WG[k, i, 1 - y, c, :, MAIN:].astype(F32)
        for other in others:
            total = total + other.astype(F32)
        WG[k, i, 1 - y, c, :, MAIN:] = total.astype(B16)

    def live(r):
        return (r >= 0) & (r < NP)

    def scatter_step(t):
        @pl.when(live(t))
        def _():
            across_c(t).start()

        @pl.when(live(t - 1))
        def _():
            r = t - 1
            k = held(r)
            across_c(r).wait_recv()

            @pl.loop(0, 4)
            def _(i):
                add(k, i, 1 - y, RC[r % 4, i, 1 - y])

            across_y(r).start()

            @pl.loop(0, 4)
            def _(i):
                add(k, i, y, RC[r % 4, i, y])

        @pl.when(live(t - 2))
        def _():
            r = t - 2
            k = held(r)
            across_y(r).wait_recv()

            @pl.loop(0, 4)
            def _(i):
                add_main(k, i, RY[r % 4, i])

            @pl.when(z == 0)
            def _():
                for i in (3, 2, 1):
                    up(r, i).start()
                    strip_up(r, i).start()

            @pl.when(z == 3)
            def _():
                for i in (0, 1, 2):
                    down(r, i).start()
                    strip_down(r, i).start()

        for q in (1, 2, 3):
            n = 4 - q

            @pl.when(live(t - 2 - q))
            def _():
                r = t - 2 - q
                k = held(r)

                @pl.when(z == q)
                def _():
                    for i in range(3, q - 1, -1):
                        up(r, i).wait_recv()
                        if i > q:
                            add(k, i, y, RU[r % 7, i - 1])
                            up(r, i).start()
                        strip_up(r, i).wait_recv()
                        if i > q:
                            add_strip(k, i, RUS[r % 7, i - 1])
                            strip_up(r, i).start()

                @pl.when(z == 3 - q)
                def _():
                    for i in range(n):
                        down(r, i).wait_recv()
                        if i < n - 1:
                            add(k, i, y, RD[r % 7, i])
                            down(r, i).start()
                        strip_down(r, i).wait_recv()
                        if i < n - 1:
                            add_strip(k, i, RDS[r % 7, i])
                            strip_down(r, i).start()

        @pl.when(live(t - 5))
        def _():
            r = t - 5
            k = held(r)

            @pl.when(z > 0)
            def _():
                add_strip(k, z, RUS[r % 7, z - 1])

            @pl.when(z < 3)
            def _():
                add_strip(k, z, RDS[r % 7, z])

            strip_y(r).start()

            @pl.when(r >= 2)
            def _():
                each_out(r - 2, lambda cp: cp.wait())

            T[r % 2] = WG[k, z, y, c].astype(F32)

            @pl.when(z > 0)
            def _():
                T[r % 2] += RU[r % 7, z - 1].astype(F32)

            @pl.when(z < 3)
            def _():
                T[r % 2] += RD[r % 7, z].astype(F32)

        @pl.when(live(t - 6))
        def _():
            r = t - 6
            strip_y(r).wait_recv()
            T[r % 2, :, MAIN:] += RYS[r % 4].astype(F32)
            each_out(r, start)

    @pl.loop(0, BACK_TICKS)
    def _(tick):
        turn = tick // SPLIT

        @pl.when((tick == 0) | (tick == 2 * (1 - s) + SPLIT * s))
        def _():
            ffn_in((tick > 0).astype(jnp.int32))

        def when(i, at0, at1, body):
            early = (1 - s) * at0 + s * i
            late = (1 - s) * at1 + s * (SPLIT + i)

            @pl.when((tick == early) | (tick == late))
            def _():
                body((tick == late).astype(jnp.int32))

        when(1, 3, 4, ffn_norm)
        when(2, 5, 7, attn_out)
        first = (tick - 3) % SPLIT * s + (tick - 5) % 2 * (1 - s)

        @pl.when(((s == 0) & (tick >= 5) & (tick < 9)) | ((s == 1) & (tick < 2 * SPLIT) & (first < 2)))
        def _():
            attn_back(first, (1 - s) * ((tick - 5) // 2) + s * turn)

        when(5, 9, 10, attn_norm)
        r = tick - 1 - (2 * SPLIT - 1) * s

        @pl.when(r == 0)
        def _():
            grad_proj()

        @pl.when((r >= 4) & (r < 8))
        def _():
            grad_fc(r - 4)

        @pl.when(r == 8)
        def _():
            grad_out()

        @pl.when((r > 8) & (r < 12))
        def _():
            grad_qkv(11 - r)

        scatter_step(r)
        for at, body in ((10, small_first), (11, small_second), (13, small_third), (16, small_last)):
            pl.when(r == at)(body)

    @pl.loop(0, NP)
    def _(r):
        @pl.when(r >= NP - 2)
        def _():
            each_out(r, lambda cp: cp.wait())

        across_c(r).wait_send()
        across_y(r).wait_send()
        strip_y(r).wait_send()
        for q in range(3):

            @pl.when(z == q)
            def _():
                for i in range(q + 1, 4):
                    up(r, i).wait_send()
                    strip_up(r, i).wait_send()

            @pl.when(z == q + 1)
            def _():
                for i in range(q + 1):
                    down(r, i).wait_send()
                    strip_down(r, i).wait_send()

    sums_out()
    pref_out()

    @pl.loop(0, 2)
    def _(b):
        dh_out(b).wait()

        @pl.when(s == 1)
        def _():
            cross(b).wait_send()


def backward_call(kept, cot, r_out, small, pkey, pval):
    W, h, a1, qkv, prob, ppre, att, res, a2, gp, act = kept
    any_, vm = pl.BlockSpec(memory_space=pl.ANY), pl.BlockSpec(memory_space=pltpu.VMEM)
    n, d = h.shape
    dma = pltpu.SemaphoreType.DMA
    wide = (4, 2, 2, 64, d)
    outs = [
        ((n, d), B16), ((1, 64, 3 * d), F32), ((1, 64, d), F32), ((1, 64, 4 * d), F32), ((1, 256, d), F32),
        ((16, 128), F32), ((16, 2 * d), B16), ((16, 512), F32),
    ]
    scratch = [
        ((NP,) + wide, B16), ((n, d), B16), ((n, d), B16), ((3, n, d), B16), ((4, n, d), B16), ((2, HALF, HALF), B16), ((n, d), B16),
        ((n, d), F32), ((n, d), B16), ((4, n, d), B16), ((n, d), B16), ((n, d), B16), ((HALF, d), B16), ((HALF, HALF), F32),
        ((HALF, HALF), B16), ((HALF, d), F32),
        ((4, 4, 2, 64, d), B16), ((4, 4, 64, MAIN), B16), ((7, 3, 64, d), B16), ((7, 3, 64, d), B16),
        ((7, 3, 64, d - MAIN), B16), ((7, 3, 64, d - MAIN), B16), ((4, 64, d - MAIN), B16), ((2, 64, d), F32),
        ((16, d), F32), ((32, d), F32), ((16, 32, 128), F32), ((16, 32, 128), F32), ((16, 128), B16), ((16, 16, 128), B16),
        ((16, 512), F32), ((16, 512), F32),
    ]
    return pl.pallas_call(
        backward_kernel,
        out_shape=[jax.ShapeDtypeStruct(*o) for o in outs],
        in_specs=[any_] * 13 + [vm] * 3,
        out_specs=[any_] * 5 + [vm] * 3,
        scratch_shapes=[pltpu.VMEM(*v) for v in scratch] + [dma((NP,))] * 7 + [dma((NP, 6))] * 4 + [dma((NP,))] * 2 + [dma((2,))] * 3 + [dma((16,))] * 4 + [dma((4,))],
        compiler_params=pltpu.CompilerParams(collective_id=1, has_side_effects=True, vmem_limit_bytes=64 << 20),
    )(W.reshape((NP,) + wide), h, a1, qkv, prob, ppre, att, res, a2, gp, act, cot, r_out, small, pkey, pval)


def finish_kernel(
    o0, o1, o2, o3, o4, o5, hid, kvb, hsum, aux, r_in, sums,
    c0, c1, c2, c3, c4, c5, g_embed, g_in, g_in_bias, g_out, g_out_bias, g_gains, g_bias,
    G_IN, G_OUT, M0, M1, M2, M3, M4, M5, sem,
):
    held = (M0, M1, M2, M3, M4, M5)
    here = [pltpu.make_async_copy(a, m, sem.at[i]) for i, (a, m) in enumerate(zip((o0, o1, o2, o3, o4, o5), held))]
    away = [pltpu.make_async_copy(m, c, sem.at[8 + i]) for i, (m, c) in enumerate(zip(held, (c0, c1, c2, c3, c4, c5)))]
    for cp in here:
        cp.start()
    h = hid[...]
    kv = kvb[...]
    G_OUT[...] = dot_tn(h.astype(B16), kv)
    out_cp = pltpu.make_async_copy(G_OUT, g_out, sem.at[6])
    out_cp.start()
    g_out_bias[...] = column_sum(kv)
    for cp, out in zip(here, away):
        cp.wait()
        out.start()
    dp = (hsum[...] * (1.0 - h * h)).astype(B16)
    G_IN[...] = dot_tn(aux[...], dp)
    in_cp = pltpu.make_async_copy(G_IN, g_in, sem.at[7])
    in_cp.start()
    g_in_bias[...] = column_sum(dp)
    g_embed[...] = dot_nt(dp, r_in[...])[:10]
    g_gains[0] = sums[11:13, :64]
    for i in range(11):
        g_bias[:, 64 * i : 64 * i + 64] = sums[i : i + 1, :64]
    for cp in away + [out_cp, in_cp]:
        cp.wait()


def finish_call(large, hid, kvb, hsum, aux, r_in, sums):
    any_, vm = pl.BlockSpec(memory_space=pl.ANY), pl.BlockSpec(memory_space=pltpu.VMEM)
    d = r_in.shape[0]
    outs = [jax.ShapeDtypeStruct(x.shape, x.dtype) for x in large]
    outs += [jax.ShapeDtypeStruct(x, F32) for x in ((10, d), (d, 512), (1, 512), (512, 2 * d), (1, 2 * d), (1, 2, 64), (1, 704))]
    return pl.pallas_call(
        finish_kernel,
        out_shape=outs,
        in_specs=[any_] * 6 + [vm] * 6,
        out_specs=[any_] * 6 + [vm, any_, vm, any_, vm, vm, vm],
        scratch_shapes=[pltpu.VMEM((d, 512), F32), pltpu.VMEM((512, 2 * d), F32)]
        + [pltpu.VMEM(x.shape, x.dtype) for x in large]
        + [pltpu.SemaphoreType.DMA((14,))],
        compiler_params=pltpu.CompilerParams(vmem_limit_bytes=63 << 20),
    )(*large, hid, kvb, hsum, aux, r_in, sums)


def on_device(
    tokens,
    segment_ids,
    cotangent,
    w_qkv,
    w_attn_out,
    w_fc,
    w_proj,
    gains,
    biases,
    prefix_embed,
    reparam_in,
    reparam_in_bias,
    reparam_out,
    reparam_out_bias,
):
    aux = prefix_rows(prefix_embed, reparam_in_bias, reparam_out_bias)
    pack = own_pack(gains, biases)
    kept = forward_call(w_qkv, w_attn_out, w_fc, w_proj, tokens, segment_ids, pack, aux, reparam_in, reparam_out)
    small, pkey, pval, hid = kept[12:]
    *large, sums, kvb, hsum = backward_call(kept[:1] + kept[2:12], cotangent, reparam_out, small, pkey, pval)
    done = finish_call([kept[1]] + large, hid, kvb, hsum, aux, reparam_in, sums)
    return (
        done[0][None],
        done[1][None],
        *done[2:6],
        done[11],
        done[12],
        done[6],
        done[7],
        done[8][0],
        done[9],
        done[10][0],
    )


def passed_along(shard, axis, by):
    size = lax.axis_size(axis)
    pairs = [(i, i + by) for i in range(size) if 0 <= i + by < size]
    return lax.ppermute(shard, axis, pairs)


def norm_rows(v, gain, shift):
    mean = jnp.mean(v, axis=-1, keepdims=True)
    cent = v - mean
    var = jnp.mean(cent * cent, axis=-1, keepdims=True)
    return cent * lax.rsqrt(var + EPS) * gain + shift


def gelu_tanh(v):
    return jax.nn.gelu(v, approximate=True)


def forward_layer(h_b, segs, pkey, pval, params):
    w_q, w_o, w_f, w_p, gain_pair, bias_all = params
    width = w_o.shape[0]
    length = h_b.shape[0]
    heads, head_dim = (pkey.shape[1], pkey.shape[2])
    scale = 1.0 / math.sqrt(head_dim)
    gain_f = gain_pair.astype(jnp.float32)
    bias_f = bias_all.astype(jnp.float32)
    hf = h_b.astype(jnp.float32)
    a1b = norm_rows(hf, gain_f[0], bias_f[9 * width : 10 * width]).astype(jnp.bfloat16)
    qkv_b = (jnp.dot(a1b, w_q, preferred_element_type=jnp.float32) + bias_f[: 3 * width]).astype(
        jnp.bfloat16
    )
    split = qkv_b.reshape(length, 3, heads, head_dim)
    query, keys, values = (split[:, 0], split[:, 1], split[:, 2])
    s_tok = jnp.einsum("lhe,mhe->hlm", query, keys, preferred_element_type=jnp.float32) * scale
    s_pre = jnp.einsum("lhe,phe->hlp", query, pkey, preferred_element_type=jnp.float32) * scale
    place = jnp.arange(length)
    allowed = (segs[:, None] == segs[None, :]) & (place[None, :] <= place[:, None])
    s_tok = jnp.where(allowed[None], s_tok, NEG)
    top = jnp.maximum(
        jnp.max(s_tok, axis=-1, keepdims=True), jnp.max(s_pre, axis=-1, keepdims=True)
    )
    e_tok = jnp.exp(s_tok - top)
    e_pre = jnp.exp(s_pre - top)
    total = jnp.sum(e_tok, axis=-1, keepdims=True) + jnp.sum(e_pre, axis=-1, keepdims=True)
    p_tok = e_tok / total
    p_pre = e_pre / total
    mixed = jnp.einsum(
        "hlm,mhe->lhe", p_tok.astype(jnp.bfloat16), values, preferred_element_type=jnp.float32
    ) + jnp.einsum(
        "hlp,phe->lhe", p_pre.astype(jnp.bfloat16), pval, preferred_element_type=jnp.float32
    )
    attn_b = mixed.reshape(length, width).astype(jnp.bfloat16)
    resid = hf + (
        jnp.dot(attn_b, w_o, preferred_element_type=jnp.float32) + bias_f[3 * width : 4 * width]
    )
    a2b = norm_rows(resid, gain_f[1], bias_f[10 * width : 11 * width]).astype(jnp.bfloat16)
    pre_act = jnp.dot(a2b, w_f, preferred_element_type=jnp.float32) + bias_f[4 * width : 8 * width]
    act_b = gelu_tanh(pre_act).astype(jnp.bfloat16)
    result = resid + (
        jnp.dot(act_b, w_p, preferred_element_type=jnp.float32) + bias_f[8 * width : 9 * width]
    )
    return (result, (hf, a1b, qkv_b, p_tok, p_pre, attn_b, resid, a2b, pre_act, act_b))


def backward_ffn(grad_out, keep, params):
    w_q, w_o, w_f, w_p, gain_pair, bias_all = params
    hf, a1b, qkv_b, p_tok, p_pre, attn_b, resid, a2b, pre_act, act_b = keep
    width = w_o.shape[0]
    gain_f = gain_pair.astype(jnp.float32)
    bias_f = bias_all.astype(jnp.float32)
    dm_b = grad_out.astype(jnp.bfloat16)
    grad_wp = jnp.einsum("lf,ld->fd", act_b, dm_b, preferred_element_type=jnp.float32)
    grad_bp = jnp.sum(dm_b.astype(jnp.float32), axis=0)
    d_act = jnp.dot(dm_b, w_p.T, preferred_element_type=jnp.float32)
    dpre_b = jax.vjp(gelu_tanh, pre_act)[1](d_act)[0].astype(jnp.bfloat16)
    grad_wf = jnp.einsum("ld,lf->df", a2b, dpre_b, preferred_element_type=jnp.float32)
    grad_bf = jnp.sum(dpre_b.astype(jnp.float32), axis=0)
    d_a2 = jnp.dot(dpre_b, w_f.T, preferred_element_type=jnp.float32)
    norm_back = jax.vjp(norm_rows, resid, gain_f[1], bias_f[10 * width : 11 * width])[1]
    d_resid_norm, grad_g2, grad_c2 = norm_back(d_a2)
    d_resid = grad_out + d_resid_norm
    return (d_resid, (grad_wf, grad_wp), (grad_bf, grad_bp, grad_g2, grad_c2))


def backward_attn(d_resid, keep, pkey, pval, params):
    w_q, w_o, w_f, w_p, gain_pair, bias_all = params
    hf, a1b, qkv_b, p_tok, p_pre, attn_b, resid, a2b, pre_act, act_b = keep
    width = w_o.shape[0]
    length = hf.shape[0]
    heads, head_dim = (pkey.shape[1], pkey.shape[2])
    prefix_len = pkey.shape[0]
    scale = 1.0 / math.sqrt(head_dim)
    gain_f = gain_pair.astype(jnp.float32)
    bias_f = bias_all.astype(jnp.float32)
    split = qkv_b.reshape(length, 3, heads, head_dim)
    query, keys, values = (split[:, 0], split[:, 1], split[:, 2])
    dat_b = d_resid.astype(jnp.bfloat16)
    grad_wo = jnp.einsum("ld,le->de", attn_b, dat_b, preferred_element_type=jnp.float32)
    grad_bo = jnp.sum(dat_b.astype(jnp.float32), axis=0)
    dattn_b = jnp.dot(dat_b, w_o.T, preferred_element_type=jnp.float32).astype(jnp.bfloat16)
    dattn_b = dattn_b.reshape(length, heads, head_dim)
    dp_tok = jnp.einsum("lhe,mhe->hlm", dattn_b, values, preferred_element_type=jnp.float32)
    dp_pre = jnp.einsum("lhe,phe->hlp", dattn_b, pval, preferred_element_type=jnp.float32)
    row_dot = jnp.sum(p_tok * dp_tok, axis=-1, keepdims=True) + jnp.sum(
        p_pre * dp_pre, axis=-1, keepdims=True
    )
    ds_tok = (p_tok * (dp_tok - row_dot)).astype(jnp.bfloat16)
    ds_pre = (p_pre * (dp_pre - row_dot)).astype(jnp.bfloat16)
    d_query = (
        jnp.einsum("hlm,mhe->lhe", ds_tok, keys, preferred_element_type=jnp.float32)
        + jnp.einsum("hlp,phe->lhe", ds_pre, pkey, preferred_element_type=jnp.float32)
    ) * scale
    d_keys = jnp.einsum("hlm,lhe->mhe", ds_tok, query, preferred_element_type=jnp.float32) * scale
    d_values = jnp.einsum(
        "hlm,lhe->mhe", p_tok.astype(jnp.bfloat16), dattn_b, preferred_element_type=jnp.float32
    )
    grad_pkey = (
        jnp.einsum("hlp,lhe->phe", ds_pre, query, preferred_element_type=jnp.float32) * scale
    )
    grad_pval = jnp.einsum(
        "hlp,lhe->phe", p_pre.astype(jnp.bfloat16), dattn_b, preferred_element_type=jnp.float32
    )
    dqkv_b = (
        jnp.stack([d_query, d_keys, d_values], axis=1)
        .reshape(length, 3 * width)
        .astype(jnp.bfloat16)
    )
    grad_wq = jnp.einsum("ld,lc->dc", a1b, dqkv_b, preferred_element_type=jnp.float32)
    grad_bq = jnp.sum(dqkv_b.astype(jnp.float32), axis=0)
    d_a1 = jnp.dot(dqkv_b, w_q.T, preferred_element_type=jnp.float32)
    norm_back_first = jax.vjp(norm_rows, hf, gain_f[0], bias_f[9 * width : 10 * width])[1]
    d_in_norm, grad_g1, grad_c1 = norm_back_first(d_a1)
    d_input = d_resid + d_in_norm
    grad_prefix = jnp.concatenate(
        [grad_pkey.reshape(prefix_len, width), grad_pval.reshape(prefix_len, width)], axis=1
    )
    return (d_input, (grad_wq, grad_wo), (grad_bq, grad_bo, grad_g1, grad_c1), grad_prefix)


def assemble(ffn_mats, ffn_small, attn_mats, attn_small):
    grad_bf, grad_bp, grad_g2, grad_c2 = ffn_small
    grad_bq, grad_bo, grad_g1, grad_c1 = attn_small
    grad_gains = jnp.stack([grad_g1, grad_g2])
    grad_bias = jnp.concatenate([grad_bq, grad_bo, grad_bf, grad_bp, grad_c1, grad_c2])
    return (attn_mats[0], attn_mats[1], ffn_mats[0], ffn_mats[1], grad_gains, grad_bias)


def on_device_general(
    tokens,
    segment_ids,
    cotangent,
    w_qkv,
    w_attn_out,
    w_fc,
    w_proj,
    gains,
    biases,
    prefix_embed,
    reparam_in,
    reparam_in_bias,
    reparam_out,
    reparam_out_bias,
):
    section = lax.axis_index("section")
    micro, row_len = segment_ids.shape
    width = tokens.shape[1]
    prefix_len = prefix_embed.shape[0]
    head_dim = width // HEADS
    gathered = (
        lax.all_gather(w_qkv, "dp", axis=1, tiled=True),
        lax.all_gather(w_attn_out, "dp", axis=1, tiled=True),
        lax.all_gather(w_fc, "dp", axis=1, tiled=True),
        lax.all_gather(w_proj, "dp", axis=1, tiled=True),
        lax.all_gather(gains, "dp", axis=2, tiled=True),
        lax.all_gather(biases, "dp", axis=1, tiled=True),
    )
    params = tuple((item[0] for item in gathered))
    pre_hidden = jnp.dot(
        prefix_embed, reparam_in, preferred_element_type=jnp.float32
    ) + reparam_in_bias.astype(jnp.float32)
    hidden = jnp.tanh(pre_hidden)
    hidden_b = hidden.astype(jnp.bfloat16)
    prefix_kv = (
        jnp.dot(hidden_b, reparam_out, preferred_element_type=jnp.float32)
        + reparam_out_bias.astype(jnp.float32)
    ).astype(jnp.bfloat16)
    pkey = prefix_kv[:, :width].reshape(prefix_len, HEADS, head_dim)
    pval = prefix_kv[:, width:].reshape(prefix_len, HEADS, head_dim)
    token_rows = tokens.reshape(micro, row_len, width)
    cot_rows = cotangent.reshape(micro, row_len, width)
    received = jnp.zeros((row_len, width), jnp.bfloat16)
    outputs = jnp.zeros((micro, row_len, width), jnp.bfloat16)
    stored = []
    for tick in range(micro + 1):
        index = tick - section
        active = (index >= 0) & (index < micro)
        slot = jnp.clip(index, 0, micro - 1)
        segs = segment_ids[slot]
        h_b = jnp.where(section == 0, token_rows[slot], received)
        result, keep = forward_layer(h_b, segs, pkey, pval, params)
        result_b = result.astype(jnp.bfloat16)
        outputs = jnp.where(active, outputs.at[slot].set(result_b), outputs)
        stored.append(keep)
        if tick < micro:
            received = passed_along(result_b, "section", 1)
    regathered = (
        lax.all_gather(w_qkv, "dp", axis=1, tiled=True),
        lax.all_gather(w_attn_out, "dp", axis=1, tiled=True),
        lax.all_gather(w_fc, "dp", axis=1, tiled=True),
        lax.all_gather(w_proj, "dp", axis=1, tiled=True),
        lax.all_gather(gains, "dp", axis=2, tiled=True),
        lax.all_gather(biases, "dp", axis=1, tiled=True),
    )
    params_back = tuple((item[0] for item in regathered))
    stacked = jax.tree.map(lambda *items: jnp.stack(items), *stored)
    coming = jnp.zeros((row_len, width), jnp.bfloat16)
    in_grads = jnp.zeros((micro, row_len, width), jnp.bfloat16)
    grad_total = None
    prefix_total = None
    for tick in range(micro + 1):
        index = micro - tick - section
        active = (index >= 0) & (index < micro)
        slot = jnp.clip(index, 0, micro - 1)
        segs = segment_ids[slot]
        saved = jax.tree.map(lambda item: item[slot + section], stacked)
        grad_out = jnp.where(
            section == 1, cot_rows[slot].astype(jnp.float32), coming.astype(jnp.float32)
        )
        keep = saved
        d_resid, ffn_mats, ffn_small = backward_ffn(grad_out, keep, params_back)
        ffn_mats = jax.tree.map(
            lambda item: jnp.where(active, item, jnp.zeros_like(item)), ffn_mats
        )
        ffn_small = jax.tree.map(
            lambda item: jnp.where(active, item, jnp.zeros_like(item)), ffn_small
        )
        d_input, attn_mats, attn_small, grad_prefix = backward_attn(
            d_resid, keep, pkey, pval, params_back
        )
        attn_mats = jax.tree.map(
            lambda item: jnp.where(active, item, jnp.zeros_like(item)), attn_mats
        )
        attn_small = jax.tree.map(
            lambda item: jnp.where(active, item, jnp.zeros_like(item)), attn_small
        )
        grad_prefix = jnp.where(active, grad_prefix, jnp.zeros_like(grad_prefix))
        grads = assemble(ffn_mats, ffn_small, attn_mats, attn_small)
        if grad_total is None:
            grad_total = grads
            prefix_total = grad_prefix
        else:
            grad_total = jax.tree.map(lambda left, right: left + right, grad_total, grads)
            prefix_total = prefix_total + grad_prefix
        d_input_b = d_input.astype(jnp.bfloat16)
        in_grads = jnp.where(active, in_grads.at[slot].set(d_input_b), in_grads)
        if tick < micro:
            coming = passed_along(d_input_b, "section", -1)
    lifted = tuple((item[None] for item in grad_total))
    weight_grads = (
        lax.psum_scatter(lifted[0], "dp", scatter_dimension=1, tiled=True),
        lax.psum_scatter(lifted[1], "dp", scatter_dimension=1, tiled=True),
        lax.psum_scatter(lifted[2], "dp", scatter_dimension=1, tiled=True),
        lax.psum_scatter(lifted[3], "dp", scatter_dimension=1, tiled=True),
        lax.psum_scatter(lifted[4], "dp", scatter_dimension=2, tiled=True),
        lax.psum_scatter(lifted[5], "dp", scatter_dimension=1, tiled=True),
    )
    prefix_grad = lax.psum(prefix_total, "dp")
    prefix_grad_b = prefix_grad.astype(jnp.bfloat16)
    grad_reparam_out = jnp.einsum(
        "pr,pc->rc", hidden_b, prefix_grad_b, preferred_element_type=jnp.float32
    )
    grad_reparam_out_bias = jnp.sum(prefix_grad_b.astype(jnp.float32), axis=0)
    hidden_part = jnp.dot(prefix_grad_b, reparam_out.T, preferred_element_type=jnp.float32)
    hidden_grad = lax.psum(hidden_part, "section")
    dpre_hidden_b = (hidden_grad * (1.0 - hidden * hidden)).astype(jnp.bfloat16)
    grad_reparam_in = jnp.einsum(
        "pd,pr->dr", prefix_embed, dpre_hidden_b, preferred_element_type=jnp.float32
    )
    grad_reparam_in_bias = jnp.sum(dpre_hidden_b.astype(jnp.float32), axis=0)
    grad_prefix_embed = jnp.dot(dpre_hidden_b, reparam_in.T, preferred_element_type=jnp.float32)
    layer_outs = outputs.reshape(1, micro * row_len, width)
    input_grads = in_grads.reshape(1, micro * row_len, width)
    return (
        layer_outs,
        input_grads,
        weight_grads[0],
        weight_grads[1],
        weight_grads[2],
        weight_grads[3],
        weight_grads[4],
        weight_grads[5],
        grad_prefix_embed,
        grad_reparam_in,
        grad_reparam_in_bias,
        grad_reparam_out,
        grad_reparam_out_bias,
    )


def solution(mesh):
    return jax.shard_map(
        on_device if mesh.shape["dp"] == 16 else on_device_general,
        mesh=mesh,
        in_specs=(
            P("dp", None),
            P("dp", None),
            P("dp", None),
            P("section", "dp", None),
            P("section", "dp", None),
            P("section", "dp", None),
            P("section", "dp", None),
            P("section", None, "dp"),
            P("section", "dp"),
            P(),
            P(),
            P(),
            P(None, "section"),
            P("section"),
        ),
        out_specs=(
            P("section", "dp", None),
            P("section", "dp", None),
            P("section", "dp", None),
            P("section", "dp", None),
            P("section", "dp", None),
            P("section", "dp", None),
            P("section", None, "dp"),
            P("section", "dp"),
            P(),
            P(),
            P(),
            P(None, "section"),
            P("section"),
        ),
        check_vma=False,
    )
```

```python
import math

import jax
import jax.numpy as jnp
from jax import lax
from jax.experimental import pallas as pl
from jax.experimental.pallas import tpu as pltpu
from jax.sharding import PartitionSpec as P

HEADS = 16
EPS = 1e-05
NEG = -1000000000.0
MESH = pl.DeviceIdType.MESH
F32 = jnp.float32
B16 = jnp.bfloat16
NP = 12
MAIN = 896
AHEAD = 1


def place():
    s = lax.axis_index("section"); d = lax.axis_index("dp")
    return s, d, d // 4, (d // 2) % 2, d % 2

def greet(s, d):
    bar = pltpu.get_barrier_semaphore()
    for i in range(1, 16):
        pl.semaphore_signal(bar, 1, device_id=(s, (d + i) % 16), device_id_type=MESH)
    pl.semaphore_signal(bar, 1, device_id=(1 - s, d), device_id_type=MESH)


def greeted():
    pl.semaphore_wait(pltpu.get_barrier_semaphore(), 16)


def to_all(src, dst, ss, rs):
    s, d = lax.axis_index("section"), lax.axis_index("dp")

    def cp(i, frm):
        to = (d + i) % 16
        return pltpu.make_async_remote_copy(
            src(to), dst.at[frm], ss.at[i], rs.at[i], device_id=(s, to), device_id_type=MESH
        )

    def start():
        for i in range(1, 16):
            cp(i, d).start()

    def arrive():
        for i in range(1, 16):
            cp(i, (d + 16 - i) % 16).wait_recv()

    def finish():
        for i in range(1, 16):
            cp(i, d).wait_send()

    return start, arrive, finish


class Gather:
    def __init__(self, W, ssem, rsem, tsem, qsem):
        self.W, self.ssem, self.rsem, self.tsem, self.qsem = W, ssem, rsem, tsem, qsem
        self.s, self.d, self.z, self.y, self.c = place()
    def blk(self, k, d):
        i = k // 8
        row = (1-i)*(1024*k+64*d) + i*(8192+256*d+64*(k-8))
        return self.W.at[pl.ds(pl.multiple_of(row, 64), 64)]
    def cp(self, k, origin, target, slot, width=1024):
        b = self.blk(k, origin)
        if width < 1024: b = b.at[:, pl.ds(0, width)]
        return pltpu.make_async_remote_copy(src_ref=b, dst_ref=b, send_sem=self.ssem.at[k, slot], recv_sem=self.rsem.at[k, origin],
            device_id=(self.s, target), device_id_type=MESH)
    def dev(self, z, y, c): return z*4+y*2+c
    def arrived(self, k, origin): self.cp(k, origin, origin, 0).wait_recv()
    def to_up(self, k, zo, op):
        op(self.cp(k, self.dev(zo, self.y, self.c), self.dev(self.z+1, self.y, self.c), zo))
    def to_down(self, k, zo, op):
        op(self.cp(k, self.dev(zo, self.y, self.c), self.dev(self.z-1, self.y, self.c), 4+zo))
    def to_y(self, k, zo, op, width=MAIN):
        op(self.cp(k, self.dev(zo, self.y, self.c), self.dev(self.z, 1-self.y, self.c), 8+zo, width))
    def strip(self, k, zo, to, slot):
        b = self.blk(k, self.dev(zo, 1-self.y, self.c)).at[:, pl.ds(MAIN, 1024-MAIN)]
        return pltpu.make_async_remote_copy(src_ref=b, dst_ref=b, send_sem=self.tsem.at[k, slot], recv_sem=self.qsem.at[k, zo],
            device_id=(self.s, self.dev(to, self.y, self.c)), device_id_type=MESH)
    def strip_up(self, k, zo, op): op(self.strip(k, zo, self.z+1, zo))
    def strip_down(self, k, zo, op): op(self.strip(k, zo, self.z-1, 4+zo))
    def to_c(self, k, zo, yo, op):
        op(self.cp(k, self.dev(zo, yo, self.c), self.dev(self.z, self.y, 1-self.c), 12+zo*2+yo))
    def step(self, t, own):
        z, y, c = self.z, self.y, self.c
        start = lambda cp: cp.start()
        def fresh(k):
            own(k)
            self.to_y(k, z, start, 1024)
            @pl.when(z < 3)
            def _(): self.to_up(k, z, start)
            @pl.when(z > 0)
            def _(): self.to_down(k, z, start)
            self.to_c(k, z, y, start)
        @pl.when(t == 0)
        def _():
            for k in range(AHEAD): fresh(k)
        @pl.when(t + AHEAD < NP)
        def _(): fresh(t + AHEAD)
        for q in (1, 2, 3, 4):
            k = t - q
            ok = (k >= 0) & (k < NP)
            if q < 4:
                @pl.when(ok & (z - q >= 0))
                def _():
                    self.arrived(k, self.dev(z-q, y, c))
                    @pl.when(z < 3)
                    def _(): self.to_up(k, z-q, start)
                    self.to_y(k, z-q, start)
                    self.to_c(k, z-q, y, start)
                @pl.when(ok & (z + q <= 3))
                def _():
                    self.arrived(k, self.dev(z+q, y, c))
                    @pl.when(z > 0)
                    def _(): self.to_down(k, z+q, start)
                    self.to_y(k, z+q, start)
                    self.to_c(k, z+q, y, start)
            e = q - 1
            def side(zo):
                o = self.dev(zo, 1-y, c)
                self.cp(k, o, o, 0, MAIN).wait_recv()
                self.to_c(k, zo, 1-y, start)
            if e == 0:
                @pl.when(ok)
                def _():
                    self.arrived(k, self.dev(z, 1-y, c))
                    @pl.when(z < 3)
                    def _(): self.strip_up(k, z, start)
                    @pl.when(z > 0)
                    def _(): self.strip_down(k, z, start)
                    self.to_c(k, z, 1-y, start)
            else:
                @pl.when(ok & (z - e >= 0))
                def _():
                    self.strip(k, z-e, z, 0).wait_recv()
                    @pl.when(z < 3)
                    def _(): self.strip_up(k, z-e, start)
                    side(z-e)
                @pl.when(ok & (z + e <= 3))
                def _():
                    self.strip(k, z+e, z, 0).wait_recv()
                    @pl.when(z > 0)
                    def _(): self.strip_down(k, z+e, start)
                    side(z+e)
    def complete(self, k):
        for i in range(8):
            self.arrived(k, 2*i + 1-self.c)
    def drain(self):
        fin = lambda cp: cp.wait_send()
        z, y = self.z, self.y
        @pl.loop(0, NP)
        def _(k):
            for zo in range(4):
                @pl.when((zo <= z) & (z < 3))
                def _(): self.to_up(k, zo, fin)
                @pl.when((zo >= z) & (z > 0))
                def _(): self.to_down(k, zo, fin)
                @pl.when(zo == z)
                def _(): self.to_y(k, zo, fin, 1024)
                @pl.when(zo != z)
                def _(): self.to_y(k, zo, fin)
                @pl.when((zo <= z) & (z < 3))
                def _(): self.strip_up(k, zo, fin)
                @pl.when((zo >= z) & (z > 0))
                def _(): self.strip_down(k, zo, fin)
                for yo in range(2): self.to_c(k, zo, yo, fin)

def own_copies(wq, wo, wf, wp, g, sem):
    out = []
    for k in range(NP):
        if k < 3: src = wq.at[0, :, pl.ds(1024*k, 1024)]
        elif k == 3: src = wo.at[0]
        elif k < 8: src = wf.at[0, :, pl.ds(1024*(k-4), 1024)]
        else: src = wp.at[0, pl.ds(64*(k-8), 64)]
        out.append(pltpu.make_async_copy(src, g.blk(jnp.int32(k), g.d), sem.at[k]))
    return out


HALF = 256
STAGES = 12
GELU_C = math.sqrt(2.0 / math.pi)


def dot_nn(a, b):
    return lax.dot_general(a, b, (((1,), (0,)), ((), ())), preferred_element_type=F32)


def dot_nt(a, b):
    return lax.dot_general(a, b, (((1,), (1,)), ((), ())), preferred_element_type=F32)


def dot_tn(a, b):
    return lax.dot_general(a, b, (((0,), (0,)), ((), ())), preferred_element_type=F32)


def whiten(v):
    mean = jnp.mean(v, axis=-1, keepdims=True)
    cent = v - mean
    rstd = lax.rsqrt(jnp.mean(cent * cent, axis=-1, keepdims=True) + EPS)
    return cent * rstd, rstd


def split_heads(pair):
    left = lax.broadcasted_iota(jnp.int32, pair.shape, 1) < 64
    zero = jnp.zeros_like(pair)
    return jnp.concatenate([jnp.where(left, pair, zero), jnp.where(left, zero, pair)], axis=0)


def forward_kernel(
    wq, wo, wf, wp, tokens, segs, gains, biases, aux, r_in, r_out,
    W_o, out_o, h_o, a1_o, qkv_o, prob_o, ppre_o, att_o, res_o, a2_o, gp_o, act_o, small_o, pkey_o, pval_o, hid_o,
    W, H, A1, QKV, PROB, PPRE, ATT, RES, A2, GP, ACT, OUT, SPRE, ACC, small, pkey, pval, hid, mask, pack, PACKS, ROWS,
    own_sem, ssem, rsem, tsem, qsem, hsem, xs, xr, save_sem, fs, ps, pr, psem,
):
    g = Gather(W, ssem, rsem, tsem, qsem)
    s = g.s
    for cp in own_copies(wq, wo, wf, wp, g, own_sem):
        cp.start()
    r_in_parts = [pltpu.make_async_copy(r_in.at[pl.ds(512 * i, 512)], ACT.at[2, :, pl.ds(512 * i, 512)], psem.at[i]) for i in range(2)]
    r_out_parts = [pltpu.make_async_copy(r_out.at[:, pl.ds(1024 * i, 1024)], ACT.at[i], psem.at[2 + i]) for i in range(2)]
    for cp in r_in_parts + r_out_parts:
        cp.start()
    greet(s, g.d)
    own_bias = biases[...].astype(F32)
    for n in range(2):
        for r in range(11):
            ROWS[0, r : r + 1, 64 * n : 64 * n + 64] = own_bias[:, 64 * r : 64 * r + 64]
        ROWS[0, 11:13, 64 * n : 64 * n + 64] = gains[0].astype(F32)
    ROWS[0, 13:16] = jnp.zeros((3, 128), F32)
    pack[...] = ROWS[0].astype(B16)
    greeted()
    send_packs, packs_in, packs_out = to_all(lambda to: pack, PACKS, ps, pr)

    def prep_saves():
        pairs = [(small, small_o), (pkey, pkey_o), (pval, pval_o), (hid, hid_o)]
        return [pltpu.make_async_copy(a, b, psem.at[4 + i]) for i, (a, b) in enumerate(pairs)]

    def prepare():
        for cp in r_in_parts + r_out_parts:
            cp.wait()
        ph = dot_nn(aux[:, :512], ACT[2, :, :512]) + dot_nn(aux[:, 512:], ACT[2, :, 512:])
        hid[...] = jnp.tanh(ph + aux[10:11, :512].astype(F32))
        hb = hid[...].astype(B16)
        head = lax.broadcasted_iota(jnp.int32, (16, 1024), 1) // 64
        for i, big in enumerate((pkey, pval)):
            kv = (dot_nn(hb, ACT[i]) + aux[11 + i : 12 + i].astype(F32)).astype(B16)
            for h in range(16):
                big[16 * h : 16 * h + 16] = jnp.where(head == h, kv, jnp.zeros_like(kv))
        key = lax.broadcasted_iota(jnp.int32, (HALF, HALF), 0)
        query = lax.broadcasted_iota(jnp.int32, (HALF, HALF), 1)
        for b in range(2):
            by_query = jnp.broadcast_to(segs[b : b + 1].astype(F32), (HALF, HALF))
            ok = (by_query.T == by_query) & (key <= query)
            mask[b] = jnp.where(ok, 0.0, NEG)
        packs_in()
        ROWS[...] = PACKS[...].astype(F32)
        left = lax.broadcasted_iota(jnp.int32, (1, 128), 1) < 64
        small[...] = jnp.zeros_like(small)
        for n in range(104):
            row, at = n // 8, 128 * (n % 8)
            if row < 11:
                (d0, r0), (d1, r1) = divmod(2 * n, 11), divmod(2 * n + 1, 11)
            else:
                (d0, r0), (d1, r1) = (2 * (n % 8), row), (2 * (n % 8) + 1, row)
            small[row : row + 1, at : at + 128] = jnp.where(left, ROWS[d0, r0 : r0 + 1], ROWS[d1, r1 : r1 + 1])
        for cp in prep_saves():
            cp.start()

    send_packs()
    PACKS[g.d] = pack[...]

    def tokens_in():
        return pltpu.make_async_copy(tokens, H, hsem)

    def half(b):
        return pl.ds(pl.multiple_of(b * HALF, HALF), HALF)

    def cross(b):
        return pltpu.make_async_remote_copy(
            OUT.at[half(b)], H.at[half(b)], xs.at[b], xr.at[b], device_id=(1 - s, g.d), device_id_type=MESH
        )

    @pl.when(s == 0)
    def _():
        tokens_in().start()

    def own(t):
        b = g.blk(t, g.d)
        pltpu.make_async_copy(b, b, own_sem.at[t]).wait()

    def rows_of(k):
        return pl.ds(pl.multiple_of(k * 1024, 1024), 1024)

    def saves(b):
        r = half(b)
        pairs = [
            (H.at[r], h_o.at[r]), (A1.at[r], a1_o.at[r]), (QKV.at[:, r], qkv_o.at[:, r]), (PROB.at[pl.ds(2 * b, 2)], prob_o.at[pl.ds(2 * b, 2)]),
            (PPRE.at[b], ppre_o.at[b]), (ATT.at[r], att_o.at[r]), (RES.at[r], res_o.at[r]), (A2.at[r], a2_o.at[r]),
            (OUT.at[r], out_o.at[r]),
        ]
        return [pltpu.make_async_copy(src, dst, save_sem.at[b, i]) for i, (src, dst) in enumerate(pairs)]

    def ffn_saves(b, j):
        r = half(b)
        return [
            pltpu.make_async_copy(GP.at[j, r], gp_o.at[j, r], fs.at[b, j]),
            pltpu.make_async_copy(ACT.at[j, r], act_o.at[j, r], fs.at[b, 4 + j]),
        ]

    def piece_out(k):
        return pltpu.make_async_copy(W.at[rows_of(k)], W_o.at[rows_of(k)], save_sem.at[2, k])

    def norm_in(b):
        @pl.when(s == 0)
        def _():
            @pl.when(b == 0)
            def _():
                tokens_in().wait()

        @pl.when(s == 1)
        def _():
            cross(b).wait_recv()

        xhat, _ = whiten(H[half(b)].astype(F32))
        A1[half(b)] = (xhat * small[11:12] + small[9:10]).astype(B16)
        saves(b)[0].start()
        saves(b)[1].start()

    def project(i, b):
        v = dot_nn(A1[half(b)], W[rows_of(i)]) + small[pl.ds(i, 1)]
        v = v.astype(B16)
        QKV[i, half(b)] = v * jnp.where(i == 0, 0.125, 1.0).astype(B16)

        @pl.when(i == 2)
        def _():
            saves(b)[2].start()

    def attend(part, b):
        @pl.when(part == 0)
        def _():
            sp = dot_nt(pkey[...], QKV[0, half(b)])
            there = lax.broadcasted_iota(jnp.int32, sp.shape, 0) % 16 < 10
            SPRE[b] = jnp.where(there, sp, NEG)

        def pair(p):
            cols = pl.ds(pl.multiple_of(p * 128, 128), 128)
            q2, k2, v2 = QKV[0, half(b), cols], QKV[1, half(b), cols], QKV[2, half(b), cols]
            st = dot_nt(split_heads(k2), q2)
            probs, pres = [], []
            for e in range(2):
                sh = st[e * HALF : (e + 1) * HALF] + mask[b]
                sp = SPRE[b, pl.ds(pl.multiple_of(p * 32 + e * 16, 16), 16)]
                top = jnp.maximum(jnp.max(sh, axis=0, keepdims=True), jnp.max(sp, axis=0, keepdims=True))
                et, ep = jnp.exp(sh - top), jnp.exp(sp - top)
                inv = 1.0 / (jnp.sum(et, axis=0, keepdims=True) + jnp.sum(ep, axis=0, keepdims=True))
                probs.append((et * inv).astype(B16))
                pres.append((ep * inv).astype(B16))
            pr = jnp.concatenate(probs, axis=0)
            PROB[2 * b + p // 4, :, pl.ds(pl.multiple_of((p % 4) * HALF, HALF), HALF)] = pr
            PPRE[b, pl.ds(pl.multiple_of(p * 32, 32), 32)] = jnp.concatenate(pres, axis=0)
            ACC[half(b), cols] = dot_tn(pr, split_heads(v2))

        for p in range(4):
            pair(part * 4 + p)

        @pl.when(part == 1)
        def _():
            ATT[half(b)] = (ACC[half(b)] + dot_tn(PPRE[b], pval[...])).astype(B16)
            saves(b)[3].start()
            saves(b)[4].start()
            saves(b)[5].start()

    def mix(b):
        r = H[half(b)].astype(F32) + (dot_nn(ATT[half(b)], W[rows_of(3)]) + small[3:4])
        RES[half(b)] = r
        xhat, _ = whiten(r)
        A2[half(b)] = (xhat * small[12:13] + small[10:11]).astype(B16)
        saves(b)[6].start()
        saves(b)[7].start()

    def widen(j, b):
        x = dot_nn(A2[half(b)], W[rows_of(4 + j)]) + small[pl.ds(4 + j, 1)]
        x2 = x * x
        h = 0.5 + 0.5 * jnp.tanh(x * (GELU_C + (0.044715 * GELU_C) * x2))
        act = x * h
        ACT[j, half(b)] = act.astype(B16)
        GP[j, half(b)] = (h + act * (1.0 - h) * (2.0 * GELU_C + (6 * 0.044715 * GELU_C) * x2)).astype(B16)

        for cp in ffn_saves(b, j):
            cp.start()

    def narrow(b):
        v = RES[half(b)] + small[8:9]
        for j in range(4):
            v = v + dot_nn(ACT[j, half(b)], W[rows_of(8 + j)])
        OUT[half(b)] = v.astype(B16)

        @pl.when(s == 0)
        def _():
            cross(b).start()

        saves(b)[8].start()

    @pl.loop(0, NP + 5 + 2 * STAGES)
    def _(tick):
        @pl.when(tick < NP + 5)
        def _():
            g.step(tick, own)

            @pl.when(tick == 3)
            def _():
                prepare()

            @pl.when(tick >= 5)
            def _():
                g.complete(tick - 5)

                @pl.when(tick < 13)
                def _():
                    piece_out(tick - 5).start()

                @pl.when(tick == NP + 4)
                def _():
                    for k in range(8, NP):
                        piece_out(k).start()

        late = tick - (NP + 5)
        stage = (1 - s) * (tick - 5) + s * ((late + STAGES) % STAGES - STAGES * (late < 0).astype(jnp.int32))
        lo = s * (late // STAGES)
        hi = (1 - s) * 2 + s * (late // STAGES + 1)

        def when(i, body):
            @pl.when(stage == i)
            def _():
                pl.loop(lo, hi)(body)

        when(0, norm_in)

        @pl.when((stage >= 1) & (stage < 4))
        def _():
            pl.loop(lo, hi)(lambda b: project(stage - 1, b))

        @pl.when((stage >= 4) & (stage < 6))
        def _():
            pl.loop(lo, hi)(lambda b: attend(stage - 4, b))

        when(6, mix)

        @pl.when((stage >= 7) & (stage < 11))
        def _():
            pl.loop(lo, hi)(lambda b: widen(stage - 7, b))

        when(11, narrow)

    g.drain()
    packs_out()
    for cp in prep_saves():
        cp.wait()

    @pl.loop(0, NP)
    def _(k):
        piece_out(k).wait()

    @pl.loop(0, 2)
    def _(b):
        for cp in saves(b) + [cp for j in range(4) for cp in ffn_saves(b, j)]:
            cp.wait()

        @pl.when(s == 0)
        def _():
            cross(b).wait_send()


def forward_call(wq, wo, wf, wp, tokens, segs, gains, biases, aux, r_in, r_out):
    any_, vm = pl.BlockSpec(memory_space=pl.ANY), pl.BlockSpec(memory_space=pltpu.VMEM)
    n, d = tokens.shape
    kept = [
        ((NP * d, d), B16), ((n, d), B16), ((n, d), B16), ((n, d), B16), ((3, n, d), B16), ((4, n, d), B16),
        ((2, HALF, HALF), B16), ((n, d), B16), ((n, d), F32), ((n, d), B16), ((4, n, d), B16), ((4, n, d), B16),
    ]
    shared = [((16, d), F32), ((HALF, d), B16), ((HALF, d), B16), ((16, 512), F32)]
    dma = pltpu.SemaphoreType.DMA
    order = [0, 2, 3, 4, 5, 6, 7, 8, 9, 10, 11, 1]
    scratch = [kept[i] for i in order] + [((2, HALF, HALF), F32), ((n, d), F32)] + shared
    scratch += [((2, HALF, HALF), F32), ((16, 128), B16), ((16, 16, 128), B16), ((16, 16, 128), F32)]
    return pl.pallas_call(
        forward_kernel,
        out_shape=[jax.ShapeDtypeStruct(*k) for k in kept + shared],
        in_specs=[any_] * 5 + [vm] * 4 + [any_] * 2,
        out_specs=[any_] * len(kept + shared),
        scratch_shapes=[pltpu.VMEM(*v) for v in scratch]
        + [dma((NP,)), dma((NP, 20)), dma((NP, 16)), dma((NP, 8)), dma((NP, 4)), dma, dma((2,)), dma((2,)), dma((3, NP)), dma((2, 8)), dma((16,)), dma((16,)), dma((8,))],
        compiler_params=pltpu.CompilerParams(collective_id=0, has_side_effects=True, vmem_limit_bytes=62 << 20),
    )(wq, wo, wf, wp, tokens, segs, gains, biases, aux, r_in, r_out)


def prefix_rows(embed, in_bias, out_bias):
    in_bias = jnp.pad(in_bias, (0, 512)).reshape(1, 1024)
    return jnp.concatenate([embed, in_bias, out_bias.reshape(2, 1024), jnp.zeros((3, 1024), B16)])


SPLIT = 6
BACK_TICKS = 2 + 2 * SPLIT + NP + 6


def unwhiten(grad, xhat, rstd):
    return rstd * (
        grad
        - jnp.mean(grad, axis=-1, keepdims=True)
        - xhat * jnp.mean(grad * xhat, axis=-1, keepdims=True)
    )


def column_sum(v):
    return jnp.sum(v.astype(F32), axis=0, keepdims=True)


def backward_kernel(
    W_i, h_i, a1_i, qkv_i, prob_i, ppre_i, att_i, res_i, a2_i, gp_i, act_i, cot, r_out, small, pkey, pval,
    dh_o, oq, oo, of, op_, own_sums, KVB, HSUM,
    WG, H, A1, QKV, BIG, PPRE, ATT, RES, A2, GP, DM, DAT, DATT, DPP, DSP, ACC,
    RC, RY, RU, RD, RUS, RDS, RYS, T, SG, DKV, SB, RB, PF, PG, HP, HPR,
    wsem, lsem, osem, cs, cr, ys, yr, us, ur, ds_, dr, yss, ysr, xs, xr, hs, bs, br, ps, pr, hx, gs,
):
    s, d, z, y, c = place()

    def slot(k):
        return k + 8 * (1 - s) if k < 4 else k

    def fetch(ks):
        return [pltpu.make_async_copy(W_i.at[k], WG.at[slot(k)], wsem.at[k]) for k in ks]

    def begin(cps):
        for cp in cps:
            cp.start()

    def loads():
        pairs = [
            (a2_i, A2), (res_i, RES), (att_i, ATT), (qkv_i, QKV), (ppre_i, PPRE), (a1_i, A1), (h_i, H),
            (act_i, BIG), (prob_i, BIG), (cot, DM),
        ]
        return [pltpu.make_async_copy(a, b, lsem.at[i]) for i, (a, b) in enumerate(pairs)]

    L_A2, L_RES, L_ATT, L_QKV, L_PPRE, L_A1, L_H, L_ACT, L_PROB, L_COT = range(10)

    def begin_loads(which):
        begin([loads()[i] for i in which])

    pl.when(s == 1)(lambda: begin_loads((L_COT,)))

    def slope(j):
        return pltpu.make_async_copy(gp_i.at[j], GP.at[j], gs.at[j])

    for j in range(4):
        begin(fetch((8 + j,)) + [slope(j)])

    pl.when(s == 0)(lambda: begin_loads((L_ACT,)))
    SG[...] = jnp.zeros_like(SG)
    DKV[...] = jnp.zeros_like(DKV)
    SB[...] = jnp.zeros_like(SB)
    greet(s, d)

    def weights(ks):
        for cp in fetch(ks):
            cp.wait()

    def half(b):
        return pl.ds(pl.multiple_of(b * HALF, HALF), HALF)

    def weight(k):
        return WG[slot(k)].reshape(1024, 1024)

    def cross(b):
        return pltpu.make_async_remote_copy(
            H.at[half(b)], DM.at[half(b)], xs.at[b], xr.at[b], device_id=(1 - s, d), device_id_type=MESH
        )

    def dh_out(b):
        return pltpu.make_async_copy(H.at[half(b)], dh_o.at[half(b)], hs.at[b])

    def more(j):
        if j < 2:
            begin(fetch((4 + 2 * j, 5 + 2 * j)))
        elif j == 2:
            begin_loads((L_A2, L_RES))
            pl.when(s == 1)(lambda: begin(fetch((3,))))
        else:
            pl.when(s == 1)(lambda: begin_loads((L_QKV, L_PPRE, L_PROB)))

    def ffn_in(b):
        if b == 0:
            pl.when(s == 1)(lambda: loads()[L_COT].wait())
            pl.when(s == 0)(lambda: cross(0).wait_recv())
        for j in range(4):
            if b == 0:
                weights((8 + j,))
                slope(j).wait()
                more(j)
            GP[j, half(b)] = (dot_nt(DM[half(b)], weight(8 + j)) * GP[j, half(b)].astype(F32)).astype(B16)
        if b == 1:

            @pl.when(s == 0)
            def _():
                begin(fetch((3, 0, 1, 2)))

    def ffn_norm(b):
        @pl.when(b == 0)
        def _():
            weights((4, 5, 6, 7))
            loads()[L_A2].wait()
            loads()[L_RES].wait()
            begin_loads((L_ATT, L_A1, L_H))

            @pl.when(s == 0)
            def _():
                begin_loads((L_QKV, L_PPRE))

            @pl.when(s == 1)
            def _():
                begin(fetch((0, 1, 2)))

        grad = dot_nt(GP[0, half(b)], weight(4))
        for j in range(1, 4):
            grad = grad + dot_nt(GP[j, half(b)], weight(4 + j))
        xhat, rstd = whiten(RES[half(b)])
        SG[10:11] += jnp.sum(grad, axis=0, keepdims=True)
        SG[12:13] += jnp.sum(grad * xhat, axis=0, keepdims=True)
        res = DM[half(b)].astype(F32) + unwhiten(grad * small[12:13], xhat, rstd)
        RES[half(b)] = res
        DAT[half(b)] = res.astype(B16)

    def attn_out(b):
        @pl.when(b == 0)
        def _():
            weights((3,))
            for i in (L_ATT, L_QKV, L_PPRE):
                loads()[i].wait()

            loads()[L_PROB].wait()

        DATT[...] = dot_nt(DAT[half(b)], weight(3)).astype(B16)
        DPP[...] = dot_nt(pval[...], DATT[...])

    def attn_back(part, b):
        @pl.loop(part * 4, part * 4 + 4)
        def _(p):
            cols = pl.ds(pl.multiple_of(p * 128, 128), 128)
            q2, k2, v2 = QKV[0, half(b), cols], QKV[1, half(b), cols], QKV[2, half(b), cols]
            do2 = DATT[:, cols]
            pr = BIG[2 * b + p // 4, :, pl.ds(pl.multiple_of((p % 4) * HALF, HALF), HALF)]
            dp = dot_nt(split_heads(v2), do2)
            dss, pres = [], []
            for e in range(2):
                ph = pr[e * HALF : (e + 1) * HALF].astype(F32)
                dh = dp[e * HALF : (e + 1) * HALF]
                at = pl.ds(pl.multiple_of(p * 32 + e * 16, 16), 16)
                pp, dpp = PPRE[b, at].astype(F32), DPP[at]
                dot = jnp.sum(ph * dh, axis=0, keepdims=True) + jnp.sum(pp * dpp, axis=0, keepdims=True)
                dss.append((ph * (dh - dot)).astype(B16))
                pres.append((pp * (dpp - dot)).astype(B16))
            ds = jnp.concatenate(dss, axis=0)
            DSP[pl.ds(pl.multiple_of(p * 32, 32), 32)] = jnp.concatenate(pres, axis=0)
            left = lax.broadcasted_iota(jnp.int32, (HALF, 128), 1) < 64
            ACC[:, cols] = dot_tn(ds, split_heads(k2))
            dk = dot_nn(ds, q2)
            dv = dot_nn(pr, do2)
            QKV[1, half(b), cols] = jnp.where(left, dk[:HALF], dk[HALF:]).astype(B16)
            QKV[2, half(b), cols] = jnp.where(left, dv[:HALF], dv[HALF:]).astype(B16)

        @pl.when(part == 1)
        def _():
            def own_rows(full):
                out = jnp.zeros((16, 1024), F32)
                head = lax.broadcasted_iota(jnp.int32, (16, 1024), 1) // 64
                for i in range(16):
                    out = out + jnp.where(head == i, full[16 * i : 16 * i + 16], 0.0)
                return out

            DKV[0:16] += own_rows(dot_nn(DSP[...], QKV[0, half(b)]))
            DKV[16:32] += own_rows(dot_nn(PPRE[b], DATT[...]))
            QKV[0, half(b)] = ((ACC[...] + dot_tn(DSP[...], pkey[...])) * 0.125).astype(B16)

    def attn_norm(b):
        @pl.when(b == 0)
        def _():
            weights((0, 1, 2))
            loads()[L_A1].wait()
            loads()[L_H].wait()

        @pl.when((s == 1) & (b == 1))
        def _():
            loads()[L_ACT].start()

        grad = dot_nt(QKV[0, half(b)], weight(0))
        for i in range(1, 3):
            grad = grad + dot_nt(QKV[i, half(b)], weight(i))
        xhat, rstd = whiten(H[half(b)].astype(F32))
        SG[9:10] += jnp.sum(grad, axis=0, keepdims=True)
        SG[11:12] += jnp.sum(grad * xhat, axis=0, keepdims=True)
        H[half(b)] = (RES[half(b)] + unwhiten(grad * small[11:12], xhat, rstd)).astype(B16)

        @pl.when(s == 1)
        def _():
            cross(b).start()

        dh_out(b).start()

    def grad_proj(j):
        if j == 0:
            loads()[L_ACT].wait()
            pl.when(s == 0)(lambda: cross(1).wait_recv())
        for i in range(4):
            cols = [BIG[i, :, 256 * q + 64 * j : 256 * q + 64 * j + 64] for q in range(4)]
            part = dot_tn(jnp.concatenate(cols, axis=1), DM[...])
            WG[8 * s + j, i] = part.astype(B16).reshape(2, 2, 64, 1024)
        if j == 3:
            pl.when(s == 0)(lambda: loads()[L_PROB].start())

    def put(k, a, v):
        for i in range(2):
            part = dot_tn(a[:, 512 * i : 512 * (i + 1)], v[...])
            WG[k, 2 * i : 2 * i + 2] = part.astype(B16).reshape(2, 2, 2, 64, 1024)

    def grad_fc(j):
        put(4 + j, A2, GP.at[j])

    def grad_out():
        put(slot(3), ATT, DAT)

    def grad_qkv(i):
        put(i + 8 * (1 - s), A1, QKV.at[i])

    send_sums, sums_in, sums_out = to_all(lambda to: SB.at[to], RB, bs, br)
    send_pref, pref_in, pref_out = to_all(lambda to: PF, PG, ps, pr)

    def r_out_in():
        return [pltpu.make_async_copy(r_out.at[:, pl.ds(1024 * i, 1024)], BIG.at[i], hx.at[i]) for i in range(2)]

    def hidden_across():
        return pltpu.make_async_remote_copy(HP, HPR, hx.at[2], hx.at[3], device_id=(1 - s, d), device_id_type=MESH)

    def small_first():
        for cp in r_out_in():
            cp.start()
        for i in range(3):
            SG[i : i + 1] = column_sum(QKV[i])
        SG[3:4] = column_sum(DAT[...])
        for j in range(4):
            SG[4 + j : 5 + j] = column_sum(GP[j])
        SG[8:9] = column_sum(DM[...])
        for i in range(16):
            for n in range(13):
                m = 11 * i + n
                row, at = (m // 16, 128 * (m % 16 // 2)) if n < 11 else (n, 128 * (i // 2))
                SB[i, n : n + 1] = SG[row : row + 1, at : at + 128]
            SB[i, 16:32] = DKV[16 * (i // 8) : 16 * (i // 8) + 16, 128 * (i % 8) : 128 * (i % 8) + 128]
        send_sums()
        RB[d] = SB[d]

    def small_second():
        sums_in()
        total = RB[0]
        for i in range(1, 16):
            total = total + RB[i]
        row = lax.broadcasted_iota(jnp.int32, (16, 128), 0)
        odd = jnp.where(row < 11, d + row, d) % 2 == 1
        own_sums[...] = jnp.where(odd, pltpu.roll(total[:16], 64, 1), total[:16])
        PF[...] = total[16:].astype(B16)
        send_pref()
        PG[d] = PF[...]

    def small_third():
        pref_in()
        for i in range(16):
            KVB[:, 128 * i : 128 * i + 128] = PG[i]
        for cp in r_out_in():
            cp.wait()
        HP[...] = dot_nt(KVB[:, :1024], BIG[0]) + dot_nt(KVB[:, 1024:], BIG[1])
        hidden_across().start()

    def small_last():
        hidden_across().wait()
        HSUM[...] = HP[...] + HPR[...]

    def held(r):
        a = r // 4
        return ((2 - a) * (1 - a) // 2) * (r + 8 * s) + a * (2 - a) * r + (a * (a - 1) // 2) * (11 - r + 8 * (1 - s))

    def across_c(r):
        return pltpu.make_async_remote_copy(
            WG.at[held(r), :, :, 1 - c], RC.at[r % 4], cs.at[r], cr.at[r],
            device_id=(s, z * 4 + y * 2 + 1 - c), device_id_type=MESH,
        )

    def across_y(r):
        return pltpu.make_async_remote_copy(
            WG.at[held(r), :, 1 - y, c, :, pl.ds(0, MAIN)], RY.at[r % 4], ys.at[r], yr.at[r],
            device_id=(s, z * 4 + (1 - y) * 2 + c), device_id_type=MESH,
        )

    def up(r, i):
        return pltpu.make_async_remote_copy(
            WG.at[held(r), i, y, c], RU.at[r % 7, i - 1], us.at[r, i - 1], ur.at[r, i - 1],
            device_id=(s, (z + 1) * 4 + y * 2 + c), device_id_type=MESH,
        )

    def down(r, i):
        return pltpu.make_async_remote_copy(
            WG.at[held(r), i, y, c], RD.at[r % 7, i], ds_.at[r, i], dr.at[r, i],
            device_id=(s, (z - 1) * 4 + y * 2 + c), device_id_type=MESH,
        )

    def strip_up(r, i):
        return pltpu.make_async_remote_copy(
            WG.at[held(r), i, 1 - y, c, :, pl.ds(MAIN, 1024 - MAIN)], RUS.at[r % 7, i - 1], us.at[r, 2 + i], ur.at[r, 2 + i],
            device_id=(s, (z + 1) * 4 + y * 2 + c), device_id_type=MESH,
        )

    def strip_down(r, i):
        return pltpu.make_async_remote_copy(
            WG.at[held(r), i, 1 - y, c, :, pl.ds(MAIN, 1024 - MAIN)], RDS.at[r % 7, i], ds_.at[r, 3 + i], dr.at[r, 3 + i],
            device_id=(s, (z - 1) * 4 + y * 2 + c), device_id_type=MESH,
        )

    def strip_y(r):
        return pltpu.make_async_remote_copy(
            WG.at[held(r), z, 1 - y, c, :, pl.ds(MAIN, 1024 - MAIN)], RYS.at[r % 4], yss.at[r], ysr.at[r],
            device_id=(s, z * 4 + (1 - y) * 2 + c), device_id_type=MESH,
        )

    def each_out(r, act):
        k = held(r)
        src = T.at[r % 2]

        @pl.when(r < 4)
        def _():
            act(pltpu.make_async_copy(src, op_.at[0, pl.ds(pl.multiple_of(64 * r, 64), 64)], osem.at[r]))

        @pl.when((r >= 4) & (r < 8))
        def _():
            act(pltpu.make_async_copy(src, of.at[0, :, pl.ds(pl.multiple_of(1024 * (r - 4), 1024), 1024)], osem.at[r]))

        @pl.when(r == 8)
        def _():
            act(pltpu.make_async_copy(src, oo.at[0], osem.at[r]))

        @pl.when(r > 8)
        def _():
            act(pltpu.make_async_copy(src, oq.at[0, :, pl.ds(pl.multiple_of(1024 * (11 - r), 1024), 1024)], osem.at[r]))

    def start(cp):
        cp.start()

    def add(k, i, j, other):
        WG[k, i, j, c] = (WG[k, i, j, c].astype(F32) + other.astype(F32)).astype(B16)

    def add_main(k, i, other):
        WG[k, i, y, c, :, :MAIN] = (WG[k, i, y, c, :, :MAIN].astype(F32) + other.astype(F32)).astype(B16)

    def add_strip(k, i, *others):
        total = WG[k, i, 1 - y, c, :, MAIN:].astype(F32)
        for other in others:
            total = total + other.astype(F32)
        WG[k, i, 1 - y, c, :, MAIN:] = total.astype(B16)

    def live(r):
        return (r >= 0) & (r < NP)

    def scatter_step(t):
        @pl.when(live(t))
        def _():
            across_c(t).start()

        @pl.when(live(t - 1))
        def _():
            r = t - 1
            k = held(r)
            across_c(r).wait_recv()

            @pl.loop(0, 4)
            def _(i):
                add(k, i, 1 - y, RC[r % 4, i, 1 - y])

            across_y(r).start()

            @pl.loop(0, 4)
            def _(i):
                add(k, i, y, RC[r % 4, i, y])

        @pl.when(live(t - 2))
        def _():
            r = t - 2
            k = held(r)
            across_y(r).wait_recv()

            @pl.loop(0, 4)
            def _(i):
                add_main(k, i, RY[r % 4, i])

            @pl.when(z == 0)
            def _():
                for i in (3, 2, 1):
                    up(r, i).start()
                    strip_up(r, i).start()

            @pl.when(z == 3)
            def _():
                for i in (0, 1, 2):
                    down(r, i).start()
                    strip_down(r, i).start()

        for q in (1, 2, 3):
            n = 4 - q

            @pl.when(live(t - 2 - q))
            def _():
                r = t - 2 - q
                k = held(r)

                @pl.when(z == q)
                def _():
                    for i in range(3, q - 1, -1):
                        up(r, i).wait_recv()
                        if i > q:
                            add(k, i, y, RU[r % 7, i - 1])
                            up(r, i).start()
                        strip_up(r, i).wait_recv()
                        if i > q:
                            add_strip(k, i, RUS[r % 7, i - 1])
                            strip_up(r, i).start()

                @pl.when(z == 3 - q)
                def _():
                    for i in range(n):
                        down(r, i).wait_recv()
                        if i < n - 1:
                            add(k, i, y, RD[r % 7, i])
                            down(r, i).start()
                        strip_down(r, i).wait_recv()
                        if i < n - 1:
                            add_strip(k, i, RDS[r % 7, i])
                            strip_down(r, i).start()

        @pl.when(live(t - 5))
        def _():
            r = t - 5
            k = held(r)

            @pl.when(z > 0)
            def _():
                add_strip(k, z, RUS[r % 7, z - 1])

            @pl.when(z < 3)
            def _():
                add_strip(k, z, RDS[r % 7, z])

            strip_y(r).start()

            @pl.when(r >= 2)
            def _():
                each_out(r - 2, lambda cp: cp.wait())

            T[r % 2] = WG[k, z, y, c].astype(F32)

            @pl.when(z > 0)
            def _():
                T[r % 2] += RU[r % 7, z - 1].astype(F32)

            @pl.when(z < 3)
            def _():
                T[r % 2] += RD[r % 7, z].astype(F32)

        @pl.when(live(t - 6))
        def _():
            r = t - 6
            strip_y(r).wait_recv()
            T[r % 2, :, MAIN:] += RYS[r % 4].astype(F32)
            each_out(r, start)

    ffn_in(0)
    greeted()

    @pl.loop(1, BACK_TICKS)
    def _(tick):
        turn = tick // SPLIT

        @pl.when(tick == 2 * (1 - s) + SPLIT * s)
        def _():
            ffn_in(1)

        def when(i, at0, at1, body):
            early = (1 - s) * at0 + s * i
            late = (1 - s) * at1 + s * (SPLIT + i)

            @pl.when((tick == early) | (tick == late))
            def _():
                body((tick == late).astype(jnp.int32))

        when(1, 3, 4, ffn_norm)
        when(2, 5, 7, attn_out)
        first = (tick - 3) % SPLIT * s + (tick - 5) % 2 * (1 - s)

        @pl.when(((s == 0) & (tick >= 5) & (tick < 9)) | ((s == 1) & (tick < 2 * SPLIT) & (first < 2)))
        def _():
            attn_back(first, (1 - s) * ((tick - 5) // 2) + s * turn)

        when(5, 9, 10, attn_norm)
        r = tick - 1 - (2 * SPLIT - 1) * s

        for j in range(4):
            pl.when(r == j)(lambda j=j: grad_proj(j))

        @pl.when((r >= 4) & (r < 8))
        def _():
            grad_fc(r - 4)

        @pl.when(r == 8)
        def _():
            grad_out()

        @pl.when((r > 8) & (r < 12))
        def _():
            grad_qkv(11 - r)

        scatter_step(r)
        for at, body in ((9, small_first), (11, small_second), (13, small_third), (17, small_last)):
            pl.when(r == at)(body)

    @pl.loop(0, NP)
    def _(r):
        @pl.when(r >= NP - 2)
        def _():
            each_out(r, lambda cp: cp.wait())

        across_c(r).wait_send()
        across_y(r).wait_send()
        strip_y(r).wait_send()
        for q in range(3):

            @pl.when(z == q)
            def _():
                for i in range(q + 1, 4):
                    up(r, i).wait_send()
                    strip_up(r, i).wait_send()

            @pl.when(z == q + 1)
            def _():
                for i in range(q + 1):
                    down(r, i).wait_send()
                    strip_down(r, i).wait_send()

    sums_out()
    pref_out()

    @pl.loop(0, 2)
    def _(b):
        dh_out(b).wait()

        @pl.when(s == 1)
        def _():
            cross(b).wait_send()


def backward_call(kept, cot, r_out, small, pkey, pval):
    W, h, a1, qkv, prob, ppre, att, res, a2, gp, act = kept
    any_, vm = pl.BlockSpec(memory_space=pl.ANY), pl.BlockSpec(memory_space=pltpu.VMEM)
    n, d = h.shape
    dma = pltpu.SemaphoreType.DMA
    wide = (4, 2, 2, 64, d)
    outs = [
        ((n, d), B16), ((1, 64, 3 * d), F32), ((1, 64, d), F32), ((1, 64, 4 * d), F32), ((1, 256, d), F32),
        ((16, 128), F32), ((16, 2 * d), B16), ((16, 512), F32),
    ]
    scratch = [
        ((NP,) + wide, B16), ((n, d), B16), ((n, d), B16), ((3, n, d), B16), ((4, n, d), B16), ((2, HALF, HALF), B16), ((n, d), B16),
        ((n, d), F32), ((n, d), B16), ((4, n, d), B16), ((n, d), B16), ((n, d), B16), ((HALF, d), B16), ((HALF, HALF), F32),
        ((HALF, HALF), B16), ((HALF, d), F32),
        ((4, 4, 2, 64, d), B16), ((4, 4, 64, MAIN), B16), ((7, 3, 64, d), B16), ((7, 3, 64, d), B16),
        ((7, 3, 64, d - MAIN), B16), ((7, 3, 64, d - MAIN), B16), ((4, 64, d - MAIN), B16), ((2, 64, d), F32),
        ((16, d), F32), ((32, d), F32), ((16, 32, 128), F32), ((16, 32, 128), F32), ((16, 128), B16), ((16, 16, 128), B16),
        ((16, 512), F32), ((16, 512), F32),
    ]
    return pl.pallas_call(
        backward_kernel,
        out_shape=[jax.ShapeDtypeStruct(*o) for o in outs],
        in_specs=[any_] * 13 + [vm] * 3,
        out_specs=[any_] * 5 + [vm] * 3,
        scratch_shapes=[pltpu.VMEM(*v) for v in scratch] + [dma((NP,))] * 7 + [dma((NP, 6))] * 4 + [dma((NP,))] * 2 + [dma((2,))] * 3 + [dma((16,))] * 4 + [dma((4,))] * 2,
        compiler_params=pltpu.CompilerParams(collective_id=1, has_side_effects=True, vmem_limit_bytes=64 << 20),
    )(W.reshape((NP,) + wide), h, a1, qkv, prob, ppre, att, res, a2, gp, act, cot, r_out, small, pkey, pval)


def finish_kernel(
    o0, o1, o2, o3, o4, o5, hid, kvb, hsum, aux, r_in, sums,
    c0, c1, c2, c3, c4, c5, g_embed, g_in, g_in_bias, g_out, g_out_bias, g_gains, g_bias,
    G_IN, G_OUT, M0, M1, M2, M3, M4, M5, sem,
):
    held = (M0, M1, M2, M3, M4, M5)
    here = [pltpu.make_async_copy(a, m, sem.at[i]) for i, (a, m) in enumerate(zip((o0, o1, o2, o3, o4, o5), held))]
    away = [pltpu.make_async_copy(m, c, sem.at[8 + i]) for i, (m, c) in enumerate(zip(held, (c0, c1, c2, c3, c4, c5)))]
    for cp in here:
        cp.start()
    h = hid[...]
    kv = kvb[...]
    G_OUT[...] = dot_tn(h.astype(B16), kv)
    out_cp = pltpu.make_async_copy(G_OUT, g_out, sem.at[6])
    out_cp.start()
    g_out_bias[...] = column_sum(kv)
    for cp, out in zip(here, away):
        cp.wait()
        out.start()
    dp = (hsum[...] * (1.0 - h * h)).astype(B16)
    G_IN[...] = dot_tn(aux[...], dp)
    in_cp = pltpu.make_async_copy(G_IN, g_in, sem.at[7])
    in_cp.start()
    g_in_bias[...] = column_sum(dp)
    g_embed[...] = dot_nt(dp, r_in[...])[:10]
    g_gains[0] = sums[11:13, :64]
    for i in range(11):
        g_bias[:, 64 * i : 64 * i + 64] = sums[i : i + 1, :64]
    for cp in away + [out_cp, in_cp]:
        cp.wait()


def finish_call(large, hid, kvb, hsum, aux, r_in, sums):
    any_, vm = pl.BlockSpec(memory_space=pl.ANY), pl.BlockSpec(memory_space=pltpu.VMEM)
    d = r_in.shape[0]
    outs = [jax.ShapeDtypeStruct(x.shape, x.dtype) for x in large]
    outs += [jax.ShapeDtypeStruct(x, F32) for x in ((10, d), (d, 512), (1, 512), (512, 2 * d), (1, 2 * d), (1, 2, 64), (1, 704))]
    return pl.pallas_call(
        finish_kernel,
        out_shape=outs,
        in_specs=[any_] * 6 + [vm] * 6,
        out_specs=[any_] * 6 + [vm, any_, vm, any_, vm, vm, vm],
        scratch_shapes=[pltpu.VMEM((d, 512), F32), pltpu.VMEM((512, 2 * d), F32)]
        + [pltpu.VMEM(x.shape, x.dtype) for x in large]
        + [pltpu.SemaphoreType.DMA((14,))],
        compiler_params=pltpu.CompilerParams(vmem_limit_bytes=63 << 20),
    )(*large, hid, kvb, hsum, aux, r_in, sums)


def on_device(
    tokens,
    segment_ids,
    cotangent,
    w_qkv,
    w_attn_out,
    w_fc,
    w_proj,
    gains,
    biases,
    prefix_embed,
    reparam_in,
    reparam_in_bias,
    reparam_out,
    reparam_out_bias,
):
    aux = prefix_rows(prefix_embed, reparam_in_bias, reparam_out_bias)
    kept = forward_call(w_qkv, w_attn_out, w_fc, w_proj, tokens, segment_ids, gains, biases, aux, reparam_in, reparam_out)
    small, pkey, pval, hid = kept[12:]
    *large, sums, kvb, hsum = backward_call(kept[:1] + kept[2:12], cotangent, reparam_out, small, pkey, pval)
    done = finish_call([kept[1]] + large, hid, kvb, hsum, aux, reparam_in, sums)
    return (
        done[0][None],
        done[1][None],
        *done[2:6],
        done[11],
        done[12],
        done[6],
        done[7],
        done[8][0],
        done[9],
        done[10][0],
    )


def passed_along(shard, axis, by):
    size = lax.axis_size(axis)
    pairs = [(i, i + by) for i in range(size) if 0 <= i + by < size]
    return lax.ppermute(shard, axis, pairs)


def norm_rows(v, gain, shift):
    mean = jnp.mean(v, axis=-1, keepdims=True)
    cent = v - mean
    var = jnp.mean(cent * cent, axis=-1, keepdims=True)
    return cent * lax.rsqrt(var + EPS) * gain + shift


def gelu_tanh(v):
    return jax.nn.gelu(v, approximate=True)


def forward_layer(h_b, segs, pkey, pval, params):
    w_q, w_o, w_f, w_p, gain_pair, bias_all = params
    width = w_o.shape[0]
    length = h_b.shape[0]
    heads, head_dim = (pkey.shape[1], pkey.shape[2])
    scale = 1.0 / math.sqrt(head_dim)
    gain_f = gain_pair.astype(jnp.float32)
    bias_f = bias_all.astype(jnp.float32)
    hf = h_b.astype(jnp.float32)
    a1b = norm_rows(hf, gain_f[0], bias_f[9 * width : 10 * width]).astype(jnp.bfloat16)
    qkv_b = (jnp.dot(a1b, w_q, preferred_element_type=jnp.float32) + bias_f[: 3 * width]).astype(
        jnp.bfloat16
    )
    split = qkv_b.reshape(length, 3, heads, head_dim)
    query, keys, values = (split[:, 0], split[:, 1], split[:, 2])
    s_tok = jnp.einsum("lhe,mhe->hlm", query, keys, preferred_element_type=jnp.float32) * scale
    s_pre = jnp.einsum("lhe,phe->hlp", query, pkey, preferred_element_type=jnp.float32) * scale
    place = jnp.arange(length)
    allowed = (segs[:, None] == segs[None, :]) & (place[None, :] <= place[:, None])
    s_tok = jnp.where(allowed[None], s_tok, NEG)
    top = jnp.maximum(
        jnp.max(s_tok, axis=-1, keepdims=True), jnp.max(s_pre, axis=-1, keepdims=True)
    )
    e_tok = jnp.exp(s_tok - top)
    e_pre = jnp.exp(s_pre - top)
    total = jnp.sum(e_tok, axis=-1, keepdims=True) + jnp.sum(e_pre, axis=-1, keepdims=True)
    p_tok = e_tok / total
    p_pre = e_pre / total
    mixed = jnp.einsum(
        "hlm,mhe->lhe", p_tok.astype(jnp.bfloat16), values, preferred_element_type=jnp.float32
    ) + jnp.einsum(
        "hlp,phe->lhe", p_pre.astype(jnp.bfloat16), pval, preferred_element_type=jnp.float32
    )
    attn_b = mixed.reshape(length, width).astype(jnp.bfloat16)
    resid = hf + (
        jnp.dot(attn_b, w_o, preferred_element_type=jnp.float32) + bias_f[3 * width : 4 * width]
    )
    a2b = norm_rows(resid, gain_f[1], bias_f[10 * width : 11 * width]).astype(jnp.bfloat16)
    pre_act = jnp.dot(a2b, w_f, preferred_element_type=jnp.float32) + bias_f[4 * width : 8 * width]
    act_b = gelu_tanh(pre_act).astype(jnp.bfloat16)
    result = resid + (
        jnp.dot(act_b, w_p, preferred_element_type=jnp.float32) + bias_f[8 * width : 9 * width]
    )
    return (result, (hf, a1b, qkv_b, p_tok, p_pre, attn_b, resid, a2b, pre_act, act_b))


def backward_ffn(grad_out, keep, params):
    w_q, w_o, w_f, w_p, gain_pair, bias_all = params
    hf, a1b, qkv_b, p_tok, p_pre, attn_b, resid, a2b, pre_act, act_b = keep
    width = w_o.shape[0]
    gain_f = gain_pair.astype(jnp.float32)
    bias_f = bias_all.astype(jnp.float32)
    dm_b = grad_out.astype(jnp.bfloat16)
    grad_wp = jnp.einsum("lf,ld->fd", act_b, dm_b, preferred_element_type=jnp.float32)
    grad_bp = jnp.sum(dm_b.astype(jnp.float32), axis=0)
    d_act = jnp.dot(dm_b, w_p.T, preferred_element_type=jnp.float32)
    dpre_b = jax.vjp(gelu_tanh, pre_act)[1](d_act)[0].astype(jnp.bfloat16)
    grad_wf = jnp.einsum("ld,lf->df", a2b, dpre_b, preferred_element_type=jnp.float32)
    grad_bf = jnp.sum(dpre_b.astype(jnp.float32), axis=0)
    d_a2 = jnp.dot(dpre_b, w_f.T, preferred_element_type=jnp.float32)
    norm_back = jax.vjp(norm_rows, resid, gain_f[1], bias_f[10 * width : 11 * width])[1]
    d_resid_norm, grad_g2, grad_c2 = norm_back(d_a2)
    d_resid = grad_out + d_resid_norm
    return (d_resid, (grad_wf, grad_wp), (grad_bf, grad_bp, grad_g2, grad_c2))


def backward_attn(d_resid, keep, pkey, pval, params):
    w_q, w_o, w_f, w_p, gain_pair, bias_all = params
    hf, a1b, qkv_b, p_tok, p_pre, attn_b, resid, a2b, pre_act, act_b = keep
    width = w_o.shape[0]
    length = hf.shape[0]
    heads, head_dim = (pkey.shape[1], pkey.shape[2])
    prefix_len = pkey.shape[0]
    scale = 1.0 / math.sqrt(head_dim)
    gain_f = gain_pair.astype(jnp.float32)
    bias_f = bias_all.astype(jnp.float32)
    split = qkv_b.reshape(length, 3, heads, head_dim)
    query, keys, values = (split[:, 0], split[:, 1], split[:, 2])
    dat_b = d_resid.astype(jnp.bfloat16)
    grad_wo = jnp.einsum("ld,le->de", attn_b, dat_b, preferred_element_type=jnp.float32)
    grad_bo = jnp.sum(dat_b.astype(jnp.float32), axis=0)
    dattn_b = jnp.dot(dat_b, w_o.T, preferred_element_type=jnp.float32).astype(jnp.bfloat16)
    dattn_b = dattn_b.reshape(length, heads, head_dim)
    dp_tok = jnp.einsum("lhe,mhe->hlm", dattn_b, values, preferred_element_type=jnp.float32)
    dp_pre = jnp.einsum("lhe,phe->hlp", dattn_b, pval, preferred_element_type=jnp.float32)
    row_dot = jnp.sum(p_tok * dp_tok, axis=-1, keepdims=True) + jnp.sum(
        p_pre * dp_pre, axis=-1, keepdims=True
    )
    ds_tok = (p_tok * (dp_tok - row_dot)).astype(jnp.bfloat16)
    ds_pre = (p_pre * (dp_pre - row_dot)).astype(jnp.bfloat16)
    d_query = (
        jnp.einsum("hlm,mhe->lhe", ds_tok, keys, preferred_element_type=jnp.float32)
        + jnp.einsum("hlp,phe->lhe", ds_pre, pkey, preferred_element_type=jnp.float32)
    ) * scale
    d_keys = jnp.einsum("hlm,lhe->mhe", ds_tok, query, preferred_element_type=jnp.float32) * scale
    d_values = jnp.einsum(
        "hlm,lhe->mhe", p_tok.astype(jnp.bfloat16), dattn_b, preferred_element_type=jnp.float32
    )
    grad_pkey = (
        jnp.einsum("hlp,lhe->phe", ds_pre, query, preferred_element_type=jnp.float32) * scale
    )
    grad_pval = jnp.einsum(
        "hlp,lhe->phe", p_pre.astype(jnp.bfloat16), dattn_b, preferred_element_type=jnp.float32
    )
    dqkv_b = (
        jnp.stack([d_query, d_keys, d_values], axis=1)
        .reshape(length, 3 * width)
        .astype(jnp.bfloat16)
    )
    grad_wq = jnp.einsum("ld,lc->dc", a1b, dqkv_b, preferred_element_type=jnp.float32)
    grad_bq = jnp.sum(dqkv_b.astype(jnp.float32), axis=0)
    d_a1 = jnp.dot(dqkv_b, w_q.T, preferred_element_type=jnp.float32)
    norm_back_first = jax.vjp(norm_rows, hf, gain_f[0], bias_f[9 * width : 10 * width])[1]
    d_in_norm, grad_g1, grad_c1 = norm_back_first(d_a1)
    d_input = d_resid + d_in_norm
    grad_prefix = jnp.concatenate(
        [grad_pkey.reshape(prefix_len, width), grad_pval.reshape(prefix_len, width)], axis=1
    )
    return (d_input, (grad_wq, grad_wo), (grad_bq, grad_bo, grad_g1, grad_c1), grad_prefix)


def assemble(ffn_mats, ffn_small, attn_mats, attn_small):
    grad_bf, grad_bp, grad_g2, grad_c2 = ffn_small
    grad_bq, grad_bo, grad_g1, grad_c1 = attn_small
    grad_gains = jnp.stack([grad_g1, grad_g2])
    grad_bias = jnp.concatenate([grad_bq, grad_bo, grad_bf, grad_bp, grad_c1, grad_c2])
    return (attn_mats[0], attn_mats[1], ffn_mats[0], ffn_mats[1], grad_gains, grad_bias)


def on_device_general(
    tokens,
    segment_ids,
    cotangent,
    w_qkv,
    w_attn_out,
    w_fc,
    w_proj,
    gains,
    biases,
    prefix_embed,
    reparam_in,
    reparam_in_bias,
    reparam_out,
    reparam_out_bias,
):
    section = lax.axis_index("section")
    micro, row_len = segment_ids.shape
    width = tokens.shape[1]
    prefix_len = prefix_embed.shape[0]
    head_dim = width // HEADS
    gathered = (
        lax.all_gather(w_qkv, "dp", axis=1, tiled=True),
        lax.all_gather(w_attn_out, "dp", axis=1, tiled=True),
        lax.all_gather(w_fc, "dp", axis=1, tiled=True),
        lax.all_gather(w_proj, "dp", axis=1, tiled=True),
        lax.all_gather(gains, "dp", axis=2, tiled=True),
        lax.all_gather(biases, "dp", axis=1, tiled=True),
    )
    params = tuple((item[0] for item in gathered))
    pre_hidden = jnp.dot(
        prefix_embed, reparam_in, preferred_element_type=jnp.float32
    ) + reparam_in_bias.astype(jnp.float32)
    hidden = jnp.tanh(pre_hidden)
    hidden_b = hidden.astype(jnp.bfloat16)
    prefix_kv = (
        jnp.dot(hidden_b, reparam_out, preferred_element_type=jnp.float32)
        + reparam_out_bias.astype(jnp.float32)
    ).astype(jnp.bfloat16)
    pkey = prefix_kv[:, :width].reshape(prefix_len, HEADS, head_dim)
    pval = prefix_kv[:, width:].reshape(prefix_len, HEADS, head_dim)
    token_rows = tokens.reshape(micro, row_len, width)
    cot_rows = cotangent.reshape(micro, row_len, width)
    received = jnp.zeros((row_len, width), jnp.bfloat16)
    outputs = jnp.zeros((micro, row_len, width), jnp.bfloat16)
    stored = []
    for tick in range(micro + 1):
        index = tick - section
        active = (index >= 0) & (index < micro)
        slot = jnp.clip(index, 0, micro - 1)
        segs = segment_ids[slot]
        h_b = jnp.where(section == 0, token_rows[slot], received)
        result, keep = forward_layer(h_b, segs, pkey, pval, params)
        result_b = result.astype(jnp.bfloat16)
        outputs = jnp.where(active, outputs.at[slot].set(result_b), outputs)
        stored.append(keep)
        if tick < micro:
            received = passed_along(result_b, "section", 1)
    regathered = (
        lax.all_gather(w_qkv, "dp", axis=1, tiled=True),
        lax.all_gather(w_attn_out, "dp", axis=1, tiled=True),
        lax.all_gather(w_fc, "dp", axis=1, tiled=True),
        lax.all_gather(w_proj, "dp", axis=1, tiled=True),
        lax.all_gather(gains, "dp", axis=2, tiled=True),
        lax.all_gather(biases, "dp", axis=1, tiled=True),
    )
    params_back = tuple((item[0] for item in regathered))
    stacked = jax.tree.map(lambda *items: jnp.stack(items), *stored)
    coming = jnp.zeros((row_len, width), jnp.bfloat16)
    in_grads = jnp.zeros((micro, row_len, width), jnp.bfloat16)
    grad_total = None
    prefix_total = None
    for tick in range(micro + 1):
        index = micro - tick - section
        active = (index >= 0) & (index < micro)
        slot = jnp.clip(index, 0, micro - 1)
        segs = segment_ids[slot]
        saved = jax.tree.map(lambda item: item[slot + section], stacked)
        grad_out = jnp.where(
            section == 1, cot_rows[slot].astype(jnp.float32), coming.astype(jnp.float32)
        )
        keep = saved
        d_resid, ffn_mats, ffn_small = backward_ffn(grad_out, keep, params_back)
        ffn_mats = jax.tree.map(
            lambda item: jnp.where(active, item, jnp.zeros_like(item)), ffn_mats
        )
        ffn_small = jax.tree.map(
            lambda item: jnp.where(active, item, jnp.zeros_like(item)), ffn_small
        )
        d_input, attn_mats, attn_small, grad_prefix = backward_attn(
            d_resid, keep, pkey, pval, params_back
        )
        attn_mats = jax.tree.map(
            lambda item: jnp.where(active, item, jnp.zeros_like(item)), attn_mats
        )
        attn_small = jax.tree.map(
            lambda item: jnp.where(active, item, jnp.zeros_like(item)), attn_small
        )
        grad_prefix = jnp.where(active, grad_prefix, jnp.zeros_like(grad_prefix))
        grads = assemble(ffn_mats, ffn_small, attn_mats, attn_small)
        if grad_total is None:
            grad_total = grads
            prefix_total = grad_prefix
        else:
            grad_total = jax.tree.map(lambda left, right: left + right, grad_total, grads)
            prefix_total = prefix_total + grad_prefix
        d_input_b = d_input.astype(jnp.bfloat16)
        in_grads = jnp.where(active, in_grads.at[slot].set(d_input_b), in_grads)
        if tick < micro:
            coming = passed_along(d_input_b, "section", -1)
    lifted = tuple((item[None] for item in grad_total))
    weight_grads = (
        lax.psum_scatter(lifted[0], "dp", scatter_dimension=1, tiled=True),
        lax.psum_scatter(lifted[1], "dp", scatter_dimension=1, tiled=True),
        lax.psum_scatter(lifted[2], "dp", scatter_dimension=1, tiled=True),
        lax.psum_scatter(lifted[3], "dp", scatter_dimension=1, tiled=True),
        lax.psum_scatter(lifted[4], "dp", scatter_dimension=2, tiled=True),
        lax.psum_scatter(lifted[5], "dp", scatter_dimension=1, tiled=True),
    )
    prefix_grad = lax.psum(prefix_total, "dp")
    prefix_grad_b = prefix_grad.astype(jnp.bfloat16)
    grad_reparam_out = jnp.einsum(
        "pr,pc->rc", hidden_b, prefix_grad_b, preferred_element_type=jnp.float32
    )
    grad_reparam_out_bias = jnp.sum(prefix_grad_b.astype(jnp.float32), axis=0)
    hidden_part = jnp.dot(prefix_grad_b, reparam_out.T, preferred_element_type=jnp.float32)
    hidden_grad = lax.psum(hidden_part, "section")
    dpre_hidden_b = (hidden_grad * (1.0 - hidden * hidden)).astype(jnp.bfloat16)
    grad_reparam_in = jnp.einsum(
        "pd,pr->dr", prefix_embed, dpre_hidden_b, preferred_element_type=jnp.float32
    )
    grad_reparam_in_bias = jnp.sum(dpre_hidden_b.astype(jnp.float32), axis=0)
    grad_prefix_embed = jnp.dot(dpre_hidden_b, reparam_in.T, preferred_element_type=jnp.float32)
    layer_outs = outputs.reshape(1, micro * row_len, width)
    input_grads = in_grads.reshape(1, micro * row_len, width)
    return (
        layer_outs,
        input_grads,
        weight_grads[0],
        weight_grads[1],
        weight_grads[2],
        weight_grads[3],
        weight_grads[4],
        weight_grads[5],
        grad_prefix_embed,
        grad_reparam_in,
        grad_reparam_in_bias,
        grad_reparam_out,
        grad_reparam_out_bias,
    )


def solution(mesh):
    return jax.shard_map(
        on_device if mesh.shape["dp"] == 16 else on_device_general,
        mesh=mesh,
        in_specs=(
            P("dp", None),
            P("dp", None),
            P("dp", None),
            P("section", "dp", None),
            P("section", "dp", None),
            P("section", "dp", None),
            P("section", "dp", None),
            P("section", None, "dp"),
            P("section", "dp"),
            P(),
            P(),
            P(),
            P(None, "section"),
            P("section"),
        ),
        out_specs=(
            P("section", "dp", None),
            P("section", "dp", None),
            P("section", "dp", None),
            P("section", "dp", None),
            P("section", "dp", None),
            P("section", "dp", None),
            P("section", None, "dp"),
            P("section", "dp"),
            P(),
            P(),
            P(),
            P(None, "section"),
            P("section"),
        ),
        check_vma=False,
    )
```

```python
import math

import jax
import jax.numpy as jnp
from jax import lax
from jax.experimental import pallas as pl
from jax.experimental.pallas import tpu as pltpu
from jax.sharding import PartitionSpec as P

HEADS = 16
EPS = 1e-05
NEG = -1000000000.0
MESH = pl.DeviceIdType.MESH
F32 = jnp.float32
B16 = jnp.bfloat16
NP = 12
MAIN = 896
AHEAD = 1


def place():
    s = lax.axis_index("section"); d = lax.axis_index("dp")
    return s, d, d // 4, (d // 2) % 2, d % 2

def greet(s, d):
    bar = pltpu.get_barrier_semaphore()
    for i in range(1, 16):
        pl.semaphore_signal(bar, 1, device_id=(s, (d + i) % 16), device_id_type=MESH)
    pl.semaphore_signal(bar, 1, device_id=(1 - s, d), device_id_type=MESH)


def greeted():
    pl.semaphore_wait(pltpu.get_barrier_semaphore(), 16)


def to_all(src, dst, ss, rs):
    s, d = lax.axis_index("section"), lax.axis_index("dp")

    def cp(i, frm):
        to = (d + i) % 16
        return pltpu.make_async_remote_copy(
            src(to), dst.at[frm], ss.at[i], rs.at[i], device_id=(s, to), device_id_type=MESH
        )

    def start():
        for i in range(1, 16):
            cp(i, d).start()

    def arrive():
        for i in range(1, 16):
            cp(i, (d + 16 - i) % 16).wait_recv()

    def finish():
        for i in range(1, 16):
            cp(i, d).wait_send()

    return start, arrive, finish


class Gather:
    def __init__(self, W, ssem, rsem, tsem, qsem):
        self.W, self.ssem, self.rsem, self.tsem, self.qsem = W, ssem, rsem, tsem, qsem
        self.s, self.d, self.z, self.y, self.c = place()
    def blk(self, k, d):
        i = k // 8
        row = (1-i)*(1024*k+64*d) + i*(8192+256*d+64*(k-8))
        return self.W.at[pl.ds(pl.multiple_of(row, 64), 64)]
    def cp(self, k, origin, target, slot, width=1024):
        b = self.blk(k, origin)
        if width < 1024: b = b.at[:, pl.ds(0, width)]
        return pltpu.make_async_remote_copy(src_ref=b, dst_ref=b, send_sem=self.ssem.at[k, slot], recv_sem=self.rsem.at[k, origin],
            device_id=(self.s, target), device_id_type=MESH)
    def dev(self, z, y, c): return z*4+y*2+c
    def arrived(self, k, origin): self.cp(k, origin, origin, 0).wait_recv()
    def to_up(self, k, zo, op):
        op(self.cp(k, self.dev(zo, self.y, self.c), self.dev(self.z+1, self.y, self.c), zo))
    def to_down(self, k, zo, op):
        op(self.cp(k, self.dev(zo, self.y, self.c), self.dev(self.z-1, self.y, self.c), 4+zo))
    def to_y(self, k, zo, op, width=MAIN):
        op(self.cp(k, self.dev(zo, self.y, self.c), self.dev(self.z, 1-self.y, self.c), 8+zo, width))
    def strip(self, k, zo, to, slot):
        b = self.blk(k, self.dev(zo, 1-self.y, self.c)).at[:, pl.ds(MAIN, 1024-MAIN)]
        return pltpu.make_async_remote_copy(src_ref=b, dst_ref=b, send_sem=self.tsem.at[k, slot], recv_sem=self.qsem.at[k, zo],
            device_id=(self.s, self.dev(to, self.y, self.c)), device_id_type=MESH)
    def strip_up(self, k, zo, op): op(self.strip(k, zo, self.z+1, zo))
    def strip_down(self, k, zo, op): op(self.strip(k, zo, self.z-1, 4+zo))
    def to_c(self, k, zo, yo, op):
        op(self.cp(k, self.dev(zo, yo, self.c), self.dev(self.z, self.y, 1-self.c), 12+zo*2+yo))
    def step(self, t, own):
        z, y, c = self.z, self.y, self.c
        start = lambda cp: cp.start()
        def fresh(k):
            own(k)
            self.to_y(k, z, start, 1024)
            @pl.when(z < 3)
            def _(): self.to_up(k, z, start)
            @pl.when(z > 0)
            def _(): self.to_down(k, z, start)
            self.to_c(k, z, y, start)
        @pl.when(t == 0)
        def _():
            for k in range(AHEAD): fresh(k)
        @pl.when(t + AHEAD < NP)
        def _(): fresh(t + AHEAD)
        for q in (1, 2, 3, 4):
            k = t - q
            ok = (k >= 0) & (k < NP)
            if q < 4:
                @pl.when(ok & (z - q >= 0))
                def _():
                    self.arrived(k, self.dev(z-q, y, c))
                    @pl.when(z < 3)
                    def _(): self.to_up(k, z-q, start)
                    self.to_y(k, z-q, start)
                    self.to_c(k, z-q, y, start)
                @pl.when(ok & (z + q <= 3))
                def _():
                    self.arrived(k, self.dev(z+q, y, c))
                    @pl.when(z > 0)
                    def _(): self.to_down(k, z+q, start)
                    self.to_y(k, z+q, start)
                    self.to_c(k, z+q, y, start)
            e = q - 1
            def side(zo):
                o = self.dev(zo, 1-y, c)
                self.cp(k, o, o, 0, MAIN).wait_recv()
                self.to_c(k, zo, 1-y, start)
            if e == 0:
                @pl.when(ok)
                def _():
                    self.arrived(k, self.dev(z, 1-y, c))
                    @pl.when(z < 3)
                    def _(): self.strip_up(k, z, start)
                    @pl.when(z > 0)
                    def _(): self.strip_down(k, z, start)
                    self.to_c(k, z, 1-y, start)
            else:
                @pl.when(ok & (z - e >= 0))
                def _():
                    self.strip(k, z-e, z, 0).wait_recv()
                    @pl.when(z < 3)
                    def _(): self.strip_up(k, z-e, start)
                    side(z-e)
                @pl.when(ok & (z + e <= 3))
                def _():
                    self.strip(k, z+e, z, 0).wait_recv()
                    @pl.when(z > 0)
                    def _(): self.strip_down(k, z+e, start)
                    side(z+e)
    def complete(self, k):
        for i in range(8):
            self.arrived(k, 2*i + 1-self.c)
    def drain(self):
        fin = lambda cp: cp.wait_send()
        z, y = self.z, self.y
        @pl.loop(0, NP)
        def _(k):
            for zo in range(4):
                @pl.when((zo <= z) & (z < 3))
                def _(): self.to_up(k, zo, fin)
                @pl.when((zo >= z) & (z > 0))
                def _(): self.to_down(k, zo, fin)
                @pl.when(zo == z)
                def _(): self.to_y(k, zo, fin, 1024)
                @pl.when(zo != z)
                def _(): self.to_y(k, zo, fin)
                @pl.when((zo <= z) & (z < 3))
                def _(): self.strip_up(k, zo, fin)
                @pl.when((zo >= z) & (z > 0))
                def _(): self.strip_down(k, zo, fin)
                for yo in range(2): self.to_c(k, zo, yo, fin)

def own_copies(wq, wo, wf, wp, g, sem):
    out = []
    for k in range(NP):
        if k < 3: src = wq.at[0, :, pl.ds(1024*k, 1024)]
        elif k == 3: src = wo.at[0]
        elif k < 8: src = wf.at[0, :, pl.ds(1024*(k-4), 1024)]
        else: src = wp.at[0, pl.ds(64*(k-8), 64)]
        out.append(pltpu.make_async_copy(src, g.blk(jnp.int32(k), g.d), sem.at[k]))
    return out


HALF = 256
STAGES = 12
GELU_C = math.sqrt(2.0 / math.pi)


def dot_nn(a, b):
    return lax.dot_general(a, b, (((1,), (0,)), ((), ())), preferred_element_type=F32)


def dot_nt(a, b):
    return lax.dot_general(a, b, (((1,), (1,)), ((), ())), preferred_element_type=F32)


def dot_tn(a, b):
    return lax.dot_general(a, b, (((0,), (0,)), ((), ())), preferred_element_type=F32)


def whiten(v):
    mean = jnp.mean(v, axis=-1, keepdims=True)
    cent = v - mean
    rstd = lax.rsqrt(jnp.mean(cent * cent, axis=-1, keepdims=True) + EPS)
    return cent * rstd, rstd


def split_heads(pair):
    left = lax.broadcasted_iota(jnp.int32, pair.shape, 1) < 64
    zero = jnp.zeros_like(pair)
    return jnp.concatenate([jnp.where(left, pair, zero), jnp.where(left, zero, pair)], axis=0)


def forward_kernel(
    wq, wo, wf, wp, tokens, segs, gains, biases, aux, r_in, r_out,
    W_o, out_o, h_o, a1_o, qkv_o, prob_o, ppre_o, att_o, res_o, a2_o, gp_o, act_o, small_o, pkey_o, pval_o, hid_o,
    W, H, A1, QKV, PROB, PPRE, ATT, RES, A2, GP, ACT, OUT, SPRE, ACC, small, pkey, pval, hid, mask, pack, PACKS, ROWS,
    own_sem, ssem, rsem, tsem, qsem, hsem, xs, xr, save_sem, fs, ps, pr, psem,
):
    g = Gather(W, ssem, rsem, tsem, qsem)
    s = g.s
    for cp in own_copies(wq, wo, wf, wp, g, own_sem):
        cp.start()
    r_in_parts = [pltpu.make_async_copy(r_in.at[pl.ds(512 * i, 512)], ACT.at[2, :, pl.ds(512 * i, 512)], psem.at[i]) for i in range(2)]
    r_out_parts = [pltpu.make_async_copy(r_out.at[:, pl.ds(1024 * i, 1024)], ACT.at[i], psem.at[2 + i]) for i in range(2)]
    for cp in r_in_parts + r_out_parts:
        cp.start()
    greet(s, g.d)
    own_bias = biases[...].astype(F32)
    for n in range(2):
        for r in range(11):
            ROWS[0, r : r + 1, 64 * n : 64 * n + 64] = own_bias[:, 64 * r : 64 * r + 64]
        ROWS[0, 11:13, 64 * n : 64 * n + 64] = gains[0].astype(F32)
    ROWS[0, 13:16] = jnp.zeros((3, 128), F32)
    pack[...] = ROWS[0].astype(B16)
    greeted()
    send_packs, packs_in, packs_out = to_all(lambda to: pack, PACKS, ps, pr)

    def prep_saves():
        pairs = [(small, small_o), (pkey, pkey_o), (pval, pval_o), (hid, hid_o)]
        return [pltpu.make_async_copy(a, b, psem.at[4 + i]) for i, (a, b) in enumerate(pairs)]

    def prepare():
        for cp in r_in_parts + r_out_parts:
            cp.wait()
        ph = dot_nn(aux[:, :512], ACT[2, :, :512]) + dot_nn(aux[:, 512:], ACT[2, :, 512:])
        hid[...] = jnp.tanh(ph + aux[10:11, :512].astype(F32))
        hb = hid[...].astype(B16)
        head = lax.broadcasted_iota(jnp.int32, (16, 1024), 1) // 64
        for i, big in enumerate((pkey, pval)):
            kv = (dot_nn(hb, ACT[i]) + aux[11 + i : 12 + i].astype(F32)).astype(B16)
            for h in range(16):
                big[16 * h : 16 * h + 16] = jnp.where(head == h, kv, jnp.zeros_like(kv))
        key = lax.broadcasted_iota(jnp.int32, (HALF, HALF), 0)
        query = lax.broadcasted_iota(jnp.int32, (HALF, HALF), 1)
        for b in range(2):
            by_query = jnp.broadcast_to(segs[b : b + 1].astype(F32), (HALF, HALF))
            ok = (by_query.T == by_query) & (key <= query)
            mask[b] = jnp.where(ok, 0.0, NEG)
        packs_in()
        ROWS[...] = PACKS[...].astype(F32)
        left = lax.broadcasted_iota(jnp.int32, (1, 128), 1) < 64
        small[...] = jnp.zeros_like(small)
        for n in range(104):
            row, at = n // 8, 128 * (n % 8)
            if row < 11:
                (d0, r0), (d1, r1) = divmod(2 * n, 11), divmod(2 * n + 1, 11)
            else:
                (d0, r0), (d1, r1) = (2 * (n % 8), row), (2 * (n % 8) + 1, row)
            small[row : row + 1, at : at + 128] = jnp.where(left, ROWS[d0, r0 : r0 + 1], ROWS[d1, r1 : r1 + 1])
        for cp in prep_saves():
            cp.start()

    send_packs()
    PACKS[g.d] = pack[...]

    def tokens_in():
        return pltpu.make_async_copy(tokens, H, hsem)

    def half(b):
        return pl.ds(pl.multiple_of(b * HALF, HALF), HALF)

    def cross(b):
        return pltpu.make_async_remote_copy(
            OUT.at[half(b)], H.at[half(b)], xs.at[b], xr.at[b], device_id=(1 - s, g.d), device_id_type=MESH
        )

    @pl.when(s == 0)
    def _():
        tokens_in().start()

    def own(t):
        b = g.blk(t, g.d)
        pltpu.make_async_copy(b, b, own_sem.at[t]).wait()

    def rows_of(k):
        return pl.ds(pl.multiple_of(k * 1024, 1024), 1024)

    def saves(b):
        r = half(b)
        pairs = [
            (H.at[r], h_o.at[r]), (A1.at[r], a1_o.at[r]), (QKV.at[:, r], qkv_o.at[:, r]), (PROB.at[pl.ds(2 * b, 2)], prob_o.at[pl.ds(2 * b, 2)]),
            (PPRE.at[b], ppre_o.at[b]), (ATT.at[r], att_o.at[r]), (RES.at[r], res_o.at[r]), (A2.at[r], a2_o.at[r]),
            (OUT.at[r], out_o.at[r]),
        ]
        return [pltpu.make_async_copy(src, dst, save_sem.at[b, i]) for i, (src, dst) in enumerate(pairs)]

    def ffn_saves(b, j):
        r = half(b)
        return [
            pltpu.make_async_copy(GP.at[j, r], gp_o.at[j, r], fs.at[b, j]),
            pltpu.make_async_copy(ACT.at[j, r], act_o.at[j, r], fs.at[b, 4 + j]),
        ]

    def piece_out(k):
        return pltpu.make_async_copy(W.at[rows_of(k)], W_o.at[rows_of(k)], save_sem.at[2, k])

    def norm_in(b):
        @pl.when(s == 0)
        def _():
            @pl.when(b == 0)
            def _():
                tokens_in().wait()

        @pl.when(s == 1)
        def _():
            cross(b).wait_recv()

        xhat, _ = whiten(H[half(b)].astype(F32))
        A1[half(b)] = (xhat * small[11:12] + small[9:10]).astype(B16)
        saves(b)[0].start()
        saves(b)[1].start()

    def project(i, b):
        v = dot_nn(A1[half(b)], W[rows_of(i)]) + small[pl.ds(i, 1)]
        v = v.astype(B16)
        QKV[i, half(b)] = v * jnp.where(i == 0, 0.125, 1.0).astype(B16)

        @pl.when(i == 2)
        def _():
            saves(b)[2].start()

    def attend(part, b):
        @pl.when(part == 0)
        def _():
            sp = dot_nt(pkey[...], QKV[0, half(b)])
            there = lax.broadcasted_iota(jnp.int32, sp.shape, 0) % 16 < 10
            SPRE[b] = jnp.where(there, sp, NEG)

        def pair(p):
            cols = pl.ds(pl.multiple_of(p * 128, 128), 128)
            q2, k2, v2 = QKV[0, half(b), cols], QKV[1, half(b), cols], QKV[2, half(b), cols]
            st = dot_nt(split_heads(k2), q2)
            probs, pres = [], []
            for e in range(2):
                sh = st[e * HALF : (e + 1) * HALF] + mask[b]
                sp = SPRE[b, pl.ds(pl.multiple_of(p * 32 + e * 16, 16), 16)]
                top = jnp.maximum(jnp.max(sh, axis=0, keepdims=True), jnp.max(sp, axis=0, keepdims=True))
                et, ep = jnp.exp(sh - top), jnp.exp(sp - top)
                inv = 1.0 / (jnp.sum(et, axis=0, keepdims=True) + jnp.sum(ep, axis=0, keepdims=True))
                probs.append((et * inv).astype(B16))
                pres.append((ep * inv).astype(B16))
            pr = jnp.concatenate(probs, axis=0)
            PROB[2 * b + p // 4, :, pl.ds(pl.multiple_of((p % 4) * HALF, HALF), HALF)] = pr
            PPRE[b, pl.ds(pl.multiple_of(p * 32, 32), 32)] = jnp.concatenate(pres, axis=0)
            ACC[half(b), cols] = dot_tn(pr, split_heads(v2))

        for p in range(4):
            pair(part * 4 + p)

        @pl.when(part == 1)
        def _():
            ATT[half(b)] = (ACC[half(b)] + dot_tn(PPRE[b], pval[...])).astype(B16)
            saves(b)[3].start()
            saves(b)[4].start()
            saves(b)[5].start()

    def mix(b):
        r = H[half(b)].astype(F32) + (dot_nn(ATT[half(b)], W[rows_of(3)]) + small[3:4])
        RES[half(b)] = r
        xhat, _ = whiten(r)
        A2[half(b)] = (xhat * small[12:13] + small[10:11]).astype(B16)
        saves(b)[6].start()
        saves(b)[7].start()

    def widen(j, b):
        x = dot_nn(A2[half(b)], W[rows_of(4 + j)]) + small[pl.ds(4 + j, 1)]
        x2 = x * x
        h = 0.5 + 0.5 * jnp.tanh(x * (GELU_C + (0.044715 * GELU_C) * x2))
        act = x * h
        ACT[j, half(b)] = act.astype(B16)
        GP[j, half(b)] = (h + act * (1.0 - h) * (2.0 * GELU_C + (6 * 0.044715 * GELU_C) * x2)).astype(B16)

        for cp in ffn_saves(b, j):
            cp.start()

    def narrow(b):
        v = RES[half(b)] + small[8:9]
        for j in range(4):
            v = v + dot_nn(ACT[j, half(b)], W[rows_of(8 + j)])
        OUT[half(b)] = v.astype(B16)

        @pl.when(s == 0)
        def _():
            cross(b).start()

        saves(b)[8].start()

    @pl.loop(0, NP + 5 + 2 * STAGES)
    def _(tick):
        @pl.when(tick < NP + 5)
        def _():
            g.step(tick, own)

            @pl.when(tick == 3)
            def _():
                prepare()

            @pl.when(tick >= 5)
            def _():
                g.complete(tick - 5)

                @pl.when(tick < 13)
                def _():
                    piece_out(tick - 5).start()

                @pl.when(tick == NP + 4)
                def _():
                    for k in range(8, NP):
                        piece_out(k).start()

        late = tick - (NP + 5)
        stage = (1 - s) * (tick - 5) + s * ((late + STAGES) % STAGES - STAGES * (late < 0).astype(jnp.int32))
        lo = s * (late // STAGES)
        hi = (1 - s) * 2 + s * (late // STAGES + 1)

        def when(i, body):
            @pl.when(stage == i)
            def _():
                pl.loop(lo, hi)(body)

        when(0, norm_in)

        @pl.when((stage >= 1) & (stage < 4))
        def _():
            pl.loop(lo, hi)(lambda b: project(stage - 1, b))

        @pl.when((stage >= 4) & (stage < 6))
        def _():
            pl.loop(lo, hi)(lambda b: attend(stage - 4, b))

        when(6, mix)

        @pl.when((stage >= 7) & (stage < 11))
        def _():
            pl.loop(lo, hi)(lambda b: widen(stage - 7, b))

        when(11, narrow)

    g.drain()
    packs_out()
    for cp in prep_saves():
        cp.wait()

    @pl.loop(0, NP)
    def _(k):
        piece_out(k).wait()

    @pl.loop(0, 2)
    def _(b):
        for cp in saves(b) + [cp for j in range(4) for cp in ffn_saves(b, j)]:
            cp.wait()

        @pl.when(s == 0)
        def _():
            cross(b).wait_send()


def forward_call(wq, wo, wf, wp, tokens, segs, gains, biases, aux, r_in, r_out):
    any_, vm = pl.BlockSpec(memory_space=pl.ANY), pl.BlockSpec(memory_space=pltpu.VMEM)
    n, d = tokens.shape
    kept = [
        ((NP * d, d), B16), ((n, d), B16), ((n, d), B16), ((n, d), B16), ((3, n, d), B16), ((4, n, d), B16),
        ((2, HALF, HALF), B16), ((n, d), B16), ((n, d), F32), ((n, d), B16), ((4, n, d), B16), ((4, n, d), B16),
    ]
    shared = [((16, d), F32), ((HALF, d), B16), ((HALF, d), B16), ((16, 512), F32)]
    dma = pltpu.SemaphoreType.DMA
    order = [0, 2, 3, 4, 5, 6, 7, 8, 9, 10, 11, 1]
    scratch = [kept[i] for i in order] + [((2, HALF, HALF), F32), ((n, d), F32)] + shared
    scratch += [((2, HALF, HALF), F32), ((16, 128), B16), ((16, 16, 128), B16), ((16, 16, 128), F32)]
    return pl.pallas_call(
        forward_kernel,
        out_shape=[jax.ShapeDtypeStruct(*k) for k in kept + shared],
        in_specs=[any_] * 5 + [vm] * 4 + [any_] * 2,
        out_specs=[any_] * len(kept + shared),
        scratch_shapes=[pltpu.VMEM(*v) for v in scratch]
        + [dma((NP,)), dma((NP, 20)), dma((NP, 16)), dma((NP, 8)), dma((NP, 4)), dma, dma((2,)), dma((2,)), dma((3, NP)), dma((2, 8)), dma((16,)), dma((16,)), dma((8,))],
        compiler_params=pltpu.CompilerParams(collective_id=0, has_side_effects=True, vmem_limit_bytes=62 << 20),
    )(wq, wo, wf, wp, tokens, segs, gains, biases, aux, r_in, r_out)


def prefix_rows(embed, in_bias, out_bias):
    in_bias = jnp.pad(in_bias, (0, 512)).reshape(1, 1024)
    return jnp.concatenate([embed, in_bias, out_bias.reshape(2, 1024), jnp.zeros((3, 1024), B16)])


SPLIT = 6
BACK_TICKS = 2 + 2 * SPLIT + NP + 6


def unwhiten(grad, xhat, rstd):
    return rstd * (
        grad
        - jnp.mean(grad, axis=-1, keepdims=True)
        - xhat * jnp.mean(grad * xhat, axis=-1, keepdims=True)
    )


def column_sum(v):
    return jnp.sum(v.astype(F32), axis=0, keepdims=True)


def backward_kernel(
    W_i, h_i, a1_i, qkv_i, prob_i, ppre_i, att_i, res_i, a2_i, gp_i, act_i, cot, r_out, small, pkey, pval,
    dh_o, oq, oo, of, op_, own_sums, KVB, HSUM,
    WG, H, A1, QKV, BIG, PPRE, ATT, RES, A2, GP, DM, DAT, DATT, DPP, DSP, ACC,
    RC, RY, RU, RD, RUS, RDS, RYS, T, SG, DKV, SB, RB, PF, PG, HP, HPR,
    wsem, lsem, osem, cs, cr, ys, yr, us, ur, ds_, dr, yss, ysr, xs, xr, hs, bs, br, ps, pr, hx, gs,
):
    s, d, z, y, c = place()

    def slot(k):
        return k + 8 * (1 - s) if k < 4 else k

    def fetch(ks):
        return [pltpu.make_async_copy(W_i.at[k], WG.at[slot(k)], wsem.at[k]) for k in ks]

    def begin(cps):
        for cp in cps:
            cp.start()

    def loads():
        pairs = [
            (a2_i, A2), (res_i, RES), (att_i, ATT), (qkv_i, QKV), (ppre_i, PPRE), (a1_i, A1), (h_i, H),
            (act_i, BIG), (prob_i, BIG), (cot, DM),
        ]
        return [pltpu.make_async_copy(a, b, lsem.at[i]) for i, (a, b) in enumerate(pairs)]

    L_A2, L_RES, L_ATT, L_QKV, L_PPRE, L_A1, L_H, L_ACT, L_PROB, L_COT = range(10)

    def begin_loads(which):
        begin([loads()[i] for i in which])

    pl.when(s == 1)(lambda: begin_loads((L_COT,)))

    def slope(j):
        return pltpu.make_async_copy(gp_i.at[j], GP.at[j], gs.at[j])

    for j in range(4):
        begin(fetch((8 + j,)) + [slope(j)])

    pl.when(s == 0)(lambda: begin_loads((L_ACT,)))
    SG[...] = jnp.zeros_like(SG)
    DKV[...] = jnp.zeros_like(DKV)
    SB[...] = jnp.zeros_like(SB)
    greet(s, d)

    def weights(ks):
        for cp in fetch(ks):
            cp.wait()

    def half(b):
        return pl.ds(pl.multiple_of(b * HALF, HALF), HALF)

    def weight(k):
        return WG[slot(k)].reshape(1024, 1024)

    def cross(b):
        return pltpu.make_async_remote_copy(
            H.at[half(b)], DM.at[half(b)], xs.at[b], xr.at[b], device_id=(1 - s, d), device_id_type=MESH
        )

    def dh_out(b):
        return pltpu.make_async_copy(H.at[half(b)], dh_o.at[half(b)], hs.at[b])

    def more(j):
        if j < 2:
            begin(fetch((4 + 2 * j, 5 + 2 * j)))
        elif j == 2:
            begin_loads((L_A2, L_RES))
            pl.when(s == 1)(lambda: begin(fetch((3,))))
        else:
            pl.when(s == 1)(lambda: begin_loads((L_QKV, L_PPRE, L_PROB)))

    def ffn_in(b):
        if b == 0:
            pl.when(s == 1)(lambda: loads()[L_COT].wait())
            pl.when(s == 0)(lambda: cross(0).wait_recv())
        for j in range(4):
            if b == 0:
                weights((8 + j,))
                slope(j).wait()
                more(j)
            GP[j, half(b)] = (dot_nt(DM[half(b)], weight(8 + j)) * GP[j, half(b)].astype(F32)).astype(B16)
        if b == 1:

            @pl.when(s == 0)
            def _():
                begin(fetch((3, 0, 1, 2)))

    def ffn_norm(b):
        @pl.when(b == 0)
        def _():
            weights((4, 5, 6, 7))
            loads()[L_A2].wait()
            loads()[L_RES].wait()
            begin_loads((L_ATT, L_A1, L_H))

            @pl.when(s == 0)
            def _():
                begin_loads((L_QKV, L_PPRE))

            @pl.when(s == 1)
            def _():
                begin(fetch((0, 1, 2)))

        grad = dot_nt(GP[0, half(b)], weight(4))
        for j in range(1, 4):
            grad = grad + dot_nt(GP[j, half(b)], weight(4 + j))
        xhat, rstd = whiten(RES[half(b)])
        SG[10:11] += jnp.sum(grad, axis=0, keepdims=True)
        SG[12:13] += jnp.sum(grad * xhat, axis=0, keepdims=True)
        res = DM[half(b)].astype(F32) + unwhiten(grad * small[12:13], xhat, rstd)
        RES[half(b)] = res
        DAT[half(b)] = res.astype(B16)

    def attn_out(b):
        @pl.when(b == 0)
        def _():
            weights((3,))
            for i in (L_ATT, L_QKV, L_PPRE):
                loads()[i].wait()

            loads()[L_PROB].wait()

        DATT[...] = dot_nt(DAT[half(b)], weight(3)).astype(B16)
        DPP[...] = dot_nt(pval[...], DATT[...])

    def attn_back(part, b):
        def pair(p):
            cols = pl.ds(pl.multiple_of(p * 128, 128), 128)
            q2, k2, v2 = QKV[0, half(b), cols], QKV[1, half(b), cols], QKV[2, half(b), cols]
            do2 = DATT[:, cols]
            pr = BIG[2 * b + p // 4, :, pl.ds(pl.multiple_of((p % 4) * HALF, HALF), HALF)]
            dp = dot_nt(split_heads(v2), do2)
            dss, pres = [], []
            for e in range(2):
                ph = pr[e * HALF : (e + 1) * HALF].astype(F32)
                dh = dp[e * HALF : (e + 1) * HALF]
                at = pl.ds(pl.multiple_of(p * 32 + e * 16, 16), 16)
                pp, dpp = PPRE[b, at].astype(F32), DPP[at]
                dot = jnp.sum(ph * dh, axis=0, keepdims=True) + jnp.sum(pp * dpp, axis=0, keepdims=True)
                dss.append((ph * (dh - dot)).astype(B16))
                pres.append((pp * (dpp - dot)).astype(B16))
            ds = jnp.concatenate(dss, axis=0)
            DSP[pl.ds(pl.multiple_of(p * 32, 32), 32)] = jnp.concatenate(pres, axis=0)
            left = lax.broadcasted_iota(jnp.int32, (HALF, 128), 1) < 64
            ACC[:, cols] = dot_tn(ds, split_heads(k2))
            dk = dot_nn(ds, q2)
            dv = dot_nn(pr, do2)
            QKV[1, half(b), cols] = jnp.where(left, dk[:HALF], dk[HALF:]).astype(B16)
            QKV[2, half(b), cols] = jnp.where(left, dv[:HALF], dv[HALF:]).astype(B16)

        for p in range(4):
            pair(part * 4 + p)

        @pl.when(part == 1)
        def _():
            def own_rows(full):
                out = jnp.zeros((16, 1024), F32)
                head = lax.broadcasted_iota(jnp.int32, (16, 1024), 1) // 64
                for i in range(16):
                    out = out + jnp.where(head == i, full[16 * i : 16 * i + 16], 0.0)
                return out

            DKV[0:16] += own_rows(dot_nn(DSP[...], QKV[0, half(b)]))
            DKV[16:32] += own_rows(dot_nn(PPRE[b], DATT[...]))
            QKV[0, half(b)] = ((ACC[...] + dot_tn(DSP[...], pkey[...])) * 0.125).astype(B16)

    def attn_norm(b):
        @pl.when(b == 0)
        def _():
            weights((0, 1, 2))
            loads()[L_A1].wait()
            loads()[L_H].wait()

        @pl.when((s == 1) & (b == 1))
        def _():
            loads()[L_ACT].start()

        grad = dot_nt(QKV[0, half(b)], weight(0))
        for i in range(1, 3):
            grad = grad + dot_nt(QKV[i, half(b)], weight(i))
        xhat, rstd = whiten(H[half(b)].astype(F32))
        SG[9:10] += jnp.sum(grad, axis=0, keepdims=True)
        SG[11:12] += jnp.sum(grad * xhat, axis=0, keepdims=True)
        H[half(b)] = (RES[half(b)] + unwhiten(grad * small[11:12], xhat, rstd)).astype(B16)

        @pl.when(s == 1)
        def _():
            cross(b).start()

        dh_out(b).start()

    def grad_proj(j):
        if j == 0:
            loads()[L_ACT].wait()
            pl.when(s == 0)(lambda: cross(1).wait_recv())
        for i in range(4):
            cols = [BIG[i, :, 256 * q + 64 * j : 256 * q + 64 * j + 64] for q in range(4)]
            part = dot_tn(jnp.concatenate(cols, axis=1), DM[...])
            WG[8 * s + j, i] = part.astype(B16).reshape(2, 2, 64, 1024)
        if j == 3:
            pl.when(s == 0)(lambda: loads()[L_PROB].start())

    def put(k, a, v):
        for i in range(2):
            part = dot_tn(a[:, 512 * i : 512 * (i + 1)], v[...])
            WG[k, 2 * i : 2 * i + 2] = part.astype(B16).reshape(2, 2, 2, 64, 1024)

    def grad_fc(j):
        put(4 + j, A2, GP.at[j])

    def grad_out():
        put(slot(3), ATT, DAT)

    def grad_qkv(i):
        put(i + 8 * (1 - s), A1, QKV.at[i])

    send_sums, sums_in, sums_out = to_all(lambda to: SB.at[to], RB, bs, br)
    send_pref, pref_in, pref_out = to_all(lambda to: PF, PG, ps, pr)

    def r_out_in():
        return [pltpu.make_async_copy(r_out.at[:, pl.ds(1024 * i, 1024)], BIG.at[i], hx.at[i]) for i in range(2)]

    def hidden_across():
        return pltpu.make_async_remote_copy(HP, HPR, hx.at[2], hx.at[3], device_id=(1 - s, d), device_id_type=MESH)

    def small_first():
        for cp in r_out_in():
            cp.start()
        for i in range(3):
            SG[i : i + 1] = column_sum(QKV[i])
        SG[3:4] = column_sum(DAT[...])
        for j in range(4):
            SG[4 + j : 5 + j] = column_sum(GP[j])
        SG[8:9] = column_sum(DM[...])
        for i in range(16):
            for n in range(13):
                m = 11 * i + n
                row, at = (m // 16, 128 * (m % 16 // 2)) if n < 11 else (n, 128 * (i // 2))
                SB[i, n : n + 1] = SG[row : row + 1, at : at + 128]
            SB[i, 16:32] = DKV[16 * (i // 8) : 16 * (i // 8) + 16, 128 * (i % 8) : 128 * (i % 8) + 128]
        send_sums()
        RB[d] = SB[d]

    def small_second():
        sums_in()
        total = RB[0]
        for i in range(1, 16):
            total = total + RB[i]
        row = lax.broadcasted_iota(jnp.int32, (16, 128), 0)
        odd = jnp.where(row < 11, d + row, d) % 2 == 1
        own_sums[...] = jnp.where(odd, pltpu.roll(total[:16], 64, 1), total[:16])
        PF[...] = total[16:].astype(B16)
        send_pref()
        PG[d] = PF[...]

    def small_third():
        pref_in()
        for i in range(16):
            KVB[:, 128 * i : 128 * i + 128] = PG[i]
        for cp in r_out_in():
            cp.wait()
        HP[...] = dot_nt(KVB[:, :1024], BIG[0]) + dot_nt(KVB[:, 1024:], BIG[1])
        hidden_across().start()

    def small_last():
        hidden_across().wait()
        HSUM[...] = HP[...] + HPR[...]

    def held(r):
        a = r // 4
        return ((2 - a) * (1 - a) // 2) * (r + 8 * s) + a * (2 - a) * r + (a * (a - 1) // 2) * (11 - r + 8 * (1 - s))

    def across_c(r):
        return pltpu.make_async_remote_copy(
            WG.at[held(r), :, :, 1 - c], RC.at[r % 4], cs.at[r], cr.at[r],
            device_id=(s, z * 4 + y * 2 + 1 - c), device_id_type=MESH,
        )

    def across_y(r):
        return pltpu.make_async_remote_copy(
            WG.at[held(r), :, 1 - y, c, :, pl.ds(0, MAIN)], RY.at[r % 4], ys.at[r], yr.at[r],
            device_id=(s, z * 4 + (1 - y) * 2 + c), device_id_type=MESH,
        )

    def up(r, i):
        return pltpu.make_async_remote_copy(
            WG.at[held(r), i, y, c], RU.at[r % 7, i - 1], us.at[r, i - 1], ur.at[r, i - 1],
            device_id=(s, (z + 1) * 4 + y * 2 + c), device_id_type=MESH,
        )

    def down(r, i):
        return pltpu.make_async_remote_copy(
            WG.at[held(r), i, y, c], RD.at[r % 7, i], ds_.at[r, i], dr.at[r, i],
            device_id=(s, (z - 1) * 4 + y * 2 + c), device_id_type=MESH,
        )

    def strip_up(r, i):
        return pltpu.make_async_remote_copy(
            WG.at[held(r), i, 1 - y, c, :, pl.ds(MAIN, 1024 - MAIN)], RUS.at[r % 7, i - 1], us.at[r, 2 + i], ur.at[r, 2 + i],
            device_id=(s, (z + 1) * 4 + y * 2 + c), device_id_type=MESH,
        )

    def strip_down(r, i):
        return pltpu.make_async_remote_copy(
            WG.at[held(r), i, 1 - y, c, :, pl.ds(MAIN, 1024 - MAIN)], RDS.at[r % 7, i], ds_.at[r, 3 + i], dr.at[r, 3 + i],
            device_id=(s, (z - 1) * 4 + y * 2 + c), device_id_type=MESH,
        )

    def strip_y(r):
        return pltpu.make_async_remote_copy(
            WG.at[held(r), z, 1 - y, c, :, pl.ds(MAIN, 1024 - MAIN)], RYS.at[r % 4], yss.at[r], ysr.at[r],
            device_id=(s, z * 4 + (1 - y) * 2 + c), device_id_type=MESH,
        )

    def each_out(r, act):
        k = held(r)
        src = T.at[r % 2]

        @pl.when(r < 4)
        def _():
            act(pltpu.make_async_copy(src, op_.at[0, pl.ds(pl.multiple_of(64 * r, 64), 64)], osem.at[r]))

        @pl.when((r >= 4) & (r < 8))
        def _():
            act(pltpu.make_async_copy(src, of.at[0, :, pl.ds(pl.multiple_of(1024 * (r - 4), 1024), 1024)], osem.at[r]))

        @pl.when(r == 8)
        def _():
            act(pltpu.make_async_copy(src, oo.at[0], osem.at[r]))

        @pl.when(r > 8)
        def _():
            act(pltpu.make_async_copy(src, oq.at[0, :, pl.ds(pl.multiple_of(1024 * (11 - r), 1024), 1024)], osem.at[r]))

    def start(cp):
        cp.start()

    def add(k, i, j, other):
        WG[k, i, j, c] = (WG[k, i, j, c].astype(F32) + other.astype(F32)).astype(B16)

    def add_main(k, i, other):
        WG[k, i, y, c, :, :MAIN] = (WG[k, i, y, c, :, :MAIN].astype(F32) + other.astype(F32)).astype(B16)

    def add_strip(k, i, *others):
        total = WG[k, i, 1 - y, c, :, MAIN:].astype(F32)
        for other in others:
            total = total + other.astype(F32)
        WG[k, i, 1 - y, c, :, MAIN:] = total.astype(B16)

    def live(r):
        return (r >= 0) & (r < NP)

    def scatter_step(t):
        @pl.when(live(t))
        def _():
            across_c(t).start()

        @pl.when(live(t - 1))
        def _():
            r = t - 1
            k = held(r)
            across_c(r).wait_recv()

            @pl.loop(0, 4)
            def _(i):
                add(k, i, 1 - y, RC[r % 4, i, 1 - y])

            across_y(r).start()

            @pl.loop(0, 4)
            def _(i):
                add(k, i, y, RC[r % 4, i, y])

        @pl.when(live(t - 2))
        def _():
            r = t - 2
            k = held(r)
            across_y(r).wait_recv()

            @pl.loop(0, 4)
            def _(i):
                add_main(k, i, RY[r % 4, i])

            @pl.when(z == 0)
            def _():
                for i in (3, 2, 1):
                    up(r, i).start()
                    strip_up(r, i).start()

            @pl.when(z == 3)
            def _():
                for i in (0, 1, 2):
                    down(r, i).start()
                    strip_down(r, i).start()

        for q in (1, 2, 3):
            n = 4 - q

            @pl.when(live(t - 2 - q))
            def _():
                r = t - 2 - q
                k = held(r)

                @pl.when(z == q)
                def _():
                    for i in range(3, q - 1, -1):
                        up(r, i).wait_recv()
                        if i > q:
                            add(k, i, y, RU[r % 7, i - 1])
                            up(r, i).start()
                        strip_up(r, i).wait_recv()
                        if i > q:
                            add_strip(k, i, RUS[r % 7, i - 1])
                            strip_up(r, i).start()

                @pl.when(z == 3 - q)
                def _():
                    for i in range(n):
                        down(r, i).wait_recv()
                        if i < n - 1:
                            add(k, i, y, RD[r % 7, i])
                            down(r, i).start()
                        strip_down(r, i).wait_recv()
                        if i < n - 1:
                            add_strip(k, i, RDS[r % 7, i])
                            strip_down(r, i).start()

        @pl.when(live(t - 5))
        def _():
            r = t - 5
            k = held(r)

            @pl.when(z > 0)
            def _():
                add_strip(k, z, RUS[r % 7, z - 1])

            @pl.when(z < 3)
            def _():
                add_strip(k, z, RDS[r % 7, z])

            strip_y(r).start()

            @pl.when(r >= 2)
            def _():
                each_out(r - 2, lambda cp: cp.wait())

            T[r % 2] = WG[k, z, y, c].astype(F32)

            @pl.when(z > 0)
            def _():
                T[r % 2] += RU[r % 7, z - 1].astype(F32)

            @pl.when(z < 3)
            def _():
                T[r % 2] += RD[r % 7, z].astype(F32)

        @pl.when(live(t - 6))
        def _():
            r = t - 6
            strip_y(r).wait_recv()
            T[r % 2, :, MAIN:] += RYS[r % 4].astype(F32)
            each_out(r, start)

    ffn_in(0)
    greeted()

    @pl.loop(1, BACK_TICKS)
    def _(tick):
        turn = tick // SPLIT

        @pl.when(tick == 2 * (1 - s) + SPLIT * s)
        def _():
            ffn_in(1)

        def when(i, at0, at1, body):
            early = (1 - s) * at0 + s * i
            late = (1 - s) * at1 + s * (SPLIT + i)

            @pl.when((tick == early) | (tick == late))
            def _():
                body((tick == late).astype(jnp.int32))

        when(1, 3, 4, ffn_norm)
        when(2, 5, 7, attn_out)
        first = (tick - 3) % SPLIT * s + (tick - 5) % 2 * (1 - s)

        @pl.when(((s == 0) & (tick >= 5) & (tick < 9)) | ((s == 1) & (tick < 2 * SPLIT) & (first < 2)))
        def _():
            attn_back(first, (1 - s) * ((tick - 5) // 2) + s * turn)

        when(5, 9, 10, attn_norm)
        r = tick - 1 - (2 * SPLIT - 1) * s

        for j in range(4):
            pl.when(r == j)(lambda j=j: grad_proj(j))

        @pl.when((r >= 4) & (r < 8))
        def _():
            grad_fc(r - 4)

        @pl.when(r == 8)
        def _():
            grad_out()

        @pl.when((r > 8) & (r < 12))
        def _():
            grad_qkv(11 - r)

        scatter_step(r)
        for at, body in ((9, small_first), (12, small_second), (15, small_third)):
            pl.when(r == at)(body)

    @pl.loop(0, NP)
    def _(r):
        @pl.when(r >= NP - 2)
        def _():
            each_out(r, lambda cp: cp.wait())

        across_c(r).wait_send()
        across_y(r).wait_send()
        strip_y(r).wait_send()
        for q in range(3):

            @pl.when(z == q)
            def _():
                for i in range(q + 1, 4):
                    up(r, i).wait_send()
                    strip_up(r, i).wait_send()

            @pl.when(z == q + 1)
            def _():
                for i in range(q + 1):
                    down(r, i).wait_send()
                    strip_down(r, i).wait_send()

    small_last()
    sums_out()
    pref_out()

    @pl.loop(0, 2)
    def _(b):
        dh_out(b).wait()

        @pl.when(s == 1)
        def _():
            cross(b).wait_send()


def backward_call(kept, cot, r_out, small, pkey, pval):
    W, h, a1, qkv, prob, ppre, att, res, a2, gp, act = kept
    any_, vm = pl.BlockSpec(memory_space=pl.ANY), pl.BlockSpec(memory_space=pltpu.VMEM)
    n, d = h.shape
    dma = pltpu.SemaphoreType.DMA
    wide = (4, 2, 2, 64, d)
    outs = [
        ((n, d), B16), ((1, 64, 3 * d), F32), ((1, 64, d), F32), ((1, 64, 4 * d), F32), ((1, 256, d), F32),
        ((16, 128), F32), ((16, 2 * d), B16), ((16, 512), F32),
    ]
    scratch = [
        ((NP,) + wide, B16), ((n, d), B16), ((n, d), B16), ((3, n, d), B16), ((4, n, d), B16), ((2, HALF, HALF), B16), ((n, d), B16),
        ((n, d), F32), ((n, d), B16), ((4, n, d), B16), ((n, d), B16), ((n, d), B16), ((HALF, d), B16), ((HALF, HALF), F32),
        ((HALF, HALF), B16), ((HALF, d), F32),
        ((4, 4, 2, 64, d), B16), ((4, 4, 64, MAIN), B16), ((7, 3, 64, d), B16), ((7, 3, 64, d), B16),
        ((7, 3, 64, d - MAIN), B16), ((7, 3, 64, d - MAIN), B16), ((4, 64, d - MAIN), B16), ((2, 64, d), F32),
        ((16, d), F32), ((32, d), F32), ((16, 32, 128), F32), ((16, 32, 128), F32), ((16, 128), B16), ((16, 16, 128), B16),
        ((16, 512), F32), ((16, 512), F32),
    ]
    return pl.pallas_call(
        backward_kernel,
        out_shape=[jax.ShapeDtypeStruct(*o) for o in outs],
        in_specs=[any_] * 13 + [vm] * 3,
        out_specs=[any_] * 5 + [vm] * 3,
        scratch_shapes=[pltpu.VMEM(*v) for v in scratch] + [dma((NP,))] * 7 + [dma((NP, 6))] * 4 + [dma((NP,))] * 2 + [dma((2,))] * 3 + [dma((16,))] * 4 + [dma((4,))] * 2,
        compiler_params=pltpu.CompilerParams(collective_id=1, has_side_effects=True, vmem_limit_bytes=64 << 20),
    )(W.reshape((NP,) + wide), h, a1, qkv, prob, ppre, att, res, a2, gp, act, cot, r_out, small, pkey, pval)


def finish_kernel(
    o0, o1, o2, o3, o4, o5, hid, kvb, hsum, aux, r_in, sums,
    c0, c1, c2, c3, c4, c5, g_embed, g_in, g_in_bias, g_out, g_out_bias, g_gains, g_bias,
    G_IN, G_OUT, M0, M1, M2, M3, M4, M5, R_IN, sem,
):
    held = (M0, M1, M2, M3, M4, M5)
    here = [pltpu.make_async_copy(a, m, sem.at[i]) for i, (a, m) in enumerate(zip((o0, o1, o2, o3, o4, o5), held))]
    away = [pltpu.make_async_copy(m, c, sem.at[8 + i]) for i, (m, c) in enumerate(zip(held, (c0, c1, c2, c3, c4, c5)))]
    for cp in here:
        cp.start()
    weight_in = pltpu.make_async_copy(r_in, R_IN, sem.at[14])
    weight_in.start()
    h = hid[...]
    kv = kvb[...]
    G_OUT[...] = dot_tn(h.astype(B16), kv)
    out_cp = pltpu.make_async_copy(G_OUT, g_out, sem.at[6])
    out_cp.start()
    g_out_bias[...] = column_sum(kv)
    for cp, out in zip(here, away):
        cp.wait()
        out.start()
    dp = (hsum[...] * (1.0 - h * h)).astype(B16)
    G_IN[...] = dot_tn(aux[...], dp)
    in_cp = pltpu.make_async_copy(G_IN, g_in, sem.at[7])
    in_cp.start()
    g_in_bias[...] = column_sum(dp)
    weight_in.wait()
    g_embed[...] = dot_nt(dp, R_IN[...])[:10]
    g_gains[0] = sums[11:13, :64]
    for i in range(11):
        g_bias[:, 64 * i : 64 * i + 64] = sums[i : i + 1, :64]
    for cp in away + [out_cp, in_cp]:
        cp.wait()


def finish_call(large, hid, kvb, hsum, aux, r_in, sums):
    any_, vm = pl.BlockSpec(memory_space=pl.ANY), pl.BlockSpec(memory_space=pltpu.VMEM)
    d = r_in.shape[0]
    outs = [jax.ShapeDtypeStruct(x.shape, x.dtype) for x in large]
    outs += [jax.ShapeDtypeStruct(x, F32) for x in ((10, d), (d, 512), (1, 512), (512, 2 * d), (1, 2 * d), (1, 2, 64), (1, 704))]
    return pl.pallas_call(
        finish_kernel,
        out_shape=outs,
        in_specs=[any_] * 6 + [vm] * 4 + [any_, vm],
        out_specs=[any_] * 6 + [vm, any_, vm, any_, vm, vm, vm],
        scratch_shapes=[pltpu.VMEM((d, 512), F32), pltpu.VMEM((512, 2 * d), F32)]
        + [pltpu.VMEM(x.shape, x.dtype) for x in large]
        + [pltpu.VMEM(r_in.shape, r_in.dtype), pltpu.SemaphoreType.DMA((15,))],
        compiler_params=pltpu.CompilerParams(vmem_limit_bytes=63 << 20),
    )(*large, hid, kvb, hsum, aux, r_in, sums)


def on_device(
    tokens,
    segment_ids,
    cotangent,
    w_qkv,
    w_attn_out,
    w_fc,
    w_proj,
    gains,
    biases,
    prefix_embed,
    reparam_in,
    reparam_in_bias,
    reparam_out,
    reparam_out_bias,
):
    aux = prefix_rows(prefix_embed, reparam_in_bias, reparam_out_bias)
    kept = forward_call(w_qkv, w_attn_out, w_fc, w_proj, tokens, segment_ids, gains, biases, aux, reparam_in, reparam_out)
    small, pkey, pval, hid = kept[12:]
    *large, sums, kvb, hsum = backward_call(kept[:1] + kept[2:12], cotangent, reparam_out, small, pkey, pval)
    done = finish_call([kept[1]] + large, hid, kvb, hsum, aux, reparam_in, sums)
    return (
        done[0][None],
        done[1][None],
        *done[2:6],
        done[11],
        done[12],
        done[6],
        done[7],
        done[8][0],
        done[9],
        done[10][0],
    )


def passed_along(shard, axis, by):
    size = lax.axis_size(axis)
    pairs = [(i, i + by) for i in range(size) if 0 <= i + by < size]
    return lax.ppermute(shard, axis, pairs)


def norm_rows(v, gain, shift):
    mean = jnp.mean(v, axis=-1, keepdims=True)
    cent = v - mean
    var = jnp.mean(cent * cent, axis=-1, keepdims=True)
    return cent * lax.rsqrt(var + EPS) * gain + shift


def gelu_tanh(v):
    return jax.nn.gelu(v, approximate=True)


def forward_layer(h_b, segs, pkey, pval, params):
    w_q, w_o, w_f, w_p, gain_pair, bias_all = params
    width = w_o.shape[0]
    length = h_b.shape[0]
    heads, head_dim = (pkey.shape[1], pkey.shape[2])
    scale = 1.0 / math.sqrt(head_dim)
    gain_f = gain_pair.astype(jnp.float32)
    bias_f = bias_all.astype(jnp.float32)
    hf = h_b.astype(jnp.float32)
    a1b = norm_rows(hf, gain_f[0], bias_f[9 * width : 10 * width]).astype(jnp.bfloat16)
    qkv_b = (jnp.dot(a1b, w_q, preferred_element_type=jnp.float32) + bias_f[: 3 * width]).astype(
        jnp.bfloat16
    )
    split = qkv_b.reshape(length, 3, heads, head_dim)
    query, keys, values = (split[:, 0], split[:, 1], split[:, 2])
    s_tok = jnp.einsum("lhe,mhe->hlm", query, keys, preferred_element_type=jnp.float32) * scale
    s_pre = jnp.einsum("lhe,phe->hlp", query, pkey, preferred_element_type=jnp.float32) * scale
    place = jnp.arange(length)
    allowed = (segs[:, None] == segs[None, :]) & (place[None, :] <= place[:, None])
    s_tok = jnp.where(allowed[None], s_tok, NEG)
    top = jnp.maximum(
        jnp.max(s_tok, axis=-1, keepdims=True), jnp.max(s_pre, axis=-1, keepdims=True)
    )
    e_tok = jnp.exp(s_tok - top)
    e_pre = jnp.exp(s_pre - top)
    total = jnp.sum(e_tok, axis=-1, keepdims=True) + jnp.sum(e_pre, axis=-1, keepdims=True)
    p_tok = e_tok / total
    p_pre = e_pre / total
    mixed = jnp.einsum(
        "hlm,mhe->lhe", p_tok.astype(jnp.bfloat16), values, preferred_element_type=jnp.float32
    ) + jnp.einsum(
        "hlp,phe->lhe", p_pre.astype(jnp.bfloat16), pval, preferred_element_type=jnp.float32
    )
    attn_b = mixed.reshape(length, width).astype(jnp.bfloat16)
    resid = hf + (
        jnp.dot(attn_b, w_o, preferred_element_type=jnp.float32) + bias_f[3 * width : 4 * width]
    )
    a2b = norm_rows(resid, gain_f[1], bias_f[10 * width : 11 * width]).astype(jnp.bfloat16)
    pre_act = jnp.dot(a2b, w_f, preferred_element_type=jnp.float32) + bias_f[4 * width : 8 * width]
    act_b = gelu_tanh(pre_act).astype(jnp.bfloat16)
    result = resid + (
        jnp.dot(act_b, w_p, preferred_element_type=jnp.float32) + bias_f[8 * width : 9 * width]
    )
    return (result, (hf, a1b, qkv_b, p_tok, p_pre, attn_b, resid, a2b, pre_act, act_b))


def backward_ffn(grad_out, keep, params):
    w_q, w_o, w_f, w_p, gain_pair, bias_all = params
    hf, a1b, qkv_b, p_tok, p_pre, attn_b, resid, a2b, pre_act, act_b = keep
    width = w_o.shape[0]
    gain_f = gain_pair.astype(jnp.float32)
    bias_f = bias_all.astype(jnp.float32)
    dm_b = grad_out.astype(jnp.bfloat16)
    grad_wp = jnp.einsum("lf,ld->fd", act_b, dm_b, preferred_element_type=jnp.float32)
    grad_bp = jnp.sum(dm_b.astype(jnp.float32), axis=0)
    d_act = jnp.dot(dm_b, w_p.T, preferred_element_type=jnp.float32)
    dpre_b = jax.vjp(gelu_tanh, pre_act)[1](d_act)[0].astype(jnp.bfloat16)
    grad_wf = jnp.einsum("ld,lf->df", a2b, dpre_b, preferred_element_type=jnp.float32)
    grad_bf = jnp.sum(dpre_b.astype(jnp.float32), axis=0)
    d_a2 = jnp.dot(dpre_b, w_f.T, preferred_element_type=jnp.float32)
    norm_back = jax.vjp(norm_rows, resid, gain_f[1], bias_f[10 * width : 11 * width])[1]
    d_resid_norm, grad_g2, grad_c2 = norm_back(d_a2)
    d_resid = grad_out + d_resid_norm
    return (d_resid, (grad_wf, grad_wp), (grad_bf, grad_bp, grad_g2, grad_c2))


def backward_attn(d_resid, keep, pkey, pval, params):
    w_q, w_o, w_f, w_p, gain_pair, bias_all = params
    hf, a1b, qkv_b, p_tok, p_pre, attn_b, resid, a2b, pre_act, act_b = keep
    width = w_o.shape[0]
    length = hf.shape[0]
    heads, head_dim = (pkey.shape[1], pkey.shape[2])
    prefix_len = pkey.shape[0]
    scale = 1.0 / math.sqrt(head_dim)
    gain_f = gain_pair.astype(jnp.float32)
    bias_f = bias_all.astype(jnp.float32)
    split = qkv_b.reshape(length, 3, heads, head_dim)
    query, keys, values = (split[:, 0], split[:, 1], split[:, 2])
    dat_b = d_resid.astype(jnp.bfloat16)
    grad_wo = jnp.einsum("ld,le->de", attn_b, dat_b, preferred_element_type=jnp.float32)
    grad_bo = jnp.sum(dat_b.astype(jnp.float32), axis=0)
    dattn_b = jnp.dot(dat_b, w_o.T, preferred_element_type=jnp.float32).astype(jnp.bfloat16)
    dattn_b = dattn_b.reshape(length, heads, head_dim)
    dp_tok = jnp.einsum("lhe,mhe->hlm", dattn_b, values, preferred_element_type=jnp.float32)
    dp_pre = jnp.einsum("lhe,phe->hlp", dattn_b, pval, preferred_element_type=jnp.float32)
    row_dot = jnp.sum(p_tok * dp_tok, axis=-1, keepdims=True) + jnp.sum(
        p_pre * dp_pre, axis=-1, keepdims=True
    )
    ds_tok = (p_tok * (dp_tok - row_dot)).astype(jnp.bfloat16)
    ds_pre = (p_pre * (dp_pre - row_dot)).astype(jnp.bfloat16)
    d_query = (
        jnp.einsum("hlm,mhe->lhe", ds_tok, keys, preferred_element_type=jnp.float32)
        + jnp.einsum("hlp,phe->lhe", ds_pre, pkey, preferred_element_type=jnp.float32)
    ) * scale
    d_keys = jnp.einsum("hlm,lhe->mhe", ds_tok, query, preferred_element_type=jnp.float32) * scale
    d_values = jnp.einsum(
        "hlm,lhe->mhe", p_tok.astype(jnp.bfloat16), dattn_b, preferred_element_type=jnp.float32
    )
    grad_pkey = (
        jnp.einsum("hlp,lhe->phe", ds_pre, query, preferred_element_type=jnp.float32) * scale
    )
    grad_pval = jnp.einsum(
        "hlp,lhe->phe", p_pre.astype(jnp.bfloat16), dattn_b, preferred_element_type=jnp.float32
    )
    dqkv_b = (
        jnp.stack([d_query, d_keys, d_values], axis=1)
        .reshape(length, 3 * width)
        .astype(jnp.bfloat16)
    )
    grad_wq = jnp.einsum("ld,lc->dc", a1b, dqkv_b, preferred_element_type=jnp.float32)
    grad_bq = jnp.sum(dqkv_b.astype(jnp.float32), axis=0)
    d_a1 = jnp.dot(dqkv_b, w_q.T, preferred_element_type=jnp.float32)
    norm_back_first = jax.vjp(norm_rows, hf, gain_f[0], bias_f[9 * width : 10 * width])[1]
    d_in_norm, grad_g1, grad_c1 = norm_back_first(d_a1)
    d_input = d_resid + d_in_norm
    grad_prefix = jnp.concatenate(
        [grad_pkey.reshape(prefix_len, width), grad_pval.reshape(prefix_len, width)], axis=1
    )
    return (d_input, (grad_wq, grad_wo), (grad_bq, grad_bo, grad_g1, grad_c1), grad_prefix)


def assemble(ffn_mats, ffn_small, attn_mats, attn_small):
    grad_bf, grad_bp, grad_g2, grad_c2 = ffn_small
    grad_bq, grad_bo, grad_g1, grad_c1 = attn_small
    grad_gains = jnp.stack([grad_g1, grad_g2])
    grad_bias = jnp.concatenate([grad_bq, grad_bo, grad_bf, grad_bp, grad_c1, grad_c2])
    return (attn_mats[0], attn_mats[1], ffn_mats[0], ffn_mats[1], grad_gains, grad_bias)


def on_device_general(
    tokens,
    segment_ids,
    cotangent,
    w_qkv,
    w_attn_out,
    w_fc,
    w_proj,
    gains,
    biases,
    prefix_embed,
    reparam_in,
    reparam_in_bias,
    reparam_out,
    reparam_out_bias,
):
    section = lax.axis_index("section")
    micro, row_len = segment_ids.shape
    width = tokens.shape[1]
    prefix_len = prefix_embed.shape[0]
    head_dim = width // HEADS
    gathered = (
        lax.all_gather(w_qkv, "dp", axis=1, tiled=True),
        lax.all_gather(w_attn_out, "dp", axis=1, tiled=True),
        lax.all_gather(w_fc, "dp", axis=1, tiled=True),
        lax.all_gather(w_proj, "dp", axis=1, tiled=True),
        lax.all_gather(gains, "dp", axis=2, tiled=True),
        lax.all_gather(biases, "dp", axis=1, tiled=True),
    )
    params = tuple((item[0] for item in gathered))
    pre_hidden = jnp.dot(
        prefix_embed, reparam_in, preferred_element_type=jnp.float32
    ) + reparam_in_bias.astype(jnp.float32)
    hidden = jnp.tanh(pre_hidden)
    hidden_b = hidden.astype(jnp.bfloat16)
    prefix_kv = (
        jnp.dot(hidden_b, reparam_out, preferred_element_type=jnp.float32)
        + reparam_out_bias.astype(jnp.float32)
    ).astype(jnp.bfloat16)
    pkey = prefix_kv[:, :width].reshape(prefix_len, HEADS, head_dim)
    pval = prefix_kv[:, width:].reshape(prefix_len, HEADS, head_dim)
    token_rows = tokens.reshape(micro, row_len, width)
    cot_rows = cotangent.reshape(micro, row_len, width)
    received = jnp.zeros((row_len, width), jnp.bfloat16)
    outputs = jnp.zeros((micro, row_len, width), jnp.bfloat16)
    stored = []
    for tick in range(micro + 1):
        index = tick - section
        active = (index >= 0) & (index < micro)
        slot = jnp.clip(index, 0, micro - 1)
        segs = segment_ids[slot]
        h_b = jnp.where(section == 0, token_rows[slot], received)
        result, keep = forward_layer(h_b, segs, pkey, pval, params)
        result_b = result.astype(jnp.bfloat16)
        outputs = jnp.where(active, outputs.at[slot].set(result_b), outputs)
        stored.append(keep)
        if tick < micro:
            received = passed_along(result_b, "section", 1)
    regathered = (
        lax.all_gather(w_qkv, "dp", axis=1, tiled=True),
        lax.all_gather(w_attn_out, "dp", axis=1, tiled=True),
        lax.all_gather(w_fc, "dp", axis=1, tiled=True),
        lax.all_gather(w_proj, "dp", axis=1, tiled=True),
        lax.all_gather(gains, "dp", axis=2, tiled=True),
        lax.all_gather(biases, "dp", axis=1, tiled=True),
    )
    params_back = tuple((item[0] for item in regathered))
    stacked = jax.tree.map(lambda *items: jnp.stack(items), *stored)
    coming = jnp.zeros((row_len, width), jnp.bfloat16)
    in_grads = jnp.zeros((micro, row_len, width), jnp.bfloat16)
    grad_total = None
    prefix_total = None
    for tick in range(micro + 1):
        index = micro - tick - section
        active = (index >= 0) & (index < micro)
        slot = jnp.clip(index, 0, micro - 1)
        segs = segment_ids[slot]
        saved = jax.tree.map(lambda item: item[slot + section], stacked)
        grad_out = jnp.where(
            section == 1, cot_rows[slot].astype(jnp.float32), coming.astype(jnp.float32)
        )
        keep = saved
        d_resid, ffn_mats, ffn_small = backward_ffn(grad_out, keep, params_back)
        ffn_mats = jax.tree.map(
            lambda item: jnp.where(active, item, jnp.zeros_like(item)), ffn_mats
        )
        ffn_small = jax.tree.map(
            lambda item: jnp.where(active, item, jnp.zeros_like(item)), ffn_small
        )
        d_input, attn_mats, attn_small, grad_prefix = backward_attn(
            d_resid, keep, pkey, pval, params_back
        )
        attn_mats = jax.tree.map(
            lambda item: jnp.where(active, item, jnp.zeros_like(item)), attn_mats
        )
        attn_small = jax.tree.map(
            lambda item: jnp.where(active, item, jnp.zeros_like(item)), attn_small
        )
        grad_prefix = jnp.where(active, grad_prefix, jnp.zeros_like(grad_prefix))
        grads = assemble(ffn_mats, ffn_small, attn_mats, attn_small)
        if grad_total is None:
            grad_total = grads
            prefix_total = grad_prefix
        else:
            grad_total = jax.tree.map(lambda left, right: left + right, grad_total, grads)
            prefix_total = prefix_total + grad_prefix
        d_input_b = d_input.astype(jnp.bfloat16)
        in_grads = jnp.where(active, in_grads.at[slot].set(d_input_b), in_grads)
        if tick < micro:
            coming = passed_along(d_input_b, "section", -1)
    lifted = tuple((item[None] for item in grad_total))
    weight_grads = (
        lax.psum_scatter(lifted[0], "dp", scatter_dimension=1, tiled=True),
        lax.psum_scatter(lifted[1], "dp", scatter_dimension=1, tiled=True),
        lax.psum_scatter(lifted[2], "dp", scatter_dimension=1, tiled=True),
        lax.psum_scatter(lifted[3], "dp", scatter_dimension=1, tiled=True),
        lax.psum_scatter(lifted[4], "dp", scatter_dimension=2, tiled=True),
        lax.psum_scatter(lifted[5], "dp", scatter_dimension=1, tiled=True),
    )
    prefix_grad = lax.psum(prefix_total, "dp")
    prefix_grad_b = prefix_grad.astype(jnp.bfloat16)
    grad_reparam_out = jnp.einsum(
        "pr,pc->rc", hidden_b, prefix_grad_b, preferred_element_type=jnp.float32
    )
    grad_reparam_out_bias = jnp.sum(prefix_grad_b.astype(jnp.float32), axis=0)
    hidden_part = jnp.dot(prefix_grad_b, reparam_out.T, preferred_element_type=jnp.float32)
    hidden_grad = lax.psum(hidden_part, "section")
    dpre_hidden_b = (hidden_grad * (1.0 - hidden * hidden)).astype(jnp.bfloat16)
    grad_reparam_in = jnp.einsum(
        "pd,pr->dr", prefix_embed, dpre_hidden_b, preferred_element_type=jnp.float32
    )
    grad_reparam_in_bias = jnp.sum(dpre_hidden_b.astype(jnp.float32), axis=0)
    grad_prefix_embed = jnp.dot(dpre_hidden_b, reparam_in.T, preferred_element_type=jnp.float32)
    layer_outs = outputs.reshape(1, micro * row_len, width)
    input_grads = in_grads.reshape(1, micro * row_len, width)
    return (
        layer_outs,
        input_grads,
        weight_grads[0],
        weight_grads[1],
        weight_grads[2],
        weight_grads[3],
        weight_grads[4],
        weight_grads[5],
        grad_prefix_embed,
        grad_reparam_in,
        grad_reparam_in_bias,
        grad_reparam_out,
        grad_reparam_out_bias,
    )


def solution(mesh):
    return jax.shard_map(
        on_device if mesh.shape["dp"] == 16 else on_device_general,
        mesh=mesh,
        in_specs=(
            P("dp", None),
            P("dp", None),
            P("dp", None),
            P("section", "dp", None),
            P("section", "dp", None),
            P("section", "dp", None),
            P("section", "dp", None),
            P("section", None, "dp"),
            P("section", "dp"),
            P(),
            P(),
            P(),
            P(None, "section"),
            P("section"),
        ),
        out_specs=(
            P("section", "dp", None),
            P("section", "dp", None),
            P("section", "dp", None),
            P("section", "dp", None),
            P("section", "dp", None),
            P("section", "dp", None),
            P("section", None, "dp"),
            P("section", "dp"),
            P(),
            P(),
            P(),
            P(None, "section"),
            P("section"),
        ),
        check_vma=False,
    )
```

```python
import math

import jax
import jax.numpy as jnp
from jax import lax
from jax.experimental import pallas as pl
from jax.experimental.pallas import tpu as pltpu
from jax.sharding import PartitionSpec as P

HEADS = 16
EPS = 1e-05
NEG = -1000000000.0
MESH = pl.DeviceIdType.MESH
F32 = jnp.float32
B16 = jnp.bfloat16
NP = 12
MAIN = 896
AHEAD = 1


def place():
    s = lax.axis_index("section"); d = lax.axis_index("dp")
    return s, d, d // 4, (d // 2) % 2, d % 2

def greet(s, d):
    bar = pltpu.get_barrier_semaphore()
    for i in range(1, 16):
        pl.semaphore_signal(bar, 1, device_id=(s, (d + i) % 16), device_id_type=MESH)
    pl.semaphore_signal(bar, 1, device_id=(1 - s, d), device_id_type=MESH)


def greeted():
    pl.semaphore_wait(pltpu.get_barrier_semaphore(), 16)


def to_all(src, dst, ss, rs):
    s, d = lax.axis_index("section"), lax.axis_index("dp")

    def cp(i, frm):
        to = (d + i) % 16
        return pltpu.make_async_remote_copy(
            src(to), dst.at[frm], ss.at[i], rs.at[i], device_id=(s, to), device_id_type=MESH
        )

    def start():
        for i in range(1, 16):
            cp(i, d).start()

    def arrive():
        for i in range(1, 16):
            cp(i, (d + 16 - i) % 16).wait_recv()

    def finish():
        for i in range(1, 16):
            cp(i, d).wait_send()

    return start, arrive, finish


class Gather:
    def __init__(self, W, ssem, rsem, tsem, qsem):
        self.W, self.ssem, self.rsem, self.tsem, self.qsem = W, ssem, rsem, tsem, qsem
        self.s, self.d, self.z, self.y, self.c = place()
    def blk(self, k, d):
        i = k // 8
        row = (1-i)*(1024*k+64*d) + i*(8192+256*d+64*(k-8))
        return self.W.at[pl.ds(pl.multiple_of(row, 64), 64)]
    def cp(self, k, origin, target, slot, width=1024):
        b = self.blk(k, origin)
        if width < 1024: b = b.at[:, pl.ds(0, width)]
        return pltpu.make_async_remote_copy(src_ref=b, dst_ref=b, send_sem=self.ssem.at[k, slot], recv_sem=self.rsem.at[k, origin],
            device_id=(self.s, target), device_id_type=MESH)
    def dev(self, z, y, c): return z*4+y*2+c
    def arrived(self, k, origin): self.cp(k, origin, origin, 0).wait_recv()
    def to_up(self, k, zo, op):
        op(self.cp(k, self.dev(zo, self.y, self.c), self.dev(self.z+1, self.y, self.c), zo))
    def to_down(self, k, zo, op):
        op(self.cp(k, self.dev(zo, self.y, self.c), self.dev(self.z-1, self.y, self.c), 4+zo))
    def to_y(self, k, zo, op, width=MAIN):
        op(self.cp(k, self.dev(zo, self.y, self.c), self.dev(self.z, 1-self.y, self.c), 8+zo, width))
    def strip(self, k, zo, to, slot):
        b = self.blk(k, self.dev(zo, 1-self.y, self.c)).at[:, pl.ds(MAIN, 1024-MAIN)]
        return pltpu.make_async_remote_copy(src_ref=b, dst_ref=b, send_sem=self.tsem.at[k, slot], recv_sem=self.qsem.at[k, zo],
            device_id=(self.s, self.dev(to, self.y, self.c)), device_id_type=MESH)
    def strip_up(self, k, zo, op): op(self.strip(k, zo, self.z+1, zo))
    def strip_down(self, k, zo, op): op(self.strip(k, zo, self.z-1, 4+zo))
    def to_c(self, k, zo, yo, op):
        op(self.cp(k, self.dev(zo, yo, self.c), self.dev(self.z, self.y, 1-self.c), 12+zo*2+yo))
    def step(self, t, own):
        z, y, c = self.z, self.y, self.c
        start = lambda cp: cp.start()
        def fresh(k):
            own(k)
            self.to_y(k, z, start, 1024)
            @pl.when(z < 3)
            def _(): self.to_up(k, z, start)
            @pl.when(z > 0)
            def _(): self.to_down(k, z, start)
            self.to_c(k, z, y, start)
        @pl.when(t == 0)
        def _():
            for k in range(AHEAD): fresh(k)
        @pl.when(t + AHEAD < NP)
        def _(): fresh(t + AHEAD)
        for q in (1, 2, 3, 4):
            k = t - q
            ok = (k >= 0) & (k < NP)
            if q < 4:
                @pl.when(ok & (z - q >= 0))
                def _():
                    self.arrived(k, self.dev(z-q, y, c))
                    @pl.when(z < 3)
                    def _(): self.to_up(k, z-q, start)
                    self.to_y(k, z-q, start)
                    self.to_c(k, z-q, y, start)
                @pl.when(ok & (z + q <= 3))
                def _():
                    self.arrived(k, self.dev(z+q, y, c))
                    @pl.when(z > 0)
                    def _(): self.to_down(k, z+q, start)
                    self.to_y(k, z+q, start)
                    self.to_c(k, z+q, y, start)
            e = q - 1
            def side(zo):
                o = self.dev(zo, 1-y, c)
                self.cp(k, o, o, 0, MAIN).wait_recv()
                self.to_c(k, zo, 1-y, start)
            if e == 0:
                @pl.when(ok)
                def _():
                    self.arrived(k, self.dev(z, 1-y, c))
                    @pl.when(z < 3)
                    def _(): self.strip_up(k, z, start)
                    @pl.when(z > 0)
                    def _(): self.strip_down(k, z, start)
                    self.to_c(k, z, 1-y, start)
            else:
                @pl.when(ok & (z - e >= 0))
                def _():
                    self.strip(k, z-e, z, 0).wait_recv()
                    @pl.when(z < 3)
                    def _(): self.strip_up(k, z-e, start)
                    side(z-e)
                @pl.when(ok & (z + e <= 3))
                def _():
                    self.strip(k, z+e, z, 0).wait_recv()
                    @pl.when(z > 0)
                    def _(): self.strip_down(k, z+e, start)
                    side(z+e)
    def complete(self, k):
        for i in range(8):
            self.arrived(k, 2*i + 1-self.c)
    def drain(self):
        fin = lambda cp: cp.wait_send()
        z, y = self.z, self.y
        @pl.loop(0, NP)
        def _(k):
            for zo in range(4):
                @pl.when((zo <= z) & (z < 3))
                def _(): self.to_up(k, zo, fin)
                @pl.when((zo >= z) & (z > 0))
                def _(): self.to_down(k, zo, fin)
                @pl.when(zo == z)
                def _(): self.to_y(k, zo, fin, 1024)
                @pl.when(zo != z)
                def _(): self.to_y(k, zo, fin)
                @pl.when((zo <= z) & (z < 3))
                def _(): self.strip_up(k, zo, fin)
                @pl.when((zo >= z) & (z > 0))
                def _(): self.strip_down(k, zo, fin)
                for yo in range(2): self.to_c(k, zo, yo, fin)

def own_copies(wq, wo, wf, wp, g, sem):
    out = []
    for k in range(NP):
        if k < 3: src = wq.at[0, :, pl.ds(1024*k, 1024)]
        elif k == 3: src = wo.at[0]
        elif k < 8: src = wf.at[0, :, pl.ds(1024*(k-4), 1024)]
        else: src = wp.at[0, pl.ds(64*(k-8), 64)]
        out.append(pltpu.make_async_copy(src, g.blk(jnp.int32(k), g.d), sem.at[k]))
    return out


HALF = 256
STAGES = 12
GELU_C = math.sqrt(2.0 / math.pi)


def dot_nn(a, b):
    return lax.dot_general(a, b, (((1,), (0,)), ((), ())), preferred_element_type=F32)


def dot_nt(a, b):
    return lax.dot_general(a, b, (((1,), (1,)), ((), ())), preferred_element_type=F32)


def dot_tn(a, b):
    return lax.dot_general(a, b, (((0,), (0,)), ((), ())), preferred_element_type=F32)


def whiten(v):
    mean = jnp.mean(v, axis=-1, keepdims=True)
    cent = v - mean
    rstd = lax.rsqrt(jnp.mean(cent * cent, axis=-1, keepdims=True) + EPS)
    return cent * rstd, rstd


def split_heads(pair):
    left = lax.broadcasted_iota(jnp.int32, pair.shape, 1) < 64
    zero = jnp.zeros_like(pair)
    return jnp.concatenate([jnp.where(left, pair, zero), jnp.where(left, zero, pair)], axis=0)


def forward_kernel(
    wq, wo, wf, wp, tokens, segs, gains, biases, aux, r_in, r_out,
    W_o, out_o, h_o, a1_o, qkv_o, prob_o, ppre_o, att_o, res_o, a2_o, gp_o, act_o, small_o, pkey_o, pval_o, hid_o,
    W, H, A1, QKV, PROB, PPRE, ATT, RES, A2, GP, ACT, OUT, SPRE, ACC, small, pkey, pval, hid, mask, pack, PACKS, ROWS,
    own_sem, ssem, rsem, tsem, qsem, hsem, xs, xr, save_sem, fs, ps, pr, psem,
):
    g = Gather(W, ssem, rsem, tsem, qsem)
    s = g.s
    for cp in own_copies(wq, wo, wf, wp, g, own_sem):
        cp.start()
    r_in_parts = [pltpu.make_async_copy(r_in.at[pl.ds(512 * i, 512)], ACT.at[2, :, pl.ds(512 * i, 512)], psem.at[i]) for i in range(2)]
    r_out_parts = [pltpu.make_async_copy(r_out.at[:, pl.ds(1024 * i, 1024)], ACT.at[i], psem.at[2 + i]) for i in range(2)]
    for cp in r_in_parts + r_out_parts:
        cp.start()
    greet(s, g.d)
    own_bias = biases[...].astype(F32)
    for n in range(2):
        for r in range(11):
            ROWS[0, r : r + 1, 64 * n : 64 * n + 64] = own_bias[:, 64 * r : 64 * r + 64]
        ROWS[0, 11:13, 64 * n : 64 * n + 64] = gains[0].astype(F32)
    ROWS[0, 13:16] = jnp.zeros((3, 128), F32)
    pack[...] = ROWS[0].astype(B16)
    greeted()
    send_packs, packs_in, packs_out = to_all(lambda to: pack, PACKS, ps, pr)

    def prep_saves():
        pairs = [(small, small_o), (pkey, pkey_o), (pval, pval_o), (hid, hid_o)]
        return [pltpu.make_async_copy(a, b, psem.at[4 + i]) for i, (a, b) in enumerate(pairs)]

    def prepare():
        for cp in r_in_parts + r_out_parts:
            cp.wait()
        ph = dot_nn(aux[:, :512], ACT[2, :, :512]) + dot_nn(aux[:, 512:], ACT[2, :, 512:])
        hid[...] = jnp.tanh(ph + aux[10:11, :512].astype(F32))
        hb = hid[...].astype(B16)
        head = lax.broadcasted_iota(jnp.int32, (16, 1024), 1) // 64
        for i, big in enumerate((pkey, pval)):
            kv = (dot_nn(hb, ACT[i]) + aux[11 + i : 12 + i].astype(F32)).astype(B16)
            for h in range(16):
                big[16 * h : 16 * h + 16] = jnp.where(head == h, kv, jnp.zeros_like(kv))
        key = lax.broadcasted_iota(jnp.int32, (HALF, HALF), 0)
        query = lax.broadcasted_iota(jnp.int32, (HALF, HALF), 1)
        for b in range(2):
            by_query = jnp.broadcast_to(segs[b : b + 1].astype(F32), (HALF, HALF))
            ok = (by_query.T == by_query) & (key <= query)
            mask[b] = jnp.where(ok, 0.0, NEG)
        packs_in()
        ROWS[...] = PACKS[...].astype(F32)
        left = lax.broadcasted_iota(jnp.int32, (1, 128), 1) < 64
        small[...] = jnp.zeros_like(small)
        for n in range(104):
            row, at = n // 8, 128 * (n % 8)
            if row < 11:
                (d0, r0), (d1, r1) = divmod(2 * n, 11), divmod(2 * n + 1, 11)
            else:
                (d0, r0), (d1, r1) = (2 * (n % 8), row), (2 * (n % 8) + 1, row)
            small[row : row + 1, at : at + 128] = jnp.where(left, ROWS[d0, r0 : r0 + 1], ROWS[d1, r1 : r1 + 1])
        for cp in prep_saves():
            cp.start()

    send_packs()
    PACKS[g.d] = pack[...]

    def tokens_in():
        return pltpu.make_async_copy(tokens, H, hsem)

    def half(b):
        return pl.ds(pl.multiple_of(b * HALF, HALF), HALF)

    def cross(b):
        return pltpu.make_async_remote_copy(
            OUT.at[half(b)], H.at[half(b)], xs.at[b], xr.at[b], device_id=(1 - s, g.d), device_id_type=MESH
        )

    @pl.when(s == 0)
    def _():
        tokens_in().start()

    def own(t):
        b = g.blk(t, g.d)
        pltpu.make_async_copy(b, b, own_sem.at[t]).wait()

    def rows_of(k):
        return pl.ds(pl.multiple_of(k * 1024, 1024), 1024)

    def saves(b):
        r = half(b)
        pairs = [
            (H.at[r], h_o.at[r]), (A1.at[r], a1_o.at[r]), (QKV.at[:, r], qkv_o.at[:, r]), (PROB.at[pl.ds(2 * b, 2)], prob_o.at[pl.ds(2 * b, 2)]),
            (PPRE.at[b], ppre_o.at[b]), (ATT.at[r], att_o.at[r]), (RES.at[r], res_o.at[r]), (A2.at[r], a2_o.at[r]),
            (OUT.at[r], out_o.at[r]),
        ]
        return [pltpu.make_async_copy(src, dst, save_sem.at[b, i]) for i, (src, dst) in enumerate(pairs)]

    def ffn_saves(b, j):
        r = half(b)
        return [
            pltpu.make_async_copy(GP.at[j, r], gp_o.at[j, r], fs.at[b, j]),
            pltpu.make_async_copy(ACT.at[j, r], act_o.at[j, r], fs.at[b, 4 + j]),
        ]

    def piece_out(k):
        return pltpu.make_async_copy(W.at[rows_of(k)], W_o.at[rows_of(k)], save_sem.at[2, k])

    def norm_in(b):
        @pl.when(s == 0)
        def _():
            @pl.when(b == 0)
            def _():
                tokens_in().wait()

        @pl.when(s == 1)
        def _():
            cross(b).wait_recv()

        xhat, _ = whiten(H[half(b)].astype(F32))
        A1[half(b)] = (xhat * small[11:12] + small[9:10]).astype(B16)
        saves(b)[0].start()
        saves(b)[1].start()

    def project(i, b):
        v = dot_nn(A1[half(b)], W[rows_of(i)]) + small[pl.ds(i, 1)]
        v = v.astype(B16)
        QKV[i, half(b)] = v * jnp.where(i == 0, 0.125, 1.0).astype(B16)

        @pl.when(i == 2)
        def _():
            saves(b)[2].start()

    def attend(part, b):
        @pl.when(part == 0)
        def _():
            sp = dot_nt(pkey[...], QKV[0, half(b)])
            there = lax.broadcasted_iota(jnp.int32, sp.shape, 0) % 16 < 10
            SPRE[b] = jnp.where(there, sp, NEG)

        def pair(p):
            cols = pl.ds(pl.multiple_of(p * 128, 128), 128)
            q2, k2, v2 = QKV[0, half(b), cols], QKV[1, half(b), cols], QKV[2, half(b), cols]
            st = dot_nt(split_heads(k2), q2)
            probs, pres = [], []
            for e in range(2):
                sh = st[e * HALF : (e + 1) * HALF] + mask[b]
                sp = SPRE[b, pl.ds(pl.multiple_of(p * 32 + e * 16, 16), 16)]
                top = jnp.maximum(jnp.max(sh, axis=0, keepdims=True), jnp.max(sp, axis=0, keepdims=True))
                et, ep = jnp.exp(sh - top), jnp.exp(sp - top)
                inv = 1.0 / (jnp.sum(et, axis=0, keepdims=True) + jnp.sum(ep, axis=0, keepdims=True))
                probs.append((et * inv).astype(B16))
                pres.append((ep * inv).astype(B16))
            pr = jnp.concatenate(probs, axis=0)
            PROB[2 * b + p // 4, :, pl.ds(pl.multiple_of((p % 4) * HALF, HALF), HALF)] = pr
            PPRE[b, pl.ds(pl.multiple_of(p * 32, 32), 32)] = jnp.concatenate(pres, axis=0)
            ACC[half(b), cols] = dot_tn(pr, split_heads(v2))

        for p in range(4):
            pair(part * 4 + p)

        @pl.when(part == 1)
        def _():
            ATT[half(b)] = (ACC[half(b)] + dot_tn(PPRE[b], pval[...])).astype(B16)
            saves(b)[3].start()
            saves(b)[4].start()
            saves(b)[5].start()

    def mix(b):
        r = H[half(b)].astype(F32) + (dot_nn(ATT[half(b)], W[rows_of(3)]) + small[3:4])
        RES[half(b)] = r
        xhat, _ = whiten(r)
        A2[half(b)] = (xhat * small[12:13] + small[10:11]).astype(B16)
        saves(b)[6].start()
        saves(b)[7].start()

    def widen(j, b):
        x = dot_nn(A2[half(b)], W[rows_of(4 + j)]) + small[pl.ds(4 + j, 1)]
        x2 = x * x
        h = 0.5 + 0.5 * jnp.tanh(x * (GELU_C + (0.044715 * GELU_C) * x2))
        act = x * h
        ACT[j, half(b)] = act.astype(B16)
        GP[j, half(b)] = (h + act * (1.0 - h) * (2.0 * GELU_C + (6 * 0.044715 * GELU_C) * x2)).astype(B16)

        for cp in ffn_saves(b, j):
            cp.start()

    def narrow(b):
        v = RES[half(b)] + small[8:9]
        for j in range(4):
            v = v + dot_nn(ACT[j, half(b)], W[rows_of(8 + j)])
        OUT[half(b)] = v.astype(B16)

        @pl.when(s == 0)
        def _():
            cross(b).start()

        saves(b)[8].start()

    @pl.loop(0, NP + 5 + 2 * STAGES)
    def _(tick):
        @pl.when(tick < NP + 5)
        def _():
            g.step(tick, own)

            @pl.when(tick == 3)
            def _():
                prepare()

            @pl.when(tick >= 5)
            def _():
                g.complete(tick - 5)

                @pl.when(tick < 13)
                def _():
                    piece_out(tick - 5).start()

                @pl.when(tick == NP + 4)
                def _():
                    for k in range(8, NP):
                        piece_out(k).start()

        late = tick - (NP + 5)
        stage = (1 - s) * (tick - 5) + s * ((late + STAGES) % STAGES - STAGES * (late < 0).astype(jnp.int32))
        lo = s * (late // STAGES)
        hi = (1 - s) * 2 + s * (late // STAGES + 1)

        def when(i, body):
            @pl.when(stage == i)
            def _():
                pl.loop(lo, hi)(body)

        when(0, norm_in)

        @pl.when((stage >= 1) & (stage < 4))
        def _():
            pl.loop(lo, hi)(lambda b: project(stage - 1, b))

        @pl.when((stage >= 4) & (stage < 6))
        def _():
            pl.loop(lo, hi)(lambda b: attend(stage - 4, b))

        when(6, mix)

        @pl.when((stage >= 7) & (stage < 11))
        def _():
            pl.loop(lo, hi)(lambda b: widen(stage - 7, b))

        when(11, narrow)

    g.drain()
    packs_out()
    for cp in prep_saves():
        cp.wait()

    @pl.loop(0, NP)
    def _(k):
        piece_out(k).wait()

    @pl.loop(0, 2)
    def _(b):
        for cp in saves(b) + [cp for j in range(4) for cp in ffn_saves(b, j)]:
            cp.wait()

        @pl.when(s == 0)
        def _():
            cross(b).wait_send()


def forward_call(wq, wo, wf, wp, tokens, segs, gains, biases, aux, r_in, r_out):
    any_, vm = pl.BlockSpec(memory_space=pl.ANY), pl.BlockSpec(memory_space=pltpu.VMEM)
    n, d = tokens.shape
    kept = [
        ((NP * d, d), B16), ((n, d), B16), ((n, d), B16), ((n, d), B16), ((3, n, d), B16), ((4, n, d), B16),
        ((2, HALF, HALF), B16), ((n, d), B16), ((n, d), F32), ((n, d), B16), ((4, n, d), B16), ((4, n, d), B16),
    ]
    shared = [((16, d), F32), ((HALF, d), B16), ((HALF, d), B16), ((16, 512), F32)]
    dma = pltpu.SemaphoreType.DMA
    order = [0, 2, 3, 4, 5, 6, 7, 8, 9, 10, 11, 1]
    scratch = [kept[i] for i in order] + [((2, HALF, HALF), F32), ((n, d), F32)] + shared
    scratch += [((2, HALF, HALF), F32), ((16, 128), B16), ((16, 16, 128), B16), ((16, 16, 128), F32)]
    return pl.pallas_call(
        forward_kernel,
        out_shape=[jax.ShapeDtypeStruct(*k) for k in kept + shared],
        in_specs=[any_] * 5 + [vm] * 4 + [any_] * 2,
        out_specs=[any_] * len(kept + shared),
        scratch_shapes=[pltpu.VMEM(*v) for v in scratch]
        + [dma((NP,)), dma((NP, 20)), dma((NP, 16)), dma((NP, 8)), dma((NP, 4)), dma, dma((2,)), dma((2,)), dma((3, NP)), dma((2, 8)), dma((16,)), dma((16,)), dma((8,))],
        compiler_params=pltpu.CompilerParams(collective_id=0, has_side_effects=True, vmem_limit_bytes=62 << 20),
    )(wq, wo, wf, wp, tokens, segs, gains, biases, aux, r_in, r_out)


def prefix_rows(embed, in_bias, out_bias):
    in_bias = jnp.pad(in_bias, (0, 512)).reshape(1, 1024)
    return jnp.concatenate([embed, in_bias, out_bias.reshape(2, 1024), jnp.zeros((3, 1024), B16)])


SPLIT = 6
BACK_TICKS = 2 + 2 * SPLIT + NP + 6


def unwhiten(grad, xhat, rstd):
    return rstd * (
        grad
        - jnp.mean(grad, axis=-1, keepdims=True)
        - xhat * jnp.mean(grad * xhat, axis=-1, keepdims=True)
    )


def column_sum(v):
    return jnp.sum(v.astype(F32), axis=0, keepdims=True)


def backward_kernel(
    W_i, h_i, a1_i, qkv_i, prob_i, ppre_i, att_i, res_i, a2_i, gp_i, act_i, cot, r_out, small, pkey, pval,
    dh_o, oq, oo, of, op_, own_sums, KVB, HSUM,
    WG, H, A1, QKV, BIG, PPRE, ATT, RES, A2, GP, DM, DAT, DATT, DPP, DSP, ACC,
    RC, RY, RU, RD, RUS, RDS, RYS, T, SG, DKV, SB, RB, PF, PG, HP, HPR,
    wsem, lsem, osem, cs, cr, ys, yr, us, ur, ds_, dr, yss, ysr, xs, xr, hs, bs, br, ps, pr, hx, gs,
):
    s, d, z, y, c = place()

    def slot(k):
        return k + 8 * (1 - s) if k < 4 else k

    def fetch(ks):
        return [pltpu.make_async_copy(W_i.at[k], WG.at[slot(k)], wsem.at[k]) for k in ks]

    def begin(cps):
        for cp in cps:
            cp.start()

    def loads():
        pairs = [
            (a2_i, A2), (res_i, RES), (att_i, ATT), (qkv_i, QKV), (ppre_i, PPRE), (a1_i, A1), (h_i, H),
            (act_i, BIG), (prob_i, BIG), (cot, DM),
        ]
        return [pltpu.make_async_copy(a, b, lsem.at[i]) for i, (a, b) in enumerate(pairs)]

    L_A2, L_RES, L_ATT, L_QKV, L_PPRE, L_A1, L_H, L_ACT, L_PROB, L_COT = range(10)

    def begin_loads(which):
        begin([loads()[i] for i in which])

    pl.when(s == 1)(lambda: begin_loads((L_COT,)))

    def slope(j):
        return pltpu.make_async_copy(gp_i.at[j], GP.at[j], gs.at[j])

    for j in range(4):
        begin(fetch((8 + j,)) + [slope(j)])

    pl.when(s == 0)(lambda: begin_loads((L_ACT,)))
    SG[...] = jnp.zeros_like(SG)
    DKV[...] = jnp.zeros_like(DKV)
    SB[...] = jnp.zeros_like(SB)
    greet(s, d)

    def weights(ks):
        for cp in fetch(ks):
            cp.wait()

    def half(b):
        return pl.ds(pl.multiple_of(b * HALF, HALF), HALF)

    def weight(k):
        return WG[slot(k)].reshape(1024, 1024)

    def cross(b):
        return pltpu.make_async_remote_copy(
            H.at[half(b)], DM.at[half(b)], xs.at[b], xr.at[b], device_id=(1 - s, d), device_id_type=MESH
        )

    def dh_out(b):
        return pltpu.make_async_copy(H.at[half(b)], dh_o.at[half(b)], hs.at[b])

    def more(j):
        if j < 2:
            begin(fetch((4 + 2 * j, 5 + 2 * j)))
        elif j == 2:
            begin_loads((L_A2, L_RES))
            pl.when(s == 1)(lambda: begin(fetch((3,))))
        else:
            pl.when(s == 1)(lambda: begin_loads((L_QKV, L_PPRE, L_PROB)))

    def ffn_in(b):
        if b == 0:
            pl.when(s == 1)(lambda: loads()[L_COT].wait())
            pl.when(s == 0)(lambda: cross(0).wait_recv())
        for j in range(4):
            if b == 0:
                weights((8 + j,))
                slope(j).wait()
                more(j)
            GP[j, half(b)] = (dot_nt(DM[half(b)], weight(8 + j)) * GP[j, half(b)].astype(F32)).astype(B16)
        if b == 1:

            @pl.when(s == 0)
            def _():
                begin(fetch((3, 0, 1, 2)))

    def ffn_norm(b):
        @pl.when(b == 0)
        def _():
            weights((4, 5, 6, 7))
            loads()[L_A2].wait()
            loads()[L_RES].wait()
            begin_loads((L_ATT, L_A1, L_H))

            @pl.when(s == 0)
            def _():
                begin_loads((L_QKV, L_PPRE))

            @pl.when(s == 1)
            def _():
                begin(fetch((0, 1, 2)))

        grad = dot_nt(GP[0, half(b)], weight(4))
        for j in range(1, 4):
            grad = grad + dot_nt(GP[j, half(b)], weight(4 + j))
        xhat, rstd = whiten(RES[half(b)])
        SG[10:11] += jnp.sum(grad, axis=0, keepdims=True)
        SG[12:13] += jnp.sum(grad * xhat, axis=0, keepdims=True)
        res = DM[half(b)].astype(F32) + unwhiten(grad * small[12:13], xhat, rstd)
        RES[half(b)] = res
        DAT[half(b)] = res.astype(B16)

    def attn_out(b):
        @pl.when(b == 0)
        def _():
            weights((3,))
            for i in (L_ATT, L_QKV, L_PPRE):
                loads()[i].wait()

            loads()[L_PROB].wait()

        DATT[...] = dot_nt(DAT[half(b)], weight(3)).astype(B16)
        DPP[...] = dot_nt(pval[...], DATT[...])

    def attn_back(part, b):
        def pair(p):
            cols = pl.ds(pl.multiple_of(p * 128, 128), 128)
            q2, k2, v2 = QKV[0, half(b), cols], QKV[1, half(b), cols], QKV[2, half(b), cols]
            do2 = DATT[:, cols]
            pr = BIG[2 * b + p // 4, :, pl.ds(pl.multiple_of((p % 4) * HALF, HALF), HALF)]
            dp = dot_nt(split_heads(v2), do2)
            dss, pres = [], []
            for e in range(2):
                ph = pr[e * HALF : (e + 1) * HALF].astype(F32)
                dh = dp[e * HALF : (e + 1) * HALF]
                at = pl.ds(pl.multiple_of(p * 32 + e * 16, 16), 16)
                pp, dpp = PPRE[b, at].astype(F32), DPP[at]
                dot = jnp.sum(ph * dh, axis=0, keepdims=True) + jnp.sum(pp * dpp, axis=0, keepdims=True)
                dss.append((ph * (dh - dot)).astype(B16))
                pres.append((pp * (dpp - dot)).astype(B16))
            ds = jnp.concatenate(dss, axis=0)
            DSP[pl.ds(pl.multiple_of(p * 32, 32), 32)] = jnp.concatenate(pres, axis=0)
            left = lax.broadcasted_iota(jnp.int32, (HALF, 128), 1) < 64
            ACC[:, cols] = dot_tn(ds, split_heads(k2))
            dk = dot_nn(ds, q2)
            dv = dot_nn(pr, do2)
            QKV[1, half(b), cols] = jnp.where(left, dk[:HALF], dk[HALF:]).astype(B16)
            QKV[2, half(b), cols] = jnp.where(left, dv[:HALF], dv[HALF:]).astype(B16)

        for p in range(4):
            pair(part * 4 + p)

        @pl.when(part == 1)
        def _():
            def own_rows(full):
                out = jnp.zeros((16, 1024), F32)
                head = lax.broadcasted_iota(jnp.int32, (16, 1024), 1) // 64
                for i in range(16):
                    out = out + jnp.where(head == i, full[16 * i : 16 * i + 16], 0.0)
                return out

            DKV[0:16] += own_rows(dot_nn(DSP[...], QKV[0, half(b)]))
            DKV[16:32] += own_rows(dot_nn(PPRE[b], DATT[...]))
            QKV[0, half(b)] = ((ACC[...] + dot_tn(DSP[...], pkey[...])) * 0.125).astype(B16)

    def attn_norm(b):
        @pl.when(b == 0)
        def _():
            weights((0, 1, 2))
            loads()[L_A1].wait()
            loads()[L_H].wait()

        @pl.when((s == 1) & (b == 1))
        def _():
            loads()[L_ACT].start()

        grad = dot_nt(QKV[0, half(b)], weight(0))
        for i in range(1, 3):
            grad = grad + dot_nt(QKV[i, half(b)], weight(i))
        xhat, rstd = whiten(H[half(b)].astype(F32))
        SG[9:10] += jnp.sum(grad, axis=0, keepdims=True)
        SG[11:12] += jnp.sum(grad * xhat, axis=0, keepdims=True)
        H[half(b)] = (RES[half(b)] + unwhiten(grad * small[11:12], xhat, rstd)).astype(B16)

        @pl.when(s == 1)
        def _():
            cross(b).start()

        dh_out(b).start()

    def grad_proj(j):
        if j == 0:
            loads()[L_ACT].wait()
            pl.when(s == 0)(lambda: cross(1).wait_recv())
        for i in range(4):
            cols = [BIG[i, :, 256 * q + 64 * j : 256 * q + 64 * j + 64] for q in range(4)]
            part = dot_tn(jnp.concatenate(cols, axis=1), DM[...])
            WG[8 * s + j, i] = part.astype(B16).reshape(2, 2, 64, 1024)
        if j == 3:
            pl.when(s == 0)(lambda: loads()[L_PROB].start())

    def put(k, a, v):
        for i in range(2):
            part = dot_tn(a[:, 512 * i : 512 * (i + 1)], v[...])
            WG[k, 2 * i : 2 * i + 2] = part.astype(B16).reshape(2, 2, 2, 64, 1024)

    def grad_fc(j):
        put(4 + j, A2, GP.at[j])

    def grad_out():
        put(slot(3), ATT, DAT)

    def grad_qkv(i):
        put(i + 8 * (1 - s), A1, QKV.at[i])

    send_sums, sums_in, sums_out = to_all(lambda to: SB.at[to], RB, bs, br)
    send_pref, pref_in, pref_out = to_all(lambda to: PF, PG, ps, pr)

    def r_out_in():
        return [pltpu.make_async_copy(r_out.at[:, pl.ds(1024 * i, 1024)], BIG.at[i], hx.at[i]) for i in range(2)]

    def hidden_across():
        return pltpu.make_async_remote_copy(HP, HPR, hx.at[2], hx.at[3], device_id=(1 - s, d), device_id_type=MESH)

    def small_first():
        for cp in r_out_in():
            cp.start()
        for i in range(3):
            SG[i : i + 1] = column_sum(QKV[i])
        SG[3:4] = column_sum(DAT[...])
        for j in range(4):
            SG[4 + j : 5 + j] = column_sum(GP[j])
        SG[8:9] = column_sum(DM[...])
        for i in range(16):
            for n in range(13):
                m = 11 * i + n
                row, at = (m // 16, 128 * (m % 16 // 2)) if n < 11 else (n, 128 * (i // 2))
                SB[i, n : n + 1] = SG[row : row + 1, at : at + 128]
            SB[i, 16:32] = DKV[16 * (i // 8) : 16 * (i // 8) + 16, 128 * (i % 8) : 128 * (i % 8) + 128]
        send_sums()
        RB[d] = SB[d]

    def small_second():
        sums_in()
        total = RB[0]
        for i in range(1, 16):
            total = total + RB[i]
        row = lax.broadcasted_iota(jnp.int32, (16, 128), 0)
        odd = jnp.where(row < 11, d + row, d) % 2 == 1
        own_sums[...] = jnp.where(odd, pltpu.roll(total[:16], 64, 1), total[:16])
        PF[...] = total[16:].astype(B16)
        send_pref()
        PG[d] = PF[...]

    def small_third():
        pref_in()
        for i in range(16):
            KVB[:, 128 * i : 128 * i + 128] = PG[i]
        for cp in r_out_in():
            cp.wait()
        HP[...] = dot_nt(KVB[:, :1024], BIG[0]) + dot_nt(KVB[:, 1024:], BIG[1])
        hidden_across().start()

    def small_last():
        hidden_across().wait()
        HSUM[...] = HP[...] + HPR[...]

    def held(r):
        a = r // 4
        return ((2 - a) * (1 - a) // 2) * (r + 8 * s) + a * (2 - a) * r + (a * (a - 1) // 2) * (11 - r + 8 * (1 - s))

    def across_c(r):
        return pltpu.make_async_remote_copy(
            WG.at[held(r), :, :, 1 - c], RC.at[r % 4], cs.at[r], cr.at[r],
            device_id=(s, z * 4 + y * 2 + 1 - c), device_id_type=MESH,
        )

    def across_y(r):
        return pltpu.make_async_remote_copy(
            WG.at[held(r), :, 1 - y, c, :, pl.ds(0, MAIN)], RY.at[r % 4], ys.at[r], yr.at[r],
            device_id=(s, z * 4 + (1 - y) * 2 + c), device_id_type=MESH,
        )

    def up(r, i):
        return pltpu.make_async_remote_copy(
            WG.at[held(r), i, y, c], RU.at[r % 7, i - 1], us.at[r, i - 1], ur.at[r, i - 1],
            device_id=(s, (z + 1) * 4 + y * 2 + c), device_id_type=MESH,
        )

    def down(r, i):
        return pltpu.make_async_remote_copy(
            WG.at[held(r), i, y, c], RD.at[r % 7, i], ds_.at[r, i], dr.at[r, i],
            device_id=(s, (z - 1) * 4 + y * 2 + c), device_id_type=MESH,
        )

    def strip_up(r, i):
        return pltpu.make_async_remote_copy(
            WG.at[held(r), i, 1 - y, c, :, pl.ds(MAIN, 1024 - MAIN)], RUS.at[r % 7, i - 1], us.at[r, 2 + i], ur.at[r, 2 + i],
            device_id=(s, (z + 1) * 4 + y * 2 + c), device_id_type=MESH,
        )

    def strip_down(r, i):
        return pltpu.make_async_remote_copy(
            WG.at[held(r), i, 1 - y, c, :, pl.ds(MAIN, 1024 - MAIN)], RDS.at[r % 7, i], ds_.at[r, 3 + i], dr.at[r, 3 + i],
            device_id=(s, (z - 1) * 4 + y * 2 + c), device_id_type=MESH,
        )

    def strip_y(r):
        return pltpu.make_async_remote_copy(
            WG.at[held(r), z, 1 - y, c, :, pl.ds(MAIN, 1024 - MAIN)], RYS.at[r % 4], yss.at[r], ysr.at[r],
            device_id=(s, z * 4 + (1 - y) * 2 + c), device_id_type=MESH,
        )

    def each_out(r, act):
        k = held(r)
        src = T.at[r % 2]

        @pl.when(r < 4)
        def _():
            act(pltpu.make_async_copy(src, op_.at[0, pl.ds(pl.multiple_of(64 * r, 64), 64)], osem.at[r]))

        @pl.when((r >= 4) & (r < 8))
        def _():
            act(pltpu.make_async_copy(src, of.at[0, :, pl.ds(pl.multiple_of(1024 * (r - 4), 1024), 1024)], osem.at[r]))

        @pl.when(r == 8)
        def _():
            act(pltpu.make_async_copy(src, oo.at[0], osem.at[r]))

        @pl.when(r > 8)
        def _():
            act(pltpu.make_async_copy(src, oq.at[0, :, pl.ds(pl.multiple_of(1024 * (11 - r), 1024), 1024)], osem.at[r]))

    def start(cp):
        cp.start()

    def add(k, i, j, other):
        WG[k, i, j, c] = (WG[k, i, j, c].astype(F32) + other.astype(F32)).astype(B16)

    def add_main(k, i, other):
        WG[k, i, y, c, :, :MAIN] = (WG[k, i, y, c, :, :MAIN].astype(F32) + other.astype(F32)).astype(B16)

    def add_strip(k, i, *others):
        total = WG[k, i, 1 - y, c, :, MAIN:].astype(F32)
        for other in others:
            total = total + other.astype(F32)
        WG[k, i, 1 - y, c, :, MAIN:] = total.astype(B16)

    def live(r):
        return (r >= 0) & (r < NP)

    def scatter_step(t):
        @pl.when(live(t))
        def _():
            across_c(t).start()

        @pl.when(live(t - 1))
        def _():
            r = t - 1
            k = held(r)
            across_c(r).wait_recv()

            @pl.loop(0, 4)
            def _(i):
                add(k, i, 1 - y, RC[r % 4, i, 1 - y])

            across_y(r).start()

            @pl.loop(0, 4)
            def _(i):
                add(k, i, y, RC[r % 4, i, y])

        for q in (1, 2, 3):
            n = 4 - q

            @pl.when(live(t - 2 - q))
            def _():
                r = t - 2 - q
                k = held(r)

                @pl.when(z == q)
                def _():
                    for i in range(3, q - 1, -1):
                        up(r, i).wait_recv()
                        if i > q:
                            add(k, i, y, RU[r % 7, i - 1])
                            up(r, i).start()
                        strip_up(r, i).wait_recv()
                        if i > q:
                            add_strip(k, i, RUS[r % 7, i - 1])
                            strip_up(r, i).start()

                @pl.when(z == 3 - q)
                def _():
                    for i in range(n):
                        down(r, i).wait_recv()
                        if i < n - 1:
                            add(k, i, y, RD[r % 7, i])
                            down(r, i).start()
                        strip_down(r, i).wait_recv()
                        if i < n - 1:
                            add_strip(k, i, RDS[r % 7, i])
                            strip_down(r, i).start()

        @pl.when(live(t - 2))
        def _():
            r = t - 2
            k = held(r)
            across_y(r).wait_recv()

            @pl.loop(0, 4)
            def _(i):
                add_main(k, i, RY[r % 4, i])

            @pl.when(z == 0)
            def _():
                for i in (3, 2, 1):
                    up(r, i).start()
                    strip_up(r, i).start()

            @pl.when(z == 3)
            def _():
                for i in (0, 1, 2):
                    down(r, i).start()
                    strip_down(r, i).start()

        @pl.when(live(t - 5))
        def _():
            r = t - 5
            k = held(r)

            @pl.when(z > 0)
            def _():
                add_strip(k, z, RUS[r % 7, z - 1])

            @pl.when(z < 3)
            def _():
                add_strip(k, z, RDS[r % 7, z])

            strip_y(r).start()

            @pl.when(r >= 2)
            def _():
                each_out(r - 2, lambda cp: cp.wait())

            T[r % 2] = WG[k, z, y, c].astype(F32)

            @pl.when(z > 0)
            def _():
                T[r % 2] += RU[r % 7, z - 1].astype(F32)

            @pl.when(z < 3)
            def _():
                T[r % 2] += RD[r % 7, z].astype(F32)

        @pl.when(live(t - 6))
        def _():
            r = t - 6
            strip_y(r).wait_recv()
            T[r % 2, :, MAIN:] += RYS[r % 4].astype(F32)
            each_out(r, start)

    ffn_in(0)
    greeted()

    @pl.loop(1, BACK_TICKS)
    def _(tick):
        turn = tick // SPLIT

        @pl.when(tick == 2 * (1 - s) + SPLIT * s)
        def _():
            ffn_in(1)

        def when(i, at0, at1, body):
            early = (1 - s) * at0 + s * i
            late = (1 - s) * at1 + s * (SPLIT + i)

            @pl.when((tick == early) | (tick == late))
            def _():
                body((tick == late).astype(jnp.int32))

        when(1, 3, 4, ffn_norm)
        when(2, 5, 7, attn_out)
        first = (tick - 3) % SPLIT * s + (tick - 5) % 2 * (1 - s)

        @pl.when(((s == 0) & (tick >= 5) & (tick < 9)) | ((s == 1) & (tick < 2 * SPLIT) & (first < 2)))
        def _():
            attn_back(first, (1 - s) * ((tick - 5) // 2) + s * turn)

        when(5, 9, 10, attn_norm)
        r = tick - 1 - (2 * SPLIT - 1) * s

        for j in range(4):
            pl.when(r == j)(lambda j=j: grad_proj(j))

        @pl.when((r >= 4) & (r < 8))
        def _():
            grad_fc(r - 4)

        @pl.when(r == 8)
        def _():
            grad_out()

        @pl.when((r > 8) & (r < 12))
        def _():
            grad_qkv(11 - r)

        scatter_step(r)
        for at, body in ((9, small_first), (12, small_second), (15, small_third)):
            pl.when(r == at)(body)

    @pl.loop(0, NP)
    def _(r):
        @pl.when(r >= NP - 2)
        def _():
            each_out(r, lambda cp: cp.wait())

        across_c(r).wait_send()
        across_y(r).wait_send()
        strip_y(r).wait_send()
        for q in range(3):

            @pl.when(z == q)
            def _():
                for i in range(q + 1, 4):
                    up(r, i).wait_send()
                    strip_up(r, i).wait_send()

            @pl.when(z == q + 1)
            def _():
                for i in range(q + 1):
                    down(r, i).wait_send()
                    strip_down(r, i).wait_send()

    small_last()
    sums_out()
    pref_out()

    @pl.loop(0, 2)
    def _(b):
        dh_out(b).wait()

        @pl.when(s == 1)
        def _():
            cross(b).wait_send()


def backward_call(kept, cot, r_out, small, pkey, pval):
    W, h, a1, qkv, prob, ppre, att, res, a2, gp, act = kept
    any_, vm = pl.BlockSpec(memory_space=pl.ANY), pl.BlockSpec(memory_space=pltpu.VMEM)
    n, d = h.shape
    dma = pltpu.SemaphoreType.DMA
    wide = (4, 2, 2, 64, d)
    outs = [
        ((n, d), B16), ((1, 64, 3 * d), F32), ((1, 64, d), F32), ((1, 64, 4 * d), F32), ((1, 256, d), F32),
        ((16, 128), F32), ((16, 2 * d), B16), ((16, 512), F32),
    ]
    scratch = [
        ((NP,) + wide, B16), ((n, d), B16), ((n, d), B16), ((3, n, d), B16), ((4, n, d), B16), ((2, HALF, HALF), B16), ((n, d), B16),
        ((n, d), F32), ((n, d), B16), ((4, n, d), B16), ((n, d), B16), ((n, d), B16), ((HALF, d), B16), ((HALF, HALF), F32),
        ((HALF, HALF), B16), ((HALF, d), F32),
        ((4, 4, 2, 64, d), B16), ((4, 4, 64, MAIN), B16), ((7, 3, 64, d), B16), ((7, 3, 64, d), B16),
        ((7, 3, 64, d - MAIN), B16), ((7, 3, 64, d - MAIN), B16), ((4, 64, d - MAIN), B16), ((2, 64, d), F32),
        ((16, d), F32), ((32, d), F32), ((16, 32, 128), F32), ((16, 32, 128), F32), ((16, 128), B16), ((16, 16, 128), B16),
        ((16, 512), F32), ((16, 512), F32),
    ]
    return pl.pallas_call(
        backward_kernel,
        out_shape=[jax.ShapeDtypeStruct(*o) for o in outs],
        in_specs=[any_] * 13 + [vm] * 3,
        out_specs=[any_] * 5 + [vm] * 3,
        scratch_shapes=[pltpu.VMEM(*v) for v in scratch] + [dma((NP,))] * 7 + [dma((NP, 6))] * 4 + [dma((NP,))] * 2 + [dma((2,))] * 3 + [dma((16,))] * 4 + [dma((4,))] * 2,
        compiler_params=pltpu.CompilerParams(collective_id=1, has_side_effects=True, vmem_limit_bytes=64 << 20),
    )(W.reshape((NP,) + wide), h, a1, qkv, prob, ppre, att, res, a2, gp, act, cot, r_out, small, pkey, pval)


def finish_kernel(
    o0, o1, o2, o3, o4, o5, hid, kvb, hsum, aux, r_in, sums,
    c0, c1, c2, c3, c4, c5, g_embed, g_in, g_in_bias, g_out, g_out_bias, g_gains, g_bias,
    G_IN, G_OUT, M0, M1, M2, M3, M4, M5, R_IN, sem,
):
    held = (M0, M1, M2, M3, M4, M5)
    here = [pltpu.make_async_copy(a, m, sem.at[i]) for i, (a, m) in enumerate(zip((o0, o1, o2, o3, o4, o5), held))]
    away = [pltpu.make_async_copy(m, c, sem.at[8 + i]) for i, (m, c) in enumerate(zip(held, (c0, c1, c2, c3, c4, c5)))]
    for cp in here:
        cp.start()
    weight_in = pltpu.make_async_copy(r_in, R_IN, sem.at[14])
    weight_in.start()
    h = hid[...]
    kv = kvb[...]
    G_OUT[...] = dot_tn(h.astype(B16), kv)
    out_cp = pltpu.make_async_copy(G_OUT, g_out, sem.at[6])
    out_cp.start()
    g_out_bias[...] = column_sum(kv)
    for cp, out in zip(here, away):
        cp.wait()
        out.start()
    dp = (hsum[...] * (1.0 - h * h)).astype(B16)
    G_IN[...] = dot_tn(aux[...], dp)
    in_cp = pltpu.make_async_copy(G_IN, g_in, sem.at[7])
    in_cp.start()
    g_in_bias[...] = column_sum(dp)
    weight_in.wait()
    g_embed[...] = dot_nt(dp, R_IN[...])[:10]
    g_gains[0] = sums[11:13, :64]
    for i in range(11):
        g_bias[:, 64 * i : 64 * i + 64] = sums[i : i + 1, :64]
    for cp in away + [out_cp, in_cp]:
        cp.wait()


def finish_call(large, hid, kvb, hsum, aux, r_in, sums):
    any_, vm = pl.BlockSpec(memory_space=pl.ANY), pl.BlockSpec(memory_space=pltpu.VMEM)
    d = r_in.shape[0]
    outs = [jax.ShapeDtypeStruct(x.shape, x.dtype) for x in large]
    outs += [jax.ShapeDtypeStruct(x, F32) for x in ((10, d), (d, 512), (1, 512), (512, 2 * d), (1, 2 * d), (1, 2, 64), (1, 704))]
    return pl.pallas_call(
        finish_kernel,
        out_shape=outs,
        in_specs=[any_] * 6 + [vm] * 4 + [any_, vm],
        out_specs=[any_] * 6 + [vm, any_, vm, any_, vm, vm, vm],
        scratch_shapes=[pltpu.VMEM((d, 512), F32), pltpu.VMEM((512, 2 * d), F32)]
        + [pltpu.VMEM(x.shape, x.dtype) for x in large]
        + [pltpu.VMEM(r_in.shape, r_in.dtype), pltpu.SemaphoreType.DMA((15,))],
        compiler_params=pltpu.CompilerParams(vmem_limit_bytes=63 << 20),
    )(*large, hid, kvb, hsum, aux, r_in, sums)


def on_device(
    tokens,
    segment_ids,
    cotangent,
    w_qkv,
    w_attn_out,
    w_fc,
    w_proj,
    gains,
    biases,
    prefix_embed,
    reparam_in,
    reparam_in_bias,
    reparam_out,
    reparam_out_bias,
):
    aux = prefix_rows(prefix_embed, reparam_in_bias, reparam_out_bias)
    kept = forward_call(w_qkv, w_attn_out, w_fc, w_proj, tokens, segment_ids, gains, biases, aux, reparam_in, reparam_out)
    small, pkey, pval, hid = kept[12:]
    *large, sums, kvb, hsum = backward_call(kept[:1] + kept[2:12], cotangent, reparam_out, small, pkey, pval)
    done = finish_call([kept[1]] + large, hid, kvb, hsum, aux, reparam_in, sums)
    return (
        done[0][None],
        done[1][None],
        *done[2:6],
        done[11],
        done[12],
        done[6],
        done[7],
        done[8][0],
        done[9],
        done[10][0],
    )


def passed_along(shard, axis, by):
    size = lax.axis_size(axis)
    pairs = [(i, i + by) for i in range(size) if 0 <= i + by < size]
    return lax.ppermute(shard, axis, pairs)


def norm_rows(v, gain, shift):
    mean = jnp.mean(v, axis=-1, keepdims=True)
    cent = v - mean
    var = jnp.mean(cent * cent, axis=-1, keepdims=True)
    return cent * lax.rsqrt(var + EPS) * gain + shift


def gelu_tanh(v):
    return jax.nn.gelu(v, approximate=True)


def forward_layer(h_b, segs, pkey, pval, params):
    w_q, w_o, w_f, w_p, gain_pair, bias_all = params
    width = w_o.shape[0]
    length = h_b.shape[0]
    heads, head_dim = (pkey.shape[1], pkey.shape[2])
    scale = 1.0 / math.sqrt(head_dim)
    gain_f = gain_pair.astype(jnp.float32)
    bias_f = bias_all.astype(jnp.float32)
    hf = h_b.astype(jnp.float32)
    a1b = norm_rows(hf, gain_f[0], bias_f[9 * width : 10 * width]).astype(jnp.bfloat16)
    qkv_b = (jnp.dot(a1b, w_q, preferred_element_type=jnp.float32) + bias_f[: 3 * width]).astype(
        jnp.bfloat16
    )
    split = qkv_b.reshape(length, 3, heads, head_dim)
    query, keys, values = (split[:, 0], split[:, 1], split[:, 2])
    s_tok = jnp.einsum("lhe,mhe->hlm", query, keys, preferred_element_type=jnp.float32) * scale
    s_pre = jnp.einsum("lhe,phe->hlp", query, pkey, preferred_element_type=jnp.float32) * scale
    place = jnp.arange(length)
    allowed = (segs[:, None] == segs[None, :]) & (place[None, :] <= place[:, None])
    s_tok = jnp.where(allowed[None], s_tok, NEG)
    top = jnp.maximum(
        jnp.max(s_tok, axis=-1, keepdims=True), jnp.max(s_pre, axis=-1, keepdims=True)
    )
    e_tok = jnp.exp(s_tok - top)
    e_pre = jnp.exp(s_pre - top)
    total = jnp.sum(e_tok, axis=-1, keepdims=True) + jnp.sum(e_pre, axis=-1, keepdims=True)
    p_tok = e_tok / total
    p_pre = e_pre / total
    mixed = jnp.einsum(
        "hlm,mhe->lhe", p_tok.astype(jnp.bfloat16), values, preferred_element_type=jnp.float32
    ) + jnp.einsum(
        "hlp,phe->lhe", p_pre.astype(jnp.bfloat16), pval, preferred_element_type=jnp.float32
    )
    attn_b = mixed.reshape(length, width).astype(jnp.bfloat16)
    resid = hf + (
        jnp.dot(attn_b, w_o, preferred_element_type=jnp.float32) + bias_f[3 * width : 4 * width]
    )
    a2b = norm_rows(resid, gain_f[1], bias_f[10 * width : 11 * width]).astype(jnp.bfloat16)
    pre_act = jnp.dot(a2b, w_f, preferred_element_type=jnp.float32) + bias_f[4 * width : 8 * width]
    act_b = gelu_tanh(pre_act).astype(jnp.bfloat16)
    result = resid + (
        jnp.dot(act_b, w_p, preferred_element_type=jnp.float32) + bias_f[8 * width : 9 * width]
    )
    return (result, (hf, a1b, qkv_b, p_tok, p_pre, attn_b, resid, a2b, pre_act, act_b))


def backward_ffn(grad_out, keep, params):
    w_q, w_o, w_f, w_p, gain_pair, bias_all = params
    hf, a1b, qkv_b, p_tok, p_pre, attn_b, resid, a2b, pre_act, act_b = keep
    width = w_o.shape[0]
    gain_f = gain_pair.astype(jnp.float32)
    bias_f = bias_all.astype(jnp.float32)
    dm_b = grad_out.astype(jnp.bfloat16)
    grad_wp = jnp.einsum("lf,ld->fd", act_b, dm_b, preferred_element_type=jnp.float32)
    grad_bp = jnp.sum(dm_b.astype(jnp.float32), axis=0)
    d_act = jnp.dot(dm_b, w_p.T, preferred_element_type=jnp.float32)
    dpre_b = jax.vjp(gelu_tanh, pre_act)[1](d_act)[0].astype(jnp.bfloat16)
    grad_wf = jnp.einsum("ld,lf->df", a2b, dpre_b, preferred_element_type=jnp.float32)
    grad_bf = jnp.sum(dpre_b.astype(jnp.float32), axis=0)
    d_a2 = jnp.dot(dpre_b, w_f.T, preferred_element_type=jnp.float32)
    norm_back = jax.vjp(norm_rows, resid, gain_f[1], bias_f[10 * width : 11 * width])[1]
    d_resid_norm, grad_g2, grad_c2 = norm_back(d_a2)
    d_resid = grad_out + d_resid_norm
    return (d_resid, (grad_wf, grad_wp), (grad_bf, grad_bp, grad_g2, grad_c2))


def backward_attn(d_resid, keep, pkey, pval, params):
    w_q, w_o, w_f, w_p, gain_pair, bias_all = params
    hf, a1b, qkv_b, p_tok, p_pre, attn_b, resid, a2b, pre_act, act_b = keep
    width = w_o.shape[0]
    length = hf.shape[0]
    heads, head_dim = (pkey.shape[1], pkey.shape[2])
    prefix_len = pkey.shape[0]
    scale = 1.0 / math.sqrt(head_dim)
    gain_f = gain_pair.astype(jnp.float32)
    bias_f = bias_all.astype(jnp.float32)
    split = qkv_b.reshape(length, 3, heads, head_dim)
    query, keys, values = (split[:, 0], split[:, 1], split[:, 2])
    dat_b = d_resid.astype(jnp.bfloat16)
    grad_wo = jnp.einsum("ld,le->de", attn_b, dat_b, preferred_element_type=jnp.float32)
    grad_bo = jnp.sum(dat_b.astype(jnp.float32), axis=0)
    dattn_b = jnp.dot(dat_b, w_o.T, preferred_element_type=jnp.float32).astype(jnp.bfloat16)
    dattn_b = dattn_b.reshape(length, heads, head_dim)
    dp_tok = jnp.einsum("lhe,mhe->hlm", dattn_b, values, preferred_element_type=jnp.float32)
    dp_pre = jnp.einsum("lhe,phe->hlp", dattn_b, pval, preferred_element_type=jnp.float32)
    row_dot = jnp.sum(p_tok * dp_tok, axis=-1, keepdims=True) + jnp.sum(
        p_pre * dp_pre, axis=-1, keepdims=True
    )
    ds_tok = (p_tok * (dp_tok - row_dot)).astype(jnp.bfloat16)
    ds_pre = (p_pre * (dp_pre - row_dot)).astype(jnp.bfloat16)
    d_query = (
        jnp.einsum("hlm,mhe->lhe", ds_tok, keys, preferred_element_type=jnp.float32)
        + jnp.einsum("hlp,phe->lhe", ds_pre, pkey, preferred_element_type=jnp.float32)
    ) * scale
    d_keys = jnp.einsum("hlm,lhe->mhe", ds_tok, query, preferred_element_type=jnp.float32) * scale
    d_values = jnp.einsum(
        "hlm,lhe->mhe", p_tok.astype(jnp.bfloat16), dattn_b, preferred_element_type=jnp.float32
    )
    grad_pkey = (
        jnp.einsum("hlp,lhe->phe", ds_pre, query, preferred_element_type=jnp.float32) * scale
    )
    grad_pval = jnp.einsum(
        "hlp,lhe->phe", p_pre.astype(jnp.bfloat16), dattn_b, preferred_element_type=jnp.float32
    )
    dqkv_b = (
        jnp.stack([d_query, d_keys, d_values], axis=1)
        .reshape(length, 3 * width)
        .astype(jnp.bfloat16)
    )
    grad_wq = jnp.einsum("ld,lc->dc", a1b, dqkv_b, preferred_element_type=jnp.float32)
    grad_bq = jnp.sum(dqkv_b.astype(jnp.float32), axis=0)
    d_a1 = jnp.dot(dqkv_b, w_q.T, preferred_element_type=jnp.float32)
    norm_back_first = jax.vjp(norm_rows, hf, gain_f[0], bias_f[9 * width : 10 * width])[1]
    d_in_norm, grad_g1, grad_c1 = norm_back_first(d_a1)
    d_input = d_resid + d_in_norm
    grad_prefix = jnp.concatenate(
        [grad_pkey.reshape(prefix_len, width), grad_pval.reshape(prefix_len, width)], axis=1
    )
    return (d_input, (grad_wq, grad_wo), (grad_bq, grad_bo, grad_g1, grad_c1), grad_prefix)


def assemble(ffn_mats, ffn_small, attn_mats, attn_small):
    grad_bf, grad_bp, grad_g2, grad_c2 = ffn_small
    grad_bq, grad_bo, grad_g1, grad_c1 = attn_small
    grad_gains = jnp.stack([grad_g1, grad_g2])
    grad_bias = jnp.concatenate([grad_bq, grad_bo, grad_bf, grad_bp, grad_c1, grad_c2])
    return (attn_mats[0], attn_mats[1], ffn_mats[0], ffn_mats[1], grad_gains, grad_bias)


def on_device_general(
    tokens,
    segment_ids,
    cotangent,
    w_qkv,
    w_attn_out,
    w_fc,
    w_proj,
    gains,
    biases,
    prefix_embed,
    reparam_in,
    reparam_in_bias,
    reparam_out,
    reparam_out_bias,
):
    section = lax.axis_index("section")
    micro, row_len = segment_ids.shape
    width = tokens.shape[1]
    prefix_len = prefix_embed.shape[0]
    head_dim = width // HEADS
    gathered = (
        lax.all_gather(w_qkv, "dp", axis=1, tiled=True),
        lax.all_gather(w_attn_out, "dp", axis=1, tiled=True),
        lax.all_gather(w_fc, "dp", axis=1, tiled=True),
        lax.all_gather(w_proj, "dp", axis=1, tiled=True),
        lax.all_gather(gains, "dp", axis=2, tiled=True),
        lax.all_gather(biases, "dp", axis=1, tiled=True),
    )
    params = tuple((item[0] for item in gathered))
    pre_hidden = jnp.dot(
        prefix_embed, reparam_in, preferred_element_type=jnp.float32
    ) + reparam_in_bias.astype(jnp.float32)
    hidden = jnp.tanh(pre_hidden)
    hidden_b = hidden.astype(jnp.bfloat16)
    prefix_kv = (
        jnp.dot(hidden_b, reparam_out, preferred_element_type=jnp.float32)
        + reparam_out_bias.astype(jnp.float32)
    ).astype(jnp.bfloat16)
    pkey = prefix_kv[:, :width].reshape(prefix_len, HEADS, head_dim)
    pval = prefix_kv[:, width:].reshape(prefix_len, HEADS, head_dim)
    token_rows = tokens.reshape(micro, row_len, width)
    cot_rows = cotangent.reshape(micro, row_len, width)
    received = jnp.zeros((row_len, width), jnp.bfloat16)
    outputs = jnp.zeros((micro, row_len, width), jnp.bfloat16)
    stored = []
    for tick in range(micro + 1):
        index = tick - section
        active = (index >= 0) & (index < micro)
        slot = jnp.clip(index, 0, micro - 1)
        segs = segment_ids[slot]
        h_b = jnp.where(section == 0, token_rows[slot], received)
        result, keep = forward_layer(h_b, segs, pkey, pval, params)
        result_b = result.astype(jnp.bfloat16)
        outputs = jnp.where(active, outputs.at[slot].set(result_b), outputs)
        stored.append(keep)
        if tick < micro:
            received = passed_along(result_b, "section", 1)
    regathered = (
        lax.all_gather(w_qkv, "dp", axis=1, tiled=True),
        lax.all_gather(w_attn_out, "dp", axis=1, tiled=True),
        lax.all_gather(w_fc, "dp", axis=1, tiled=True),
        lax.all_gather(w_proj, "dp", axis=1, tiled=True),
        lax.all_gather(gains, "dp", axis=2, tiled=True),
        lax.all_gather(biases, "dp", axis=1, tiled=True),
    )
    params_back = tuple((item[0] for item in regathered))
    stacked = jax.tree.map(lambda *items: jnp.stack(items), *stored)
    coming = jnp.zeros((row_len, width), jnp.bfloat16)
    in_grads = jnp.zeros((micro, row_len, width), jnp.bfloat16)
    grad_total = None
    prefix_total = None
    for tick in range(micro + 1):
        index = micro - tick - section
        active = (index >= 0) & (index < micro)
        slot = jnp.clip(index, 0, micro - 1)
        segs = segment_ids[slot]
        saved = jax.tree.map(lambda item: item[slot + section], stacked)
        grad_out = jnp.where(
            section == 1, cot_rows[slot].astype(jnp.float32), coming.astype(jnp.float32)
        )
        keep = saved
        d_resid, ffn_mats, ffn_small = backward_ffn(grad_out, keep, params_back)
        ffn_mats = jax.tree.map(
            lambda item: jnp.where(active, item, jnp.zeros_like(item)), ffn_mats
        )
        ffn_small = jax.tree.map(
            lambda item: jnp.where(active, item, jnp.zeros_like(item)), ffn_small
        )
        d_input, attn_mats, attn_small, grad_prefix = backward_attn(
            d_resid, keep, pkey, pval, params_back
        )
        attn_mats = jax.tree.map(
            lambda item: jnp.where(active, item, jnp.zeros_like(item)), attn_mats
        )
        attn_small = jax.tree.map(
            lambda item: jnp.where(active, item, jnp.zeros_like(item)), attn_small
        )
        grad_prefix = jnp.where(active, grad_prefix, jnp.zeros_like(grad_prefix))
        grads = assemble(ffn_mats, ffn_small, attn_mats, attn_small)
        if grad_total is None:
            grad_total = grads
            prefix_total = grad_prefix
        else:
            grad_total = jax.tree.map(lambda left, right: left + right, grad_total, grads)
            prefix_total = prefix_total + grad_prefix
        d_input_b = d_input.astype(jnp.bfloat16)
        in_grads = jnp.where(active, in_grads.at[slot].set(d_input_b), in_grads)
        if tick < micro:
            coming = passed_along(d_input_b, "section", -1)
    lifted = tuple((item[None] for item in grad_total))
    weight_grads = (
        lax.psum_scatter(lifted[0], "dp", scatter_dimension=1, tiled=True),
        lax.psum_scatter(lifted[1], "dp", scatter_dimension=1, tiled=True),
        lax.psum_scatter(lifted[2], "dp", scatter_dimension=1, tiled=True),
        lax.psum_scatter(lifted[3], "dp", scatter_dimension=1, tiled=True),
        lax.psum_scatter(lifted[4], "dp", scatter_dimension=2, tiled=True),
        lax.psum_scatter(lifted[5], "dp", scatter_dimension=1, tiled=True),
    )
    prefix_grad = lax.psum(prefix_total, "dp")
    prefix_grad_b = prefix_grad.astype(jnp.bfloat16)
    grad_reparam_out = jnp.einsum(
        "pr,pc->rc", hidden_b, prefix_grad_b, preferred_element_type=jnp.float32
    )
    grad_reparam_out_bias = jnp.sum(prefix_grad_b.astype(jnp.float32), axis=0)
    hidden_part = jnp.dot(prefix_grad_b, reparam_out.T, preferred_element_type=jnp.float32)
    hidden_grad = lax.psum(hidden_part, "section")
    dpre_hidden_b = (hidden_grad * (1.0 - hidden * hidden)).astype(jnp.bfloat16)
    grad_reparam_in = jnp.einsum(
        "pd,pr->dr", prefix_embed, dpre_hidden_b, preferred_element_type=jnp.float32
    )
    grad_reparam_in_bias = jnp.sum(dpre_hidden_b.astype(jnp.float32), axis=0)
    grad_prefix_embed = jnp.dot(dpre_hidden_b, reparam_in.T, preferred_element_type=jnp.float32)
    layer_outs = outputs.reshape(1, micro * row_len, width)
    input_grads = in_grads.reshape(1, micro * row_len, width)
    return (
        layer_outs,
        input_grads,
        weight_grads[0],
        weight_grads[1],
        weight_grads[2],
        weight_grads[3],
        weight_grads[4],
        weight_grads[5],
        grad_prefix_embed,
        grad_reparam_in,
        grad_reparam_in_bias,
        grad_reparam_out,
        grad_reparam_out_bias,
    )


def solution(mesh):
    return jax.shard_map(
        on_device if mesh.shape["dp"] == 16 else on_device_general,
        mesh=mesh,
        in_specs=(
            P("dp", None),
            P("dp", None),
            P("dp", None),
            P("section", "dp", None),
            P("section", "dp", None),
            P("section", "dp", None),
            P("section", "dp", None),
            P("section", None, "dp"),
            P("section", "dp"),
            P(),
            P(),
            P(),
            P(None, "section"),
            P("section"),
        ),
        out_specs=(
            P("section", "dp", None),
            P("section", "dp", None),
            P("section", "dp", None),
            P("section", "dp", None),
            P("section", "dp", None),
            P("section", "dp", None),
            P("section", None, "dp"),
            P("section", "dp"),
            P(),
            P(),
            P(),
            P(None, "section"),
            P("section"),
        ),
        check_vma=False,
    )
```
